32 devices in a mesh: dp: 4 (over y, core), expert: 2 (over x), tensor: 4 (over z).
Axes of the slice: x: 2, y: 2, z: 4, core: 2. Of those that a mesh axis runs over, the one named last changes fastest.
Arguments:
- tokens: bfloat16 [1024, 2048], P(('dp', 'expert')), may hold values from -6 to 6
- cotangent: bfloat16 [1024, 2048], P(('dp', 'expert')), may hold values from -6 to 6
- expert_ids: int32 [1024, 1], P(('dp', 'expert')), may hold values from 0 to 31; in each aligned block of 128 rows (0 to 127, 128 to 255, ...) at most 8 rows name the same one
- gate_weight: bfloat16 [32, 2048, 1408], P('expert', 'dp', 'tensor'), may hold values from -0.125 to 0.125
- up_weight: bfloat16 [32, 2048, 1408], P('expert', 'dp', 'tensor'), may hold values from -0.125 to 0.125
- down_weight: bfloat16 [32, 2048, 1408], P('expert', 'dp', 'tensor'), may hold values from -0.15625 to 0.15625
Outputs:
- grad_tokens: bfloat16 [1024, 2048], P(('dp', 'expert'), 'tensor')
- grad_gate: bfloat16 [32, 2048, 1408], P('expert', 'dp', 'tensor')
- grad_up: bfloat16 [32, 2048, 1408], P('expert', 'dp', 'tensor')
The draws below stay inside these ranges and needn't reach their ends.
Inputs may be any that keep to these rules, and one draw needn't show every extreme that they name: `expert_ids`: among the 128 tokens of one block no expert id occurs more than 8 times, and in every draw some block holds some id exactly 8 times.
All inputs are finite; a program needn't handle non-finite values.
Results may differ from the reference program's by a relative error of at most 0.013.
Values may be sent and summed in bfloat16 or wider, within the bound.
No kernel may reach another device: no remote copies, remote signals or barrier semaphores. Data moves between devices by JAX's collectives and lax.ppermute only.
A program may use at most 192 MiB of HBM per device.

```python
import math
import jax
import jax.numpy as jnp
import numpy as np
from jax import lax

D = 2048
FF = 1408
EXPERTS = 32
TOK_DEV = 128
CAP = 8
TOKENS = 1024
N_DP = 4
N_EXPERT = 2
N_TENSOR = 4


def steps_of(key, extent, split, smallest, top_value):
    loudness, own = 1.0, jax.random.fold_in(key, 6)
    for axis_at, blocks in split:
        heights = jnp.exp(jax.random.uniform(jax.random.fold_in(own, axis_at), (blocks,), jnp.float32, smallest / len(split), top_value / len(split)))
        loudness = loudness * jnp.repeat(heights, extent[axis_at] // blocks).reshape([-1 if axis == axis_at else 1 for axis in range(len(extent))])
    return loudness


def assign_block(key, own, number, rows, count, top, most, skew):
    order = jax.random.permutation(key, count)
    heavy_load, usual = portions_of(count, rows * top, most, skew, True), portions_of(count, rows * top, most, skew, False)
    places = jnp.arange(count)

    def named(sizes, rotation):
        used = int((sizes > 0).sum())
        fixed = max(1, used // 4)
        passed = fixed + (places - fixed + rotation * (used - fixed)) % max(1, count - fixed)
        return jnp.zeros((count,), jnp.int32).at[order[jnp.where(places < fixed, places, passed)]].set(jnp.asarray(sizes, jnp.int32))

    sizes = jnp.where(number % 4 == 0, named(heavy_load, number // 4), named(usual, number - number // 4 - 1))
    mixed = jax.random.permutation(jax.random.fold_in(own, 3), count)
    source_of, receiver = mixed[0:count // 2 * 2:2], mixed[1:count // 2 * 2:2]
    margin = jnp.minimum(sizes[source_of] - 1, most - sizes[receiver]) // 2
    margin = jnp.where((source_of == order[0]) | (receiver == order[0]) | (sizes[receiver] == 0), 0, jnp.maximum(margin, 0))
    passed = jax.random.randint(jax.random.fold_in(own, 4), (count // 2,), 0, 1 << 20) % (margin + 1)
    sizes = sizes.at[source_of].add(-passed).at[receiver].add(passed)
    members = jnp.searchsorted(jnp.cumsum(sizes), jnp.arange(rows * top), side="right").astype(jnp.int32)
    grid = members.reshape(top, rows).T
    grid = grid[jax.random.permutation(jax.random.fold_in(own, 1), rows)]
    rotation = jax.random.randint(jax.random.fold_in(own, 2), (rows, 1), 0, top)
    return jnp.take_along_axis(grid, (jnp.arange(top)[None, :] + rotation) % top, axis=1)


def portions_of(amount, total, bound, slope, full):
    weights = [(1 << 20) // math.isqrt(standing ** slope) + 1 for standing in range(1, amount + 1)]
    largest = bound if full else min(bound, max(-(-total // amount), total * weights[0] // sum(weights)))
    least = 1 if total - largest >= amount - 1 else 0
    counts, rest = [largest] + [least] * (amount - 1), total - largest - least * (amount - 1)
    while rest > 0:
        movable = [i for i in range(1, amount) if counts[i] < largest] or [i for i in range(1, amount) if counts[i] < bound]
        whole, budget = sum([weights[i] for i in movable]), rest
        for i in movable:
            addition = min(bound - counts[i], max(1, budget * weights[i] // whole), rest)
            counts[i] = counts[i] + addition
            rest = rest - addition
    return np.array(counts)


def centred(own_key, dims, scale, bound, cuts=(), kind=jnp.bfloat16):
    gain = steps_of(own_key, dims, cuts, -0.22, 0.18) if cuts else 1.0
    drawn = jax.random.normal(own_key, dims, jnp.float32) * scale * gain
    return jnp.minimum(jnp.maximum(drawn, -bound), bound).astype(kind)


def setup_inputs(seed: int = 0) -> dict:
    key_of = jax.random.split(jax.random.key(seed), 7)
    tokens = centred(key_of[0], (TOKENS, D), 1.0, 6.0, ((0, 8),))
    cotangent = centred(key_of[1], (TOKENS, D), 1.0, 6.0, ((0, 8),))
    expert_ids_keys = jax.random.split(jax.random.fold_in(key_of[2], 1), TOKENS // TOK_DEV)
    expert_ids_turns = jax.random.permutation(jax.random.fold_in(key_of[2], 3), TOKENS // TOK_DEV)
    expert_ids = jax.vmap(lambda own, number: assign_block(jax.random.fold_in(key_of[2], 2), own, number, TOK_DEV, EXPERTS, 1, CAP, 2))(expert_ids_keys, expert_ids_turns).reshape((TOKENS, 1))
    gate_weight = centred(key_of[3], (EXPERTS, D, FF), D ** -0.5, 0.125, ((0, 2), (1, 4), (2, 4)))
    up_weight = centred(key_of[4], (EXPERTS, D, FF), D ** -0.5, 0.125, ((0, 2), (1, 4), (2, 4)))
    down_weight = centred(key_of[5], (EXPERTS, D, FF), FF ** -0.5, 0.15625, ((0, 2), (1, 4), (2, 4)))
    return {"tokens": tokens, "cotangent": cotangent, "expert_ids": expert_ids, "gate_weight": gate_weight, "up_weight": up_weight, "down_weight": down_weight}


def reference(tokens, cotangent, expert_ids, gate_weight, up_weight, down_weight):
    block_count = N_DP * N_EXPERT
    chosen = expert_ids[:, 0].reshape(block_count, TOK_DEV)
    columns = jnp.arange(EXPERTS, dtype=jnp.int32)
    onehot = (chosen[:, :, None] == columns[None, None, :]).astype(jnp.int32)
    earlier = jnp.cumsum(onehot, axis=1) - onehot
    position = jnp.sum(earlier * onehot, axis=2).astype(jnp.int32)
    block_index = jnp.arange(block_count, dtype=jnp.int32)[:, None]
    group_index = block_index // N_EXPERT
    source = block_index % N_EXPERT
    flat_rows = ((chosen * N_DP + group_index) * N_EXPERT + source) * CAP + position
    slot_table = jnp.full((EXPERTS * N_DP * N_EXPERT * CAP,), TOKENS, jnp.int32)
    slot_table = slot_table.at[flat_rows.reshape(-1).astype(jnp.int32)].set(jnp.arange(TOKENS, dtype=jnp.int32))
    slot_index = slot_table.reshape(EXPERTS, N_DP * N_EXPERT * CAP)
    zero_row = jnp.zeros((1, D), jnp.bfloat16)
    tokens_padded = jnp.concatenate([tokens, zero_row.astype(tokens.dtype)], 0)
    cotangent_padded = jnp.concatenate([cotangent, zero_row.astype(cotangent.dtype)], 0)
    shard_width = FF // N_TENSOR
    group_rows = N_EXPERT * CAP

    def one_expert(operands):
        row_index, gate_mat, up_mat, down_mat = operands
        slot_tokens = tokens_padded[row_index]
        slot_cotangent = cotangent_padded[row_index]
        gate_act = jnp.dot(slot_tokens, gate_mat, preferred_element_type=jnp.float32)
        up_act = jnp.dot(slot_tokens, up_mat, preferred_element_type=jnp.float32)
        hidden_grad = jnp.dot(slot_cotangent, down_mat, preferred_element_type=jnp.float32)
        sigmoid_gate = jax.nn.sigmoid(gate_act)
        up_grad = (hidden_grad * gate_act * sigmoid_gate).astype(jnp.bfloat16)
        gate_grad = (hidden_grad * up_act * sigmoid_gate * (1.0 + gate_act * (1.0 - sigmoid_gate))).astype(jnp.bfloat16)
        summed = jnp.zeros((slot_tokens.shape[0], D), jnp.float32)
        for shard in range(N_TENSOR):
            start = shard * shard_width
            shard_term = jnp.dot(gate_grad[:, start:start + shard_width], gate_mat[:, start:start + shard_width].T, preferred_element_type=jnp.float32)
            shard_term = shard_term + jnp.dot(up_grad[:, start:start + shard_width], up_mat[:, start:start + shard_width].T, preferred_element_type=jnp.float32)
            rounded = lax.optimization_barrier(shard_term.astype(jnp.bfloat16))
            summed = summed + rounded.astype(jnp.float32)
        token_rows = summed.astype(jnp.bfloat16)
        grouped_tokens = slot_tokens.reshape(N_DP, group_rows, D).astype(jnp.float32)
        grouped_gate = gate_grad.reshape(N_DP, group_rows, FF).astype(jnp.float32)
        grouped_up = up_grad.reshape(N_DP, group_rows, FF).astype(jnp.float32)
        gate_terms = jnp.einsum("gsd,gsf->gdf", grouped_tokens, grouped_gate)
        up_terms = jnp.einsum("gsd,gsf->gdf", grouped_tokens, grouped_up)
        gate_terms = lax.optimization_barrier(gate_terms.astype(jnp.bfloat16))
        up_terms = lax.optimization_barrier(up_terms.astype(jnp.bfloat16))
        gate_total = jnp.sum(gate_terms.astype(jnp.float32), axis=0).astype(jnp.bfloat16)
        up_total = jnp.sum(up_terms.astype(jnp.float32), axis=0).astype(jnp.bfloat16)
        return token_rows, gate_total, up_total

    token_rows, grad_gate, grad_up = lax.map(one_expert, (slot_index, gate_weight, up_weight, down_weight))
    grad_tokens = jnp.zeros((TOKENS + 1, D), token_rows.dtype)
    grad_tokens = grad_tokens.at[slot_index.reshape(-1)].set(token_rows.reshape(-1, D))
    return grad_tokens[:TOKENS], grad_gate, grad_up
```

```python
import jax
import jax.numpy as jnp
from jax import lax
from jax.sharding import PartitionSpec as P

CAP = 8


def swap(value, axis, count, bit):
    return lax.ppermute(value, axis, [(i, i ^ bit) for i in range(count)])


def bits_of(count):
    bits = []
    bit = 1
    while bit < count:
        bits.append(bit)
        bit *= 2
    return bits


def halving_sum(parts, axis, count, last=None):
    parts = dict(parts)
    for bit in bits_of(count):
        leaving = sorted(r for r in parts if r & bit)
        arrived = swap(jnp.stack([parts[r].astype(jnp.bfloat16) for r in leaving]), axis, count, bit)
        for at, r in enumerate(leaving):
            parts[r ^ bit] = parts[r ^ bit].astype(jnp.float32) + arrived[at].astype(jnp.float32)
            del parts[r]
    return parts[0]


def doubling_gather(value, axis, count):
    held = {0: value}
    for bit in reversed(bits_of(count)):
        known = sorted(held)
        arrived = swap(jnp.stack([held[r] for r in known]), axis, count, bit)
        for at, r in enumerate(known):
            held[r ^ bit] = arrived[at]
    return [held[r] for r in range(count)]


def on_device(tokens, cotangent, expert_ids, gate_weight, up_weight, down_weight):
    n_dp, n_x, n_t = lax.axis_size("dp"), lax.axis_size("expert"), lax.axis_size("tensor")
    k, x, t = lax.axis_index("dp"), lax.axis_index("expert"), lax.axis_index("tensor")
    local_experts, width, hidden = gate_weight.shape
    rows = tokens.shape[0]
    slots = n_x * CAP

    ids_row = expert_ids.reshape(1, rows)
    order = jnp.arange(rows, dtype=jnp.int32)
    earlier = (expert_ids == ids_row) & (order[:, None] < order[None, :])
    position = jnp.sum(earlier.astype(jnp.int32), axis=0)
    target = ids_row[0] * CAP + position
    targets = lax.all_gather(target, ("dp", "expert"), axis=0, tiled=False).reshape(n_dp, n_x, rows)

    pair = jnp.stack([tokens, cotangent])
    placers, slot_rows = [], []
    for rel in range(n_dp):
        columns = lax.dynamic_slice_in_dim(pair, (k ^ rel) * width, width, axis=2)
        mine = columns if rel == 0 else swap(columns, "dp", n_dp, rel)
        if n_x == 2:
            blocks = jnp.concatenate([mine, swap(mine, "expert", n_x, 1)], axis=1)
            sources = jnp.stack([x, x ^ 1])
        else:
            blocks = lax.all_gather(mine, "expert", axis=1, tiled=True)
            sources = jnp.arange(n_x, dtype=jnp.int32)
        goal = lax.dynamic_index_in_dim(targets, k ^ rel, axis=0, keepdims=False)[sources]
        expert = goal // CAP - x * local_experts
        place = jnp.arange(n_x, dtype=jnp.int32)[:, None] * CAP + goal % CAP
        row = jnp.where((expert >= 0) & (expert < local_experts), expert * slots + place, -1)
        row = row.reshape(1, n_x * rows)
        every = jnp.arange(local_experts * slots, dtype=jnp.int32)[:, None]
        placer = (every == row).astype(jnp.bfloat16)
        placers.append(placer)
        slot_rows.append(
            jnp.einsum("sn,and->asd", placer, blocks, preferred_element_type=jnp.float32)
            .astype(jnp.bfloat16)
            .reshape(2, local_experts, slots, width)
        )
    slot_rows = jnp.concatenate(slot_rows, axis=2)
    inputs, grads_in = slot_rows[0], slot_rows[1]

    def project(values, weight):
        return jnp.einsum("esd,edf->esf", values, weight, preferred_element_type=jnp.float32).astype(jnp.bfloat16)

    acts = jnp.stack([project(inputs, gate_weight), project(inputs, up_weight), project(grads_in, down_weight)])
    acts = acts.reshape(3, local_experts, n_dp, slots, hidden)
    gate_act, up_act, hidden_grad = halving_sum({r: acts[:, :, r] for r in range(n_dp)}, "dp", n_dp)
    sigmoid_gate = jax.nn.sigmoid(gate_act)
    up_grad = (hidden_grad * gate_act * sigmoid_gate).astype(jnp.bfloat16)
    gate_grad = (
        hidden_grad * up_act * sigmoid_gate * (1.0 + gate_act * (1.0 - sigmoid_gate))
    ).astype(jnp.bfloat16)
    grads = doubling_gather(jnp.stack([gate_grad, up_grad]), "dp", n_dp)
    grads = jnp.concatenate(grads, axis=2)
    gate_grad, up_grad = grads[0], grads[1]

    partial_value = jnp.einsum("esf,edf->esd", gate_grad, gate_weight, preferred_element_type=jnp.float32)
    partial_value = partial_value + jnp.einsum("esf,edf->esd", up_grad, up_weight, preferred_element_type=jnp.float32)
    partial_value = partial_value.astype(jnp.bfloat16).reshape(local_experts, n_dp, slots, width)
    per_token = []
    for rel in range(n_dp):
        flat = partial_value[:, rel].reshape(local_experts * slots, width)
        back = lax.dot_general(
            placers[rel], flat, (((0,), (0,)), ((), ())), preferred_element_type=jnp.float32
        ).astype(jnp.bfloat16).reshape(n_x, rows, width)
        if n_x == 2:
            back = back[0] + swap(back[1], "expert", n_x, 1)
        else:
            back = lax.psum_scatter(back, "expert", scatter_dimension=0, tiled=False)
        per_token.append(back)
    per_token = jnp.stack(per_token)
    terms = {r: lax.dynamic_index_in_dim(per_token, k ^ t ^ r, axis=0, keepdims=False) for r in range(n_t)}
    summed = halving_sum(terms, "tensor", n_t).astype(jnp.bfloat16)
    summed = lax.ppermute(
        summed, ("dp", "tensor"), [(i * n_t + j, j * n_t + i) for i in range(n_dp) for j in range(n_t)]
    )

    grad_gate = jnp.einsum("esd,esf->edf", inputs, gate_grad, preferred_element_type=jnp.float32).astype(jnp.bfloat16)
    grad_up = jnp.einsum("esd,esf->edf", inputs, up_grad, preferred_element_type=jnp.float32).astype(jnp.bfloat16)
    return summed, grad_gate, grad_up


def solution(mesh):
    placed = (
        P(("dp", "expert"), None),
        P(("dp", "expert"), None),
        P(("dp", "expert"), None),
        P("expert", "dp", "tensor"),
        P("expert", "dp", "tensor"),
        P("expert", "dp", "tensor"),
    )
    return jax.shard_map(
        on_device,
        mesh=mesh,
        in_specs=placed,
        out_specs=(
            P(("dp", "expert"), "tensor"),
            P("expert", "dp", "tensor"),
            P("expert", "dp", "tensor"),
        ),
        check_vma=False,
    )
```

```python
import functools

import jax
import jax.numpy as jnp
from jax import lax
from jax.experimental import pallas as pl
from jax.experimental.pallas import tpu as pltpu
from jax.sharding import PartitionSpec as P

CAP = 8
META = 16
F32 = jnp.float32
BF16 = jnp.bfloat16
VMEM_LIMIT = 48 * 1024 * 1024


def swap(value, axis, count, bit):
    return lax.ppermute(value, axis, [(i, i ^ bit) for i in range(count)])


def whole_spec(shape):
    return pl.BlockSpec(shape, lambda *_: (0,) * len(shape))


def params():
    return pltpu.CompilerParams(vmem_limit_bytes=VMEM_LIMIT)


def split_kernel(width, n_dp, where, ids, rows_ref, *outs):
    k, x = where[0], where[1]
    rows = rows_ref.shape[0]
    for rel in range(n_dp):
        start = pl.multiple_of((k ^ rel) * width, 128)
        outs[rel][0:rows, :] = rows_ref[:, pl.ds(start, width)]
    if outs[0].shape[0] == rows:
        return
    column = ids[...]
    line = lax.broadcasted_iota(jnp.int32, (rows, rows), 0)
    lane = lax.broadcasted_iota(jnp.int32, (rows, rows), 1)
    named = jnp.broadcast_to(column, (rows, rows)).astype(F32)
    along = jnp.sum(jnp.where(line == lane, named, 0.0), axis=0, keepdims=True)
    earlier = jnp.where((named == along) & (line < lane), 1.0, 0.0)
    place = jnp.sum(earlier, axis=0, keepdims=True) + (x * CAP).astype(F32)
    at = lax.broadcasted_iota(jnp.int32, (META, rows), 0)
    meta = jnp.where(at == 0, along, jnp.where(at == 1, place, 0.0)).astype(BF16)
    for rel in range(n_dp):
        outs[rel][rows:, :] = jnp.zeros((META, width), BF16)
        outs[rel][rows:, 0:rows] = meta


def split(where, ids, values, width, n_dp, with_meta):
    rows = values.shape[0]
    tall = rows + META if with_meta else rows
    return pl.pallas_call(
        functools.partial(split_kernel, width, n_dp),
        out_shape=[jax.ShapeDtypeStruct((tall, width), BF16)] * n_dp,
        in_specs=[
            pl.BlockSpec(memory_space=pltpu.SMEM),
            whole_spec(ids.shape),
            whole_spec(values.shape),
        ],
        out_specs=[whole_spec((tall, width))] * n_dp,
        compiler_params=params(),
    )(where, ids, values)


def placer_of(row, slot_count):
    every = lax.broadcasted_iota(jnp.int32, (slot_count, row.shape[1]), 0)
    return (every == row).astype(F32).astype(BF16)


def project_kernel(n_dp, weights, first, where, *refs):
    blocks, refs = refs[: 2 * n_dp], refs[2 * n_dp :]
    if not first:
        lines, refs = refs[0], refs[1:]
    weight_refs, refs = refs[:weights], refs[weights:]
    if first:
        keep, send, placed, lines = refs
    else:
        keep, send, placed = refs
    step = pl.program_id(0)
    per_step = weight_refs[0].shape[0]
    local_experts, slot_rows, width = placed.shape
    slots = slot_rows // n_dp
    rows = blocks[0].shape[0] - (META if first else 0)

    @pl.when(step == 0)
    def _():
        for rel in range(n_dp):
            pair = blocks[2 * rel], blocks[2 * rel + 1]
            if first:
                metas = [b[rows:, 0:rows].astype(F32) for b in pair]
                ids = jnp.concatenate([m[0:1] for m in metas], axis=1)
                place = jnp.concatenate([m[1:2] for m in metas], axis=1)
                low = (where[1] * local_experts).astype(F32)
                row = ((ids - low) * slots + place).astype(jnp.int32)
                lines[rel] = jnp.broadcast_to(row, (8, row.shape[1]))
            else:
                row = lines[rel][0:1]
            placer = placer_of(row, local_experts * slots)
            values = jnp.concatenate([b[0:rows, :] for b in pair], axis=0)
            found = jnp.dot(placer, values, preferred_element_type=F32).astype(BF16)
            placed[:, rel * slots : (rel + 1) * slots, :] = found.reshape(local_experts, slots, width)

    for i in range(per_step):
        mine = placed[step * per_step + i]
        for w in range(weights):
            act = jnp.dot(mine, weight_refs[w][i], preferred_element_type=F32).astype(BF16)
            for rel in range(n_dp):
                out = send if rel & 1 else keep
                out[w, rel // 2, i] = act[rel * slots : (rel + 1) * slots]


def project(where, blocks, lines, weights, n_dp, per_step):
    first = lines is None
    local_experts, width, hidden = weights[0].shape
    slots = 2 * CAP
    rows = blocks[0].shape[0] - (META if first else 0)
    count = len(weights)
    act = (count, n_dp // 2, local_experts, slots, hidden)
    act_block = (count, n_dp // 2, per_step, slots, hidden)
    act_spec = pl.BlockSpec(act_block, lambda e: (0, 0, e, 0, 0))
    placed = (local_experts, n_dp * slots, width)
    line = (n_dp, 8, 2 * rows)
    weight_spec = pl.BlockSpec((per_step, width, hidden), lambda e: (e, 0, 0))
    out_shape = [jax.ShapeDtypeStruct(act, BF16), jax.ShapeDtypeStruct(act, BF16)]
    out_specs = [act_spec, act_spec]
    scratch = []
    operands = [where, *blocks]
    in_specs = [pl.BlockSpec(memory_space=pltpu.SMEM)] + [whole_spec(b.shape) for b in blocks]
    if first:
        out_shape += [jax.ShapeDtypeStruct(placed, BF16), jax.ShapeDtypeStruct(line, jnp.int32)]
        out_specs += [whole_spec(placed), whole_spec(line)]
    else:
        operands.append(lines)
        in_specs.append(whole_spec(line))
        scratch.append(pltpu.VMEM(placed, BF16))
    flops = 2 * count * local_experts * n_dp * slots * width * hidden
    return pl.pallas_call(
        functools.partial(project_kernel, n_dp, count, first),
        grid=(local_experts // per_step,),
        out_shape=out_shape,
        in_specs=in_specs + [weight_spec] * count,
        out_specs=out_specs,
        scratch_shapes=scratch,
        compiler_params=params(),
        cost_estimate=pl.CostEstimate(
            flops=4 * flops, bytes_accessed=count * local_experts * width * hidden * 2, transcendentals=0
        ),
    )(*operands, *weights)


def back_kernel(n_dp, where, lines, h0, h1, h2, h3, gate, up, keep_x, send_x, keep_z, send_z, held):
    step = pl.program_id(0)
    held_hidden = (h0, h1, h2, h3)
    per_step = gate.shape[0]
    slots = h0.shape[2]
    for i in range(per_step):
        gate_grad = jnp.concatenate([h[0, i] for h in held_hidden], axis=0)
        up_grad = jnp.concatenate([h[1, i] for h in held_hidden], axis=0)
        dims = (((1,), (1,)), ((), ()))
        value = lax.dot_general(gate_grad, gate[i], dims, preferred_element_type=F32)
        value = value + lax.dot_general(up_grad, up[i], dims, preferred_element_type=F32)
        value = value.astype(BF16)
        start = pl.multiple_of((step * per_step + i) * slots, 16)
        for rel in range(n_dp):
            held[rel, pl.ds(start, slots), :] = value[rel * slots : (rel + 1) * slots]

    @pl.when(step == pl.num_programs(0) - 1)
    def _():
        rows, half = keep_x.shape[1], keep_x.shape[2]
        for r in range(n_dp):
            rel = where[2] ^ r
            placer = placer_of(lines[rel][0:1], held.shape[1])
            token_rows = lax.dot_general(
                placer, held[rel], (((0,), (0,)), ((), ())), preferred_element_type=F32
            ).astype(BF16)
            keep_x[r] = token_rows[0:rows, 0:half]
            send_x[r] = token_rows[rows:, 0:half]
            out = send_z if r & 1 else keep_z
            out[0, r // 2] = token_rows[0:rows, half:]
            out[1, r // 2] = token_rows[rows:, half:]


def back(where, lines, parts, gate, up, rows, per_step):
    n_dp = len(parts)
    local_experts, width, hidden = gate.shape
    slots = parts[0].shape[2]
    part_spec = pl.BlockSpec((2, per_step, slots, hidden), lambda e: (0, e, 0, 0))
    weight_spec = pl.BlockSpec((per_step, width, hidden), lambda e: (e, 0, 0))
    shape_x = (n_dp, rows, width // 2)
    shape_z = (2, n_dp // 2, rows, width // 2)
    flops = 4 * local_experts * n_dp * slots * width * hidden
    return pl.pallas_call(
        functools.partial(back_kernel, n_dp),
        grid=(local_experts // per_step,),
        out_shape=[jax.ShapeDtypeStruct(s, BF16) for s in (shape_x, shape_x, shape_z, shape_z)],
        in_specs=[pl.BlockSpec(memory_space=pltpu.SMEM), whole_spec(lines.shape)]
        + [part_spec] * n_dp
        + [weight_spec] * 2,
        out_specs=[whole_spec(s) for s in (shape_x, shape_x, shape_z, shape_z)],
        scratch_shapes=[pltpu.VMEM((n_dp, local_experts * slots, width), BF16)],
        compiler_params=params(),
        cost_estimate=pl.CostEstimate(
            flops=4 * flops, bytes_accessed=2 * local_experts * width * hidden * 2, transcendentals=0
        ),
    )(where, lines, *parts, gate, up)


def weight_kernel(which, placed, h0, h1, h2, h3, out):
    for i in range(out.shape[0]):
        grad = jnp.concatenate([h[which, i] for h in (h0, h1, h2, h3)], axis=0)
        out[i] = lax.dot_general(
            placed[i], grad, (((0,), (0,)), ((), ())), preferred_element_type=F32
        ).astype(BF16)


def weight_grad(which, placed, parts, per_step):
    local_experts, slot_rows, width = placed.shape
    _, _, slots, hidden = parts[0].shape
    part_spec = pl.BlockSpec((2, per_step, slots, hidden), lambda e: (0, e, 0, 0))
    flops = 2 * local_experts * slot_rows * width * hidden
    return pl.pallas_call(
        functools.partial(weight_kernel, which),
        grid=(local_experts // per_step,),
        out_shape=jax.ShapeDtypeStruct((local_experts, width, hidden), BF16),
        in_specs=[pl.BlockSpec((per_step, slot_rows, width), lambda e: (e, 0, 0))] + [part_spec] * len(parts),
        out_specs=pl.BlockSpec((per_step, width, hidden), lambda e: (e, 0, 0)),
        compiler_params=params(),
        cost_estimate=pl.CostEstimate(
            flops=4 * flops, bytes_accessed=local_experts * width * hidden * 2, transcendentals=0
        ),
    )(placed, *parts)


def plus(first, second):
    return first.astype(F32) + second.astype(F32)


def swiglu_grads(gate_act, up_act, hidden_grad):
    sigmoid_gate = jax.nn.sigmoid(gate_act)
    up_grad = (hidden_grad * gate_act * sigmoid_gate).astype(BF16)
    gate_grad = (
        hidden_grad * up_act * sigmoid_gate * (1.0 + gate_act * (1.0 - sigmoid_gate))
    ).astype(BF16)
    return gate_grad, up_grad


def on_small_slice(tokens, cotangent, expert_ids, gate_weight, up_weight, down_weight):
    n_dp, n_x, n_t = 4, 2, 4
    k, x, t = lax.axis_index("dp"), lax.axis_index("expert"), lax.axis_index("tensor")
    width = gate_weight.shape[1]
    rows = tokens.shape[0]
    half = width // 2
    where = jnp.stack([k, x, k ^ t]).astype(jnp.int32)

    def collect(values, with_meta):
        chunks = split(where, expert_ids, values, width, n_dp, with_meta)
        blocks = []
        for rel in range(n_dp):
            mine = chunks[0] if rel == 0 else swap(chunks[rel], "dp", n_dp, rel)
            blocks += [mine, swap(mine, "expert", n_x, 1)]
        return blocks

    token_blocks = collect(tokens, True)
    grad_blocks = collect(cotangent, False)
    keep, send, placed, lines = project(where, token_blocks, None, [gate_weight, up_weight], n_dp, 2)

    def over_dp(keep, send):
        arrived = swap(send, "dp", n_dp, 1)
        near = plus(keep[:, 0], arrived[:, 0])
        far = plus(keep[:, 1], arrived[:, 1]).astype(BF16)
        return near + swap(far, "dp", n_dp, 2).astype(F32)

    acts = over_dp(keep, send)
    keep, send = project(where, grad_blocks, lines, [down_weight], n_dp, 2)
    hidden_grad = over_dp(keep, send)[0]
    part = jnp.stack(swiglu_grads(acts[0], acts[1], hidden_grad))
    far = swap(part, "dp", n_dp, 2)
    parts = [part, swap(part, "dp", n_dp, 1), far, swap(far, "dp", n_dp, 1)]

    keep_x, send_x, keep_z, send_z = back(where, lines, parts, gate_weight, up_weight, rows, 2)
    sum_x = plus(keep_x, swap(send_x, "expert", n_x, 1))
    sum_z = plus(keep_z, swap(send_z, "tensor", n_t, 1))
    from_z = swap(jnp.stack([sum_x[1], sum_x[3]]).astype(BF16), "tensor", n_t, 1)
    from_x = swap(sum_z[1].astype(BF16), "expert", n_x, 1)
    near = jnp.concatenate([plus(sum_x[0], from_z[0]), plus(sum_z[0, 0], from_x[0])], axis=1).astype(BF16)
    far = jnp.concatenate([plus(sum_x[2], from_z[1]), plus(sum_z[0, 1], from_x[1])], axis=1).astype(BF16)
    pairs = [(i, j) for i in range(n_dp) for j in range(n_t)]
    near = lax.ppermute(near, ("dp", "tensor"), [(i * n_t + j, j * n_t + i) for i, j in pairs])
    far = lax.ppermute(far, ("dp", "tensor"), [(i * n_t + j, (j ^ 2) * n_t + i) for i, j in pairs])
    grad_tokens = plus(near, far).astype(BF16)

    grad_gate = weight_grad(0, placed, parts, 2)
    grad_up = weight_grad(1, placed, parts, 2)
    return grad_tokens, grad_gate, grad_up


def bits_of(count):
    bits = []
    bit = 1
    while bit < count:
        bits.append(bit)
        bit *= 2
    return bits


def halving_sum(parts, axis, count):
    parts = dict(parts)
    for bit in bits_of(count):
        leaving = sorted(r for r in parts if r & bit)
        arrived = swap(jnp.stack([parts[r].astype(BF16) for r in leaving]), axis, count, bit)
        for at, r in enumerate(leaving):
            parts[r ^ bit] = plus(parts[r ^ bit], arrived[at])
            del parts[r]
    return parts[0]


def doubling_gather(value, axis, count):
    held = {0: value}
    for bit in reversed(bits_of(count)):
        known = sorted(held)
        arrived = swap(jnp.stack([held[r] for r in known]), axis, count, bit)
        for at, r in enumerate(known):
            held[r ^ bit] = arrived[at]
    return [held[r] for r in range(count)]


def on_any_slice(tokens, cotangent, expert_ids, gate_weight, up_weight, down_weight):
    n_dp, n_x, n_t = lax.axis_size("dp"), lax.axis_size("expert"), lax.axis_size("tensor")
    k, x, t = lax.axis_index("dp"), lax.axis_index("expert"), lax.axis_index("tensor")
    local_experts, width, hidden = gate_weight.shape
    rows = tokens.shape[0]
    slots = n_x * CAP
    ids_row = expert_ids.reshape(1, rows)
    order = jnp.arange(rows, dtype=jnp.int32)
    earlier = (expert_ids == ids_row) & (order[:, None] < order[None, :])
    position = jnp.sum(earlier.astype(jnp.int32), axis=0)
    target = ids_row[0] * CAP + position
    targets = lax.all_gather(target, ("dp", "expert"), axis=0, tiled=False).reshape(n_dp, n_x, rows)
    pair = jnp.stack([tokens, cotangent])
    placers, slot_rows = [], []
    for rel in range(n_dp):
        columns = lax.dynamic_slice_in_dim(pair, (k ^ rel) * width, width, axis=2)
        mine = columns if rel == 0 else swap(columns, "dp", n_dp, rel)
        blocks = lax.all_gather(mine, "expert", axis=1, tiled=True)
        goal = lax.dynamic_index_in_dim(targets, k ^ rel, axis=0, keepdims=False)
        expert = goal // CAP - x * local_experts
        place = jnp.arange(n_x, dtype=jnp.int32)[:, None] * CAP + goal % CAP
        row = jnp.where((expert >= 0) & (expert < local_experts), expert * slots + place, -1)
        row = row.reshape(1, n_x * rows)
        every = jnp.arange(local_experts * slots, dtype=jnp.int32)[:, None]
        placer = (every == row).astype(BF16)
        placers.append(placer)
        slot_rows.append(
            jnp.einsum("sn,and->asd", placer, blocks, preferred_element_type=F32)
            .astype(BF16)
            .reshape(2, local_experts, slots, width)
        )
    slot_rows = jnp.concatenate(slot_rows, axis=2)
    inputs, grads_in = slot_rows[0], slot_rows[1]

    def act(values, weight):
        return jnp.einsum("esd,edf->esf", values, weight, preferred_element_type=F32).astype(BF16)

    acts = jnp.stack([act(inputs, gate_weight), act(inputs, up_weight), act(grads_in, down_weight)])
    acts = acts.reshape(3, local_experts, n_dp, slots, hidden)
    acts = halving_sum({r: acts[:, :, r] for r in range(n_dp)}, "dp", n_dp)
    grads = doubling_gather(jnp.stack(swiglu_grads(acts[0], acts[1], acts[2])), "dp", n_dp)
    grads = jnp.concatenate(grads, axis=2)
    gate_grad, up_grad = grads[0], grads[1]
    partial_value = jnp.einsum("esf,edf->esd", gate_grad, gate_weight, preferred_element_type=F32)
    partial_value = partial_value + jnp.einsum("esf,edf->esd", up_grad, up_weight, preferred_element_type=F32)
    partial_value = partial_value.astype(BF16).reshape(local_experts, n_dp, slots, width)
    per_token = []
    for rel in range(n_dp):
        flat = partial_value[:, rel].reshape(local_experts * slots, width)
        spread = lax.dot_general(placers[rel], flat, (((0,), (0,)), ((), ())), preferred_element_type=F32)
        spread = spread.astype(BF16).reshape(n_x, rows, width)
        per_token.append(lax.psum_scatter(spread, "expert", scatter_dimension=0, tiled=False))
    per_token = jnp.stack(per_token)
    terms = {r: lax.dynamic_index_in_dim(per_token, k ^ t ^ r, axis=0, keepdims=False) for r in range(n_t)}
    summed = halving_sum(terms, "tensor", n_t).astype(BF16)
    summed = lax.ppermute(
        summed, ("dp", "tensor"), [(i * n_t + j, j * n_t + i) for i in range(n_dp) for j in range(n_t)]
    )
    grad_gate = jnp.einsum("esd,esf->edf", inputs, gate_grad, preferred_element_type=F32).astype(BF16)
    grad_up = jnp.einsum("esd,esf->edf", inputs, up_grad, preferred_element_type=F32).astype(BF16)
    return summed, grad_gate, grad_up


def solution(mesh):
    placed = (
        P(("dp", "expert"), None),
        P(("dp", "expert"), None),
        P(("dp", "expert"), None),
        P("expert", "dp", "tensor"),
        P("expert", "dp", "tensor"),
        P("expert", "dp", "tensor"),
    )
    sizes = tuple(mesh.shape[name] for name in ("dp", "expert", "tensor"))
    return jax.shard_map(
        on_small_slice if sizes == (4, 2, 4) else on_any_slice,
        mesh=mesh,
        in_specs=placed,
        out_specs=(
            P(("dp", "expert"), "tensor"),
            P("expert", "dp", "tensor"),
            P("expert", "dp", "tensor"),
        ),
        check_vma=False,
    )
```

```python
import functools

import jax
import jax.numpy as jnp
from jax import lax
from jax.experimental import pallas as pl
from jax.experimental.pallas import tpu as pltpu
from jax.sharding import PartitionSpec as P

CAP = 8
META = 16
F32 = jnp.float32
BF16 = jnp.bfloat16
VMEM_LIMIT = 48 * 1024 * 1024


def swap(value, axis, count, bit):
    return lax.ppermute(value, axis, [(i, i ^ bit) for i in range(count)])


def whole_spec(shape):
    return pl.BlockSpec(shape, lambda *_: (0,) * len(shape))


def params():
    return pltpu.CompilerParams(vmem_limit_bytes=VMEM_LIMIT)


def split_kernel(width, n_dp, where, ids, tokens, cotangent, *outs):
    k, x = where[0], where[1]
    rows = tokens.shape[0]
    along = ids[...].astype(F32)
    line = lax.broadcasted_iota(jnp.int32, (rows, rows), 0)
    lane = lax.broadcasted_iota(jnp.int32, (rows, rows), 1)
    named = jnp.broadcast_to(along, (rows, rows))
    down = jnp.sum(jnp.where(line == lane, named, 0.0), axis=1, keepdims=True)
    earlier = jnp.where((named == down) & (line < lane), 1.0, 0.0)
    place = jnp.sum(earlier, axis=0, keepdims=True) + (x * CAP).astype(F32)
    at = lax.broadcasted_iota(jnp.int32, (META, rows), 0)
    meta = jnp.where(at == 0, along, jnp.where(at == 1, place, 0.0)).astype(BF16)
    for rel in range(n_dp):
        start = pl.multiple_of((k ^ rel) * width, 128)
        outs[rel][0:rows, :] = tokens[:, pl.ds(start, width)]
        outs[rel][rows:, :] = jnp.zeros((META, width), BF16)
        outs[rel][rows:, 0:rows] = meta
        outs[n_dp + rel][...] = cotangent[:, pl.ds(start, width)]


def split(where, ids, tokens, cotangent, width, n_dp):
    rows = tokens.shape[0]
    tall, low = (rows + META, width), (rows, width)
    return pl.pallas_call(
        functools.partial(split_kernel, width, n_dp),
        out_shape=[jax.ShapeDtypeStruct(s, BF16) for s in [tall] * n_dp + [low] * n_dp],
        in_specs=[
            pl.BlockSpec(memory_space=pltpu.SMEM),
            whole_spec(ids.shape),
            whole_spec(tokens.shape),
            whole_spec(cotangent.shape),
        ],
        out_specs=[whole_spec(s) for s in [tall] * n_dp + [low] * n_dp],
        compiler_params=params(),
    )(where, ids, tokens, cotangent)


def placer_of(row, slot_count):
    every = lax.broadcasted_iota(jnp.int32, (slot_count, row.shape[1]), 0)
    return (every == row).astype(F32).astype(BF16)


def project_kernel(n_dp, weights, first, after, where, *refs):
    blocks, refs = refs[: 2 * n_dp], refs[2 * n_dp + after :]
    if not first:
        lines, refs = refs[0], refs[1:]
    weight_refs, refs = refs[:weights], refs[weights:]
    if first:
        keep, send, placed, lines = refs
    else:
        keep, send, placed = refs
    step = pl.program_id(0)
    per_step = weight_refs[0].shape[0]
    local_experts, slot_rows, width = placed.shape
    slots = slot_rows // n_dp
    rows = blocks[0].shape[0] - (META if first else 0)

    @pl.when(step == 0)
    def _():
        for rel in range(n_dp):
            pair = blocks[2 * rel], blocks[2 * rel + 1]
            if first:
                metas = [b[rows:, 0:rows].astype(F32) for b in pair]
                ids = jnp.concatenate([m[0:1] for m in metas], axis=1)
                place = jnp.concatenate([m[1:2] for m in metas], axis=1)
                low = (where[1] * local_experts).astype(F32)
                row = ((ids - low) * slots + place).astype(jnp.int32)
                lines[rel] = jnp.broadcast_to(row, (8, row.shape[1]))
            else:
                row = lines[rel][0:1]
            placer = placer_of(row, local_experts * slots)
            values = jnp.concatenate([b[0:rows, :] for b in pair], axis=0)
            found = jnp.dot(placer, values, preferred_element_type=F32).astype(BF16)
            placed[:, rel * slots : (rel + 1) * slots, :] = found.reshape(local_experts, slots, width)

    for i in range(per_step):
        mine = placed[step * per_step + i]
        for w in range(weights):
            act = lax.dot_general(
                mine, weight_refs[w][i], (((1,), (1,)), ((), ())), preferred_element_type=F32
            ).astype(BF16)
            for rel in range(n_dp):
                out = send if rel & 1 else keep
                out[rel // 2, w, i] = act[rel * slots : (rel + 1) * slots]


def project(where, blocks, lines, weights, n_dp, per_step, after=()):
    first = lines is None
    local_experts, hidden, width = weights[0].shape
    slots = 2 * CAP
    rows = blocks[0].shape[0] - (META if first else 0)
    count = len(weights)
    act = (n_dp // 2, count, local_experts, slots, hidden)
    act_block = (n_dp // 2, count, per_step, slots, hidden)
    act_spec = pl.BlockSpec(act_block, lambda e: (0, 0, e, 0, 0))
    placed = (local_experts, n_dp * slots, width)
    line = (n_dp, 8, 2 * rows)
    weight_spec = pl.BlockSpec((per_step, hidden, width), lambda e: (e, 0, 0))
    out_shape = [jax.ShapeDtypeStruct(act, BF16), jax.ShapeDtypeStruct(act, BF16)]
    out_specs = [act_spec, act_spec]
    scratch = []
    operands = [where, *blocks]
    in_specs = [pl.BlockSpec(memory_space=pltpu.SMEM)] + [whole_spec(b.shape) for b in blocks]
    if first:
        operands += after
        in_specs += [pl.BlockSpec(memory_space=pl.ANY)] * len(after)
        out_shape += [jax.ShapeDtypeStruct(placed, BF16), jax.ShapeDtypeStruct(line, jnp.int32)]
        out_specs += [whole_spec(placed), whole_spec(line)]
    else:
        operands.append(lines)
        in_specs.append(whole_spec(line))
        scratch.append(pltpu.VMEM(placed, BF16))
    flops = 2 * count * local_experts * n_dp * slots * width * hidden
    return pl.pallas_call(
        functools.partial(project_kernel, n_dp, count, first, len(after)),
        grid=(local_experts // per_step,),
        out_shape=out_shape,
        in_specs=in_specs + [weight_spec] * count,
        out_specs=out_specs,
        scratch_shapes=scratch,
        compiler_params=params(),
        cost_estimate=pl.CostEstimate(
            flops=4 * flops, bytes_accessed=count * local_experts * width * hidden * 2, transcendentals=0
        ),
    )(*operands, *weights)


def back_kernel(n_dp, where, lines, h0, h1, h2, h3, gate, up, keep_x, send_x, keep_z, send_z, held):
    step = pl.program_id(0)
    held_hidden = (h0, h1, h2, h3)
    per_step = gate.shape[0]
    slots = h0.shape[2]
    for i in range(per_step):
        gate_grad = jnp.concatenate([h[0, i] for h in held_hidden], axis=0)
        up_grad = jnp.concatenate([h[1, i] for h in held_hidden], axis=0)
        value = jnp.dot(gate_grad, gate[i], preferred_element_type=F32)
        value = value + jnp.dot(up_grad, up[i], preferred_element_type=F32)
        value = value.astype(BF16)
        start = pl.multiple_of((step * per_step + i) * slots, 16)
        for rel in range(n_dp):
            held[rel, pl.ds(start, slots), :] = value[rel * slots : (rel + 1) * slots]

    @pl.when(step == pl.num_programs(0) - 1)
    def _():
        rows, half = keep_x.shape[1], keep_x.shape[2]
        for r in range(n_dp):
            rel = where[2] ^ r
            placer = placer_of(lines[rel][0:1], held.shape[1])
            token_rows = lax.dot_general(
                placer, held[rel], (((0,), (0,)), ((), ())), preferred_element_type=F32
            ).astype(BF16)
            keep_x[r] = token_rows[0:rows, 0:half]
            send_x[r] = token_rows[rows:, 0:half]
            out = send_z if r & 1 else keep_z
            out[0, r // 2] = token_rows[0:rows, half:]
            out[1, r // 2] = token_rows[rows:, half:]


def back(where, lines, parts, gate, up, rows, per_step):
    n_dp = len(parts)
    local_experts, hidden, width = gate.shape
    slots = parts[0].shape[2]
    part_spec = pl.BlockSpec((2, per_step, slots, hidden), lambda e: (0, e, 0, 0))
    weight_spec = pl.BlockSpec((per_step, hidden, width), lambda e: (e, 0, 0))
    shape_x = (n_dp, rows, width // 2)
    shape_z = (2, n_dp // 2, rows, width // 2)
    flops = 4 * local_experts * n_dp * slots * width * hidden
    return pl.pallas_call(
        functools.partial(back_kernel, n_dp),
        grid=(local_experts // per_step,),
        out_shape=[jax.ShapeDtypeStruct(s, BF16) for s in (shape_x, shape_x, shape_z, shape_z)],
        in_specs=[pl.BlockSpec(memory_space=pltpu.SMEM), whole_spec(lines.shape)]
        + [part_spec] * n_dp
        + [weight_spec] * 2,
        out_specs=[whole_spec(s) for s in (shape_x, shape_x, shape_z, shape_z)],
        scratch_shapes=[pltpu.VMEM((n_dp, local_experts * slots, width), BF16)],
        compiler_params=params(),
        cost_estimate=pl.CostEstimate(
            flops=4 * flops, bytes_accessed=2 * local_experts * width * hidden * 2, transcendentals=0
        ),
    )(where, lines, *parts, gate, up)


def weight_kernel(which, placed, h0, h1, h2, h3, out):
    for i in range(out.shape[0]):
        grad = jnp.concatenate([h[which, i] for h in (h0, h1, h2, h3)], axis=0)
        out[i] = lax.dot_general(
            grad, placed[i], (((0,), (0,)), ((), ())), preferred_element_type=F32
        ).astype(BF16)


def weight_grad(which, placed, parts, per_step):
    local_experts, slot_rows, width = placed.shape
    _, _, slots, hidden = parts[0].shape
    part_spec = pl.BlockSpec((2, per_step, slots, hidden), lambda e: (0, e, 0, 0))
    flops = 2 * local_experts * slot_rows * width * hidden
    return pl.pallas_call(
        functools.partial(weight_kernel, which),
        grid=(local_experts // per_step,),
        out_shape=jax.ShapeDtypeStruct((local_experts, hidden, width), BF16),
        in_specs=[pl.BlockSpec((per_step, slot_rows, width), lambda e: (e, 0, 0))] + [part_spec] * len(parts),
        out_specs=pl.BlockSpec((per_step, hidden, width), lambda e: (e, 0, 0)),
        compiler_params=params(),
        cost_estimate=pl.CostEstimate(
            flops=4 * flops, bytes_accessed=local_experts * width * hidden * 2, transcendentals=0
        ),
    )(placed, *parts)


def plus(first, second):
    return first.astype(F32) + second.astype(F32)


def swiglu_grads(gate_act, up_act, hidden_grad):
    sigmoid_gate = jax.nn.sigmoid(gate_act)
    up_grad = (hidden_grad * gate_act * sigmoid_gate).astype(BF16)
    gate_grad = (
        hidden_grad * up_act * sigmoid_gate * (1.0 + gate_act * (1.0 - sigmoid_gate))
    ).astype(BF16)
    return gate_grad, up_grad


def on_small_slice(tokens, cotangent, expert_ids, gate_weight, up_weight, down_weight):
    n_dp, n_x, n_t = 4, 2, 4
    k, x, t = lax.axis_index("dp"), lax.axis_index("expert"), lax.axis_index("tensor")
    width = gate_weight.shape[1]
    rows = tokens.shape[0]
    half = width // 2
    where = jnp.stack([k, x, k ^ t]).astype(jnp.int32)

    chunks = split(where, expert_ids.reshape(1, rows), tokens, cotangent, width, n_dp)

    def collect(chunks):
        blocks = []
        for rel in range(n_dp):
            mine = chunks[0] if rel == 0 else swap(chunks[rel], "dp", n_dp, rel)
            blocks += [mine, swap(mine, "expert", n_x, 1)]
        return blocks

    token_blocks = collect(chunks[:n_dp])
    grad_blocks = collect(chunks[n_dp:])
    gate_weight, up_weight, down_weight = (
        jnp.swapaxes(weight, 1, 2) for weight in (gate_weight, up_weight, down_weight)
    )
    keep, send, placed, lines = project(
        where, token_blocks, None, [gate_weight, up_weight], n_dp, 2, after=grad_blocks[::2]
    )

    def over_dp(keep, send):
        arrived = swap(send, "dp", n_dp, 1)
        near = plus(keep[0], arrived[0])
        far = plus(keep[1], arrived[1]).astype(BF16)
        return near + swap(far, "dp", n_dp, 2).astype(F32)

    acts = over_dp(keep, send)
    keep, send = project(where, grad_blocks, lines, [down_weight], n_dp, 2)
    hidden_grad = over_dp(keep, send)[0]
    part = jnp.stack(swiglu_grads(acts[0], acts[1], hidden_grad))
    far = swap(part, "dp", n_dp, 2)
    parts = [part, swap(part, "dp", n_dp, 1), far, swap(far, "dp", n_dp, 1)]

    keep_x, send_x, keep_z, send_z = back(where, lines, parts, gate_weight, up_weight, rows, 2)
    sum_x = plus(keep_x, swap(send_x, "expert", n_x, 1))
    sum_z = plus(keep_z, swap(send_z, "tensor", n_t, 1))
    from_z = swap(jnp.stack([sum_x[1], sum_x[3]]).astype(BF16), "tensor", n_t, 1)
    from_x = swap(sum_z[1].astype(BF16), "expert", n_x, 1)
    near = jnp.concatenate([plus(sum_x[0], from_z[0]), plus(sum_z[0, 0], from_x[0])], axis=1).astype(BF16)
    far = jnp.concatenate([plus(sum_x[2], from_z[1]), plus(sum_z[0, 1], from_x[1])], axis=1).astype(BF16)
    pairs = [(i, j) for i in range(n_dp) for j in range(n_t)]
    near = lax.ppermute(near, ("dp", "tensor"), [(i * n_t + j, j * n_t + i) for i, j in pairs])
    far = lax.ppermute(far, ("dp", "tensor"), [(i * n_t + j, (j ^ 2) * n_t + i) for i, j in pairs])
    grad_tokens = plus(near, far).astype(BF16)

    grad_gate = jnp.swapaxes(weight_grad(0, placed, parts, 2), 1, 2)
    grad_up = jnp.swapaxes(weight_grad(1, placed, parts, 2), 1, 2)
    return grad_tokens, grad_gate, grad_up


def bits_of(count):
    bits = []
    bit = 1
    while bit < count:
        bits.append(bit)
        bit *= 2
    return bits


def halving_sum(parts, axis, count):
    parts = dict(parts)
    for bit in bits_of(count):
        leaving = sorted(r for r in parts if r & bit)
        arrived = swap(jnp.stack([parts[r].astype(BF16) for r in leaving]), axis, count, bit)
        for at, r in enumerate(leaving):
            parts[r ^ bit] = plus(parts[r ^ bit], arrived[at])
            del parts[r]
    return parts[0]


def doubling_gather(value, axis, count):
    held = {0: value}
    for bit in reversed(bits_of(count)):
        known = sorted(held)
        arrived = swap(jnp.stack([held[r] for r in known]), axis, count, bit)
        for at, r in enumerate(known):
            held[r ^ bit] = arrived[at]
    return [held[r] for r in range(count)]


def on_any_slice(tokens, cotangent, expert_ids, gate_weight, up_weight, down_weight):
    n_dp, n_x, n_t = lax.axis_size("dp"), lax.axis_size("expert"), lax.axis_size("tensor")
    k, x, t = lax.axis_index("dp"), lax.axis_index("expert"), lax.axis_index("tensor")
    local_experts, width, hidden = gate_weight.shape
    rows = tokens.shape[0]
    slots = n_x * CAP
    ids_row = expert_ids.reshape(1, rows)
    order = jnp.arange(rows, dtype=jnp.int32)
    earlier = (expert_ids == ids_row) & (order[:, None] < order[None, :])
    position = jnp.sum(earlier.astype(jnp.int32), axis=0)
    target = ids_row[0] * CAP + position
    targets = lax.all_gather(target, ("dp", "expert"), axis=0, tiled=False).reshape(n_dp, n_x, rows)
    pair = jnp.stack([tokens, cotangent])
    placers, slot_rows = [], []
    for rel in range(n_dp):
        columns = lax.dynamic_slice_in_dim(pair, (k ^ rel) * width, width, axis=2)
        mine = columns if rel == 0 else swap(columns, "dp", n_dp, rel)
        blocks = lax.all_gather(mine, "expert", axis=1, tiled=True)
        goal = lax.dynamic_index_in_dim(targets, k ^ rel, axis=0, keepdims=False)
        expert = goal // CAP - x * local_experts
        place = jnp.arange(n_x, dtype=jnp.int32)[:, None] * CAP + goal % CAP
        row = jnp.where((expert >= 0) & (expert < local_experts), expert * slots + place, -1)
        row = row.reshape(1, n_x * rows)
        every = jnp.arange(local_experts * slots, dtype=jnp.int32)[:, None]
        placer = (every == row).astype(BF16)
        placers.append(placer)
        slot_rows.append(
            jnp.einsum("sn,and->asd", placer, blocks, preferred_element_type=F32)
            .astype(BF16)
            .reshape(2, local_experts, slots, width)
        )
    slot_rows = jnp.concatenate(slot_rows, axis=2)
    inputs, grads_in = slot_rows[0], slot_rows[1]

    def act(values, weight):
        return jnp.einsum("esd,edf->esf", values, weight, preferred_element_type=F32).astype(BF16)

    acts = jnp.stack([act(inputs, gate_weight), act(inputs, up_weight), act(grads_in, down_weight)])
    acts = acts.reshape(3, local_experts, n_dp, slots, hidden)
    acts = halving_sum({r: acts[:, :, r] for r in range(n_dp)}, "dp", n_dp)
    grads = doubling_gather(jnp.stack(swiglu_grads(acts[0], acts[1], acts[2])), "dp", n_dp)
    grads = jnp.concatenate(grads, axis=2)
    gate_grad, up_grad = grads[0], grads[1]
    partial_value = jnp.einsum("esf,edf->esd", gate_grad, gate_weight, preferred_element_type=F32)
    partial_value = partial_value + jnp.einsum("esf,edf->esd", up_grad, up_weight, preferred_element_type=F32)
    partial_value = partial_value.astype(BF16).reshape(local_experts, n_dp, slots, width)
    per_token = []
    for rel in range(n_dp):
        flat = partial_value[:, rel].reshape(local_experts * slots, width)
        spread = lax.dot_general(placers[rel], flat, (((0,), (0,)), ((), ())), preferred_element_type=F32)
        spread = spread.astype(BF16).reshape(n_x, rows, width)
        per_token.append(lax.psum_scatter(spread, "expert", scatter_dimension=0, tiled=False))
    per_token = jnp.stack(per_token)
    terms = {r: lax.dynamic_index_in_dim(per_token, k ^ t ^ r, axis=0, keepdims=False) for r in range(n_t)}
    summed = halving_sum(terms, "tensor", n_t).astype(BF16)
    summed = lax.ppermute(
        summed, ("dp", "tensor"), [(i * n_t + j, j * n_t + i) for i in range(n_dp) for j in range(n_t)]
    )
    grad_gate = jnp.einsum("esd,esf->edf", inputs, gate_grad, preferred_element_type=F32).astype(BF16)
    grad_up = jnp.einsum("esd,esf->edf", inputs, up_grad, preferred_element_type=F32).astype(BF16)
    return summed, grad_gate, grad_up


def solution(mesh):
    placed = (
        P(("dp", "expert"), None),
        P(("dp", "expert"), None),
        P(("dp", "expert"), None),
        P("expert", "dp", "tensor"),
        P("expert", "dp", "tensor"),
        P("expert", "dp", "tensor"),
    )
    sizes = tuple(mesh.shape[name] for name in ("dp", "expert", "tensor"))
    return jax.shard_map(
        on_small_slice if sizes == (4, 2, 4) else on_any_slice,
        mesh=mesh,
        in_specs=placed,
        out_specs=(
            P(("dp", "expert"), "tensor"),
            P("expert", "dp", "tensor"),
            P("expert", "dp", "tensor"),
        ),
        check_vma=False,
    )
```

```python
import functools

import jax
import jax.numpy as jnp
from jax import lax
from jax.experimental import pallas as pl
from jax.experimental.pallas import tpu as pltpu
from jax.sharding import PartitionSpec as P

CAP = 8
META = 16
F32 = jnp.float32
BF16 = jnp.bfloat16
VMEM_LIMIT = 48 * 1024 * 1024


def swap(value, axis, count, bit):
    return lax.ppermute(value, axis, [(i, i ^ bit) for i in range(count)])


def whole_spec(shape):
    return pl.BlockSpec(shape, lambda *_: (0,) * len(shape))


def params():
    return pltpu.CompilerParams(vmem_limit_bytes=VMEM_LIMIT)


def split_kernel(width, n_dp, where, ids, tokens, cotangent, *refs):
    outs, (meta, sems) = refs[:-2], refs[-2:]
    k, x = where[0], where[1]
    rows = tokens.shape[0]
    copies = []
    for rel in range(n_dp):
        start = pl.multiple_of((k ^ rel) * width, 128)
        for which, source in enumerate((tokens, cotangent)):
            out = outs[which * n_dp + rel]
            copy = pltpu.make_async_copy(
                source.at[:, pl.ds(start, width)], out.at[pl.ds(0, rows), :], sems.at[which * n_dp + rel]
            )
            copy.start()
            copies.append(copy)
    along = ids[...].astype(F32)
    line = lax.broadcasted_iota(jnp.int32, (rows, rows), 0)
    lane = lax.broadcasted_iota(jnp.int32, (rows, rows), 1)
    named = jnp.broadcast_to(along, (rows, rows))
    down = jnp.sum(jnp.where(line == lane, named, 0.0), axis=1, keepdims=True)
    earlier = jnp.where((named == down) & (line < lane), 1.0, 0.0)
    place = jnp.sum(earlier, axis=0, keepdims=True) + (x * CAP).astype(F32)
    at = lax.broadcasted_iota(jnp.int32, (META, rows), 0)
    meta[...] = jnp.zeros(meta.shape, BF16)
    meta[:, 0:rows] = jnp.where(at == 0, along, jnp.where(at == 1, place, 0.0)).astype(BF16)
    for rel in range(n_dp):
        copy = pltpu.make_async_copy(meta, outs[rel].at[pl.ds(rows, META), :], sems.at[2 * n_dp + rel])
        copy.start()
        copies.append(copy)
    for copy in copies:
        copy.wait()


def split(where, ids, tokens, cotangent, width, n_dp):
    rows = tokens.shape[0]
    tall, low = (rows + META, width), (rows, width)
    anywhere = pl.BlockSpec(memory_space=pl.ANY)
    return pl.pallas_call(
        functools.partial(split_kernel, width, n_dp),
        out_shape=[jax.ShapeDtypeStruct(s, BF16) for s in [tall] * n_dp + [low] * n_dp],
        in_specs=[
            pl.BlockSpec(memory_space=pltpu.SMEM),
            pl.BlockSpec(memory_space=pltpu.VMEM),
            anywhere,
            anywhere,
        ],
        out_specs=[anywhere] * (2 * n_dp),
        scratch_shapes=[pltpu.VMEM((META, width), BF16), pltpu.SemaphoreType.DMA((3 * n_dp,))],
        compiler_params=params(),
    )(where, ids, tokens, cotangent)


def placer_of(row, slot_count):
    every = lax.broadcasted_iota(jnp.int32, (slot_count, row.shape[1]), 0)
    return (every == row).astype(F32).astype(BF16)


def place_kernel(order, first, after, where, *refs):
    n_dp = len(order)
    if first:
        mine, other, refs = refs[:n_dp], refs[n_dp : 2 * n_dp], refs[2 * n_dp + after :]
        placed, lines = refs
    else:
        mine, lines, refs = refs[:n_dp], refs[n_dp], refs[n_dp + 1 :]
        halves, (placed,) = refs[: len(refs) - after - 1], refs[-1:]
        other = [half.at[i] for half in halves for i in range(half.shape[0])]
    local_experts, slot_rows, width = placed.shape
    slots = slot_rows // n_dp
    rows = mine[0].shape[0] - (META if first else 0)
    for at, rel in enumerate(order):
        pair = mine[rel], other[rel]
        if first:
            metas = [b[rows:, 0:rows].astype(F32) for b in pair]
            ids = jnp.concatenate([m[0:1] for m in metas], axis=1)
            place = jnp.concatenate([m[1:2] for m in metas], axis=1)
            low = (where[1] * local_experts).astype(F32)
            row = ((ids - low) * slots + place).astype(jnp.int32)
            lines[rel] = jnp.broadcast_to(row, (8, row.shape[1]))
        else:
            row = lines[rel][0:1]
        placer = placer_of(row, local_experts * slots)
        values = jnp.concatenate([b[0:rows, :] for b in pair], axis=0)
        found = jnp.dot(placer, values, preferred_element_type=F32).astype(BF16)
        placed[:, at * slots : (at + 1) * slots, :] = found.reshape(local_experts, slots, width)


def place(order, where, mine, other, lines, local_experts, after, cost):
    first = lines is None
    n_dp, slots = len(order), 2 * CAP
    width = mine[0].shape[1]
    rows = mine[0].shape[0] - (META if first else 0)
    placed = jax.ShapeDtypeStruct((local_experts, n_dp * slots, width), BF16)
    line = jax.ShapeDtypeStruct((n_dp, 8, 2 * rows), jnp.int32)
    near = pl.BlockSpec(memory_space=pltpu.VMEM)
    operands = [*mine] + ([] if first else [lines]) + [*other]
    return pl.pallas_call(
        functools.partial(place_kernel, order, first, len(after)),
        out_shape=[placed, line] if first else placed,
        in_specs=[pl.BlockSpec(memory_space=pltpu.SMEM)]
        + [near] * len(operands)
        + [pl.BlockSpec(memory_space=pl.ANY)] * len(after),
        out_specs=[near, near] if first else near,
        compiler_params=params(),
        cost_estimate=pl.CostEstimate(flops=cost, bytes_accessed=4 * rows * width * n_dp, transcendentals=0),
    )(where, *operands, *after)


def back_kernel(n_dp, where, lines, h0, h1, h2, h3, gate, up, keep_x, send_x, keep_z, send_z, near, held, sems):
    parts = (h0, h1, h2, h3)
    local_experts, slots = h0.shape[1], h0.shape[2]
    per_copy = local_experts // sems.shape[1]

    def copy_of(which, at):
        group = pl.ds(at * per_copy, per_copy)
        return pltpu.make_async_copy((gate, up)[which].at[group], near.at[which, group], sems.at[which, at])

    for at in range(sems.shape[1]):
        for which in range(2):
            copy_of(which, at).start()
    for at in range(sems.shape[1]):
        for which in range(2):
            copy_of(which, at).wait()
        for e in range(at * per_copy, (at + 1) * per_copy):
            gate_grad = jnp.concatenate([h[0, e] for h in parts], axis=0)
            up_grad = jnp.concatenate([h[1, e] for h in parts], axis=0)
            value = jnp.dot(gate_grad, near[0, e], preferred_element_type=F32)
            value = value + jnp.dot(up_grad, near[1, e], preferred_element_type=F32)
            value = value.astype(BF16)
            for rel in range(n_dp):
                held[rel, e * slots : (e + 1) * slots, :] = value[rel * slots : (rel + 1) * slots]

    rows, half = keep_x.shape[1], keep_x.shape[2]
    for r in range(n_dp):
        rel = where[2] ^ r
        placer = placer_of(lines[rel][0:1], held.shape[1])
        token_rows = lax.dot_general(
            placer, held[rel], (((0,), (0,)), ((), ())), preferred_element_type=F32
        ).astype(BF16)
        keep_x[r] = token_rows[0:rows, 0:half]
        send_x[r] = token_rows[rows:, 0:half]
        out = send_z if r & 1 else keep_z
        out[0, r // 2] = token_rows[0:rows, half:]
        out[1, r // 2] = token_rows[rows:, half:]


def back(where, lines, parts, gate, up, rows):
    n_dp = len(parts)
    local_experts, hidden, width = gate.shape
    slots = parts[0].shape[2]
    shape_x = (n_dp, rows, width // 2)
    shape_z = (2, n_dp // 2, rows, width // 2)
    near = pl.BlockSpec(memory_space=pltpu.VMEM)
    flops = 4 * local_experts * n_dp * slots * width * hidden
    return pl.pallas_call(
        functools.partial(back_kernel, n_dp),
        out_shape=[jax.ShapeDtypeStruct(s, BF16) for s in (shape_x, shape_x, shape_z, shape_z)],
        in_specs=[pl.BlockSpec(memory_space=pltpu.SMEM)]
        + [near] * (1 + n_dp)
        + [pl.BlockSpec(memory_space=pl.ANY)] * 2,
        out_specs=[near] * 4,
        scratch_shapes=[
            pltpu.VMEM((2, local_experts, hidden, width), BF16),
            pltpu.VMEM((n_dp, local_experts * slots, width), BF16),
            pltpu.SemaphoreType.DMA((2, 8 if local_experts % 8 == 0 else 1)),
        ],
        compiler_params=params(),
        cost_estimate=pl.CostEstimate(
            flops=4 * flops, bytes_accessed=2 * local_experts * width * hidden * 2, transcendentals=0
        ),
    )(where, lines, *parts, gate, up)


def weight_kernel(which, order, placed, h0, h1, h2, h3, out):
    parts = (h0, h1, h2, h3)
    for i in range(out.shape[0]):
        grad = jnp.concatenate([parts[rel][which, i] for rel in order], axis=0)
        out[i] = lax.dot_general(
            grad, placed[i], (((0,), (0,)), ((), ())), preferred_element_type=F32
        ).astype(BF16)


def weight_grad(which, order, placed, parts, per_step):
    local_experts, slot_rows, width = placed.shape
    _, _, slots, hidden = parts[0].shape
    part_spec = pl.BlockSpec((2, per_step, slots, hidden), lambda e: (0, e, 0, 0))
    flops = 2 * local_experts * slot_rows * width * hidden
    return pl.pallas_call(
        functools.partial(weight_kernel, which, order),
        grid=(local_experts // per_step,),
        out_shape=jax.ShapeDtypeStruct((local_experts, hidden, width), BF16),
        in_specs=[pl.BlockSpec((per_step, slot_rows, width), lambda e: (e, 0, 0))] + [part_spec] * len(parts),
        out_specs=pl.BlockSpec((per_step, hidden, width), lambda e: (e, 0, 0)),
        compiler_params=params(),
        cost_estimate=pl.CostEstimate(
            flops=4 * flops, bytes_accessed=local_experts * width * hidden * 2, transcendentals=0
        ),
    )(placed, *parts)


def plus(first, second):
    return first.astype(F32) + second.astype(F32)


def swiglu_grads(gate_act, up_act, hidden_grad):
    sigmoid_gate = jax.nn.sigmoid(gate_act)
    up_grad = (hidden_grad * gate_act * sigmoid_gate).astype(BF16)
    gate_grad = (
        hidden_grad * up_act * sigmoid_gate * (1.0 + gate_act * (1.0 - sigmoid_gate))
    ).astype(BF16)
    return gate_grad, up_grad


def on_small_slice(tokens, cotangent, expert_ids, gate_weight, up_weight, down_weight):
    n_dp, n_x, n_t = 4, 2, 4
    k, x, t = lax.axis_index("dp"), lax.axis_index("expert"), lax.axis_index("tensor")
    width = gate_weight.shape[1]
    rows = tokens.shape[0]
    half = width // 2
    where = jnp.stack([k, x, k ^ t]).astype(jnp.int32)

    chunks = split(where, expert_ids.reshape(1, rows), tokens, cotangent, width, n_dp)

    own = [c if i % n_dp == 0 else swap(c, "dp", n_dp, i % n_dp) for i, c in enumerate(chunks)]
    own_tokens, own_grads = own[:n_dp], own[n_dp:]
    other_tokens = [swap(c, "expert", n_x, 1) for c in own_tokens]
    all_grads = jnp.stack(own_grads)
    other_grads = swap(all_grads, "expert", n_x, 1)
    gate_weight, up_weight, down_weight = (
        jnp.swapaxes(weight, 1, 2) for weight in (gate_weight, up_weight, down_weight)
    )
    local_experts = gate_weight.shape[0]
    order = (0, 1, 2, 3)

    def project(values, weight):
        act = jnp.einsum("esd,ehd->esh", values, weight, preferred_element_type=F32).astype(BF16)
        return jnp.split(act, n_dp, axis=1)

    def near_and_far(act):
        near, far = swap(act[1], "dp", n_dp, 1), swap(act[3], "dp", n_dp, 1)
        return plus(act[0], near), plus(act[2], far).astype(BF16)

    placed, lines = place(order, where, own_tokens, other_tokens, None, local_experts, [all_grads], 1 << 34)
    gate_near, gate_far = near_and_far(project(placed, gate_weight))
    up_near, up_far = near_and_far(project(placed, up_weight))
    far = jnp.stack([gate_far, up_far])
    there = swap(far, "dp", n_dp, 2)
    placed_grads = place(order, where, own_grads, [other_grads], lines, local_experts, [far], 1 << 34)
    hidden_act = project(placed_grads, down_weight)
    hidden_grad = hidden_act[0].astype(F32)
    for rel in range(1, n_dp):
        hidden_grad = hidden_grad + swap(hidden_act[rel], "dp", n_dp, rel).astype(F32)
    acts = plus(gate_near, there[0]), plus(up_near, there[1])
    part = jnp.stack(swiglu_grads(acts[0], acts[1], hidden_grad))
    far = swap(part, "dp", n_dp, 2)
    parts = [part, swap(part, "dp", n_dp, 1), far, swap(far, "dp", n_dp, 1)]

    keep_x, send_x, keep_z, send_z = back(where, lines, parts, gate_weight, up_weight, rows)
    sum_x = plus(keep_x, swap(send_x, "expert", n_x, 1))
    sum_z = plus(keep_z, swap(send_z, "tensor", n_t, 1))
    from_z = swap(jnp.stack([sum_x[1], sum_x[3]]).astype(BF16), "tensor", n_t, 1)
    from_x = swap(sum_z[1].astype(BF16), "expert", n_x, 1)
    near = jnp.concatenate([plus(sum_x[0], from_z[0]), plus(sum_z[0, 0], from_x[0])], axis=1).astype(BF16)
    far = jnp.concatenate([plus(sum_x[2], from_z[1]), plus(sum_z[0, 1], from_x[1])], axis=1).astype(BF16)
    pairs = [(i, j) for i in range(n_dp) for j in range(n_t)]
    near = lax.ppermute(near, ("dp", "tensor"), [(i * n_t + j, j * n_t + i) for i, j in pairs])
    far = lax.ppermute(far, ("dp", "tensor"), [(i * n_t + j, (j ^ 2) * n_t + i) for i, j in pairs])
    grad_tokens = plus(near, far).astype(BF16)

    grad_gate = jnp.swapaxes(weight_grad(0, order, placed, parts, 4), 1, 2)
    grad_up = jnp.swapaxes(weight_grad(1, order, placed, parts, 4), 1, 2)
    return grad_tokens, grad_gate, grad_up


def bits_of(count):
    bits = []
    bit = 1
    while bit < count:
        bits.append(bit)
        bit *= 2
    return bits


def halving_sum(parts, axis, count):
    parts = dict(parts)
    for bit in bits_of(count):
        leaving = sorted(r for r in parts if r & bit)
        arrived = swap(jnp.stack([parts[r].astype(BF16) for r in leaving]), axis, count, bit)
        for at, r in enumerate(leaving):
            parts[r ^ bit] = plus(parts[r ^ bit], arrived[at])
            del parts[r]
    return parts[0]


def doubling_gather(value, axis, count):
    held = {0: value}
    for bit in reversed(bits_of(count)):
        known = sorted(held)
        arrived = swap(jnp.stack([held[r] for r in known]), axis, count, bit)
        for at, r in enumerate(known):
            held[r ^ bit] = arrived[at]
    return [held[r] for r in range(count)]


def on_any_slice(tokens, cotangent, expert_ids, gate_weight, up_weight, down_weight):
    n_dp, n_x, n_t = lax.axis_size("dp"), lax.axis_size("expert"), lax.axis_size("tensor")
    k, x, t = lax.axis_index("dp"), lax.axis_index("expert"), lax.axis_index("tensor")
    local_experts, width, hidden = gate_weight.shape
    rows = tokens.shape[0]
    slots = n_x * CAP
    ids_row = expert_ids.reshape(1, rows)
    order = jnp.arange(rows, dtype=jnp.int32)
    earlier = (expert_ids == ids_row) & (order[:, None] < order[None, :])
    position = jnp.sum(earlier.astype(jnp.int32), axis=0)
    target = ids_row[0] * CAP + position
    targets = lax.all_gather(target, ("dp", "expert"), axis=0, tiled=False).reshape(n_dp, n_x, rows)
    pair = jnp.stack([tokens, cotangent])
    placers, slot_rows = [], []
    for rel in range(n_dp):
        columns = lax.dynamic_slice_in_dim(pair, (k ^ rel) * width, width, axis=2)
        mine = columns if rel == 0 else swap(columns, "dp", n_dp, rel)
        blocks = lax.all_gather(mine, "expert", axis=1, tiled=True)
        goal = lax.dynamic_index_in_dim(targets, k ^ rel, axis=0, keepdims=False)
        expert = goal // CAP - x * local_experts
        place = jnp.arange(n_x, dtype=jnp.int32)[:, None] * CAP + goal % CAP
        row = jnp.where((expert >= 0) & (expert < local_experts), expert * slots + place, -1)
        row = row.reshape(1, n_x * rows)
        every = jnp.arange(local_experts * slots, dtype=jnp.int32)[:, None]
        placer = (every == row).astype(BF16)
        placers.append(placer)
        slot_rows.append(
            jnp.einsum("sn,and->asd", placer, blocks, preferred_element_type=F32)
            .astype(BF16)
            .reshape(2, local_experts, slots, width)
        )
    slot_rows = jnp.concatenate(slot_rows, axis=2)
    inputs, grads_in = slot_rows[0], slot_rows[1]

    def act(values, weight):
        return jnp.einsum("esd,edf->esf", values, weight, preferred_element_type=F32).astype(BF16)

    acts = jnp.stack([act(inputs, gate_weight), act(inputs, up_weight), act(grads_in, down_weight)])
    acts = acts.reshape(3, local_experts, n_dp, slots, hidden)
    acts = halving_sum({r: acts[:, :, r] for r in range(n_dp)}, "dp", n_dp)
    grads = doubling_gather(jnp.stack(swiglu_grads(acts[0], acts[1], acts[2])), "dp", n_dp)
    grads = jnp.concatenate(grads, axis=2)
    gate_grad, up_grad = grads[0], grads[1]
    partial_value = jnp.einsum("esf,edf->esd", gate_grad, gate_weight, preferred_element_type=F32)
    partial_value = partial_value + jnp.einsum("esf,edf->esd", up_grad, up_weight, preferred_element_type=F32)
    partial_value = partial_value.astype(BF16).reshape(local_experts, n_dp, slots, width)
    per_token = []
    for rel in range(n_dp):
        flat = partial_value[:, rel].reshape(local_experts * slots, width)
        spread = lax.dot_general(placers[rel], flat, (((0,), (0,)), ((), ())), preferred_element_type=F32)
        spread = spread.astype(BF16).reshape(n_x, rows, width)
        per_token.append(lax.psum_scatter(spread, "expert", scatter_dimension=0, tiled=False))
    per_token = jnp.stack(per_token)
    terms = {r: lax.dynamic_index_in_dim(per_token, k ^ t ^ r, axis=0, keepdims=False) for r in range(n_t)}
    summed = halving_sum(terms, "tensor", n_t).astype(BF16)
    summed = lax.ppermute(
        summed, ("dp", "tensor"), [(i * n_t + j, j * n_t + i) for i in range(n_dp) for j in range(n_t)]
    )
    grad_gate = jnp.einsum("esd,esf->edf", inputs, gate_grad, preferred_element_type=F32).astype(BF16)
    grad_up = jnp.einsum("esd,esf->edf", inputs, up_grad, preferred_element_type=F32).astype(BF16)
    return summed, grad_gate, grad_up


def solution(mesh):
    placed = (
        P(("dp", "expert"), None),
        P(("dp", "expert"), None),
        P(("dp", "expert"), None),
        P("expert", "dp", "tensor"),
        P("expert", "dp", "tensor"),
        P("expert", "dp", "tensor"),
    )
    sizes = tuple(mesh.shape[name] for name in ("dp", "expert", "tensor"))
    return jax.shard_map(
        on_small_slice if sizes == (4, 2, 4) else on_any_slice,
        mesh=mesh,
        in_specs=placed,
        out_specs=(
            P(("dp", "expert"), "tensor"),
            P("expert", "dp", "tensor"),
            P("expert", "dp", "tensor"),
        ),
        check_vma=False,
    )
```

```python
import functools

import jax
import jax.numpy as jnp
from jax import lax
from jax.experimental import pallas as pl
from jax.experimental.pallas import tpu as pltpu
from jax.sharding import PartitionSpec as P

CAP = 8
META = 16
F32 = jnp.float32
BF16 = jnp.bfloat16
VMEM_LIMIT = 48 * 1024 * 1024
PLACE_COST = 1 << 34


def swap(value, axis, count, bit):
    return lax.ppermute(value, axis, [(i, i ^ bit) for i in range(count)])


def whole_spec(shape):
    return pl.BlockSpec(shape, lambda *_: (0,) * len(shape))


def params():
    return pltpu.CompilerParams(vmem_limit_bytes=VMEM_LIMIT)


def split_kernel(width, n_dp, where, ids, tokens, cotangent, *refs):
    outs, (meta, sems) = refs[:-2], refs[-2:]
    k, x = where[0], where[1]
    rows = tokens.shape[0]
    copies = []
    for rel in range(n_dp):
        start = pl.multiple_of((k ^ rel) * width, 128)
        for which, (source, first) in enumerate(((tokens, 0), (cotangent, rows + META))):
            copy = pltpu.make_async_copy(
                source.at[:, pl.ds(start, width)],
                outs[rel].at[pl.ds(first, rows), :],
                sems.at[which * n_dp + rel],
            )
            copy.start()
            copies.append(copy)
    along = ids[...].astype(F32)
    line = lax.broadcasted_iota(jnp.int32, (rows, rows), 0)
    lane = lax.broadcasted_iota(jnp.int32, (rows, rows), 1)
    named = jnp.broadcast_to(along, (rows, rows))
    down = jnp.sum(jnp.where(line == lane, named, 0.0), axis=1, keepdims=True)
    earlier = jnp.where((named == down) & (line < lane), 1.0, 0.0)
    place = jnp.sum(earlier, axis=0, keepdims=True) + (x * CAP).astype(F32)
    at = lax.broadcasted_iota(jnp.int32, (META, rows), 0)
    meta[...] = jnp.zeros(meta.shape, BF16)
    meta[:, 0:rows] = jnp.where(at == 0, along, jnp.where(at == 1, place, 0.0)).astype(BF16)
    for rel in range(n_dp):
        copy = pltpu.make_async_copy(meta, outs[rel].at[pl.ds(rows, META), :], sems.at[2 * n_dp + rel])
        copy.start()
        copies.append(copy)
    for copy in copies:
        copy.wait()


def split(where, ids, tokens, cotangent, width, n_dp):
    rows = tokens.shape[0]
    pack = (2 * rows + META, width)
    anywhere = pl.BlockSpec(memory_space=pl.ANY)
    return pl.pallas_call(
        functools.partial(split_kernel, width, n_dp),
        out_shape=[jax.ShapeDtypeStruct(pack, BF16)] * n_dp,
        in_specs=[
            pl.BlockSpec(memory_space=pltpu.SMEM),
            pl.BlockSpec(memory_space=pltpu.VMEM),
            anywhere,
            anywhere,
        ],
        out_specs=[anywhere] * n_dp,
        scratch_shapes=[pltpu.VMEM((META, width), BF16), pltpu.SemaphoreType.DMA((3 * n_dp,))],
        compiler_params=params(),
    )(where, ids, tokens, cotangent)


def placer_of(row, slot_count):
    every = lax.broadcasted_iota(jnp.int32, (slot_count, row.shape[1]), 0)
    return (every == row).astype(F32).astype(BF16)


def place_kernel(first, rows, where, mine, near, late, *refs):
    n_dp = len(mine)
    other = [near.at[0], near.at[1], late.at[0], late.at[1]]
    if first:
        placed, lines = refs[-2:]
    else:
        lines, placed = refs[0], refs[-1]
    local_experts, slot_rows, width = placed.shape
    slots = slot_rows // n_dp
    for rel in range(n_dp):
        if first:
            pair = [b[0 : rows + META, :] for b in (mine[rel], other[rel])]
            metas = [b[rows:, 0:rows].astype(F32) for b in pair]
            ids = jnp.concatenate([m[0:1] for m in metas], axis=1)
            place = jnp.concatenate([m[1:2] for m in metas], axis=1)
            low = (where[1] * local_experts).astype(F32)
            row = ((ids - low) * slots + place).astype(jnp.int32)
            lines[rel] = jnp.broadcast_to(row, (8, row.shape[1]))
            pair = [b[0:rows] for b in pair]
        else:
            row = lines[rel][0:1]
            pair = [b[b.shape[0] - rows :, :] for b in (mine[rel], other[rel])]
        placer = placer_of(row, local_experts * slots)
        found = jnp.dot(placer, jnp.concatenate(pair, axis=0), preferred_element_type=F32).astype(BF16)
        placed[:, rel * slots : (rel + 1) * slots, :] = found.reshape(local_experts, slots, width)


def place(where, mine, near, late, lines, rows, local_experts, after):
    first = lines is None
    n_dp, slots = len(mine), 2 * CAP
    width = mine[0].shape[1]
    placed = jax.ShapeDtypeStruct((local_experts, n_dp * slots, width), BF16)
    line = jax.ShapeDtypeStruct((n_dp, 8, 2 * rows), jnp.int32)
    vmem = pl.BlockSpec(memory_space=pltpu.VMEM)
    operands = [near, late] + ([] if first else [lines])

    def kernel(where, *refs):
        place_kernel(first, rows, where, refs[:n_dp], *refs[n_dp:])

    return pl.pallas_call(
        kernel,
        out_shape=[placed, line] if first else placed,
        in_specs=[pl.BlockSpec(memory_space=pltpu.SMEM)]
        + [vmem] * (n_dp + len(operands))
        + [pl.BlockSpec(memory_space=pl.ANY)] * len(after),
        out_specs=[vmem, vmem] if first else vmem,
        compiler_params=params(),
        cost_estimate=pl.CostEstimate(flops=PLACE_COST, bytes_accessed=4 * rows * width * n_dp, transcendentals=0),
    )(where, *mine, *operands, *after)


def back_kernel(rels, lines, h0, h1, gate, up, own0, own1, other0, other1, near, held, sems):
    parts = (h0, h1)
    local_experts, slots = h0.shape[1], h0.shape[2]
    per_copy = local_experts // sems.shape[1]

    def copy_of(which, at):
        group = pl.ds(at * per_copy, per_copy)
        return pltpu.make_async_copy((gate, up)[which].at[group], near.at[which, group], sems.at[which, at])

    for at in range(sems.shape[1]):
        for which in range(2):
            copy_of(which, at).start()
    for at in range(sems.shape[1]):
        for which in range(2):
            copy_of(which, at).wait()
        for e in range(at * per_copy, (at + 1) * per_copy):
            gate_grad = jnp.concatenate([h[0, e] for h in parts], axis=0)
            up_grad = jnp.concatenate([h[1, e] for h in parts], axis=0)
            value = jnp.dot(gate_grad, near[0, e], preferred_element_type=F32)
            value = value + jnp.dot(up_grad, near[1, e], preferred_element_type=F32)
            value = value.astype(BF16)
            for i in range(2):
                held[i, e * slots : (e + 1) * slots, :] = value[i * slots : (i + 1) * slots]

    rows = own0.shape[0]
    for i, (own, other) in enumerate(((own0, other0), (own1, other1))):
        placer = placer_of(lines[rels[i]][0:1], held.shape[1])
        token_rows = lax.dot_general(
            placer, held[i], (((0,), (0,)), ((), ())), preferred_element_type=F32
        ).astype(BF16)
        own[...] = token_rows[0:rows]
        other[...] = token_rows[rows:]


def back(rels, lines, parts, gate, up, rows):
    local_experts, hidden, width = gate.shape
    slots = parts[0].shape[2]
    vmem = pl.BlockSpec(memory_space=pltpu.VMEM)
    flops = 4 * local_experts * 2 * slots * width * hidden
    return pl.pallas_call(
        functools.partial(back_kernel, rels),
        out_shape=[jax.ShapeDtypeStruct((rows, width), BF16)] * 4,
        in_specs=[vmem] * 3 + [pl.BlockSpec(memory_space=pl.ANY)] * 2,
        out_specs=[vmem] * 4,
        scratch_shapes=[
            pltpu.VMEM((2, local_experts, hidden, width), BF16),
            pltpu.VMEM((2, local_experts * slots, width), BF16),
            pltpu.SemaphoreType.DMA((2, 8 if local_experts % 8 == 0 else 1)),
        ],
        compiler_params=params(),
        cost_estimate=pl.CostEstimate(
            flops=4 * flops, bytes_accessed=2 * local_experts * width * hidden * 2, transcendentals=0
        ),
    )(lines, *parts, gate, up)


def weight_kernel(which, order, placed, h0, h1, h2, h3, out):
    parts = (h0, h1, h2, h3)
    for i in range(out.shape[0]):
        grad = jnp.concatenate([parts[rel][which, i] for rel in order], axis=0)
        out[i] = lax.dot_general(
            grad, placed[i], (((0,), (0,)), ((), ())), preferred_element_type=F32
        ).astype(BF16)


def weight_grad(which, order, placed, parts, per_step):
    local_experts, slot_rows, width = placed.shape
    _, _, slots, hidden = parts[0].shape
    part_spec = pl.BlockSpec((2, per_step, slots, hidden), lambda e: (0, e, 0, 0))
    flops = 2 * local_experts * slot_rows * width * hidden
    return pl.pallas_call(
        functools.partial(weight_kernel, which, order),
        grid=(local_experts // per_step,),
        out_shape=jax.ShapeDtypeStruct((local_experts, hidden, width), BF16),
        in_specs=[pl.BlockSpec((per_step, slot_rows, width), lambda e: (e, 0, 0))] + [part_spec] * len(parts),
        out_specs=pl.BlockSpec((per_step, hidden, width), lambda e: (e, 0, 0)),
        compiler_params=params(),
        cost_estimate=pl.CostEstimate(
            flops=4 * flops, bytes_accessed=local_experts * width * hidden * 2, transcendentals=0
        ),
    )(placed, *parts)


def plus(first, second):
    return first.astype(F32) + second.astype(F32)


def swiglu_grads(gate_act, up_act, hidden_grad):
    sigmoid_gate = jax.nn.sigmoid(gate_act)
    up_grad = (hidden_grad * gate_act * sigmoid_gate).astype(BF16)
    gate_grad = (
        hidden_grad * up_act * sigmoid_gate * (1.0 + gate_act * (1.0 - sigmoid_gate))
    ).astype(BF16)
    return gate_grad, up_grad


def on_small_slice(tokens, cotangent, expert_ids, gate_weight, up_weight, down_weight):
    n_dp, n_x, n_t = 4, 2, 4
    k, x, t = lax.axis_index("dp"), lax.axis_index("expert"), lax.axis_index("tensor")
    width = gate_weight.shape[1]
    rows = tokens.shape[0]
    where = jnp.stack([k, x]).astype(jnp.int32)
    packs = split(where, expert_ids.reshape(1, rows), tokens, cotangent, width, n_dp)
    own = [pack if rel == 0 else swap(pack, "dp", n_dp, rel) for rel, pack in enumerate(packs)]
    near_packs = swap(jnp.stack(own[:2]), "expert", n_x, 1)
    leaving_tokens = jnp.stack([o[: rows + META] for o in own[2:]])
    near_packs, leaving_tokens = lax.optimization_barrier((near_packs, leaving_tokens))
    late_tokens = swap(leaving_tokens, "expert", n_x, 1)
    leaving_grads = jnp.stack([o[rows + META :] for o in own[2:]])
    late_grads = swap(leaving_grads, "expert", n_x, 1)
    gate_weight, up_weight, down_weight = (
        jnp.swapaxes(weight, 1, 2) for weight in (gate_weight, up_weight, down_weight)
    )
    local_experts = gate_weight.shape[0]
    order = (0, 1, 2, 3)

    def project(values, weight):
        act = jnp.einsum("esd,ehd->esh", values, weight, preferred_element_type=F32).astype(BF16)
        return jnp.split(act, n_dp, axis=1)

    def near_and_far(act):
        near, far = swap(act[1], "dp", n_dp, 1), swap(act[3], "dp", n_dp, 1)
        return plus(act[0], near), plus(act[2], far).astype(BF16)

    placed, lines = place(where, own, near_packs, late_tokens, None, rows, local_experts, [leaving_grads])
    gate_near, gate_far = near_and_far(project(placed, gate_weight))
    up_near, up_far = near_and_far(project(placed, up_weight))
    far = jnp.stack([gate_far, up_far])
    there = swap(far, "dp", n_dp, 2)
    placed_grads = place(where, own, near_packs, late_grads, lines, rows, local_experts, [far])
    hidden_act = project(placed_grads, down_weight)
    hidden_grad = hidden_act[0].astype(F32)
    for rel in range(1, n_dp):
        hidden_grad = hidden_grad + swap(hidden_act[rel], "dp", n_dp, rel).astype(F32)
    acts = plus(gate_near, there[0]), plus(up_near, there[1])
    part = jnp.stack(swiglu_grads(acts[0], acts[1], hidden_grad))
    far = swap(part, "dp", n_dp, 2)
    beside = swap(part, "dp", n_dp, 1)
    near_back = back((0, 1), lines, [part, beside], gate_weight, up_weight, rows)
    far, near_back = lax.optimization_barrier((far, near_back))
    parts = [part, beside, far, swap(far, "dp", n_dp, 1)]
    far_back = back((2, 3), lines, parts[2:], gate_weight, up_weight, rows)

    def to_owner(value, rel, flip):
        if rel == 0 and flip == 0:
            return value
        pairs = [
            (i * n_x + j, (i ^ rel) * n_x + (j ^ flip)) for i in range(n_dp) for j in range(n_x)
        ]
        return lax.ppermute(value, ("dp", "expert"), pairs)

    def blocks(rels, own0, own1, other0, other1):
        terms = [
            plus(to_owner(own_r, rel, 0), to_owner(other_r, rel, 1)).astype(BF16)
            for rel, own_r, other_r in zip(rels, (own0, own1), (other0, other1))
        ]
        odd = ((k ^ t) & 1) == 1
        keep = jnp.where(odd, terms[1], terms[0])
        leaving = jnp.where(odd, terms[0], terms[1])
        return plus(keep, swap(leaving, "tensor", n_t, 1))

    first, second = blocks((0, 1), *near_back), blocks((2, 3), *far_back)
    swapped = ((k ^ t) & 2) == 2
    keep = jnp.where(swapped, second, first)
    leaving = jnp.where(swapped, first, second).astype(BF16)
    grad_tokens = plus(keep, swap(leaving, "tensor", n_t, 2)).astype(BF16)

    grad_gate = jnp.swapaxes(weight_grad(0, order, placed, parts, 4), 1, 2)
    grad_up = jnp.swapaxes(weight_grad(1, order, placed, parts, 4), 1, 2)
    return grad_tokens, grad_gate, grad_up


def bits_of(count):
    bits = []
    bit = 1
    while bit < count:
        bits.append(bit)
        bit *= 2
    return bits


def halving_sum(parts, axis, count):
    parts = dict(parts)
    for bit in bits_of(count):
        leaving = sorted(r for r in parts if r & bit)
        arrived = swap(jnp.stack([parts[r].astype(BF16) for r in leaving]), axis, count, bit)
        for at, r in enumerate(leaving):
            parts[r ^ bit] = plus(parts[r ^ bit], arrived[at])
            del parts[r]
    return parts[0]


def doubling_gather(value, axis, count):
    held = {0: value}
    for bit in reversed(bits_of(count)):
        known = sorted(held)
        arrived = swap(jnp.stack([held[r] for r in known]), axis, count, bit)
        for at, r in enumerate(known):
            held[r ^ bit] = arrived[at]
    return [held[r] for r in range(count)]


def on_any_slice(tokens, cotangent, expert_ids, gate_weight, up_weight, down_weight):
    n_dp, n_x, n_t = lax.axis_size("dp"), lax.axis_size("expert"), lax.axis_size("tensor")
    k, x, t = lax.axis_index("dp"), lax.axis_index("expert"), lax.axis_index("tensor")
    local_experts, width, hidden = gate_weight.shape
    rows = tokens.shape[0]
    slots = n_x * CAP
    ids_row = expert_ids.reshape(1, rows)
    order = jnp.arange(rows, dtype=jnp.int32)
    earlier = (expert_ids == ids_row) & (order[:, None] < order[None, :])
    position = jnp.sum(earlier.astype(jnp.int32), axis=0)
    target = ids_row[0] * CAP + position
    targets = lax.all_gather(target, ("dp", "expert"), axis=0, tiled=False).reshape(n_dp, n_x, rows)
    pair = jnp.stack([tokens, cotangent])
    placers, slot_rows = [], []
    for rel in range(n_dp):
        columns = lax.dynamic_slice_in_dim(pair, (k ^ rel) * width, width, axis=2)
        mine = columns if rel == 0 else swap(columns, "dp", n_dp, rel)
        blocks = lax.all_gather(mine, "expert", axis=1, tiled=True)
        goal = lax.dynamic_index_in_dim(targets, k ^ rel, axis=0, keepdims=False)
        expert = goal // CAP - x * local_experts
        place = jnp.arange(n_x, dtype=jnp.int32)[:, None] * CAP + goal % CAP
        row = jnp.where((expert >= 0) & (expert < local_experts), expert * slots + place, -1)
        row = row.reshape(1, n_x * rows)
        every = jnp.arange(local_experts * slots, dtype=jnp.int32)[:, None]
        placer = (every == row).astype(BF16)
        placers.append(placer)
        slot_rows.append(
            jnp.einsum("sn,and->asd", placer, blocks, preferred_element_type=F32)
            .astype(BF16)
            .reshape(2, local_experts, slots, width)
        )
    slot_rows = jnp.concatenate(slot_rows, axis=2)
    inputs, grads_in = slot_rows[0], slot_rows[1]

    def act(values, weight):
        return jnp.einsum("esd,edf->esf", values, weight, preferred_element_type=F32).astype(BF16)

    acts = jnp.stack([act(inputs, gate_weight), act(inputs, up_weight), act(grads_in, down_weight)])
    acts = acts.reshape(3, local_experts, n_dp, slots, hidden)
    acts = halving_sum({r: acts[:, :, r] for r in range(n_dp)}, "dp", n_dp)
    grads = doubling_gather(jnp.stack(swiglu_grads(acts[0], acts[1], acts[2])), "dp", n_dp)
    grads = jnp.concatenate(grads, axis=2)
    gate_grad, up_grad = grads[0], grads[1]
    partial_value = jnp.einsum("esf,edf->esd", gate_grad, gate_weight, preferred_element_type=F32)
    partial_value = partial_value + jnp.einsum("esf,edf->esd", up_grad, up_weight, preferred_element_type=F32)
    partial_value = partial_value.astype(BF16).reshape(local_experts, n_dp, slots, width)
    per_token = []
    for rel in range(n_dp):
        flat = partial_value[:, rel].reshape(local_experts * slots, width)
        spread = lax.dot_general(placers[rel], flat, (((0,), (0,)), ((), ())), preferred_element_type=F32)
        spread = spread.astype(BF16).reshape(n_x, rows, width)
        per_token.append(lax.psum_scatter(spread, "expert", scatter_dimension=0, tiled=False))
    per_token = jnp.stack(per_token)
    terms = {r: lax.dynamic_index_in_dim(per_token, k ^ t ^ r, axis=0, keepdims=False) for r in range(n_t)}
    summed = halving_sum(terms, "tensor", n_t).astype(BF16)
    summed = lax.ppermute(
        summed, ("dp", "tensor"), [(i * n_t + j, j * n_t + i) for i in range(n_dp) for j in range(n_t)]
    )
    grad_gate = jnp.einsum("esd,esf->edf", inputs, gate_grad, preferred_element_type=F32).astype(BF16)
    grad_up = jnp.einsum("esd,esf->edf", inputs, up_grad, preferred_element_type=F32).astype(BF16)
    return summed, grad_gate, grad_up


def solution(mesh):
    placed = (
        P(("dp", "expert"), None),
        P(("dp", "expert"), None),
        P(("dp", "expert"), None),
        P("expert", "dp", "tensor"),
        P("expert", "dp", "tensor"),
        P("expert", "dp", "tensor"),
    )
    sizes = tuple(mesh.shape[name] for name in ("dp", "expert", "tensor"))
    return jax.shard_map(
        on_small_slice if sizes == (4, 2, 4) else on_any_slice,
        mesh=mesh,
        in_specs=placed,
        out_specs=(
            P(("dp", "expert"), "tensor"),
            P("expert", "dp", "tensor"),
            P("expert", "dp", "tensor"),
        ),
        check_vma=False,
    )
```

```python
import functools

import jax
import jax.numpy as jnp
from jax import lax
from jax.experimental import pallas as pl
from jax.experimental.pallas import tpu as pltpu
from jax.sharding import PartitionSpec as P

CAP = 8
META = 16
F32 = jnp.float32
BF16 = jnp.bfloat16
VMEM_LIMIT = 24 * 1024 * 1024
SPLIT_VMEM_LIMIT = 63 * 1024 * 1024
PLACE_COST = 1 << 34


def swap(value, axis, count, bit):
    return lax.ppermute(value, axis, [(i, i ^ bit) for i in range(count)])


def whole_spec(shape):
    return pl.BlockSpec(shape, lambda *_: (0,) * len(shape))


def params():
    return pltpu.CompilerParams(vmem_limit_bytes=VMEM_LIMIT)


def split_kernel(width, n_dp, where, ids, tokens, cotangent, *refs):
    outs, (meta, sems) = refs[:-2], refs[-2:]
    k, x = where[0], where[1]
    rows = tokens.shape[0]
    copies = []
    for rel in range(n_dp):
        start = pl.multiple_of((k ^ rel) * width, 128)
        for which, source in enumerate((tokens, cotangent)):
            copy = pltpu.make_async_copy(
                source.at[:, pl.ds(start, width)],
                outs[which * n_dp + rel].at[pl.ds(0, rows), :],
                sems.at[which * n_dp + rel],
            )
            copy.start()
            copies.append(copy)
    along = ids[...].astype(F32)
    line = lax.broadcasted_iota(jnp.int32, (rows, rows), 0)
    lane = lax.broadcasted_iota(jnp.int32, (rows, rows), 1)
    named = jnp.broadcast_to(along, (rows, rows))
    down = jnp.sum(jnp.where(line == lane, named, 0.0), axis=1, keepdims=True)
    earlier = jnp.where((named == down) & (line < lane), 1.0, 0.0)
    place = jnp.sum(earlier, axis=0, keepdims=True) + (x * CAP).astype(F32)
    at = lax.broadcasted_iota(jnp.int32, (META, rows), 0)
    meta[...] = jnp.zeros(meta.shape, BF16)
    meta[:, 0:rows] = jnp.where(at == 0, along, jnp.where(at == 1, place, 0.0)).astype(BF16)
    for rel in range(n_dp):
        copy = pltpu.make_async_copy(meta, outs[rel].at[pl.ds(rows, META), :], sems.at[2 * n_dp + rel])
        copy.start()
        copies.append(copy)
    for copy in copies:
        copy.wait()


def split(where, ids, tokens, cotangent, width, n_dp):
    rows = tokens.shape[0]
    shapes = [(rows + META, width)] * n_dp + [(rows, width)] * n_dp
    anywhere = pl.BlockSpec(memory_space=pl.ANY)
    return pl.pallas_call(
        functools.partial(split_kernel, width, n_dp),
        out_shape=[jax.ShapeDtypeStruct(s, BF16) for s in shapes],
        in_specs=[
            pl.BlockSpec(memory_space=pltpu.SMEM),
            pl.BlockSpec(memory_space=pltpu.VMEM),
            anywhere,
            anywhere,
        ],
        out_specs=[anywhere] * (2 * n_dp),
        scratch_shapes=[pltpu.VMEM((META, width), BF16), pltpu.SemaphoreType.DMA((3 * n_dp,))],
        compiler_params=pltpu.CompilerParams(vmem_limit_bytes=SPLIT_VMEM_LIMIT),
    )(where, ids, tokens, cotangent)


def placer_of(row, slot_count):
    every = lax.broadcasted_iota(jnp.int32, (slot_count, row.shape[1]), 0)
    return (every == row).astype(F32).astype(BF16)


def place_kernel(first, rows, where, mine, others, *refs):
    n_dp = len(mine)
    other = []
    for group in others:
        other += [group] if len(group.shape) == 2 else [group.at[i] for i in range(group.shape[0])]
    if first:
        placed, lines = refs[-2:]
    else:
        lines, placed = refs[0], refs[-1]
    local_experts, slot_rows, width = placed.shape
    slots = slot_rows // n_dp
    for rel in range(n_dp):
        if first:
            pair = [b[0 : rows + META, :] for b in (mine[rel], other[rel])]
            metas = [b[rows:, 0:rows].astype(F32) for b in pair]
            ids = jnp.concatenate([m[0:1] for m in metas], axis=1)
            place = jnp.concatenate([m[1:2] for m in metas], axis=1)
            low = (where[1] * local_experts).astype(F32)
            row = ((ids - low) * slots + place).astype(jnp.int32)
            lines[rel] = jnp.broadcast_to(row, (8, row.shape[1]))
            pair = [b[0:rows] for b in pair]
        else:
            row = lines[rel][0:1]
            pair = [b[...] for b in (mine[rel], other[rel])]
        placer = placer_of(row, local_experts * slots)
        found = jnp.dot(placer, jnp.concatenate(pair, axis=0), preferred_element_type=F32).astype(BF16)
        placed[:, rel * slots : (rel + 1) * slots, :] = found.reshape(local_experts, slots, width)


def place(where, mine, others, lines, rows, local_experts, after):
    first = lines is None
    n_dp, slots = len(mine), 2 * CAP
    width = mine[0].shape[1]
    placed = jax.ShapeDtypeStruct((local_experts, n_dp * slots, width), BF16)
    line = jax.ShapeDtypeStruct((n_dp, 8, 2 * rows), jnp.int32)
    vmem = pl.BlockSpec(memory_space=pltpu.VMEM)
    operands = [*others] + ([] if first else [lines])

    def kernel(where, *refs):
        split_at = n_dp + len(others)
        place_kernel(first, rows, where, refs[:n_dp], refs[n_dp:split_at], *refs[split_at:])

    return pl.pallas_call(
        kernel,
        out_shape=[placed, line] if first else placed,
        in_specs=[pl.BlockSpec(memory_space=pltpu.SMEM)]
        + [vmem] * (n_dp + len(operands))
        + [pl.BlockSpec(memory_space=pl.ANY)] * len(after),
        out_specs=[vmem, vmem] if first else vmem,
        compiler_params=params(),
        cost_estimate=pl.CostEstimate(flops=PLACE_COST, bytes_accessed=4 * rows * width * n_dp, transcendentals=0),
    )(where, *mine, *operands, *after)


def back_kernel(rels, lines, h0, h1, gate, up, own0, own1, other0, other1, near, held, sems):
    parts = (h0, h1)
    local_experts, slots = h0.shape[1], h0.shape[2]
    per_copy = local_experts // sems.shape[1]

    def copy_of(which, at):
        group = pl.ds(at * per_copy, per_copy)
        return pltpu.make_async_copy((gate, up)[which].at[group], near.at[which, group], sems.at[which, at])

    for at in range(sems.shape[1]):
        for which in range(2):
            copy_of(which, at).start()
    for at in range(sems.shape[1]):
        for which in range(2):
            copy_of(which, at).wait()
        for e in range(at * per_copy, (at + 1) * per_copy):
            gate_grad = jnp.concatenate([h[0, e] for h in parts], axis=0)
            up_grad = jnp.concatenate([h[1, e] for h in parts], axis=0)
            value = jnp.dot(gate_grad, near[0, e], preferred_element_type=F32)
            value = value + jnp.dot(up_grad, near[1, e], preferred_element_type=F32)
            value = value.astype(BF16)
            for i in range(2):
                held[i, e * slots : (e + 1) * slots, :] = value[i * slots : (i + 1) * slots]

    rows = own0.shape[0]
    for i, (own, other) in enumerate(((own0, other0), (own1, other1))):
        placer = placer_of(lines[rels[i]][0:1], held.shape[1])
        token_rows = lax.dot_general(
            placer, held[i], (((0,), (0,)), ((), ())), preferred_element_type=F32
        ).astype(BF16)
        own[...] = token_rows[0:rows]
        other[...] = token_rows[rows:]


def back(rels, lines, parts, gate, up, rows):
    local_experts, hidden, width = gate.shape
    slots = parts[0].shape[2]
    vmem = pl.BlockSpec(memory_space=pltpu.VMEM)
    flops = 4 * local_experts * 2 * slots * width * hidden
    return pl.pallas_call(
        functools.partial(back_kernel, rels),
        out_shape=[jax.ShapeDtypeStruct((rows, width), BF16)] * 4,
        in_specs=[vmem] * 3 + [pl.BlockSpec(memory_space=pl.ANY)] * 2,
        out_specs=[vmem] * 4,
        scratch_shapes=[
            pltpu.VMEM((2, local_experts, hidden, width), BF16),
            pltpu.VMEM((2, local_experts * slots, width), BF16),
            pltpu.SemaphoreType.DMA((2, 8 if local_experts % 8 == 0 else 1)),
        ],
        compiler_params=params(),
        cost_estimate=pl.CostEstimate(
            flops=4 * flops, bytes_accessed=2 * local_experts * width * hidden * 2, transcendentals=0
        ),
    )(lines, *parts, gate, up)


def weight_kernel(which, order, placed, h0, h1, h2, h3, out):
    parts = (h0, h1, h2, h3)
    for i in range(out.shape[0]):
        grad = jnp.concatenate([parts[rel][which, i] for rel in order], axis=0)
        out[i] = lax.dot_general(
            grad, placed[i], (((0,), (0,)), ((), ())), preferred_element_type=F32
        ).astype(BF16)


def weight_grad(which, order, placed, parts, per_step):
    local_experts, slot_rows, width = placed.shape
    _, _, slots, hidden = parts[0].shape
    part_spec = pl.BlockSpec((2, per_step, slots, hidden), lambda e: (0, e, 0, 0))
    flops = 2 * local_experts * slot_rows * width * hidden
    return pl.pallas_call(
        functools.partial(weight_kernel, which, order),
        grid=(local_experts // per_step,),
        out_shape=jax.ShapeDtypeStruct((local_experts, hidden, width), BF16),
        in_specs=[pl.BlockSpec((per_step, slot_rows, width), lambda e: (e, 0, 0))] + [part_spec] * len(parts),
        out_specs=pl.BlockSpec((per_step, hidden, width), lambda e: (e, 0, 0)),
        compiler_params=params(),
        cost_estimate=pl.CostEstimate(
            flops=4 * flops, bytes_accessed=local_experts * width * hidden * 2, transcendentals=0
        ),
    )(placed, *parts)


def plus(first, second):
    return first.astype(F32) + second.astype(F32)


def swiglu_grads(gate_act, up_act, hidden_grad):
    sigmoid_gate = jax.nn.sigmoid(gate_act)
    up_grad = (hidden_grad * gate_act * sigmoid_gate).astype(BF16)
    gate_grad = (
        hidden_grad * up_act * sigmoid_gate * (1.0 + gate_act * (1.0 - sigmoid_gate))
    ).astype(BF16)
    return gate_grad, up_grad


def on_small_slice(tokens, cotangent, expert_ids, gate_weight, up_weight, down_weight):
    n_dp, n_x, n_t = 4, 2, 4
    k, x, t = lax.axis_index("dp"), lax.axis_index("expert"), lax.axis_index("tensor")
    width = gate_weight.shape[1]
    rows = tokens.shape[0]
    where = jnp.stack([k, x]).astype(jnp.int32)
    chunks = split(where, expert_ids.reshape(1, rows), tokens, cotangent, width, n_dp)
    def to_owner(value, rel, flip):
        if rel == 0 and flip == 0:
            return value
        pairs = [
            (i * n_x + j, (i ^ rel) * n_x + (j ^ flip)) for i in range(n_dp) for j in range(n_x)
        ]
        return lax.ppermute(value, ("dp", "expert"), pairs)

    own_tokens = [to_owner(c, rel, 0) for rel, c in enumerate(chunks[:n_dp])]
    near_tokens = [to_owner(c, rel, 1) for rel, c in enumerate(chunks[:2])]
    far_tokens, *grads = lax.optimization_barrier((jnp.stack(own_tokens[2:]), *chunks[n_dp:]))
    near_tokens, far_tokens = lax.optimization_barrier((near_tokens, far_tokens))
    far_tokens = swap(far_tokens, "expert", n_x, 1)
    own_grads = [to_owner(c, rel, 0) for rel, c in enumerate(grads)]
    leaving_grads = jnp.stack(own_grads)
    far_tokens, leaving_grads = lax.optimization_barrier((far_tokens, leaving_grads))
    other_grads = swap(leaving_grads, "expert", n_x, 1)
    gate_weight, up_weight, down_weight = (
        jnp.swapaxes(weight, 1, 2) for weight in (gate_weight, up_weight, down_weight)
    )
    local_experts = gate_weight.shape[0]
    order = (0, 1, 2, 3)

    def project(values, weight):
        act = jnp.einsum("esd,ehd->esh", values, weight, preferred_element_type=F32).astype(BF16)
        return jnp.split(act, n_dp, axis=1)

    def near_and_far(act):
        near, far = swap(act[1], "dp", n_dp, 1), swap(act[3], "dp", n_dp, 1)
        return plus(act[0], near), plus(act[2], far).astype(BF16)

    placed, lines = place(where, own_tokens, [*near_tokens, far_tokens], None, rows, local_experts, [leaving_grads])
    gate_near, gate_far = near_and_far(project(placed, gate_weight))
    up_near, up_far = near_and_far(project(placed, up_weight))
    far = jnp.stack([gate_far, up_far])
    there = swap(far, "dp", n_dp, 2)
    placed_grads = place(where, own_grads, [other_grads], lines, rows, local_experts, [far])
    hidden_act = project(placed_grads, down_weight)
    hidden_grad = hidden_act[0].astype(F32)
    for rel in range(1, n_dp):
        hidden_grad = hidden_grad + swap(hidden_act[rel], "dp", n_dp, rel).astype(F32)
    acts = plus(gate_near, there[0]), plus(up_near, there[1])
    part = jnp.stack(swiglu_grads(acts[0], acts[1], hidden_grad))
    far = swap(part, "dp", n_dp, 2)
    beside = swap(part, "dp", n_dp, 1)
    near_back = back((0, 1), lines, [part, beside], gate_weight, up_weight, rows)
    far, near_back = lax.optimization_barrier((far, near_back))
    parts = [part, beside, far, swap(far, "dp", n_dp, 1)]
    far_back = back((2, 3), lines, parts[2:], gate_weight, up_weight, rows)

    def blocks(rels, own0, own1, other0, other1):
        terms = [
            plus(to_owner(own_r, rel, 0), to_owner(other_r, rel, 1)).astype(BF16)
            for rel, own_r, other_r in zip(rels, (own0, own1), (other0, other1))
        ]
        odd = ((k ^ t) & 1) == 1
        keep = jnp.where(odd, terms[1], terms[0])
        leaving = jnp.where(odd, terms[0], terms[1])
        return plus(keep, swap(leaving, "tensor", n_t, 1))

    first, second = blocks((0, 1), *near_back), blocks((2, 3), *far_back)
    swapped = ((k ^ t) & 2) == 2
    keep = jnp.where(swapped, second, first)
    leaving = jnp.where(swapped, first, second).astype(BF16)
    grad_tokens = plus(keep, swap(leaving, "tensor", n_t, 2)).astype(BF16)

    grad_gate = jnp.swapaxes(weight_grad(0, order, placed, parts, 4), 1, 2)
    grad_up = jnp.swapaxes(weight_grad(1, order, placed, parts, 4), 1, 2)
    return grad_tokens, grad_gate, grad_up


def bits_of(count):
    bits = []
    bit = 1
    while bit < count:
        bits.append(bit)
        bit *= 2
    return bits


def halving_sum(parts, axis, count):
    parts = dict(parts)
    for bit in bits_of(count):
        leaving = sorted(r for r in parts if r & bit)
        arrived = swap(jnp.stack([parts[r].astype(BF16) for r in leaving]), axis, count, bit)
        for at, r in enumerate(leaving):
            parts[r ^ bit] = plus(parts[r ^ bit], arrived[at])
            del parts[r]
    return parts[0]


def doubling_gather(value, axis, count):
    held = {0: value}
    for bit in reversed(bits_of(count)):
        known = sorted(held)
        arrived = swap(jnp.stack([held[r] for r in known]), axis, count, bit)
        for at, r in enumerate(known):
            held[r ^ bit] = arrived[at]
    return [held[r] for r in range(count)]


def on_any_slice(tokens, cotangent, expert_ids, gate_weight, up_weight, down_weight):
    n_dp, n_x, n_t = lax.axis_size("dp"), lax.axis_size("expert"), lax.axis_size("tensor")
    k, x, t = lax.axis_index("dp"), lax.axis_index("expert"), lax.axis_index("tensor")
    local_experts, width, hidden = gate_weight.shape
    rows = tokens.shape[0]
    slots = n_x * CAP
    ids_row = expert_ids.reshape(1, rows)
    order = jnp.arange(rows, dtype=jnp.int32)
    earlier = (expert_ids == ids_row) & (order[:, None] < order[None, :])
    position = jnp.sum(earlier.astype(jnp.int32), axis=0)
    target = ids_row[0] * CAP + position
    targets = lax.all_gather(target, ("dp", "expert"), axis=0, tiled=False).reshape(n_dp, n_x, rows)
    pair = jnp.stack([tokens, cotangent])
    placers, slot_rows = [], []
    for rel in range(n_dp):
        columns = lax.dynamic_slice_in_dim(pair, (k ^ rel) * width, width, axis=2)
        mine = columns if rel == 0 else swap(columns, "dp", n_dp, rel)
        blocks = lax.all_gather(mine, "expert", axis=1, tiled=True)
        goal = lax.dynamic_index_in_dim(targets, k ^ rel, axis=0, keepdims=False)
        expert = goal // CAP - x * local_experts
        place = jnp.arange(n_x, dtype=jnp.int32)[:, None] * CAP + goal % CAP
        row = jnp.where((expert >= 0) & (expert < local_experts), expert * slots + place, -1)
        row = row.reshape(1, n_x * rows)
        every = jnp.arange(local_experts * slots, dtype=jnp.int32)[:, None]
        placer = (every == row).astype(BF16)
        placers.append(placer)
        slot_rows.append(
            jnp.einsum("sn,and->asd", placer, blocks, preferred_element_type=F32)
            .astype(BF16)
            .reshape(2, local_experts, slots, width)
        )
    slot_rows = jnp.concatenate(slot_rows, axis=2)
    inputs, grads_in = slot_rows[0], slot_rows[1]

    def act(values, weight):
        return jnp.einsum("esd,edf->esf", values, weight, preferred_element_type=F32).astype(BF16)

    acts = jnp.stack([act(inputs, gate_weight), act(inputs, up_weight), act(grads_in, down_weight)])
    acts = acts.reshape(3, local_experts, n_dp, slots, hidden)
    acts = halving_sum({r: acts[:, :, r] for r in range(n_dp)}, "dp", n_dp)
    grads = doubling_gather(jnp.stack(swiglu_grads(acts[0], acts[1], acts[2])), "dp", n_dp)
    grads = jnp.concatenate(grads, axis=2)
    gate_grad, up_grad = grads[0], grads[1]
    partial_value = jnp.einsum("esf,edf->esd", gate_grad, gate_weight, preferred_element_type=F32)
    partial_value = partial_value + jnp.einsum("esf,edf->esd", up_grad, up_weight, preferred_element_type=F32)
    partial_value = partial_value.astype(BF16).reshape(local_experts, n_dp, slots, width)
    per_token = []
    for rel in range(n_dp):
        flat = partial_value[:, rel].reshape(local_experts * slots, width)
        spread = lax.dot_general(placers[rel], flat, (((0,), (0,)), ((), ())), preferred_element_type=F32)
        spread = spread.astype(BF16).reshape(n_x, rows, width)
        per_token.append(lax.psum_scatter(spread, "expert", scatter_dimension=0, tiled=False))
    per_token = jnp.stack(per_token)
    terms = {r: lax.dynamic_index_in_dim(per_token, k ^ t ^ r, axis=0, keepdims=False) for r in range(n_t)}
    summed = halving_sum(terms, "tensor", n_t).astype(BF16)
    summed = lax.ppermute(
        summed, ("dp", "tensor"), [(i * n_t + j, j * n_t + i) for i in range(n_dp) for j in range(n_t)]
    )
    grad_gate = jnp.einsum("esd,esf->edf", inputs, gate_grad, preferred_element_type=F32).astype(BF16)
    grad_up = jnp.einsum("esd,esf->edf", inputs, up_grad, preferred_element_type=F32).astype(BF16)
    return summed, grad_gate, grad_up


def solution(mesh):
    placed = (
        P(("dp", "expert"), None),
        P(("dp", "expert"), None),
        P(("dp", "expert"), None),
        P("expert", "dp", "tensor"),
        P("expert", "dp", "tensor"),
        P("expert", "dp", "tensor"),
    )
    sizes = tuple(mesh.shape[name] for name in ("dp", "expert", "tensor"))
    return jax.shard_map(
        on_small_slice if sizes == (4, 2, 4) else on_any_slice,
        mesh=mesh,
        in_specs=placed,
        out_specs=(
            P(("dp", "expert"), "tensor"),
            P("expert", "dp", "tensor"),
            P("expert", "dp", "tensor"),
        ),
        check_vma=False,
    )
```

```python
import functools

import jax
import jax.numpy as jnp
from jax import lax
from jax.experimental import pallas as pl
from jax.experimental.pallas import tpu as pltpu
from jax.sharding import PartitionSpec as P

CAP = 8
META = 16
F32 = jnp.float32
BF16 = jnp.bfloat16
MIB = 1024 * 1024
PLACE_COST = 1 << 34


def swap(value, axis, count, bit):
    return lax.ppermute(value, axis, [(i, i ^ bit) for i in range(count)])


def whole_spec(shape):
    return pl.BlockSpec(shape, lambda *_: (0,) * len(shape))


def params(mib=16):
    return pltpu.CompilerParams(vmem_limit_bytes=mib * MIB)


def split_kernel(width, n_dp, where, ids, tokens, *refs):
    outs, (meta, sems) = refs[:-2], refs[-2:]
    k, x = where[0], where[1]
    rows = tokens.shape[0]
    copies = []
    for rel in range(n_dp):
        start = pl.multiple_of((k ^ rel) * width, 128)
        copy = pltpu.make_async_copy(
            tokens.at[:, pl.ds(start, width)], outs[rel].at[pl.ds(0, rows), :], sems.at[rel]
        )
        copy.start()
        copies.append(copy)
    along = ids[...].astype(F32)
    line = lax.broadcasted_iota(jnp.int32, (rows, rows), 0)
    lane = lax.broadcasted_iota(jnp.int32, (rows, rows), 1)
    named = jnp.broadcast_to(along, (rows, rows))
    down = jnp.sum(jnp.where(line == lane, named, 0.0), axis=1, keepdims=True)
    earlier = jnp.where((named == down) & (line < lane), 1.0, 0.0)
    place = jnp.sum(earlier, axis=0, keepdims=True) + (x * CAP).astype(F32)
    at = lax.broadcasted_iota(jnp.int32, (META, rows), 0)
    meta[...] = jnp.zeros(meta.shape, BF16)
    meta[:, 0:rows] = jnp.where(at == 0, along, jnp.where(at == 1, place, 0.0)).astype(BF16)
    for rel in range(n_dp):
        copy = pltpu.make_async_copy(meta, outs[rel].at[pl.ds(rows, META), :], sems.at[n_dp + rel])
        copy.start()
        copies.append(copy)
    for copy in copies:
        copy.wait()


def split(where, ids, tokens, width, n_dp):
    rows = tokens.shape[0]
    anywhere = pl.BlockSpec(memory_space=pl.ANY)
    return pl.pallas_call(
        functools.partial(split_kernel, width, n_dp),
        out_shape=[jax.ShapeDtypeStruct((rows + META, width), BF16)] * n_dp,
        in_specs=[
            pl.BlockSpec(memory_space=pltpu.SMEM),
            pl.BlockSpec(memory_space=pltpu.VMEM),
            anywhere,
        ],
        out_specs=[anywhere] * n_dp,
        scratch_shapes=[pltpu.VMEM((META, width), BF16), pltpu.SemaphoreType.DMA((2 * n_dp,))],
        compiler_params=params(),
    )(where, ids, tokens)


def placer_of(row, slot_count):
    every = lax.broadcasted_iota(jnp.int32, (slot_count, row.shape[1]), 0)
    return (every == row).astype(F32).astype(BF16)


def place_kernel(first, rows, where, mine, others, *refs):
    n_dp = len(mine)
    other = []
    for group in others:
        other += [group] if len(group.shape) == 2 else [group.at[i] for i in range(group.shape[0])]
    if first:
        placed, lines = refs[-2:]
    else:
        lines, placed = refs[0], refs[-1]
    local_experts, slot_rows, width = placed.shape
    slots = slot_rows // n_dp
    for rel in range(n_dp):
        if first:
            pair = [b[0 : rows + META, :] for b in (mine[rel], other[rel])]
            metas = [b[rows:, 0:rows].astype(F32) for b in pair]
            ids = jnp.concatenate([m[0:1] for m in metas], axis=1)
            place = jnp.concatenate([m[1:2] for m in metas], axis=1)
            low = (where[1] * local_experts).astype(F32)
            row = ((ids - low) * slots + place).astype(jnp.int32)
            lines[rel] = jnp.broadcast_to(row, (8, row.shape[1]))
            pair = [b[0:rows] for b in pair]
        else:
            row = lines[rel][0:1]
            pair = [b[...] for b in (mine[rel], other[rel])]
        placer = placer_of(row, local_experts * slots)
        found = jnp.dot(placer, jnp.concatenate(pair, axis=0), preferred_element_type=F32).astype(BF16)
        placed[:, rel * slots : (rel + 1) * slots, :] = found.reshape(local_experts, slots, width)


def place(where, mine, others, lines, rows, local_experts, after):
    first = lines is None
    n_dp, slots = len(mine), 2 * CAP
    width = mine[0].shape[1]
    placed = jax.ShapeDtypeStruct((local_experts, n_dp * slots, width), BF16)
    line = jax.ShapeDtypeStruct((n_dp, 8, 2 * rows), jnp.int32)
    vmem = pl.BlockSpec(memory_space=pltpu.VMEM)
    operands = [*others] + ([] if first else [lines])

    def kernel(where, *refs):
        split_at = n_dp + len(others)
        place_kernel(first, rows, where, refs[:n_dp], refs[n_dp:split_at], *refs[split_at:])

    return pl.pallas_call(
        kernel,
        out_shape=[placed, line] if first else placed,
        in_specs=[pl.BlockSpec(memory_space=pltpu.SMEM)]
        + [vmem] * (n_dp + len(operands))
        + [pl.BlockSpec(memory_space=pl.ANY)] * len(after),
        out_specs=[vmem, vmem] if first else vmem,
        compiler_params=params(),
        cost_estimate=pl.CostEstimate(flops=PLACE_COST, bytes_accessed=4 * rows * width * n_dp, transcendentals=0),
    )(where, *mine, *operands, *after)


def back_kernel(rels, lines, h0, h1, gate, up, own0, own1, other0, other1, near, held, sems):
    parts = (h0, h1)
    local_experts, slots = h0.shape[1], h0.shape[2]
    per_copy = local_experts // sems.shape[1]

    def copy_of(which, at):
        group = pl.ds(at * per_copy, per_copy)
        return pltpu.make_async_copy((gate, up)[which].at[group], near.at[which, group], sems.at[which, at])

    for at in range(sems.shape[1]):
        for which in range(2):
            copy_of(which, at).start()
    for at in range(sems.shape[1]):
        for which in range(2):
            copy_of(which, at).wait()
        for e in range(at * per_copy, (at + 1) * per_copy):
            gate_grad = jnp.concatenate([h[0, e] for h in parts], axis=0)
            up_grad = jnp.concatenate([h[1, e] for h in parts], axis=0)
            value = jnp.dot(gate_grad, near[0, e], preferred_element_type=F32)
            value = value + jnp.dot(up_grad, near[1, e], preferred_element_type=F32)
            value = value.astype(BF16)
            for i in range(2):
                held[i, e * slots : (e + 1) * slots, :] = value[i * slots : (i + 1) * slots]

    rows = own0.shape[0]
    for i, (own, other) in enumerate(((own0, other0), (own1, other1))):
        placer = placer_of(lines[rels[i]][0:1], held.shape[1])
        token_rows = lax.dot_general(
            placer, held[i], (((0,), (0,)), ((), ())), preferred_element_type=F32
        ).astype(BF16)
        own[...] = token_rows[0:rows]
        other[...] = token_rows[rows:]


def back(rels, lines, parts, gate, up, rows):
    local_experts, hidden, width = gate.shape
    slots = parts[0].shape[2]
    vmem = pl.BlockSpec(memory_space=pltpu.VMEM)
    flops = 4 * local_experts * 2 * slots * width * hidden
    return pl.pallas_call(
        functools.partial(back_kernel, rels),
        out_shape=[jax.ShapeDtypeStruct((rows, width), BF16)] * 4,
        in_specs=[vmem] * 3 + [pl.BlockSpec(memory_space=pl.ANY)] * 2,
        out_specs=[vmem] * 4,
        scratch_shapes=[
            pltpu.VMEM((2, local_experts, hidden, width), BF16),
            pltpu.VMEM((2, local_experts * slots, width), BF16),
            pltpu.SemaphoreType.DMA((2, 8 if local_experts % 8 == 0 else 1)),
        ],
        compiler_params=params(48),
        cost_estimate=pl.CostEstimate(
            flops=4 * flops, bytes_accessed=2 * local_experts * width * hidden * 2, transcendentals=0
        ),
    )(lines, *parts, gate, up)


def weight_kernel(which, order, placed, h0, h1, h2, h3, out):
    parts = (h0, h1, h2, h3)
    for i in range(out.shape[0]):
        grad = jnp.concatenate([parts[rel][which, i] for rel in order], axis=0)
        out[i] = lax.dot_general(
            grad, placed[i], (((0,), (0,)), ((), ())), preferred_element_type=F32
        ).astype(BF16)


def weight_grad(which, order, placed, parts, per_step):
    local_experts, slot_rows, width = placed.shape
    _, _, slots, hidden = parts[0].shape
    part_spec = pl.BlockSpec((2, per_step, slots, hidden), lambda e: (0, e, 0, 0))
    flops = 2 * local_experts * slot_rows * width * hidden
    return pl.pallas_call(
        functools.partial(weight_kernel, which, order),
        grid=(local_experts // per_step,),
        out_shape=jax.ShapeDtypeStruct((local_experts, hidden, width), BF16),
        in_specs=[pl.BlockSpec((per_step, slot_rows, width), lambda e: (e, 0, 0))] + [part_spec] * len(parts),
        out_specs=pl.BlockSpec((per_step, hidden, width), lambda e: (e, 0, 0)),
        compiler_params=params(48),
        cost_estimate=pl.CostEstimate(
            flops=4 * flops, bytes_accessed=local_experts * width * hidden * 2, transcendentals=0
        ),
    )(placed, *parts)


def plus(first, second):
    return first.astype(F32) + second.astype(F32)


def swiglu_grads(gate_act, up_act, hidden_grad):
    sigmoid_gate = jax.nn.sigmoid(gate_act)
    up_grad = (hidden_grad * gate_act * sigmoid_gate).astype(BF16)
    gate_grad = (
        hidden_grad * up_act * sigmoid_gate * (1.0 + gate_act * (1.0 - sigmoid_gate))
    ).astype(BF16)
    return gate_grad, up_grad


def on_small_slice(tokens, cotangent, expert_ids, gate_weight, up_weight, down_weight):
    n_dp, n_x, n_t = 4, 2, 4
    k, x, t = lax.axis_index("dp"), lax.axis_index("expert"), lax.axis_index("tensor")
    width = gate_weight.shape[1]
    rows = tokens.shape[0]
    where = jnp.stack([k, x]).astype(jnp.int32)
    chunks = split(where, expert_ids.reshape(1, rows), tokens, width, n_dp)
    def to_owner(value, rel, flip):
        if rel == 0 and flip == 0:
            return value
        pairs = [
            (i * n_x + j, (i ^ rel) * n_x + (j ^ flip)) for i in range(n_dp) for j in range(n_x)
        ]
        return lax.ppermute(value, ("dp", "expert"), pairs)

    own_tokens = [to_owner(c, rel, 0) for rel, c in enumerate(chunks)]
    near_tokens = [to_owner(c, rel, 1) for rel, c in enumerate(chunks[:2])]
    far_tokens, cotangent = lax.optimization_barrier((jnp.stack(own_tokens[2:]), cotangent))
    grads = [lax.dynamic_slice_in_dim(cotangent, (k ^ rel) * width, width, axis=1) for rel in range(n_dp)]
    near_tokens, far_tokens = lax.optimization_barrier((near_tokens, far_tokens))
    far_tokens = swap(far_tokens, "expert", n_x, 1)
    own_grads = [to_owner(c, rel, 0) for rel, c in enumerate(grads)]
    leaving_grads = jnp.stack(own_grads)
    far_tokens, leaving_grads = lax.optimization_barrier((far_tokens, leaving_grads))
    other_grads = swap(leaving_grads, "expert", n_x, 1)
    gate_weight, up_weight, down_weight = (
        jnp.swapaxes(weight, 1, 2) for weight in (gate_weight, up_weight, down_weight)
    )
    local_experts = gate_weight.shape[0]
    order = (0, 1, 2, 3)

    def project(values, weight):
        act = jnp.einsum("esd,ehd->esh", values, weight, preferred_element_type=F32).astype(BF16)
        return jnp.split(act, n_dp, axis=1)

    def near_and_far(act):
        near, far = swap(act[1], "dp", n_dp, 1), swap(act[3], "dp", n_dp, 1)
        return plus(act[0], near), plus(act[2], far).astype(BF16)

    placed, lines = place(where, own_tokens, [*near_tokens, far_tokens], None, rows, local_experts, [leaving_grads])
    gate_near, gate_far = near_and_far(project(placed, gate_weight))
    up_near, up_far = near_and_far(project(placed, up_weight))
    far = jnp.stack([gate_far, up_far])
    there = swap(far, "dp", n_dp, 2)
    placed_grads = place(where, own_grads, [other_grads], lines, rows, local_experts, [far])
    hidden_act = project(placed_grads, down_weight)
    hidden_grad = hidden_act[0].astype(F32)
    for rel in range(1, n_dp):
        hidden_grad = hidden_grad + swap(hidden_act[rel], "dp", n_dp, rel).astype(F32)
    acts = plus(gate_near, there[0]), plus(up_near, there[1])
    part = jnp.stack(swiglu_grads(acts[0], acts[1], hidden_grad))
    far = swap(part, "dp", n_dp, 2)
    beside = swap(part, "dp", n_dp, 1)
    near_back = back((0, 1), lines, [part, beside], gate_weight, up_weight, rows)
    far, near_back = lax.optimization_barrier((far, near_back))
    parts = [part, beside, far, swap(far, "dp", n_dp, 1)]
    far_back = back((2, 3), lines, parts[2:], gate_weight, up_weight, rows)

    def blocks(rels, own0, own1, other0, other1):
        terms = [
            plus(to_owner(own_r, rel, 0), to_owner(other_r, rel, 1)).astype(BF16)
            for rel, own_r, other_r in zip(rels, (own0, own1), (other0, other1))
        ]
        odd = ((k ^ t) & 1) == 1
        keep = jnp.where(odd, terms[1], terms[0])
        leaving = jnp.where(odd, terms[0], terms[1])
        return plus(keep, swap(leaving, "tensor", n_t, 1))

    first, second = blocks((0, 1), *near_back), blocks((2, 3), *far_back)
    swapped = ((k ^ t) & 2) == 2
    keep = jnp.where(swapped, second, first)
    leaving = jnp.where(swapped, first, second).astype(BF16)
    grad_tokens = plus(keep, swap(leaving, "tensor", n_t, 2)).astype(BF16)

    grad_gate = jnp.swapaxes(weight_grad(0, order, placed, parts, 4), 1, 2)
    grad_up = jnp.swapaxes(weight_grad(1, order, placed, parts, 4), 1, 2)
    return grad_tokens, grad_gate, grad_up


def bits_of(count):
    bits = []
    bit = 1
    while bit < count:
        bits.append(bit)
        bit *= 2
    return bits


def halving_sum(parts, axis, count):
    parts = dict(parts)
    for bit in bits_of(count):
        leaving = sorted(r for r in parts if r & bit)
        arrived = swap(jnp.stack([parts[r].astype(BF16) for r in leaving]), axis, count, bit)
        for at, r in enumerate(leaving):
            parts[r ^ bit] = plus(parts[r ^ bit], arrived[at])
            del parts[r]
    return parts[0]


def doubling_gather(value, axis, count):
    held = {0: value}
    for bit in reversed(bits_of(count)):
        known = sorted(held)
        arrived = swap(jnp.stack([held[r] for r in known]), axis, count, bit)
        for at, r in enumerate(known):
            held[r ^ bit] = arrived[at]
    return [held[r] for r in range(count)]


def on_any_slice(tokens, cotangent, expert_ids, gate_weight, up_weight, down_weight):
    n_dp, n_x, n_t = lax.axis_size("dp"), lax.axis_size("expert"), lax.axis_size("tensor")
    k, x, t = lax.axis_index("dp"), lax.axis_index("expert"), lax.axis_index("tensor")
    local_experts, width, hidden = gate_weight.shape
    rows = tokens.shape[0]
    slots = n_x * CAP
    ids_row = expert_ids.reshape(1, rows)
    order = jnp.arange(rows, dtype=jnp.int32)
    earlier = (expert_ids == ids_row) & (order[:, None] < order[None, :])
    position = jnp.sum(earlier.astype(jnp.int32), axis=0)
    target = ids_row[0] * CAP + position
    targets = lax.all_gather(target, ("dp", "expert"), axis=0, tiled=False).reshape(n_dp, n_x, rows)
    pair = jnp.stack([tokens, cotangent])
    placers, slot_rows = [], []
    for rel in range(n_dp):
        columns = lax.dynamic_slice_in_dim(pair, (k ^ rel) * width, width, axis=2)
        mine = columns if rel == 0 else swap(columns, "dp", n_dp, rel)
        blocks = lax.all_gather(mine, "expert", axis=1, tiled=True)
        goal = lax.dynamic_index_in_dim(targets, k ^ rel, axis=0, keepdims=False)
        expert = goal // CAP - x * local_experts
        place = jnp.arange(n_x, dtype=jnp.int32)[:, None] * CAP + goal % CAP
        row = jnp.where((expert >= 0) & (expert < local_experts), expert * slots + place, -1)
        row = row.reshape(1, n_x * rows)
        every = jnp.arange(local_experts * slots, dtype=jnp.int32)[:, None]
        placer = (every == row).astype(BF16)
        placers.append(placer)
        slot_rows.append(
            jnp.einsum("sn,and->asd", placer, blocks, preferred_element_type=F32)
            .astype(BF16)
            .reshape(2, local_experts, slots, width)
        )
    slot_rows = jnp.concatenate(slot_rows, axis=2)
    inputs, grads_in = slot_rows[0], slot_rows[1]

    def act(values, weight):
        return jnp.einsum("esd,edf->esf", values, weight, preferred_element_type=F32).astype(BF16)

    acts = jnp.stack([act(inputs, gate_weight), act(inputs, up_weight), act(grads_in, down_weight)])
    acts = acts.reshape(3, local_experts, n_dp, slots, hidden)
    acts = halving_sum({r: acts[:, :, r] for r in range(n_dp)}, "dp", n_dp)
    grads = doubling_gather(jnp.stack(swiglu_grads(acts[0], acts[1], acts[2])), "dp", n_dp)
    grads = jnp.concatenate(grads, axis=2)
    gate_grad, up_grad = grads[0], grads[1]
    partial_value = jnp.einsum("esf,edf->esd", gate_grad, gate_weight, preferred_element_type=F32)
    partial_value = partial_value + jnp.einsum("esf,edf->esd", up_grad, up_weight, preferred_element_type=F32)
    partial_value = partial_value.astype(BF16).reshape(local_experts, n_dp, slots, width)
    per_token = []
    for rel in range(n_dp):
        flat = partial_value[:, rel].reshape(local_experts * slots, width)
        spread = lax.dot_general(placers[rel], flat, (((0,), (0,)), ((), ())), preferred_element_type=F32)
        spread = spread.astype(BF16).reshape(n_x, rows, width)
        per_token.append(lax.psum_scatter(spread, "expert", scatter_dimension=0, tiled=False))
    per_token = jnp.stack(per_token)
    terms = {r: lax.dynamic_index_in_dim(per_token, k ^ t ^ r, axis=0, keepdims=False) for r in range(n_t)}
    summed = halving_sum(terms, "tensor", n_t).astype(BF16)
    summed = lax.ppermute(
        summed, ("dp", "tensor"), [(i * n_t + j, j * n_t + i) for i in range(n_dp) for j in range(n_t)]
    )
    grad_gate = jnp.einsum("esd,esf->edf", inputs, gate_grad, preferred_element_type=F32).astype(BF16)
    grad_up = jnp.einsum("esd,esf->edf", inputs, up_grad, preferred_element_type=F32).astype(BF16)
    return summed, grad_gate, grad_up


def solution(mesh):
    placed = (
        P(("dp", "expert"), None),
        P(("dp", "expert"), None),
        P(("dp", "expert"), None),
        P("expert", "dp", "tensor"),
        P("expert", "dp", "tensor"),
        P("expert", "dp", "tensor"),
    )
    sizes = tuple(mesh.shape[name] for name in ("dp", "expert", "tensor"))
    return jax.shard_map(
        on_small_slice if sizes == (4, 2, 4) else on_any_slice,
        mesh=mesh,
        in_specs=placed,
        out_specs=(
            P(("dp", "expert"), "tensor"),
            P("expert", "dp", "tensor"),
            P("expert", "dp", "tensor"),
        ),
        check_vma=False,
    )
```

```python
import functools

import jax
import jax.numpy as jnp
from jax import lax
from jax.experimental import pallas as pl
from jax.experimental.pallas import tpu as pltpu
from jax.sharding import PartitionSpec as P

CAP = 8
META = 16
F32 = jnp.float32
BF16 = jnp.bfloat16
MIB = 1024 * 1024
PLACE_COST = 1 << 34


def swap(value, axis, count, bit):
    return lax.ppermute(value, axis, [(i, i ^ bit) for i in range(count)])


def whole_spec(shape):
    return pl.BlockSpec(shape, lambda *_: (0,) * len(shape))


def params(mib=16):
    return pltpu.CompilerParams(vmem_limit_bytes=mib * MIB)


def split_kernel(width, n_dp, where, ids, tokens, *refs):
    outs, (meta, sems) = refs[:-2], refs[-2:]
    k, x = where[0], where[1]
    rows = tokens.shape[0]
    copies = []
    for rel in range(n_dp):
        start = pl.multiple_of((k ^ rel) * width, 128)
        copy = pltpu.make_async_copy(
            tokens.at[:, pl.ds(start, width)], outs[rel].at[pl.ds(0, rows), :], sems.at[rel]
        )
        copy.start()
        copies.append(copy)
    along = ids[...].astype(F32)
    line = lax.broadcasted_iota(jnp.int32, (rows, rows), 0)
    lane = lax.broadcasted_iota(jnp.int32, (rows, rows), 1)
    named = jnp.broadcast_to(along, (rows, rows))
    down = jnp.sum(jnp.where(line == lane, named, 0.0), axis=1, keepdims=True)
    earlier = jnp.where((named == down) & (line < lane), 1.0, 0.0)
    place = jnp.sum(earlier, axis=0, keepdims=True) + (x * CAP).astype(F32)
    at = lax.broadcasted_iota(jnp.int32, (META, rows), 0)
    meta[...] = jnp.zeros(meta.shape, BF16)
    meta[:, 0:rows] = jnp.where(at == 0, along, jnp.where(at == 1, place, 0.0)).astype(BF16)
    for rel in range(n_dp):
        copy = pltpu.make_async_copy(meta, outs[rel].at[pl.ds(rows, META), :], sems.at[n_dp + rel])
        copy.start()
        copies.append(copy)
    for copy in copies:
        copy.wait()


def split(where, ids, tokens, width, n_dp):
    rows = tokens.shape[0]
    anywhere = pl.BlockSpec(memory_space=pl.ANY)
    return pl.pallas_call(
        functools.partial(split_kernel, width, n_dp),
        out_shape=[jax.ShapeDtypeStruct((rows + META, width), BF16)] * n_dp,
        in_specs=[
            pl.BlockSpec(memory_space=pltpu.SMEM),
            pl.BlockSpec(memory_space=pltpu.VMEM),
            anywhere,
        ],
        out_specs=[anywhere] * n_dp,
        scratch_shapes=[pltpu.VMEM((META, width), BF16), pltpu.SemaphoreType.DMA((2 * n_dp,))],
        compiler_params=params(),
    )(where, ids, tokens)


def placer_of(row, slot_count):
    every = lax.broadcasted_iota(jnp.int32, (slot_count, row.shape[1]), 0)
    return (every == row).astype(F32).astype(BF16)


def place_kernel(first, rows, where, mine, others, *refs):
    n_dp = len(mine)
    other = []
    for group in others:
        other += [group] if len(group.shape) == 2 else [group.at[i] for i in range(group.shape[0])]
    if first:
        placed, lines = refs[-2:]
    else:
        lines, placed = refs[0], refs[-1]
    local_experts, slot_rows, width = placed.shape
    slots = slot_rows // n_dp
    for rel in range(n_dp):
        if first:
            pair = [b[0 : rows + META, :] for b in (mine[rel], other[rel])]
            metas = [b[rows:, 0:rows].astype(F32) for b in pair]
            ids = jnp.concatenate([m[0:1] for m in metas], axis=1)
            place = jnp.concatenate([m[1:2] for m in metas], axis=1)
            low = (where[1] * local_experts).astype(F32)
            row = ((ids - low) * slots + place).astype(jnp.int32)
            lines[rel] = jnp.broadcast_to(row, (8, row.shape[1]))
            pair = [b[0:rows] for b in pair]
        else:
            row = lines[rel][0:1]
            pair = [b[...] for b in (mine[rel], other[rel])]
        placer = placer_of(row, local_experts * slots)
        found = jnp.dot(placer, jnp.concatenate(pair, axis=0), preferred_element_type=F32).astype(BF16)
        placed[:, rel * slots : (rel + 1) * slots, :] = found.reshape(local_experts, slots, width)


def place(where, mine, others, lines, rows, local_experts, after):
    first = lines is None
    n_dp, slots = len(mine), 2 * CAP
    width = mine[0].shape[1]
    placed = jax.ShapeDtypeStruct((local_experts, n_dp * slots, width), BF16)
    line = jax.ShapeDtypeStruct((n_dp, 8, 2 * rows), jnp.int32)
    vmem = pl.BlockSpec(memory_space=pltpu.VMEM)
    operands = [*others] + ([] if first else [lines])

    def kernel(where, *refs):
        split_at = n_dp + len(others)
        place_kernel(first, rows, where, refs[:n_dp], refs[n_dp:split_at], *refs[split_at:])

    return pl.pallas_call(
        kernel,
        out_shape=[placed, line] if first else placed,
        in_specs=[pl.BlockSpec(memory_space=pltpu.SMEM)]
        + [vmem] * (n_dp + len(operands))
        + [pl.BlockSpec(memory_space=pl.ANY)] * len(after),
        out_specs=[vmem, vmem] if first else vmem,
        compiler_params=params(48),
        cost_estimate=pl.CostEstimate(flops=PLACE_COST, bytes_accessed=4 * rows * width * n_dp, transcendentals=0),
    )(where, *mine, *operands, *after)


def back_kernel(rels, lines, h0, h1, gate, up, own0, own1, other0, other1, near, held, sems):
    parts = (h0, h1)
    local_experts, slots, _ = h0.shape
    hidden = gate.shape[1]
    per_copy = local_experts // sems.shape[1]

    def copy_of(which, at):
        group = pl.ds(at * per_copy, per_copy)
        rows = pl.ds(which * hidden, hidden)
        return pltpu.make_async_copy((gate, up)[which].at[group], near.at[group, rows], sems.at[which, at])

    for at in range(sems.shape[1]):
        for which in range(2):
            copy_of(which, at).start()
    for at in range(sems.shape[1]):
        for which in range(2):
            copy_of(which, at).wait()
        for e in range(at * per_copy, (at + 1) * per_copy):
            grads = jnp.concatenate([h[e] for h in parts], axis=0)
            value = jnp.dot(grads, near[e], preferred_element_type=F32).astype(BF16)
            for i in range(2):
                held[i, e * slots : (e + 1) * slots, :] = value[i * slots : (i + 1) * slots]

    rows = own0.shape[0]
    for i, (own, other) in enumerate(((own0, other0), (own1, other1))):
        placer = placer_of(lines[rels[i]][0:1], held.shape[1])
        token_rows = lax.dot_general(
            placer, held[i], (((0,), (0,)), ((), ())), preferred_element_type=F32
        ).astype(BF16)
        own[...] = token_rows[0:rows]
        other[...] = token_rows[rows:]


def back(rels, lines, parts, gate, up, rows):
    local_experts, hidden, width = gate.shape
    slots = parts[0].shape[1]
    vmem = pl.BlockSpec(memory_space=pltpu.VMEM)
    flops = 4 * local_experts * 2 * slots * width * hidden
    return pl.pallas_call(
        functools.partial(back_kernel, rels),
        out_shape=[jax.ShapeDtypeStruct((rows, width), BF16)] * 4,
        in_specs=[vmem] * 3 + [pl.BlockSpec(memory_space=pl.ANY)] * 2,
        out_specs=[vmem] * 4,
        scratch_shapes=[
            pltpu.VMEM((local_experts, 2 * hidden, width), BF16),
            pltpu.VMEM((2, local_experts * slots, width), BF16),
            pltpu.SemaphoreType.DMA((2, 8 if local_experts % 8 == 0 else 1)),
        ],
        compiler_params=params(48),
        cost_estimate=pl.CostEstimate(
            flops=4 * flops, bytes_accessed=2 * local_experts * width * hidden * 2, transcendentals=0
        ),
    )(lines, *parts, gate, up)


def weight_kernel(placed, h0, h1, h2, h3, gate, up):
    hidden = gate.shape[1]
    for i in range(gate.shape[0]):
        grads = jnp.concatenate([h[i] for h in (h0, h1, h2, h3)], axis=0)
        both = lax.dot_general(
            grads, placed[i], (((0,), (0,)), ((), ())), preferred_element_type=F32
        ).astype(BF16)
        gate[i] = both[0:hidden]
        up[i] = both[hidden:]


def weight_grads(placed, parts, per_step):
    local_experts, slot_rows, width = placed.shape
    _, slots, both = parts[0].shape
    hidden = both // 2
    part_spec = pl.BlockSpec((per_step, slots, both), lambda e: (e, 0, 0))
    out_spec = pl.BlockSpec((per_step, hidden, width), lambda e: (e, 0, 0))
    flops = 2 * local_experts * slot_rows * width * both
    return pl.pallas_call(
        weight_kernel,
        grid=(local_experts // per_step,),
        out_shape=[jax.ShapeDtypeStruct((local_experts, hidden, width), BF16)] * 2,
        in_specs=[pl.BlockSpec((per_step, slot_rows, width), lambda e: (e, 0, 0))] + [part_spec] * len(parts),
        out_specs=[out_spec] * 2,
        compiler_params=params(48),
        cost_estimate=pl.CostEstimate(
            flops=4 * flops, bytes_accessed=local_experts * width * both * 2, transcendentals=0
        ),
    )(placed, *parts)


def plus(first, second):
    return first.astype(F32) + second.astype(F32)


def swiglu_grads(gate_act, up_act, hidden_grad):
    sigmoid_gate = jax.nn.sigmoid(gate_act)
    up_grad = (hidden_grad * gate_act * sigmoid_gate).astype(BF16)
    gate_grad = (
        hidden_grad * up_act * sigmoid_gate * (1.0 + gate_act * (1.0 - sigmoid_gate))
    ).astype(BF16)
    return gate_grad, up_grad


def on_small_slice(tokens, cotangent, expert_ids, gate_weight, up_weight, down_weight):
    n_dp, n_x, n_t = 4, 2, 4
    k, x, t = lax.axis_index("dp"), lax.axis_index("expert"), lax.axis_index("tensor")
    width = gate_weight.shape[1]
    rows = tokens.shape[0]
    where = jnp.stack([k, x]).astype(jnp.int32)
    chunks = split(where, expert_ids.reshape(1, rows), tokens, width, n_dp)
    def to_owner(value, rel, flip):
        if rel == 0 and flip == 0:
            return value
        pairs = [
            (i * n_x + j, (i ^ rel) * n_x + (j ^ flip)) for i in range(n_dp) for j in range(n_x)
        ]
        return lax.ppermute(value, ("dp", "expert"), pairs)

    own_tokens = [to_owner(c, rel, 0) for rel, c in enumerate(chunks)]
    near_tokens = [to_owner(c, rel, 1) for rel, c in enumerate(chunks[:2])]
    grads = [lax.dynamic_slice_in_dim(cotangent, (k ^ rel) * width, width, axis=1) for rel in range(n_dp)]
    far_tokens, grads = lax.optimization_barrier((own_tokens[2:], grads))
    near_tokens, far_tokens = lax.optimization_barrier((near_tokens, far_tokens))
    far_tokens = [swap(c, "expert", n_x, 1) for c in far_tokens]
    own_grads = [to_owner(c, rel, 0) for rel, c in enumerate(grads)]
    leaving_grads = jnp.stack(own_grads)
    far_tokens, leaving_grads = lax.optimization_barrier((far_tokens, leaving_grads))
    other_grads = swap(leaving_grads, "expert", n_x, 1)
    gate_weight, up_weight, down_weight = (
        jnp.swapaxes(weight, 1, 2) for weight in (gate_weight, up_weight, down_weight)
    )
    local_experts = gate_weight.shape[0]

    def project(values, weight):
        act = jnp.einsum("esd,ehd->esh", values, weight, preferred_element_type=F32).astype(BF16)
        return jnp.split(act, n_dp, axis=1)

    def near_and_far(act):
        near, far = swap(act[1], "dp", n_dp, 1), swap(act[3], "dp", n_dp, 1)
        return plus(act[0], near), plus(act[2], far).astype(BF16)

    placed, lines = place(where, own_tokens, near_tokens + far_tokens, None, rows, local_experts, [leaving_grads])
    gate_near, gate_far = near_and_far(project(placed, gate_weight))
    up_near, up_far = near_and_far(project(placed, up_weight))
    far = jnp.stack([gate_far, up_far])
    there = swap(far, "dp", n_dp, 2)
    placed_grads = place(where, own_grads, [other_grads], lines, rows, local_experts, [far])
    hidden_act = project(placed_grads, down_weight)
    beside, there = lax.optimization_barrier((swap(hidden_act[3], "dp", n_dp, 1), there))
    hidden_far = plus(hidden_act[2], beside).astype(BF16)
    hidden_near = plus(hidden_act[0], swap(hidden_act[1], "dp", n_dp, 1))
    gate_act, up_act = plus(gate_near, there[0]), plus(up_near, there[1])
    sigmoid_gate = jax.nn.sigmoid(gate_act)
    up_factor = gate_act * sigmoid_gate
    gate_factor = up_act * sigmoid_gate * (1.0 + gate_act * (1.0 - sigmoid_gate))
    hidden_grad = plus(hidden_near, swap(hidden_far, "dp", n_dp, 2))
    part = jnp.concatenate([hidden_grad * gate_factor, hidden_grad * up_factor], axis=2).astype(BF16)
    far = swap(part, "dp", n_dp, 2)
    beside = swap(part, "dp", n_dp, 1)
    near_back = back((0, 1), lines, [part, beside], gate_weight, up_weight, rows)
    far, _ = lax.optimization_barrier((far, near_back[0]))
    parts = [part, beside, far, swap(far, "dp", n_dp, 1)]
    far_back = back((2, 3), lines, parts[2:], gate_weight, up_weight, rows)
    weight_grad = weight_grads(placed, parts, 4)

    def blocks(rels, after, own0, own1, other0, other1):
        terms = [
            plus(to_owner(own_r, rel, 0), to_owner(other_r, rel, 1)).astype(BF16)
            for rel, own_r, other_r in zip(rels, (own0, own1), (other0, other1))
        ]
        odd = ((k ^ t) & 1) == 1
        keep = jnp.where(odd, terms[1], terms[0])
        leaving = jnp.where(odd, terms[0], terms[1])
        leaving, _ = lax.optimization_barrier((leaving, after))
        return plus(keep, swap(leaving, "tensor", n_t, 1))

    first, second = blocks((0, 1), [], *near_back), blocks((2, 3), weight_grad, *far_back)
    swapped = ((k ^ t) & 2) == 2
    keep = jnp.where(swapped, second, first)
    leaving = jnp.where(swapped, first, second).astype(BF16)
    grad_tokens = plus(keep, swap(leaving, "tensor", n_t, 2)).astype(BF16)

    grad_gate, grad_up = (jnp.swapaxes(grad, 1, 2) for grad in weight_grad)
    return grad_tokens, grad_gate, grad_up


def bits_of(count):
    bits = []
    bit = 1
    while bit < count:
        bits.append(bit)
        bit *= 2
    return bits


def halving_sum(parts, axis, count):
    parts = dict(parts)
    for bit in bits_of(count):
        leaving = sorted(r for r in parts if r & bit)
        arrived = swap(jnp.stack([parts[r].astype(BF16) for r in leaving]), axis, count, bit)
        for at, r in enumerate(leaving):
            parts[r ^ bit] = plus(parts[r ^ bit], arrived[at])
            del parts[r]
    return parts[0]


def doubling_gather(value, axis, count):
    held = {0: value}
    for bit in reversed(bits_of(count)):
        known = sorted(held)
        arrived = swap(jnp.stack([held[r] for r in known]), axis, count, bit)
        for at, r in enumerate(known):
            held[r ^ bit] = arrived[at]
    return [held[r] for r in range(count)]


def on_any_slice(tokens, cotangent, expert_ids, gate_weight, up_weight, down_weight):
    n_dp, n_x, n_t = lax.axis_size("dp"), lax.axis_size("expert"), lax.axis_size("tensor")
    k, x, t = lax.axis_index("dp"), lax.axis_index("expert"), lax.axis_index("tensor")
    local_experts, width, hidden = gate_weight.shape
    rows = tokens.shape[0]
    slots = n_x * CAP
    ids_row = expert_ids.reshape(1, rows)
    order = jnp.arange(rows, dtype=jnp.int32)
    earlier = (expert_ids == ids_row) & (order[:, None] < order[None, :])
    position = jnp.sum(earlier.astype(jnp.int32), axis=0)
    target = ids_row[0] * CAP + position
    targets = lax.all_gather(target, ("dp", "expert"), axis=0, tiled=False).reshape(n_dp, n_x, rows)
    pair = jnp.stack([tokens, cotangent])
    placers, slot_rows = [], []
    for rel in range(n_dp):
        columns = lax.dynamic_slice_in_dim(pair, (k ^ rel) * width, width, axis=2)
        mine = columns if rel == 0 else swap(columns, "dp", n_dp, rel)
        blocks = lax.all_gather(mine, "expert", axis=1, tiled=True)
        goal = lax.dynamic_index_in_dim(targets, k ^ rel, axis=0, keepdims=False)
        expert = goal // CAP - x * local_experts
        place = jnp.arange(n_x, dtype=jnp.int32)[:, None] * CAP + goal % CAP
        row = jnp.where((expert >= 0) & (expert < local_experts), expert * slots + place, -1)
        row = row.reshape(1, n_x * rows)
        every = jnp.arange(local_experts * slots, dtype=jnp.int32)[:, None]
        placer = (every == row).astype(BF16)
        placers.append(placer)
        slot_rows.append(
            jnp.einsum("sn,and->asd", placer, blocks, preferred_element_type=F32)
            .astype(BF16)
            .reshape(2, local_experts, slots, width)
        )
    slot_rows = jnp.concatenate(slot_rows, axis=2)
    inputs, grads_in = slot_rows[0], slot_rows[1]

    def act(values, weight):
        return jnp.einsum("esd,edf->esf", values, weight, preferred_element_type=F32).astype(BF16)

    acts = jnp.stack([act(inputs, gate_weight), act(inputs, up_weight), act(grads_in, down_weight)])
    acts = acts.reshape(3, local_experts, n_dp, slots, hidden)
    acts = halving_sum({r: acts[:, :, r] for r in range(n_dp)}, "dp", n_dp)
    grads = doubling_gather(jnp.stack(swiglu_grads(acts[0], acts[1], acts[2])), "dp", n_dp)
    grads = jnp.concatenate(grads, axis=2)
    gate_grad, up_grad = grads[0], grads[1]
    partial_value = jnp.einsum("esf,edf->esd", gate_grad, gate_weight, preferred_element_type=F32)
    partial_value = partial_value + jnp.einsum("esf,edf->esd", up_grad, up_weight, preferred_element_type=F32)
    partial_value = partial_value.astype(BF16).reshape(local_experts, n_dp, slots, width)
    per_token = []
    for rel in range(n_dp):
        flat = partial_value[:, rel].reshape(local_experts * slots, width)
        spread = lax.dot_general(placers[rel], flat, (((0,), (0,)), ((), ())), preferred_element_type=F32)
        spread = spread.astype(BF16).reshape(n_x, rows, width)
        per_token.append(lax.psum_scatter(spread, "expert", scatter_dimension=0, tiled=False))
    per_token = jnp.stack(per_token)
    terms = {r: lax.dynamic_index_in_dim(per_token, k ^ t ^ r, axis=0, keepdims=False) for r in range(n_t)}
    summed = halving_sum(terms, "tensor", n_t).astype(BF16)
    summed = lax.ppermute(
        summed, ("dp", "tensor"), [(i * n_t + j, j * n_t + i) for i in range(n_dp) for j in range(n_t)]
    )
    grad_gate = jnp.einsum("esd,esf->edf", inputs, gate_grad, preferred_element_type=F32).astype(BF16)
    grad_up = jnp.einsum("esd,esf->edf", inputs, up_grad, preferred_element_type=F32).astype(BF16)
    return summed, grad_gate, grad_up


def solution(mesh):
    placed = (
        P(("dp", "expert"), None),
        P(("dp", "expert"), None),
        P(("dp", "expert"), None),
        P("expert", "dp", "tensor"),
        P("expert", "dp", "tensor"),
        P("expert", "dp", "tensor"),
    )
    sizes = tuple(mesh.shape[name] for name in ("dp", "expert", "tensor"))
    return jax.shard_map(
        on_small_slice if sizes == (4, 2, 4) else on_any_slice,
        mesh=mesh,
        in_specs=placed,
        out_specs=(
            P(("dp", "expert"), "tensor"),
            P("expert", "dp", "tensor"),
            P("expert", "dp", "tensor"),
        ),
        check_vma=False,
    )
```

```python
import functools

import jax
import jax.numpy as jnp
from jax import lax
from jax.experimental import pallas as pl
from jax.experimental.pallas import tpu as pltpu
from jax.sharding import PartitionSpec as P

CAP = 8
META = 16
F32 = jnp.float32
BF16 = jnp.bfloat16
MIB = 1024 * 1024
PLACE_COST = 1 << 34


def swap(value, axis, count, bit):
    return lax.ppermute(value, axis, [(i, i ^ bit) for i in range(count)])


def whole_spec(shape):
    return pl.BlockSpec(shape, lambda *_: (0,) * len(shape))


def params(mib=16):
    return pltpu.CompilerParams(vmem_limit_bytes=mib * MIB)


def split_kernel(width, n_dp, where, ids, tokens, *refs):
    outs, (meta, sems) = refs[:-2], refs[-2:]
    k, x = where[0], where[1]
    rows = tokens.shape[0]
    copies = []
    for rel in range(n_dp):
        start = pl.multiple_of((k ^ rel) * width, 128)
        copy = pltpu.make_async_copy(
            tokens.at[:, pl.ds(start, width)], outs[rel].at[pl.ds(0, rows), :], sems.at[rel]
        )
        copy.start()
        copies.append(copy)
    along = ids[...].astype(F32)
    line = lax.broadcasted_iota(jnp.int32, (rows, rows), 0)
    lane = lax.broadcasted_iota(jnp.int32, (rows, rows), 1)
    named = jnp.broadcast_to(along, (rows, rows))
    down = jnp.sum(jnp.where(line == lane, named, 0.0), axis=1, keepdims=True)
    earlier = jnp.where((named == down) & (line < lane), 1.0, 0.0)
    place = jnp.sum(earlier, axis=0, keepdims=True) + (x * CAP).astype(F32)
    at = lax.broadcasted_iota(jnp.int32, (META, rows), 0)
    meta[...] = jnp.zeros(meta.shape, BF16)
    meta[:, 0:rows] = jnp.where(at == 0, along, jnp.where(at == 1, place, 0.0)).astype(BF16)
    for rel in range(n_dp):
        copy = pltpu.make_async_copy(meta, outs[rel].at[pl.ds(rows, META), :], sems.at[n_dp + rel])
        copy.start()
        copies.append(copy)
    for copy in copies:
        copy.wait()


def split(where, ids, tokens, width, n_dp):
    rows = tokens.shape[0]
    anywhere = pl.BlockSpec(memory_space=pl.ANY)
    return pl.pallas_call(
        functools.partial(split_kernel, width, n_dp),
        out_shape=[jax.ShapeDtypeStruct((rows + META, width), BF16)] * n_dp,
        in_specs=[
            pl.BlockSpec(memory_space=pltpu.SMEM),
            pl.BlockSpec(memory_space=pltpu.VMEM),
            anywhere,
        ],
        out_specs=[anywhere] * n_dp,
        scratch_shapes=[pltpu.VMEM((META, width), BF16), pltpu.SemaphoreType.DMA((2 * n_dp,))],
        compiler_params=params(),
    )(where, ids, tokens)


def placer_of(row, slot_count):
    every = lax.broadcasted_iota(jnp.int32, (slot_count, row.shape[1]), 0)
    return (every == row).astype(F32).astype(BF16)


def place_kernel(first, rows, where, mine, others, *refs):
    n_dp = len(mine)
    other = []
    for group in others:
        other += [group] if len(group.shape) == 2 else [group.at[i] for i in range(group.shape[0])]
    if first:
        placed, lines = refs[-2:]
    else:
        lines, placed = refs[0], refs[-1]
    local_experts, slot_rows, width = placed.shape
    slots = slot_rows // n_dp
    for rel in range(n_dp):
        if first:
            pair = [b[0 : rows + META, :] for b in (mine[rel], other[rel])]
            metas = [b[rows:, 0:rows].astype(F32) for b in pair]
            ids = jnp.concatenate([m[0:1] for m in metas], axis=1)
            place = jnp.concatenate([m[1:2] for m in metas], axis=1)
            low = (where[1] * local_experts).astype(F32)
            row = ((ids - low) * slots + place).astype(jnp.int32)
            lines[rel] = jnp.broadcast_to(row, (8, row.shape[1]))
            pair = [b[0:rows] for b in pair]
        else:
            row = lines[rel][0:1]
            pair = [b[...] for b in (mine[rel], other[rel])]
        placer = placer_of(row, local_experts * slots)
        found = jnp.dot(placer, jnp.concatenate(pair, axis=0), preferred_element_type=F32).astype(BF16)
        placed[:, rel * slots : (rel + 1) * slots, :] = found.reshape(local_experts, slots, width)


def place(where, mine, others, lines, rows, local_experts, after):
    first = lines is None
    n_dp, slots = len(mine), 2 * CAP
    width = mine[0].shape[1]
    placed = jax.ShapeDtypeStruct((local_experts, n_dp * slots, width), BF16)
    line = jax.ShapeDtypeStruct((n_dp, 8, 2 * rows), jnp.int32)
    vmem = pl.BlockSpec(memory_space=pltpu.VMEM)
    operands = [*others] + ([] if first else [lines])

    def kernel(where, *refs):
        split_at = n_dp + len(others)
        place_kernel(first, rows, where, refs[:n_dp], refs[n_dp:split_at], *refs[split_at:])

    return pl.pallas_call(
        kernel,
        out_shape=[placed, line] if first else placed,
        in_specs=[pl.BlockSpec(memory_space=pltpu.SMEM)]
        + [vmem] * (n_dp + len(operands))
        + [pl.BlockSpec(memory_space=pl.ANY)] * len(after),
        out_specs=[vmem, vmem] if first else vmem,
        compiler_params=params(),
        cost_estimate=pl.CostEstimate(flops=PLACE_COST, bytes_accessed=4 * rows * width * n_dp, transcendentals=0),
    )(where, *mine, *operands, *after)


def back_kernel(rels, lines, h0, h1, gate, up, own0, own1, other0, other1, near, held, sems):
    parts = (h0, h1)
    local_experts, slots, _ = h0.shape
    hidden = gate.shape[1]
    per_copy = local_experts // sems.shape[1]

    def copy_of(which, at):
        group = pl.ds(at * per_copy, per_copy)
        rows = pl.ds(which * hidden, hidden)
        return pltpu.make_async_copy((gate, up)[which].at[group], near.at[group, rows], sems.at[which, at])

    for at in range(sems.shape[1]):
        for which in range(2):
            copy_of(which, at).start()
    for at in range(sems.shape[1]):
        for which in range(2):
            copy_of(which, at).wait()
        for e in range(at * per_copy, (at + 1) * per_copy):
            grads = jnp.concatenate([h[e] for h in parts], axis=0)
            value = jnp.dot(grads, near[e], preferred_element_type=F32).astype(BF16)
            for i in range(2):
                held[i, e * slots : (e + 1) * slots, :] = value[i * slots : (i + 1) * slots]

    rows = own0.shape[0]
    for i, (own, other) in enumerate(((own0, other0), (own1, other1))):
        placer = placer_of(lines[rels[i]][0:1], held.shape[1])
        token_rows = lax.dot_general(
            placer, held[i], (((0,), (0,)), ((), ())), preferred_element_type=F32
        ).astype(BF16)
        own[...] = token_rows[0:rows]
        other[...] = token_rows[rows:]


def back(rels, lines, parts, gate, up, rows):
    local_experts, hidden, width = gate.shape
    slots = parts[0].shape[1]
    vmem = pl.BlockSpec(memory_space=pltpu.VMEM)
    flops = 4 * local_experts * 2 * slots * width * hidden
    return pl.pallas_call(
        functools.partial(back_kernel, rels),
        out_shape=[jax.ShapeDtypeStruct((rows, width), BF16)] * 4,
        in_specs=[vmem] * 3 + [pl.BlockSpec(memory_space=pl.ANY)] * 2,
        out_specs=[vmem] * 4,
        scratch_shapes=[
            pltpu.VMEM((local_experts, 2 * hidden, width), BF16),
            pltpu.VMEM((2, local_experts * slots, width), BF16),
            pltpu.SemaphoreType.DMA((2, 8 if local_experts % 8 == 0 else 1)),
        ],
        compiler_params=params(48),
        cost_estimate=pl.CostEstimate(
            flops=4 * flops, bytes_accessed=2 * local_experts * width * hidden * 2, transcendentals=0
        ),
    )(lines, *parts, gate, up)


def weight_kernel(placed, h0, h1, h2, h3, gate, up):
    hidden = gate.shape[1]
    for i in range(gate.shape[0]):
        grads = jnp.concatenate([h[i] for h in (h0, h1, h2, h3)], axis=0)
        both = lax.dot_general(
            grads, placed[i], (((0,), (0,)), ((), ())), preferred_element_type=F32
        ).astype(BF16)
        gate[i] = both[0:hidden]
        up[i] = both[hidden:]


def weight_grads(placed, parts, per_step):
    local_experts, slot_rows, width = placed.shape
    _, slots, both = parts[0].shape
    hidden = both // 2
    part_spec = pl.BlockSpec((per_step, slots, both), lambda e: (e, 0, 0))
    out_spec = pl.BlockSpec((per_step, hidden, width), lambda e: (e, 0, 0))
    flops = 2 * local_experts * slot_rows * width * both
    return pl.pallas_call(
        weight_kernel,
        grid=(local_experts // per_step,),
        out_shape=[jax.ShapeDtypeStruct((local_experts, hidden, width), BF16)] * 2,
        in_specs=[pl.BlockSpec((per_step, slot_rows, width), lambda e: (e, 0, 0))] + [part_spec] * len(parts),
        out_specs=[out_spec] * 2,
        compiler_params=params(24),
        cost_estimate=pl.CostEstimate(
            flops=4 * flops, bytes_accessed=local_experts * width * both * 2, transcendentals=0
        ),
    )(placed, *parts)


def plus(first, second):
    return first.astype(F32) + second.astype(F32)


def swiglu_grads(gate_act, up_act, hidden_grad):
    sigmoid_gate = jax.nn.sigmoid(gate_act)
    up_grad = (hidden_grad * gate_act * sigmoid_gate).astype(BF16)
    gate_grad = (
        hidden_grad * up_act * sigmoid_gate * (1.0 + gate_act * (1.0 - sigmoid_gate))
    ).astype(BF16)
    return gate_grad, up_grad


def on_small_slice(tokens, cotangent, expert_ids, gate_weight, up_weight, down_weight):
    n_dp, n_x, n_t = 4, 2, 4
    k, x, t = lax.axis_index("dp"), lax.axis_index("expert"), lax.axis_index("tensor")
    width = gate_weight.shape[1]
    rows = tokens.shape[0]
    where = jnp.stack([k, x]).astype(jnp.int32)
    chunks = split(where, expert_ids.reshape(1, rows), tokens, width, n_dp)
    def to_owner(value, rel, flip):
        if rel == 0 and flip == 0:
            return value
        pairs = [
            (i * n_x + j, (i ^ rel) * n_x + (j ^ flip)) for i in range(n_dp) for j in range(n_x)
        ]
        return lax.ppermute(value, ("dp", "expert"), pairs)

    own_tokens = [to_owner(c, rel, 0) for rel, c in enumerate(chunks)]
    near_tokens = [to_owner(c, rel, 1) for rel, c in enumerate(chunks[:2])]
    grads = [lax.dynamic_slice_in_dim(cotangent, (k ^ rel) * width, width, axis=1) for rel in range(n_dp)]
    far_tokens, grads = lax.optimization_barrier((own_tokens[2:], grads))
    near_tokens, far_tokens = lax.optimization_barrier((near_tokens, far_tokens))
    far_tokens = [swap(c, "expert", n_x, 1) for c in far_tokens]
    own_grads = [to_owner(c, rel, 0) for rel, c in enumerate(grads)]
    leaving_grads = jnp.stack(own_grads)
    far_tokens, leaving_grads = lax.optimization_barrier((far_tokens, leaving_grads))
    other_grads = swap(leaving_grads, "expert", n_x, 1)
    gate_weight, up_weight, down_weight = (
        jnp.swapaxes(weight, 1, 2) for weight in (gate_weight, up_weight, down_weight)
    )
    local_experts = gate_weight.shape[0]

    def project(values, weight):
        act = jnp.einsum("esd,ehd->esh", values, weight, preferred_element_type=F32).astype(BF16)
        return jnp.split(act, n_dp, axis=1)

    def near_and_far(act):
        near, far = swap(act[1], "dp", n_dp, 1), swap(act[3], "dp", n_dp, 1)
        return plus(act[0], near), plus(act[2], far).astype(BF16)

    placed, lines = place(where, own_tokens, near_tokens + far_tokens, None, rows, local_experts, [leaving_grads])
    gate_near, gate_far = near_and_far(project(placed, gate_weight))
    up_near, up_far = near_and_far(project(placed, up_weight))
    far = jnp.stack([gate_far, up_far])
    there = swap(far, "dp", n_dp, 2)
    placed_grads = place(where, own_grads, [other_grads], lines, rows, local_experts, [far])
    hidden_act = project(placed_grads, down_weight)
    beside, there = lax.optimization_barrier((swap(hidden_act[3], "dp", n_dp, 1), there))
    hidden_far = plus(hidden_act[2], beside).astype(BF16)
    hidden_near = plus(hidden_act[0], swap(hidden_act[1], "dp", n_dp, 1))
    gate_act, up_act = plus(gate_near, there[0]), plus(up_near, there[1])
    sigmoid_gate = jax.nn.sigmoid(gate_act)
    up_factor = gate_act * sigmoid_gate
    gate_factor = up_act * sigmoid_gate * (1.0 + gate_act * (1.0 - sigmoid_gate))
    hidden_grad = plus(hidden_near, swap(hidden_far, "dp", n_dp, 2))
    part = jnp.concatenate([hidden_grad * gate_factor, hidden_grad * up_factor], axis=2).astype(BF16)
    far = swap(part, "dp", n_dp, 2)
    beside = swap(part, "dp", n_dp, 1)
    near_back = back((0, 1), lines, [part, beside], gate_weight, up_weight, rows)
    far, _ = lax.optimization_barrier((far, near_back[0]))
    parts = [part, beside, far, swap(far, "dp", n_dp, 1)]
    far_back = back((2, 3), lines, parts[2:], gate_weight, up_weight, rows)
    weight_grad = weight_grads(placed, parts, 4)

    def blocks(rels, after, own0, own1, other0, other1):
        owns = [to_owner(own, rel, 0) for rel, own in zip(rels, (own0, own1))]
        others = [to_owner(other, rel, 1) for rel, other in zip(rels, (other0, other1))]
        owns, others, _ = lax.optimization_barrier((owns, others, after))
        terms = [plus(own, other).astype(BF16) for own, other in zip(owns, others)]
        odd = ((k ^ t) & 1) == 1
        keep = jnp.where(odd, terms[1], terms[0])
        leaving = jnp.where(odd, terms[0], terms[1])
        return plus(keep, swap(leaving, "tensor", n_t, 1))

    first, second = blocks((0, 1), far_back[0], *near_back), blocks((2, 3), weight_grad, *far_back)
    swapped = ((k ^ t) & 2) == 2
    keep = jnp.where(swapped, second, first)
    leaving = jnp.where(swapped, first, second).astype(BF16)
    grad_tokens = plus(keep, swap(leaving, "tensor", n_t, 2)).astype(BF16)

    grad_gate, grad_up = (jnp.swapaxes(grad, 1, 2) for grad in weight_grad)
    return grad_tokens, grad_gate, grad_up


def bits_of(count):
    bits = []
    bit = 1
    while bit < count:
        bits.append(bit)
        bit *= 2
    return bits


def halving_sum(parts, axis, count):
    parts = dict(parts)
    for bit in bits_of(count):
        leaving = sorted(r for r in parts if r & bit)
        arrived = swap(jnp.stack([parts[r].astype(BF16) for r in leaving]), axis, count, bit)
        for at, r in enumerate(leaving):
            parts[r ^ bit] = plus(parts[r ^ bit], arrived[at])
            del parts[r]
    return parts[0]


def doubling_gather(value, axis, count):
    held = {0: value}
    for bit in reversed(bits_of(count)):
        known = sorted(held)
        arrived = swap(jnp.stack([held[r] for r in known]), axis, count, bit)
        for at, r in enumerate(known):
            held[r ^ bit] = arrived[at]
    return [held[r] for r in range(count)]


def on_any_slice(tokens, cotangent, expert_ids, gate_weight, up_weight, down_weight):
    n_dp, n_x, n_t = lax.axis_size("dp"), lax.axis_size("expert"), lax.axis_size("tensor")
    k, x, t = lax.axis_index("dp"), lax.axis_index("expert"), lax.axis_index("tensor")
    local_experts, width, hidden = gate_weight.shape
    rows = tokens.shape[0]
    slots = n_x * CAP
    ids_row = expert_ids.reshape(1, rows)
    order = jnp.arange(rows, dtype=jnp.int32)
    earlier = (expert_ids == ids_row) & (order[:, None] < order[None, :])
    position = jnp.sum(earlier.astype(jnp.int32), axis=0)
    target = ids_row[0] * CAP + position
    targets = lax.all_gather(target, ("dp", "expert"), axis=0, tiled=False).reshape(n_dp, n_x, rows)
    pair = jnp.stack([tokens, cotangent])
    placers, slot_rows = [], []
    for rel in range(n_dp):
        columns = lax.dynamic_slice_in_dim(pair, (k ^ rel) * width, width, axis=2)
        mine = columns if rel == 0 else swap(columns, "dp", n_dp, rel)
        blocks = lax.all_gather(mine, "expert", axis=1, tiled=True)
        goal = lax.dynamic_index_in_dim(targets, k ^ rel, axis=0, keepdims=False)
        expert = goal // CAP - x * local_experts
        place = jnp.arange(n_x, dtype=jnp.int32)[:, None] * CAP + goal % CAP
        row = jnp.where((expert >= 0) & (expert < local_experts), expert * slots + place, -1)
        row = row.reshape(1, n_x * rows)
        every = jnp.arange(local_experts * slots, dtype=jnp.int32)[:, None]
        placer = (every == row).astype(BF16)
        placers.append(placer)
        slot_rows.append(
            jnp.einsum("sn,and->asd", placer, blocks, preferred_element_type=F32)
            .astype(BF16)
            .reshape(2, local_experts, slots, width)
        )
    slot_rows = jnp.concatenate(slot_rows, axis=2)
    inputs, grads_in = slot_rows[0], slot_rows[1]

    def act(values, weight):
        return jnp.einsum("esd,edf->esf", values, weight, preferred_element_type=F32).astype(BF16)

    acts = jnp.stack([act(inputs, gate_weight), act(inputs, up_weight), act(grads_in, down_weight)])
    acts = acts.reshape(3, local_experts, n_dp, slots, hidden)
    acts = halving_sum({r: acts[:, :, r] for r in range(n_dp)}, "dp", n_dp)
    grads = doubling_gather(jnp.stack(swiglu_grads(acts[0], acts[1], acts[2])), "dp", n_dp)
    grads = jnp.concatenate(grads, axis=2)
    gate_grad, up_grad = grads[0], grads[1]
    partial_value = jnp.einsum("esf,edf->esd", gate_grad, gate_weight, preferred_element_type=F32)
    partial_value = partial_value + jnp.einsum("esf,edf->esd", up_grad, up_weight, preferred_element_type=F32)
    partial_value = partial_value.astype(BF16).reshape(local_experts, n_dp, slots, width)
    per_token = []
    for rel in range(n_dp):
        flat = partial_value[:, rel].reshape(local_experts * slots, width)
        spread = lax.dot_general(placers[rel], flat, (((0,), (0,)), ((), ())), preferred_element_type=F32)
        spread = spread.astype(BF16).reshape(n_x, rows, width)
        per_token.append(lax.psum_scatter(spread, "expert", scatter_dimension=0, tiled=False))
    per_token = jnp.stack(per_token)
    terms = {r: lax.dynamic_index_in_dim(per_token, k ^ t ^ r, axis=0, keepdims=False) for r in range(n_t)}
    summed = halving_sum(terms, "tensor", n_t).astype(BF16)
    summed = lax.ppermute(
        summed, ("dp", "tensor"), [(i * n_t + j, j * n_t + i) for i in range(n_dp) for j in range(n_t)]
    )
    grad_gate = jnp.einsum("esd,esf->edf", inputs, gate_grad, preferred_element_type=F32).astype(BF16)
    grad_up = jnp.einsum("esd,esf->edf", inputs, up_grad, preferred_element_type=F32).astype(BF16)
    return summed, grad_gate, grad_up


def solution(mesh):
    placed = (
        P(("dp", "expert"), None),
        P(("dp", "expert"), None),
        P(("dp", "expert"), None),
        P("expert", "dp", "tensor"),
        P("expert", "dp", "tensor"),
        P("expert", "dp", "tensor"),
    )
    sizes = tuple(mesh.shape[name] for name in ("dp", "expert", "tensor"))
    return jax.shard_map(
        on_small_slice if sizes == (4, 2, 4) else on_any_slice,
        mesh=mesh,
        in_specs=placed,
        out_specs=(
            P(("dp", "expert"), "tensor"),
            P("expert", "dp", "tensor"),
            P("expert", "dp", "tensor"),
        ),
        check_vma=False,
    )
```

```python
import functools

import jax
import jax.numpy as jnp
from jax import lax
from jax.experimental import pallas as pl
from jax.experimental.pallas import tpu as pltpu
from jax.sharding import PartitionSpec as P

CAP = 8
META = 16
F32 = jnp.float32
BF16 = jnp.bfloat16
MIB = 1024 * 1024
PLACE_COST = 1 << 34


def swap(value, axis, count, bit):
    return lax.ppermute(value, axis, [(i, i ^ bit) for i in range(count)])


def whole_spec(shape):
    return pl.BlockSpec(shape, lambda *_: (0,) * len(shape))


def params(mib=16):
    return pltpu.CompilerParams(vmem_limit_bytes=mib * MIB)


def placer_of(row, slot_count):
    every = lax.broadcasted_iota(jnp.int32, (slot_count, row.shape[1]), 0)
    return (every == row).astype(F32).astype(BF16)


def place_kernel(first, rows, where, mine, others, *refs):
    n_dp = len(mine)
    other = []
    for group in others:
        other += [group] if len(group.shape) == 2 else [group.at[i] for i in range(group.shape[0])]
    if first:
        placed, lines = refs[-2:]
    else:
        lines, placed = refs[0], refs[-1]
    local_experts, slot_rows, width = placed.shape
    slots = slot_rows // n_dp
    for rel in range(n_dp):
        if first:
            pair = [b[0 : rows + META, :] for b in (mine[rel], other[rel])]
            metas = [b[rows:, 0:rows].astype(F32) for b in pair]
            ids = jnp.concatenate([m[0:1] for m in metas], axis=1)
            place = jnp.concatenate([m[1:2] for m in metas], axis=1)
            low = (where[1] * local_experts).astype(F32)
            row = ((ids - low) * slots + place).astype(jnp.int32)
            lines[rel] = jnp.broadcast_to(row, (8, row.shape[1]))
            pair = [b[0:rows] for b in pair]
        else:
            row = lines[rel][0:1]
            pair = [b[...] for b in (mine[rel], other[rel])]
        placer = placer_of(row, local_experts * slots)
        found = jnp.dot(placer, jnp.concatenate(pair, axis=0), preferred_element_type=F32).astype(BF16)
        placed[:, rel * slots : (rel + 1) * slots, :] = found.reshape(local_experts, slots, width)


def place(where, mine, others, lines, rows, local_experts, after):
    first = lines is None
    n_dp, slots = len(mine), 2 * CAP
    width = mine[0].shape[1]
    placed = jax.ShapeDtypeStruct((local_experts, n_dp * slots, width), BF16)
    line = jax.ShapeDtypeStruct((n_dp, 8, 2 * rows), jnp.int32)
    vmem = pl.BlockSpec(memory_space=pltpu.VMEM)
    operands = [*others] + ([] if first else [lines])

    def kernel(where, *refs):
        split_at = n_dp + len(others)
        place_kernel(first, rows, where, refs[:n_dp], refs[n_dp:split_at], *refs[split_at:])

    return pl.pallas_call(
        kernel,
        out_shape=[placed, line] if first else placed,
        in_specs=[pl.BlockSpec(memory_space=pltpu.SMEM)]
        + [vmem] * (n_dp + len(operands))
        + [pl.BlockSpec(memory_space=pl.ANY)] * len(after),
        out_specs=[vmem, vmem] if first else vmem,
        compiler_params=params(),
        cost_estimate=pl.CostEstimate(flops=PLACE_COST, bytes_accessed=4 * rows * width * n_dp, transcendentals=0),
    )(where, *mine, *operands, *after)


def back_kernel(rels, first, last, *refs):
    if first:
        earlier, refs = refs[0], refs[1:]
    if last:
        lines, refs = refs[0], refs[1:]
    h0, h1, gate, up = refs[:4]
    outs, near, sems = refs[4:-2], refs[-2], refs[-1]
    parts = (h0, h1)
    count, slots, _ = h0.shape
    hidden = gate.shape[1]
    per_copy = count // sems.shape[1]

    def copy_of(which, at):
        rows = pl.ds(which * hidden, hidden)
        source = (gate, up)[which].at[pl.ds(first + at * per_copy, per_copy)]
        return pltpu.make_async_copy(source, near.at[pl.ds(at * per_copy, per_copy), rows], sems.at[which, at])

    for at in range(sems.shape[1]):
        for which in range(2):
            copy_of(which, at).start()
    for at in range(sems.shape[1]):
        for which in range(2):
            copy_of(which, at).wait()
        for e in range(at * per_copy, (at + 1) * per_copy):
            grads = jnp.concatenate([h[e] for h in parts], axis=0)
            value = jnp.dot(grads, near[e], preferred_element_type=F32).astype(BF16)
            for i in range(2):
                rows = value[i * slots : (i + 1) * slots]
                if last:
                    outs[-1][i, (first + e) * slots : (first + e + 1) * slots, :] = rows
                else:
                    outs[0][i, e * slots : (e + 1) * slots, :] = rows
    if not last:
        return
    own0, own1, other0, other1, held = outs
    if first:
        held[:, 0 : first * slots, :] = earlier[...]
    rows = own0.shape[0]
    for i, (own, other) in enumerate(((own0, other0), (own1, other1))):
        placer = placer_of(lines[rels[i]][0:1], held.shape[1])
        token_rows = lax.dot_general(
            placer, held[i], (((0,), (0,)), ((), ())), preferred_element_type=F32
        ).astype(BF16)
        own[...] = token_rows[0:rows]
        other[...] = token_rows[rows:]


def back(rels, lines, parts, gate, up, rows, first=0, earlier=None):
    local_experts, hidden, width = gate.shape
    count, slots, _ = parts[0].shape
    last = first + count == local_experts
    vmem = pl.BlockSpec(memory_space=pltpu.VMEM)
    flops = (16 if last else 1) * count * 2 * slots * width * hidden
    operands = ([earlier] if first else []) + ([lines] if last else []) + [*parts]
    near = [
        pltpu.VMEM((count, 2 * hidden, width), BF16),
        pltpu.SemaphoreType.DMA((2, count // 2 if count % 2 == 0 else count)),
    ]
    if last:
        out_shape = [jax.ShapeDtypeStruct((rows, width), BF16)] * 4
        near = [pltpu.VMEM((2, local_experts * slots, width), BF16)] + near
    else:
        out_shape = jax.ShapeDtypeStruct((2, count * slots, width), BF16)
    return pl.pallas_call(
        functools.partial(back_kernel, rels, first, last),
        out_shape=out_shape,
        in_specs=[vmem] * len(operands) + [pl.BlockSpec(memory_space=pltpu.HBM)] * 2,
        out_specs=[vmem] * 4 if last else vmem,
        scratch_shapes=near,
        compiler_params=params(48),
        cost_estimate=pl.CostEstimate(
            flops=flops, bytes_accessed=2 * count * width * hidden * 2 if last else width, transcendentals=0
        ),
    )(*operands, gate, up)


def weight_kernel(placed, h0, h1, h2, h3, gate, up):
    hidden = gate.shape[1]
    for i in range(gate.shape[0]):
        grads = jnp.concatenate([h[i] for h in (h0, h1, h2, h3)], axis=0)
        both = lax.dot_general(
            grads, placed[i], (((0,), (0,)), ((), ())), preferred_element_type=F32
        ).astype(BF16)
        gate[i] = both[0:hidden]
        up[i] = both[hidden:]


def weight_grads(placed, parts, per_step):
    local_experts, slot_rows, width = placed.shape
    _, slots, both = parts[0].shape
    hidden = both // 2
    part_spec = pl.BlockSpec((per_step, slots, both), lambda e: (e, 0, 0))
    out_spec = pl.BlockSpec((per_step, hidden, width), lambda e: (e, 0, 0))
    flops = 2 * local_experts * slot_rows * width * both
    return pl.pallas_call(
        weight_kernel,
        grid=(local_experts // per_step,),
        out_shape=[jax.ShapeDtypeStruct((local_experts, hidden, width), BF16)] * 2,
        in_specs=[pl.BlockSpec((per_step, slot_rows, width), lambda e: (e, 0, 0))] + [part_spec] * len(parts),
        out_specs=[out_spec] * 2,
        compiler_params=params(12),
        cost_estimate=pl.CostEstimate(
            flops=4 * flops, bytes_accessed=local_experts * width * both * 2, transcendentals=0
        ),
    )(placed, *parts)


def plus(first, second):
    return first.astype(F32) + second.astype(F32)


def swiglu_grads(gate_act, up_act, hidden_grad):
    sigmoid_gate = jax.nn.sigmoid(gate_act)
    up_grad = (hidden_grad * gate_act * sigmoid_gate).astype(BF16)
    gate_grad = (
        hidden_grad * up_act * sigmoid_gate * (1.0 + gate_act * (1.0 - sigmoid_gate))
    ).astype(BF16)
    return gate_grad, up_grad


def on_small_slice(tokens, cotangent, expert_ids, gate_weight, up_weight, down_weight):
    n_dp, n_x, n_t = 4, 2, 4
    k, x, t = lax.axis_index("dp"), lax.axis_index("expert"), lax.axis_index("tensor")
    width = gate_weight.shape[1]
    rows = tokens.shape[0]
    where = jnp.stack([k, x]).astype(jnp.int32)
    ids_row = expert_ids.reshape(1, rows)
    order = jnp.arange(rows, dtype=jnp.int32)
    earlier = (expert_ids == ids_row) & (order[:, None] < order[None, :])
    position = jnp.sum(earlier.astype(jnp.int32), axis=0, keepdims=True) + x * CAP
    meta = jnp.concatenate([ids_row, position], axis=0).astype(BF16)
    meta = jnp.pad(meta, ((0, META - 2), (0, width - rows)))

    def columns(values, rel):
        return lax.dynamic_slice_in_dim(values, (k ^ rel) * width, width, axis=1)

    chunks = [jnp.concatenate([columns(tokens, rel), meta], axis=0) for rel in range(n_dp)]

    def to_owner(value, rel, flip):
        if rel == 0 and flip == 0:
            return value
        pairs = [
            (i * n_x + j, (i ^ rel) * n_x + (j ^ flip)) for i in range(n_dp) for j in range(n_x)
        ]
        return lax.ppermute(value, ("dp", "expert"), pairs)

    own_tokens = [to_owner(c, rel, 0) for rel, c in enumerate(chunks)]
    near_tokens = [to_owner(c, rel, 1) for rel, c in enumerate(chunks[:2])]
    grads = [columns(cotangent, rel) for rel in range(n_dp)]
    far_tokens, grads = lax.optimization_barrier((own_tokens[2:], grads))
    near_tokens, far_tokens = lax.optimization_barrier((near_tokens, far_tokens))
    far_tokens = [swap(c, "expert", n_x, 1) for c in far_tokens]
    own_grads = [to_owner(c, rel, 0) for rel, c in enumerate(grads)]
    leaving_grads = jnp.stack(own_grads)
    far_tokens, leaving_grads = lax.optimization_barrier((far_tokens, leaving_grads))
    other_grads = swap(leaving_grads, "expert", n_x, 1)
    gate_weight, up_weight, down_weight = (
        jnp.swapaxes(weight, 1, 2) for weight in (gate_weight, up_weight, down_weight)
    )
    local_experts = gate_weight.shape[0]

    def project(values, weight):
        act = jnp.einsum("esd,ehd->esh", values, weight, preferred_element_type=F32).astype(BF16)
        return jnp.split(act, n_dp, axis=1)

    def near_and_far(act):
        near, far = swap(act[1], "dp", n_dp, 1), swap(act[3], "dp", n_dp, 1)
        return plus(act[0], near), plus(act[2], far).astype(BF16)

    placed, lines = place(where, own_tokens, near_tokens + far_tokens, None, rows, local_experts, [leaving_grads])
    gate_near, gate_far = near_and_far(project(placed, gate_weight))
    up_near, up_far = near_and_far(project(placed, up_weight))
    far = jnp.stack([gate_far, up_far])
    there = swap(far, "dp", n_dp, 2)
    placed_grads = place(where, own_grads, [other_grads], lines, rows, local_experts, [far])
    hidden_act = project(placed_grads, down_weight)
    beside, there = lax.optimization_barrier((swap(hidden_act[3], "dp", n_dp, 1), there))
    hidden_far = plus(hidden_act[2], beside).astype(BF16)
    hidden_near = plus(hidden_act[0], swap(hidden_act[1], "dp", n_dp, 1))
    gate_act, up_act = plus(gate_near, there[0]), plus(up_near, there[1])
    sigmoid_gate = jax.nn.sigmoid(gate_act)
    up_factor = gate_act * sigmoid_gate
    gate_factor = up_act * sigmoid_gate * (1.0 + gate_act * (1.0 - sigmoid_gate))
    hidden_grad = plus(hidden_near, swap(hidden_far, "dp", n_dp, 2))
    part = jnp.concatenate([hidden_grad * gate_factor, hidden_grad * up_factor], axis=2).astype(BF16)
    count = local_experts * 3 // 8
    far = [swap(piece, "dp", n_dp, 2) for piece in jnp.split(part, [count], axis=0)]
    beside = swap(part, "dp", n_dp, 1)
    near_back = back((0, 1), lines, [part, beside], gate_weight, up_weight, rows)
    far[0], _ = lax.optimization_barrier((far[0], near_back[0]))
    far_beside = [swap(far[0], "dp", n_dp, 1)]
    early = back((2, 3), lines, [far[0], far_beside[0]], gate_weight, up_weight, rows)
    far[1], _ = lax.optimization_barrier((far[1], early))
    far_beside.append(swap(far[1], "dp", n_dp, 1))
    far_back = back((2, 3), lines, [far[1], far_beside[1]], gate_weight, up_weight, rows, count, early)
    parts = [part, beside, jnp.concatenate(far, axis=0), jnp.concatenate(far_beside, axis=0)]
    after_back, _ = lax.optimization_barrier((placed, far_back[0]))
    weight_grad = weight_grads(after_back, parts, 4)

    def blocks(rels, after, own0, own1, other0, other1):
        owns = [to_owner(own, rel, 0) for rel, own in zip(rels, (own0, own1))]
        others = [to_owner(other, rel, 1) for rel, other in zip(rels, (other0, other1))]
        owns, others, _ = lax.optimization_barrier((owns, others, after))
        terms = [plus(own, other).astype(BF16) for own, other in zip(owns, others)]
        odd = ((k ^ t) & 1) == 1
        keep = jnp.where(odd, terms[1], terms[0])
        leaving = jnp.where(odd, terms[0], terms[1])
        return plus(keep, swap(leaving, "tensor", n_t, 1))

    first, second = blocks((0, 1), far_back[0], *near_back), blocks((2, 3), weight_grad, *far_back)
    swapped = ((k ^ t) & 2) == 2
    keep = jnp.where(swapped, second, first)
    leaving = jnp.where(swapped, first, second).astype(BF16)
    grad_tokens = plus(keep, swap(leaving, "tensor", n_t, 2)).astype(BF16)

    grad_gate, grad_up = (jnp.swapaxes(grad, 1, 2) for grad in weight_grad)
    return grad_tokens, grad_gate, grad_up


def bits_of(count):
    bits = []
    bit = 1
    while bit < count:
        bits.append(bit)
        bit *= 2
    return bits


def halving_sum(parts, axis, count):
    parts = dict(parts)
    for bit in bits_of(count):
        leaving = sorted(r for r in parts if r & bit)
        arrived = swap(jnp.stack([parts[r].astype(BF16) for r in leaving]), axis, count, bit)
        for at, r in enumerate(leaving):
            parts[r ^ bit] = plus(parts[r ^ bit], arrived[at])
            del parts[r]
    return parts[0]


def doubling_gather(value, axis, count):
    held = {0: value}
    for bit in reversed(bits_of(count)):
        known = sorted(held)
        arrived = swap(jnp.stack([held[r] for r in known]), axis, count, bit)
        for at, r in enumerate(known):
            held[r ^ bit] = arrived[at]
    return [held[r] for r in range(count)]


def on_any_slice(tokens, cotangent, expert_ids, gate_weight, up_weight, down_weight):
    n_dp, n_x, n_t = lax.axis_size("dp"), lax.axis_size("expert"), lax.axis_size("tensor")
    k, x, t = lax.axis_index("dp"), lax.axis_index("expert"), lax.axis_index("tensor")
    local_experts, width, hidden = gate_weight.shape
    rows = tokens.shape[0]
    slots = n_x * CAP
    ids_row = expert_ids.reshape(1, rows)
    order = jnp.arange(rows, dtype=jnp.int32)
    earlier = (expert_ids == ids_row) & (order[:, None] < order[None, :])
    position = jnp.sum(earlier.astype(jnp.int32), axis=0)
    target = ids_row[0] * CAP + position
    targets = lax.all_gather(target, ("dp", "expert"), axis=0, tiled=False).reshape(n_dp, n_x, rows)
    pair = jnp.stack([tokens, cotangent])
    placers, slot_rows = [], []
    for rel in range(n_dp):
        columns = lax.dynamic_slice_in_dim(pair, (k ^ rel) * width, width, axis=2)
        mine = columns if rel == 0 else swap(columns, "dp", n_dp, rel)
        blocks = lax.all_gather(mine, "expert", axis=1, tiled=True)
        goal = lax.dynamic_index_in_dim(targets, k ^ rel, axis=0, keepdims=False)
        expert = goal // CAP - x * local_experts
        place = jnp.arange(n_x, dtype=jnp.int32)[:, None] * CAP + goal % CAP
        row = jnp.where((expert >= 0) & (expert < local_experts), expert * slots + place, -1)
        row = row.reshape(1, n_x * rows)
        every = jnp.arange(local_experts * slots, dtype=jnp.int32)[:, None]
        placer = (every == row).astype(BF16)
        placers.append(placer)
        slot_rows.append(
            jnp.einsum("sn,and->asd", placer, blocks, preferred_element_type=F32)
            .astype(BF16)
            .reshape(2, local_experts, slots, width)
        )
    slot_rows = jnp.concatenate(slot_rows, axis=2)
    inputs, grads_in = slot_rows[0], slot_rows[1]

    def act(values, weight):
        return jnp.einsum("esd,edf->esf", values, weight, preferred_element_type=F32).astype(BF16)

    acts = jnp.stack([act(inputs, gate_weight), act(inputs, up_weight), act(grads_in, down_weight)])
    acts = acts.reshape(3, local_experts, n_dp, slots, hidden)
    acts = halving_sum({r: acts[:, :, r] for r in range(n_dp)}, "dp", n_dp)
    grads = doubling_gather(jnp.stack(swiglu_grads(acts[0], acts[1], acts[2])), "dp", n_dp)
    grads = jnp.concatenate(grads, axis=2)
    gate_grad, up_grad = grads[0], grads[1]
    partial_value = jnp.einsum("esf,edf->esd", gate_grad, gate_weight, preferred_element_type=F32)
    partial_value = partial_value + jnp.einsum("esf,edf->esd", up_grad, up_weight, preferred_element_type=F32)
    partial_value = partial_value.astype(BF16).reshape(local_experts, n_dp, slots, width)
    per_token = []
    for rel in range(n_dp):
        flat = partial_value[:, rel].reshape(local_experts * slots, width)
        spread = lax.dot_general(placers[rel], flat, (((0,), (0,)), ((), ())), preferred_element_type=F32)
        spread = spread.astype(BF16).reshape(n_x, rows, width)
        per_token.append(lax.psum_scatter(spread, "expert", scatter_dimension=0, tiled=False))
    per_token = jnp.stack(per_token)
    terms = {r: lax.dynamic_index_in_dim(per_token, k ^ t ^ r, axis=0, keepdims=False) for r in range(n_t)}
    summed = halving_sum(terms, "tensor", n_t).astype(BF16)
    summed = lax.ppermute(
        summed, ("dp", "tensor"), [(i * n_t + j, j * n_t + i) for i in range(n_dp) for j in range(n_t)]
    )
    grad_gate = jnp.einsum("esd,esf->edf", inputs, gate_grad, preferred_element_type=F32).astype(BF16)
    grad_up = jnp.einsum("esd,esf->edf", inputs, up_grad, preferred_element_type=F32).astype(BF16)
    return summed, grad_gate, grad_up


def solution(mesh):
    placed = (
        P(("dp", "expert"), None),
        P(("dp", "expert"), None),
        P(("dp", "expert"), None),
        P("expert", "dp", "tensor"),
        P("expert", "dp", "tensor"),
        P("expert", "dp", "tensor"),
    )
    sizes = tuple(mesh.shape[name] for name in ("dp", "expert", "tensor"))
    return jax.shard_map(
        on_small_slice if sizes == (4, 2, 4) else on_any_slice,
        mesh=mesh,
        in_specs=placed,
        out_specs=(
            P(("dp", "expert"), "tensor"),
            P("expert", "dp", "tensor"),
            P("expert", "dp", "tensor"),
        ),
        check_vma=False,
    )
```

```python
import functools

import jax
import jax.numpy as jnp
from jax import lax
from jax.experimental import pallas as pl
from jax.experimental.pallas import tpu as pltpu
from jax.sharding import PartitionSpec as P

CAP = 8
META = 16
F32 = jnp.float32
BF16 = jnp.bfloat16
MIB = 1024 * 1024
PLACE_COST = 1 << 34


def swap(value, axis, count, bit):
    return lax.ppermute(value, axis, [(i, i ^ bit) for i in range(count)])


def whole_spec(shape):
    return pl.BlockSpec(shape, lambda *_: (0,) * len(shape))


def params(mib=16):
    return pltpu.CompilerParams(vmem_limit_bytes=mib * MIB)


def placer_of(row, slot_count):
    every = lax.broadcasted_iota(jnp.int32, (slot_count, row.shape[1]), 0)
    return (every == row).astype(F32).astype(BF16)


def place_kernel(first, rows, where, mine, others, *refs):
    n_dp = len(mine)
    other = []
    for group in others:
        other += [group] if len(group.shape) == 2 else [group.at[i] for i in range(group.shape[0])]
    if first:
        placed, lines = refs[-2:]
    else:
        lines, placed = refs[0], refs[-1]
    local_experts, slot_rows, width = placed.shape
    slots = slot_rows // n_dp
    for rel in range(n_dp):
        if first:
            pair = [b[0 : rows + META, :] for b in (mine[rel], other[rel])]
            metas = [b[rows:, 0:rows].astype(F32) for b in pair]
            ids = jnp.concatenate([m[0:1] for m in metas], axis=1)
            place = jnp.concatenate([m[1:2] for m in metas], axis=1)
            low = (where[1] * local_experts).astype(F32)
            row = ((ids - low) * slots + place).astype(jnp.int32)
            lines[rel] = jnp.broadcast_to(row, (8, row.shape[1]))
            pair = [b[0:rows] for b in pair]
        else:
            row = lines[rel][0:1]
            pair = [b[...] for b in (mine[rel], other[rel])]
        placer = placer_of(row, local_experts * slots)
        found = jnp.dot(placer, jnp.concatenate(pair, axis=0), preferred_element_type=F32).astype(BF16)
        placed[:, rel * slots : (rel + 1) * slots, :] = found.reshape(local_experts, slots, width)


def place(where, mine, others, lines, rows, local_experts, after):
    first = lines is None
    n_dp, slots = len(mine), 2 * CAP
    width = mine[0].shape[1]
    placed = jax.ShapeDtypeStruct((local_experts, n_dp * slots, width), BF16)
    line = jax.ShapeDtypeStruct((n_dp, 8, 2 * rows), jnp.int32)
    vmem = pl.BlockSpec(memory_space=pltpu.VMEM)
    operands = [*others] + ([] if first else [lines])

    def kernel(where, *refs):
        split_at = n_dp + len(others)
        place_kernel(first, rows, where, refs[:n_dp], refs[n_dp:split_at], *refs[split_at:])

    return pl.pallas_call(
        kernel,
        out_shape=[placed, line] if first else placed,
        in_specs=[pl.BlockSpec(memory_space=pltpu.SMEM)]
        + [vmem] * (n_dp + len(operands))
        + [pl.BlockSpec(memory_space=pl.ANY)] * len(after),
        out_specs=[vmem, vmem] if first else vmem,
        compiler_params=params(),
        cost_estimate=pl.CostEstimate(flops=PLACE_COST, bytes_accessed=4 * rows * width * n_dp, transcendentals=0),
    )(where, *mine, *operands, *after)


def back_kernel(low, first, last, where, *refs):
    if first:
        earlier, refs = refs[0], refs[1:]
    if last:
        lines, refs = refs[0], refs[1:]
    h0, h1, gate, up = refs[:4]
    outs, near, sems = refs[4:-2], refs[-2], refs[-1]
    parts = (h0, h1)
    count, slots, _ = h0.shape
    hidden = gate.shape[1]
    per_copy = count // sems.shape[1]

    def copy_of(which, at):
        rows = pl.ds(which * hidden, hidden)
        source = (gate, up)[which].at[pl.ds(first + at * per_copy, per_copy)]
        return pltpu.make_async_copy(source, near.at[pl.ds(at * per_copy, per_copy), rows], sems.at[which, at])

    for at in range(sems.shape[1]):
        for which in range(2):
            copy_of(which, at).start()
    for at in range(sems.shape[1]):
        for which in range(2):
            copy_of(which, at).wait()
        for e in range(at * per_copy, (at + 1) * per_copy):
            grads = jnp.concatenate([h[e] for h in parts], axis=0)
            value = jnp.dot(grads, near[e], preferred_element_type=F32).astype(BF16)
            for i in range(2):
                rows = value[i * slots : (i + 1) * slots]
                if last:
                    outs[-1][i, (first + e) * slots : (first + e + 1) * slots, :] = rows
                else:
                    outs[0][i, e * slots : (e + 1) * slots, :] = rows
    if not last:
        return
    held = outs[-1]
    if first:
        held[:, 0 : first * slots, :] = earlier[...]
    rows = outs[0].shape[0]
    for i in range(2):
        which = where[2] ^ i
        placer = placer_of(lines[low + which][0:1], held.shape[1])
        token_rows = lax.dot_general(
            placer, held[which], (((0,), (0,)), ((), ())), preferred_element_type=F32
        ).astype(BF16)
        outs[2 * i][...] = token_rows[0:rows]
        outs[2 * i + 1][...] = token_rows[rows:]


def back(low, where, lines, parts, gate, up, rows, first=0, earlier=None):
    local_experts, hidden, width = gate.shape
    count, slots, _ = parts[0].shape
    last = first + count == local_experts
    vmem = pl.BlockSpec(memory_space=pltpu.VMEM)
    flops = (16 if last else 1) * count * 2 * slots * width * hidden
    operands = ([earlier] if first else []) + ([lines] if last else []) + [*parts]
    near = [
        pltpu.VMEM((count, 2 * hidden, width), BF16),
        pltpu.SemaphoreType.DMA((2, count // 2 if count % 2 == 0 else count)),
    ]
    if last:
        out_shape = [jax.ShapeDtypeStruct((rows, width), BF16)] * 4
        near = [pltpu.VMEM((2, local_experts * slots, width), BF16)] + near
    else:
        out_shape = jax.ShapeDtypeStruct((2, count * slots, width), BF16)
    return pl.pallas_call(
        functools.partial(back_kernel, low, first, last),
        out_shape=out_shape,
        in_specs=[pl.BlockSpec(memory_space=pltpu.SMEM)]
        + [vmem] * len(operands)
        + [pl.BlockSpec(memory_space=pl.ANY)] * 2,
        out_specs=[vmem] * 4 if last else vmem,
        scratch_shapes=near,
        compiler_params=params(48),
        cost_estimate=pl.CostEstimate(
            flops=flops, bytes_accessed=2 * count * width * hidden * 2 if last else width, transcendentals=0
        ),
    )(where, *operands, gate, up)


def weight_kernel(placed, h0, h1, h2, h3, gate, up):
    hidden = gate.shape[1]
    for i in range(gate.shape[0]):
        grads = jnp.concatenate([h[i] for h in (h0, h1, h2, h3)], axis=0)
        both = lax.dot_general(
            grads, placed[i], (((0,), (0,)), ((), ())), preferred_element_type=F32
        ).astype(BF16)
        gate[i] = both[0:hidden]
        up[i] = both[hidden:]


def weight_grads(placed, parts, per_step):
    local_experts, slot_rows, width = placed.shape
    _, slots, both = parts[0].shape
    hidden = both // 2
    part_spec = pl.BlockSpec((per_step, slots, both), lambda e: (e, 0, 0))
    out_spec = pl.BlockSpec((per_step, hidden, width), lambda e: (e, 0, 0))
    flops = 2 * local_experts * slot_rows * width * both
    return pl.pallas_call(
        weight_kernel,
        grid=(local_experts // per_step,),
        out_shape=[jax.ShapeDtypeStruct((local_experts, hidden, width), BF16)] * 2,
        in_specs=[pl.BlockSpec((per_step, slot_rows, width), lambda e: (e, 0, 0))] + [part_spec] * len(parts),
        out_specs=[out_spec] * 2,
        compiler_params=params(12),
        cost_estimate=pl.CostEstimate(
            flops=4 * flops, bytes_accessed=local_experts * width * both * 2, transcendentals=0
        ),
    )(placed, *parts)


def plus(first, second):
    return first.astype(F32) + second.astype(F32)


def swiglu_grads(gate_act, up_act, hidden_grad):
    sigmoid_gate = jax.nn.sigmoid(gate_act)
    up_grad = (hidden_grad * gate_act * sigmoid_gate).astype(BF16)
    gate_grad = (
        hidden_grad * up_act * sigmoid_gate * (1.0 + gate_act * (1.0 - sigmoid_gate))
    ).astype(BF16)
    return gate_grad, up_grad


def on_small_slice(tokens, cotangent, expert_ids, gate_weight, up_weight, down_weight):
    n_dp, n_x, n_t = 4, 2, 4
    k, x, t = lax.axis_index("dp"), lax.axis_index("expert"), lax.axis_index("tensor")
    width = gate_weight.shape[1]
    rows = tokens.shape[0]
    where = jnp.stack([k, x, (k ^ t) & 1]).astype(jnp.int32)
    ids_row = expert_ids.reshape(1, rows)
    order = jnp.arange(rows, dtype=jnp.int32)
    earlier = (expert_ids == ids_row) & (order[:, None] < order[None, :])
    position = jnp.sum(earlier.astype(jnp.int32), axis=0, keepdims=True) + x * CAP
    meta = jnp.concatenate([ids_row, position], axis=0).astype(BF16)
    meta = jnp.pad(meta, ((0, META - 2), (0, width - rows)))

    def columns(values, rel):
        return lax.dynamic_slice_in_dim(values, (k ^ rel) * width, width, axis=1)

    chunks = [jnp.concatenate([columns(tokens, rel), meta], axis=0) for rel in range(n_dp)]

    def to_owner(value, rel, flip):
        if rel == 0 and flip == 0:
            return value
        pairs = [
            (i * n_x + j, (i ^ rel) * n_x + (j ^ flip)) for i in range(n_dp) for j in range(n_x)
        ]
        return lax.ppermute(value, ("dp", "expert"), pairs)

    own_tokens = [to_owner(c, rel, 0) for rel, c in enumerate(chunks)]
    near_tokens = [to_owner(c, rel, 1) for rel, c in enumerate(chunks[:2])]
    grads = [columns(cotangent, rel) for rel in range(n_dp)]
    far_tokens, grads = lax.optimization_barrier((own_tokens[2:], grads))
    near_tokens, far_tokens = lax.optimization_barrier((near_tokens, far_tokens))
    far_tokens = [swap(c, "expert", n_x, 1) for c in far_tokens]
    own_grads = [to_owner(c, rel, 0) for rel, c in enumerate(grads)]
    leaving_grads = jnp.stack(own_grads)
    far_tokens, leaving_grads = lax.optimization_barrier((far_tokens, leaving_grads))
    other_grads = swap(leaving_grads, "expert", n_x, 1)
    gate_weight, up_weight, down_weight = (
        jnp.swapaxes(weight, 1, 2) for weight in (gate_weight, up_weight, down_weight)
    )
    local_experts = gate_weight.shape[0]

    def project(values, weight):
        act = jnp.einsum("esd,ehd->esh", values, weight, preferred_element_type=F32).astype(BF16)
        return jnp.split(act, n_dp, axis=1)

    def near_and_far(act):
        near, far = swap(act[1], "dp", n_dp, 1), swap(act[3], "dp", n_dp, 1)
        return plus(act[0], near), plus(act[2], far).astype(BF16)

    placed, lines = place(where, own_tokens, near_tokens + far_tokens, None, rows, local_experts, [leaving_grads])
    gate_near, gate_far = near_and_far(project(placed, gate_weight))
    up_near, up_far = near_and_far(project(placed, up_weight))
    far = jnp.stack([gate_far, up_far])
    there = swap(far, "dp", n_dp, 2)
    placed_grads = place(where, own_grads, [other_grads], lines, rows, local_experts, [far])
    hidden_act = project(placed_grads, down_weight)
    beside, there = lax.optimization_barrier((swap(hidden_act[3], "dp", n_dp, 1), there))
    hidden_far = plus(hidden_act[2], beside).astype(BF16)
    hidden_near = plus(hidden_act[0], swap(hidden_act[1], "dp", n_dp, 1))
    gate_act, up_act = plus(gate_near, there[0]), plus(up_near, there[1])
    sigmoid_gate = jax.nn.sigmoid(gate_act)
    up_factor = gate_act * sigmoid_gate
    gate_factor = up_act * sigmoid_gate * (1.0 + gate_act * (1.0 - sigmoid_gate))
    hidden_grad = plus(hidden_near, swap(hidden_far, "dp", n_dp, 2))
    part = jnp.concatenate([hidden_grad * gate_factor, hidden_grad * up_factor], axis=2).astype(BF16)
    count = local_experts * 3 // 8
    far = [swap(piece, "dp", n_dp, 2) for piece in jnp.split(part, [count], axis=0)]
    beside = swap(part, "dp", n_dp, 1)
    near_back = back(0, where, lines, [part, beside], gate_weight, up_weight, rows)
    far[0], _ = lax.optimization_barrier((far[0], near_back[0]))
    far_beside = [swap(far[0], "dp", n_dp, 1)]
    early = back(2, where, lines, [far[0], far_beside[0]], gate_weight, up_weight, rows)
    far[1], _ = lax.optimization_barrier((far[1], early))
    far_beside.append(swap(far[1], "dp", n_dp, 1))
    far_back = back(2, where, lines, [far[1], far_beside[1]], gate_weight, up_weight, rows, count, early)
    parts = [part, beside, jnp.concatenate(far, axis=0), jnp.concatenate(far_beside, axis=0)]
    after_back, _ = lax.optimization_barrier((placed, far_back[0]))
    weight_grad = weight_grads(after_back, parts, 4)

    def to_keeper(value, low, turn, flip):
        pairs = []
        for i in range(n_dp):
            for j in range(n_x):
                for l in range(n_t):
                    odd = (i ^ l) & 1
                    to = ((i ^ low ^ odd ^ turn) * n_x + (j ^ flip)) * n_t + (l ^ odd)
                    pairs.append(((i * n_x + j) * n_t + l, to))
        return lax.ppermute(value, ("dp", "expert", "tensor"), pairs)

    def arrive(low, values):
        return [to_keeper(v, low, at // 2, at % 2) for at, v in enumerate(values)]

    near_terms, far_back = lax.optimization_barrier((arrive(0, near_back), far_back))
    far_terms = arrive(2, far_back)
    far_terms, _ = lax.optimization_barrier((far_terms, weight_grad))
    first, second = (sum(v.astype(F32) for v in terms) for terms in (near_terms, far_terms))
    swapped = ((k ^ t) & 2) == 2
    keep = jnp.where(swapped, second, first)
    leaving = jnp.where(swapped, first, second).astype(BF16)
    grad_tokens = plus(keep, swap(leaving, "tensor", n_t, 2)).astype(BF16)

    grad_gate, grad_up = (jnp.swapaxes(grad, 1, 2) for grad in weight_grad)
    return grad_tokens, grad_gate, grad_up


def bits_of(count):
    bits = []
    bit = 1
    while bit < count:
        bits.append(bit)
        bit *= 2
    return bits


def halving_sum(parts, axis, count):
    parts = dict(parts)
    for bit in bits_of(count):
        leaving = sorted(r for r in parts if r & bit)
        arrived = swap(jnp.stack([parts[r].astype(BF16) for r in leaving]), axis, count, bit)
        for at, r in enumerate(leaving):
            parts[r ^ bit] = plus(parts[r ^ bit], arrived[at])
            del parts[r]
    return parts[0]


def doubling_gather(value, axis, count):
    held = {0: value}
    for bit in reversed(bits_of(count)):
        known = sorted(held)
        arrived = swap(jnp.stack([held[r] for r in known]), axis, count, bit)
        for at, r in enumerate(known):
            held[r ^ bit] = arrived[at]
    return [held[r] for r in range(count)]


def on_any_slice(tokens, cotangent, expert_ids, gate_weight, up_weight, down_weight):
    n_dp, n_x, n_t = lax.axis_size("dp"), lax.axis_size("expert"), lax.axis_size("tensor")
    k, x, t = lax.axis_index("dp"), lax.axis_index("expert"), lax.axis_index("tensor")
    local_experts, width, hidden = gate_weight.shape
    rows = tokens.shape[0]
    slots = n_x * CAP
    ids_row = expert_ids.reshape(1, rows)
    order = jnp.arange(rows, dtype=jnp.int32)
    earlier = (expert_ids == ids_row) & (order[:, None] < order[None, :])
    position = jnp.sum(earlier.astype(jnp.int32), axis=0)
    target = ids_row[0] * CAP + position
    targets = lax.all_gather(target, ("dp", "expert"), axis=0, tiled=False).reshape(n_dp, n_x, rows)
    pair = jnp.stack([tokens, cotangent])
    placers, slot_rows = [], []
    for rel in range(n_dp):
        columns = lax.dynamic_slice_in_dim(pair, (k ^ rel) * width, width, axis=2)
        mine = columns if rel == 0 else swap(columns, "dp", n_dp, rel)
        blocks = lax.all_gather(mine, "expert", axis=1, tiled=True)
        goal = lax.dynamic_index_in_dim(targets, k ^ rel, axis=0, keepdims=False)
        expert = goal // CAP - x * local_experts
        place = jnp.arange(n_x, dtype=jnp.int32)[:, None] * CAP + goal % CAP
        row = jnp.where((expert >= 0) & (expert < local_experts), expert * slots + place, -1)
        row = row.reshape(1, n_x * rows)
        every = jnp.arange(local_experts * slots, dtype=jnp.int32)[:, None]
        placer = (every == row).astype(BF16)
        placers.append(placer)
        slot_rows.append(
            jnp.einsum("sn,and->asd", placer, blocks, preferred_element_type=F32)
            .astype(BF16)
            .reshape(2, local_experts, slots, width)
        )
    slot_rows = jnp.concatenate(slot_rows, axis=2)
    inputs, grads_in = slot_rows[0], slot_rows[1]

    def act(values, weight):
        return jnp.einsum("esd,edf->esf", values, weight, preferred_element_type=F32).astype(BF16)

    acts = jnp.stack([act(inputs, gate_weight), act(inputs, up_weight), act(grads_in, down_weight)])
    acts = acts.reshape(3, local_experts, n_dp, slots, hidden)
    acts = halving_sum({r: acts[:, :, r] for r in range(n_dp)}, "dp", n_dp)
    grads = doubling_gather(jnp.stack(swiglu_grads(acts[0], acts[1], acts[2])), "dp", n_dp)
    grads = jnp.concatenate(grads, axis=2)
    gate_grad, up_grad = grads[0], grads[1]
    partial_value = jnp.einsum("esf,edf->esd", gate_grad, gate_weight, preferred_element_type=F32)
    partial_value = partial_value + jnp.einsum("esf,edf->esd", up_grad, up_weight, preferred_element_type=F32)
    partial_value = partial_value.astype(BF16).reshape(local_experts, n_dp, slots, width)
    per_token = []
    for rel in range(n_dp):
        flat = partial_value[:, rel].reshape(local_experts * slots, width)
        spread = lax.dot_general(placers[rel], flat, (((0,), (0,)), ((), ())), preferred_element_type=F32)
        spread = spread.astype(BF16).reshape(n_x, rows, width)
        per_token.append(lax.psum_scatter(spread, "expert", scatter_dimension=0, tiled=False))
    per_token = jnp.stack(per_token)
    terms = {r: lax.dynamic_index_in_dim(per_token, k ^ t ^ r, axis=0, keepdims=False) for r in range(n_t)}
    summed = halving_sum(terms, "tensor", n_t).astype(BF16)
    summed = lax.ppermute(
        summed, ("dp", "tensor"), [(i * n_t + j, j * n_t + i) for i in range(n_dp) for j in range(n_t)]
    )
    grad_gate = jnp.einsum("esd,esf->edf", inputs, gate_grad, preferred_element_type=F32).astype(BF16)
    grad_up = jnp.einsum("esd,esf->edf", inputs, up_grad, preferred_element_type=F32).astype(BF16)
    return summed, grad_gate, grad_up


def solution(mesh):
    placed = (
        P(("dp", "expert"), None),
        P(("dp", "expert"), None),
        P(("dp", "expert"), None),
        P("expert", "dp", "tensor"),
        P("expert", "dp", "tensor"),
        P("expert", "dp", "tensor"),
    )
    sizes = tuple(mesh.shape[name] for name in ("dp", "expert", "tensor"))
    return jax.shard_map(
        on_small_slice if sizes == (4, 2, 4) else on_any_slice,
        mesh=mesh,
        in_specs=placed,
        out_specs=(
            P(("dp", "expert"), "tensor"),
            P("expert", "dp", "tensor"),
            P("expert", "dp", "tensor"),
        ),
        check_vma=False,
    )
```

```python
import functools

import jax
import jax.numpy as jnp
from jax import lax
from jax.experimental import pallas as pl
from jax.experimental.pallas import tpu as pltpu
from jax.sharding import PartitionSpec as P

CAP = 8
META = 16
F32 = jnp.float32
BF16 = jnp.bfloat16
MIB = 1024 * 1024
PLACE_COST = 1 << 34


def swap(value, axis, count, bit):
    return lax.ppermute(value, axis, [(i, i ^ bit) for i in range(count)])


def whole_spec(shape):
    return pl.BlockSpec(shape, lambda *_: (0,) * len(shape))


def params(mib=16):
    return pltpu.CompilerParams(vmem_limit_bytes=mib * MIB)


def placer_of(row, slot_count):
    every = lax.broadcasted_iota(jnp.int32, (slot_count, row.shape[1]), 0)
    return (every == row).astype(F32).astype(BF16)


def place_kernel(first, rows, mine, others, *refs):
    n_dp = len(mine)
    other = []
    for group in others:
        other += [group] if len(group.shape) == 2 else [group.at[i] for i in range(group.shape[0])]
    if first:
        placed, lines = refs[-2:]
    else:
        lines, placed = refs[0], refs[-1]
    local_experts, slot_rows, width = placed.shape
    slots = slot_rows // n_dp
    for rel in range(n_dp):
        if first:
            pair = [b[0 : rows + META, :] for b in (mine[rel], other[rel])]
            metas = [b[rows:, 0:rows].astype(F32) for b in pair]
            ids = jnp.concatenate([m[0:1] for m in metas], axis=1)
            place = jnp.concatenate([m[1:2] for m in metas], axis=1)
            low = (lax.axis_index("expert") * local_experts).astype(F32)
            row = ((ids - low) * slots + place).astype(jnp.int32)
            lines[rel] = jnp.broadcast_to(row, (8, row.shape[1]))
            pair = [b[0:rows] for b in pair]
        else:
            row = lines[rel][0:1]
            pair = [b[...] for b in (mine[rel], other[rel])]
        placer = placer_of(row, local_experts * slots)
        found = jnp.dot(placer, jnp.concatenate(pair, axis=0), preferred_element_type=F32).astype(BF16)
        placed[:, rel * slots : (rel + 1) * slots, :] = found.reshape(local_experts, slots, width)


def place(mine, others, lines, rows, local_experts, after):
    first = lines is None
    n_dp, slots = len(mine), 2 * CAP
    width = mine[0].shape[1]
    placed = jax.ShapeDtypeStruct((local_experts, n_dp * slots, width), BF16)
    line = jax.ShapeDtypeStruct((n_dp, 8, 2 * rows), jnp.int32)
    vmem = pl.BlockSpec(memory_space=pltpu.VMEM)
    operands = [*others] + ([] if first else [lines])

    def kernel(*refs):
        split_at = n_dp + len(others)
        place_kernel(first, rows, refs[:n_dp], refs[n_dp:split_at], *refs[split_at:])

    return pl.pallas_call(
        kernel,
        out_shape=[placed, line] if first else placed,
        in_specs=[vmem] * (n_dp + len(operands))
        + [pl.BlockSpec(memory_space=pl.ANY)] * len(after),
        out_specs=[vmem, vmem] if first else vmem,
        compiler_params=params(),
        cost_estimate=pl.CostEstimate(flops=PLACE_COST, bytes_accessed=4 * rows * width * n_dp, transcendentals=0),
    )(*mine, *operands, *after)


def back_kernel(low, first, last, *refs):
    if first:
        earlier, refs = refs[0], refs[1:]
    if last:
        lines, refs = refs[0], refs[1:]
    h0, h1, gate, up = refs[:4]
    outs, near, sems = refs[4:-2], refs[-2], refs[-1]
    parts = (h0, h1)
    count, slots, _ = h0.shape
    hidden = gate.shape[1]
    per_copy = count // sems.shape[1]

    def copy_of(which, at):
        rows = pl.ds(which * hidden, hidden)
        source = (gate, up)[which].at[pl.ds(first + at * per_copy, per_copy)]
        return pltpu.make_async_copy(source, near.at[pl.ds(at * per_copy, per_copy), rows], sems.at[which, at])

    for at in range(sems.shape[1]):
        for which in range(2):
            copy_of(which, at).start()
    for at in range(sems.shape[1]):
        for which in range(2):
            copy_of(which, at).wait()
        for e in range(at * per_copy, (at + 1) * per_copy):
            grads = jnp.concatenate([h[e] for h in parts], axis=0)
            value = jnp.dot(grads, near[e], preferred_element_type=F32).astype(BF16)
            for i in range(2):
                rows = value[i * slots : (i + 1) * slots]
                if last:
                    outs[-1][i, (first + e) * slots : (first + e + 1) * slots, :] = rows
                else:
                    outs[0][i, e * slots : (e + 1) * slots, :] = rows
    if not last:
        return
    held = outs[-1]
    if first:
        held[:, 0 : first * slots, :] = earlier[...]
    rows = outs[0].shape[0]
    odd = (lax.axis_index("dp") ^ lax.axis_index("tensor")) & 1
    for i in range(2):
        which = odd ^ i
        placer = placer_of(lines[low + which][0:1], held.shape[1])
        token_rows = lax.dot_general(
            placer, held[which], (((0,), (0,)), ((), ())), preferred_element_type=F32
        ).astype(BF16)
        outs[2 * i][...] = token_rows[0:rows]
        outs[2 * i + 1][...] = token_rows[rows:]


def back(low, lines, parts, gate, up, rows, first=0, earlier=None):
    local_experts, hidden, width = gate.shape
    count, slots, _ = parts[0].shape
    last = first + count == local_experts
    vmem = pl.BlockSpec(memory_space=pltpu.VMEM)
    flops = (16 if last else 1) * count * 2 * slots * width * hidden
    operands = ([earlier] if first else []) + ([lines] if last else []) + [*parts]
    near = [
        pltpu.VMEM((count, 2 * hidden, width), BF16),
        pltpu.SemaphoreType.DMA((2, count // 2 if count % 2 == 0 else count)),
    ]
    if last:
        out_shape = [jax.ShapeDtypeStruct((rows, width), BF16)] * 4
        near = [pltpu.VMEM((2, local_experts * slots, width), BF16)] + near
    else:
        out_shape = jax.ShapeDtypeStruct((2, count * slots, width), BF16)
    return pl.pallas_call(
        functools.partial(back_kernel, low, first, last),
        out_shape=out_shape,
        in_specs=[vmem] * len(operands) + [pl.BlockSpec(memory_space=pl.ANY)] * 2,
        out_specs=[vmem] * 4 if last else vmem,
        scratch_shapes=near,
        compiler_params=params(48),
        cost_estimate=pl.CostEstimate(
            flops=flops, bytes_accessed=2 * count * width * hidden * 2 if last else width, transcendentals=0
        ),
    )(*operands, gate, up)


def weight_kernel(placed, h0, h1, h2, h3, gate, up):
    hidden = gate.shape[1]
    for i in range(gate.shape[0]):
        grads = jnp.concatenate([h[i] for h in (h0, h1, h2, h3)], axis=0)
        both = lax.dot_general(
            grads, placed[i], (((0,), (0,)), ((), ())), preferred_element_type=F32
        ).astype(BF16)
        gate[i] = both[0:hidden]
        up[i] = both[hidden:]


def weight_grads(placed, parts, per_step):
    local_experts, slot_rows, width = placed.shape
    _, slots, both = parts[0].shape
    hidden = both // 2
    part_spec = pl.BlockSpec((per_step, slots, both), lambda e: (e, 0, 0))
    out_spec = pl.BlockSpec((per_step, hidden, width), lambda e: (e, 0, 0))
    flops = 2 * local_experts * slot_rows * width * both
    return pl.pallas_call(
        weight_kernel,
        grid=(local_experts // per_step,),
        out_shape=[jax.ShapeDtypeStruct((local_experts, hidden, width), BF16)] * 2,
        in_specs=[pl.BlockSpec((per_step, slot_rows, width), lambda e: (e, 0, 0))] + [part_spec] * len(parts),
        out_specs=[out_spec] * 2,
        compiler_params=params(12),
        cost_estimate=pl.CostEstimate(
            flops=4 * flops, bytes_accessed=local_experts * width * both * 2, transcendentals=0
        ),
    )(placed, *parts)


def plus(first, second):
    return first.astype(F32) + second.astype(F32)


def swiglu_grads(gate_act, up_act, hidden_grad):
    sigmoid_gate = jax.nn.sigmoid(gate_act)
    up_grad = (hidden_grad * gate_act * sigmoid_gate).astype(BF16)
    gate_grad = (
        hidden_grad * up_act * sigmoid_gate * (1.0 + gate_act * (1.0 - sigmoid_gate))
    ).astype(BF16)
    return gate_grad, up_grad


def on_small_slice(tokens, cotangent, expert_ids, gate_weight, up_weight, down_weight):
    n_dp, n_x, n_t = 4, 2, 4
    k, x, t = lax.axis_index("dp"), lax.axis_index("expert"), lax.axis_index("tensor")
    width = gate_weight.shape[1]
    rows = tokens.shape[0]
    ids_row = expert_ids.reshape(1, rows)
    order = jnp.arange(rows, dtype=jnp.int32)
    earlier = (expert_ids == ids_row) & (order[:, None] < order[None, :])
    position = jnp.sum(earlier.astype(jnp.int32), axis=0, keepdims=True) + x * CAP
    meta = jnp.concatenate([ids_row, position], axis=0).astype(BF16)
    meta = jnp.pad(meta, ((0, META - 2), (0, width - rows)))

    def columns(values, rel):
        return lax.dynamic_slice_in_dim(values, (k ^ rel) * width, width, axis=1)

    chunks = [jnp.concatenate([columns(tokens, rel), meta], axis=0) for rel in range(n_dp)]

    def to_owner(value, rel, flip):
        if rel == 0 and flip == 0:
            return value
        pairs = [
            (i * n_x + j, (i ^ rel) * n_x + (j ^ flip)) for i in range(n_dp) for j in range(n_x)
        ]
        return lax.ppermute(value, ("dp", "expert"), pairs)

    own_tokens = [to_owner(c, rel, 0) for rel, c in enumerate(chunks)]
    near_tokens = [to_owner(c, rel, 1) for rel, c in enumerate(chunks[:2])]
    grads = [columns(cotangent, rel) for rel in range(n_dp)]
    far_tokens, grads = lax.optimization_barrier((own_tokens[2:], grads))
    near_tokens, far_tokens = lax.optimization_barrier((near_tokens, far_tokens))
    far_tokens = [swap(c, "expert", n_x, 1) for c in far_tokens]
    own_grads = [to_owner(c, rel, 0) for rel, c in enumerate(grads)]
    leaving_grads = jnp.stack(own_grads)
    far_tokens, leaving_grads = lax.optimization_barrier((far_tokens, leaving_grads))
    other_grads = swap(leaving_grads, "expert", n_x, 1)
    gate_weight, up_weight, down_weight = (
        jnp.swapaxes(weight, 1, 2) for weight in (gate_weight, up_weight, down_weight)
    )
    local_experts = gate_weight.shape[0]

    def project(values, weight):
        act = jnp.einsum("esd,ehd->esh", values, weight, preferred_element_type=F32).astype(BF16)
        return jnp.split(act, n_dp, axis=1)

    def near_and_far(act):
        near, far = swap(act[1], "dp", n_dp, 1), swap(act[3], "dp", n_dp, 1)
        return plus(act[0], near), plus(act[2], far).astype(BF16)

    placed, lines = place(own_tokens, near_tokens + far_tokens, None, rows, local_experts, [leaving_grads])
    gate_near, gate_far = near_and_far(project(placed, gate_weight))
    up_near, up_far = near_and_far(project(placed, up_weight))
    far = jnp.stack([gate_far, up_far])
    there = swap(far, "dp", n_dp, 2)
    placed_grads = place(own_grads, [other_grads], lines, rows, local_experts, [far])
    hidden_act = project(placed_grads, down_weight)
    beside, there = lax.optimization_barrier((swap(hidden_act[3], "dp", n_dp, 1), there))
    hidden_far = plus(hidden_act[2], beside).astype(BF16)
    hidden_near = plus(hidden_act[0], swap(hidden_act[1], "dp", n_dp, 1))
    gate_act, up_act = plus(gate_near, there[0]), plus(up_near, there[1])
    sigmoid_gate = jax.nn.sigmoid(gate_act)
    up_factor = gate_act * sigmoid_gate
    gate_factor = up_act * sigmoid_gate * (1.0 + gate_act * (1.0 - sigmoid_gate))
    hidden_grad = plus(hidden_near, swap(hidden_far, "dp", n_dp, 2))
    part = jnp.concatenate([hidden_grad * gate_factor, hidden_grad * up_factor], axis=2).astype(BF16)
    count = local_experts * 3 // 8
    far = [swap(piece, "dp", n_dp, 2) for piece in jnp.split(part, [count], axis=0)]
    beside = swap(part, "dp", n_dp, 1)
    near_back = back(0, lines, [part, beside], gate_weight, up_weight, rows)
    far[0], _ = lax.optimization_barrier((far[0], near_back[0]))
    far_beside = [swap(far[0], "dp", n_dp, 1)]
    early = back(2, lines, [far[0], far_beside[0]], gate_weight, up_weight, rows)
    far[1], _ = lax.optimization_barrier((far[1], early))
    far_beside.append(swap(far[1], "dp", n_dp, 1))
    far_back = back(2, lines, [far[1], far_beside[1]], gate_weight, up_weight, rows, count, early)
    parts = [part, beside, jnp.concatenate(far, axis=0), jnp.concatenate(far_beside, axis=0)]
    others = swap(jnp.stack(near_back[1::2]), "expert", n_x, 1)
    others, after_back, _ = lax.optimization_barrier((others, placed, far_back[0]))
    weight_grad = weight_grads(after_back, parts, 4)

    def to_keeper(value, low, turn, flip):
        pairs = []
        for i in range(n_dp):
            for j in range(n_x):
                for l in range(n_t):
                    odd = (i ^ l) & 1
                    to = ((i ^ low ^ odd ^ turn) * n_x + (j ^ flip)) * n_t + (l ^ odd)
                    pairs.append(((i * n_x + j) * n_t + l, to))
        return lax.ppermute(value, ("dp", "expert", "tensor"), pairs)

    merged = [plus(own, other).astype(BF16) for own, other in zip(near_back[::2], others)]
    far_terms = [to_keeper(value, 2, at // 2, at % 2) for at, value in enumerate(far_back)]
    merged, _ = lax.optimization_barrier((merged, weight_grad))
    near_terms = [to_keeper(value, 0, turn, 0) for turn, value in enumerate(merged)]
    first, second = (sum(v.astype(F32) for v in terms) for terms in (near_terms, far_terms))
    swapped = ((k ^ t) & 2) == 2
    keep = jnp.where(swapped, second, first)
    leaving = jnp.where(swapped, first, second).astype(BF16)
    grad_tokens = plus(keep, swap(leaving, "tensor", n_t, 2)).astype(BF16)

    grad_gate, grad_up = (jnp.swapaxes(grad, 1, 2) for grad in weight_grad)
    return grad_tokens, grad_gate, grad_up


def bits_of(count):
    bits = []
    bit = 1
    while bit < count:
        bits.append(bit)
        bit *= 2
    return bits


def halving_sum(parts, axis, count):
    parts = dict(parts)
    for bit in bits_of(count):
        leaving = sorted(r for r in parts if r & bit)
        arrived = swap(jnp.stack([parts[r].astype(BF16) for r in leaving]), axis, count, bit)
        for at, r in enumerate(leaving):
            parts[r ^ bit] = plus(parts[r ^ bit], arrived[at])
            del parts[r]
    return parts[0]


def doubling_gather(value, axis, count):
    held = {0: value}
    for bit in reversed(bits_of(count)):
        known = sorted(held)
        arrived = swap(jnp.stack([held[r] for r in known]), axis, count, bit)
        for at, r in enumerate(known):
            held[r ^ bit] = arrived[at]
    return [held[r] for r in range(count)]


def on_any_slice(tokens, cotangent, expert_ids, gate_weight, up_weight, down_weight):
    n_dp, n_x, n_t = lax.axis_size("dp"), lax.axis_size("expert"), lax.axis_size("tensor")
    k, x, t = lax.axis_index("dp"), lax.axis_index("expert"), lax.axis_index("tensor")
    local_experts, width, hidden = gate_weight.shape
    rows = tokens.shape[0]
    slots = n_x * CAP
    ids_row = expert_ids.reshape(1, rows)
    order = jnp.arange(rows, dtype=jnp.int32)
    earlier = (expert_ids == ids_row) & (order[:, None] < order[None, :])
    position = jnp.sum(earlier.astype(jnp.int32), axis=0)
    target = ids_row[0] * CAP + position
    targets = lax.all_gather(target, ("dp", "expert"), axis=0, tiled=False).reshape(n_dp, n_x, rows)
    pair = jnp.stack([tokens, cotangent])
    placers, slot_rows = [], []
    for rel in range(n_dp):
        columns = lax.dynamic_slice_in_dim(pair, (k ^ rel) * width, width, axis=2)
        mine = columns if rel == 0 else swap(columns, "dp", n_dp, rel)
        blocks = lax.all_gather(mine, "expert", axis=1, tiled=True)
        goal = lax.dynamic_index_in_dim(targets, k ^ rel, axis=0, keepdims=False)
        expert = goal // CAP - x * local_experts
        place = jnp.arange(n_x, dtype=jnp.int32)[:, None] * CAP + goal % CAP
        row = jnp.where((expert >= 0) & (expert < local_experts), expert * slots + place, -1)
        row = row.reshape(1, n_x * rows)
        every = jnp.arange(local_experts * slots, dtype=jnp.int32)[:, None]
        placer = (every == row).astype(BF16)
        placers.append(placer)
        slot_rows.append(
            jnp.einsum("sn,and->asd", placer, blocks, preferred_element_type=F32)
            .astype(BF16)
            .reshape(2, local_experts, slots, width)
        )
    slot_rows = jnp.concatenate(slot_rows, axis=2)
    inputs, grads_in = slot_rows[0], slot_rows[1]

    def act(values, weight):
        return jnp.einsum("esd,edf->esf", values, weight, preferred_element_type=F32).astype(BF16)

    acts = jnp.stack([act(inputs, gate_weight), act(inputs, up_weight), act(grads_in, down_weight)])
    acts = acts.reshape(3, local_experts, n_dp, slots, hidden)
    acts = halving_sum({r: acts[:, :, r] for r in range(n_dp)}, "dp", n_dp)
    grads = doubling_gather(jnp.stack(swiglu_grads(acts[0], acts[1], acts[2])), "dp", n_dp)
    grads = jnp.concatenate(grads, axis=2)
    gate_grad, up_grad = grads[0], grads[1]
    partial_value = jnp.einsum("esf,edf->esd", gate_grad, gate_weight, preferred_element_type=F32)
    partial_value = partial_value + jnp.einsum("esf,edf->esd", up_grad, up_weight, preferred_element_type=F32)
    partial_value = partial_value.astype(BF16).reshape(local_experts, n_dp, slots, width)
    per_token = []
    for rel in range(n_dp):
        flat = partial_value[:, rel].reshape(local_experts * slots, width)
        spread = lax.dot_general(placers[rel], flat, (((0,), (0,)), ((), ())), preferred_element_type=F32)
        spread = spread.astype(BF16).reshape(n_x, rows, width)
        per_token.append(lax.psum_scatter(spread, "expert", scatter_dimension=0, tiled=False))
    per_token = jnp.stack(per_token)
    terms = {r: lax.dynamic_index_in_dim(per_token, k ^ t ^ r, axis=0, keepdims=False) for r in range(n_t)}
    summed = halving_sum(terms, "tensor", n_t).astype(BF16)
    summed = lax.ppermute(
        summed, ("dp", "tensor"), [(i * n_t + j, j * n_t + i) for i in range(n_dp) for j in range(n_t)]
    )
    grad_gate = jnp.einsum("esd,esf->edf", inputs, gate_grad, preferred_element_type=F32).astype(BF16)
    grad_up = jnp.einsum("esd,esf->edf", inputs, up_grad, preferred_element_type=F32).astype(BF16)
    return summed, grad_gate, grad_up


def solution(mesh):
    placed = (
        P(("dp", "expert"), None),
        P(("dp", "expert"), None),
        P(("dp", "expert"), None),
        P("expert", "dp", "tensor"),
        P("expert", "dp", "tensor"),
        P("expert", "dp", "tensor"),
    )
    sizes = tuple(mesh.shape[name] for name in ("dp", "expert", "tensor"))
    return jax.shard_map(
        on_small_slice if sizes == (4, 2, 4) else on_any_slice,
        mesh=mesh,
        in_specs=placed,
        out_specs=(
            P(("dp", "expert"), "tensor"),
            P("expert", "dp", "tensor"),
            P("expert", "dp", "tensor"),
        ),
        check_vma=False,
    )
```

```python
import functools

import jax
import jax.numpy as jnp
from jax import lax
from jax.experimental import pallas as pl
from jax.experimental.pallas import tpu as pltpu
from jax.sharding import PartitionSpec as P

CAP = 8
META = 16
F32 = jnp.float32
BF16 = jnp.bfloat16
MIB = 1024 * 1024
PLACE_COST = 1 << 34


def swap(value, axis, count, bit):
    return lax.ppermute(value, axis, [(i, i ^ bit) for i in range(count)])


def whole_spec(shape):
    return pl.BlockSpec(shape, lambda *_: (0,) * len(shape))


def params(mib=16):
    return pltpu.CompilerParams(vmem_limit_bytes=mib * MIB)


def placer_of(row, slot_count):
    every = lax.broadcasted_iota(jnp.int32, (slot_count, row.shape[1]), 0)
    return (every == row).astype(F32).astype(BF16)


def place_kernel(first, rows, mine, others, *refs):
    n_dp = len(mine)
    other = []
    for group in others:
        other += [group] if len(group.shape) == 2 else [group.at[i] for i in range(group.shape[0])]
    if first:
        placed, lines = refs[-2:]
    else:
        lines, placed = refs[0], refs[-1]
    local_experts, slot_rows, width = placed.shape
    slots = slot_rows // n_dp
    for rel in range(n_dp):
        if first:
            pair = [b[0 : rows + META, :] for b in (mine[rel], other[rel])]
            metas = [b[rows:, 0:rows].astype(F32) for b in pair]
            ids = jnp.concatenate([m[0:1] for m in metas], axis=1)
            place = jnp.concatenate([m[1:2] for m in metas], axis=1)
            low = (lax.axis_index("expert") * local_experts).astype(F32)
            row = ((ids - low) * slots + place).astype(jnp.int32)
            lines[rel] = jnp.broadcast_to(row, (8, row.shape[1]))
            pair = [b[0:rows] for b in pair]
        else:
            row = lines[rel][0:1]
            pair = [b[...] for b in (mine[rel], other[rel])]
        placer = placer_of(row, local_experts * slots)
        found = jnp.dot(placer, jnp.concatenate(pair, axis=0), preferred_element_type=F32).astype(BF16)
        placed[:, rel * slots : (rel + 1) * slots, :] = found.reshape(local_experts, slots, width)


def place(mine, others, lines, rows, local_experts, after):
    first = lines is None
    n_dp, slots = len(mine), 2 * CAP
    width = mine[0].shape[1]
    placed = jax.ShapeDtypeStruct((local_experts, n_dp * slots, width), BF16)
    line = jax.ShapeDtypeStruct((n_dp, 8, 2 * rows), jnp.int32)
    vmem = pl.BlockSpec(memory_space=pltpu.VMEM)
    operands = [*others] + ([] if first else [lines])

    def kernel(*refs):
        split_at = n_dp + len(others)
        place_kernel(first, rows, refs[:n_dp], refs[n_dp:split_at], *refs[split_at:])

    return pl.pallas_call(
        kernel,
        out_shape=[placed, line] if first else placed,
        in_specs=[vmem] * (n_dp + len(operands))
        + [pl.BlockSpec(memory_space=pl.ANY)] * len(after),
        out_specs=[vmem, vmem] if first else vmem,
        compiler_params=params(),
        cost_estimate=pl.CostEstimate(flops=PLACE_COST, bytes_accessed=4 * rows * width * n_dp, transcendentals=0),
    )(*mine, *operands, *after)


def back_kernel(low, first, last, *refs):
    if first:
        earlier, refs = refs[0], refs[1:]
    if last:
        lines, refs = refs[0], refs[1:]
    h0, h1, gate, up = refs[:4]
    outs, near, sems = refs[4:-2], refs[-2], refs[-1]
    parts = (h0, h1)
    count, slots, _ = h0.shape
    hidden = gate.shape[1]
    per_copy = count // sems.shape[1]

    def copy_of(which, at):
        rows = pl.ds(which * hidden, hidden)
        source = (gate, up)[which].at[pl.ds(first + at * per_copy, per_copy)]
        return pltpu.make_async_copy(source, near.at[pl.ds(at * per_copy, per_copy), rows], sems.at[which, at])

    for at in range(sems.shape[1]):
        for which in range(2):
            copy_of(which, at).start()
    for at in range(sems.shape[1]):
        for which in range(2):
            copy_of(which, at).wait()
        for e in range(at * per_copy, (at + 1) * per_copy):
            grads = jnp.concatenate([h[e] for h in parts], axis=0)
            value = jnp.dot(grads, near[e], preferred_element_type=F32).astype(BF16)
            for i in range(2):
                rows = value[i * slots : (i + 1) * slots]
                if last:
                    outs[-1][i, (first + e) * slots : (first + e + 1) * slots, :] = rows
                else:
                    outs[0][i, e * slots : (e + 1) * slots, :] = rows
    if not last:
        return
    held = outs[-1]
    if first:
        held[:, 0 : first * slots, :] = earlier[...]
    rows = outs[0].shape[0]
    odd = (lax.axis_index("dp") ^ lax.axis_index("tensor")) & 1
    for i in range(2):
        which = odd ^ i if low else i
        placer = placer_of(lines[low + which][0:1], held.shape[1])
        token_rows = lax.dot_general(
            placer, held[which], (((0,), (0,)), ((), ())), preferred_element_type=F32
        ).astype(BF16)
        outs[2 * i][...] = token_rows[0:rows]
        outs[2 * i + 1][...] = token_rows[rows:]


def back(low, lines, parts, gate, up, rows, first=0, earlier=None):
    local_experts, hidden, width = gate.shape
    count, slots, _ = parts[0].shape
    last = first + count == local_experts
    vmem = pl.BlockSpec(memory_space=pltpu.VMEM)
    flops = (16 if last else 1) * count * 2 * slots * width * hidden
    operands = ([earlier] if first else []) + ([lines] if last else []) + [*parts]
    near = [
        pltpu.VMEM((count, 2 * hidden, width), BF16),
        pltpu.SemaphoreType.DMA((2, count // 2 if count % 2 == 0 else count)),
    ]
    if last:
        out_shape = [jax.ShapeDtypeStruct((rows, width), BF16)] * 4
        near = [pltpu.VMEM((2, local_experts * slots, width), BF16)] + near
    else:
        out_shape = jax.ShapeDtypeStruct((2, count * slots, width), BF16)
    return pl.pallas_call(
        functools.partial(back_kernel, low, first, last),
        out_shape=out_shape,
        in_specs=[vmem] * len(operands) + [pl.BlockSpec(memory_space=pl.ANY)] * 2,
        out_specs=[vmem] * 4 if last else vmem,
        scratch_shapes=near,
        compiler_params=params(48),
        cost_estimate=pl.CostEstimate(
            flops=flops, bytes_accessed=2 * count * width * hidden * 2 if last else width, transcendentals=0
        ),
    )(*operands, gate, up)


def weight_kernel(placed, h0, h1, h2, h3, gate, up):
    hidden = gate.shape[1]
    for i in range(gate.shape[0]):
        grads = jnp.concatenate([h[i] for h in (h0, h1, h2, h3)], axis=0)
        both = lax.dot_general(
            grads, placed[i], (((0,), (0,)), ((), ())), preferred_element_type=F32
        ).astype(BF16)
        gate[i] = both[0:hidden]
        up[i] = both[hidden:]


def weight_grads(placed, parts, per_step):
    local_experts, slot_rows, width = placed.shape
    _, slots, both = parts[0].shape
    hidden = both // 2
    part_spec = pl.BlockSpec((per_step, slots, both), lambda e: (e, 0, 0))
    out_spec = pl.BlockSpec((per_step, hidden, width), lambda e: (e, 0, 0))
    flops = 2 * local_experts * slot_rows * width * both
    return pl.pallas_call(
        weight_kernel,
        grid=(local_experts // per_step,),
        out_shape=[jax.ShapeDtypeStruct((local_experts, hidden, width), BF16)] * 2,
        in_specs=[pl.BlockSpec((per_step, slot_rows, width), lambda e: (e, 0, 0))] + [part_spec] * len(parts),
        out_specs=[out_spec] * 2,
        compiler_params=params(12),
        cost_estimate=pl.CostEstimate(
            flops=4 * flops, bytes_accessed=local_experts * width * both * 2, transcendentals=0
        ),
    )(placed, *parts)


def plus(first, second):
    return first.astype(F32) + second.astype(F32)


def swiglu_grads(gate_act, up_act, hidden_grad):
    sigmoid_gate = jax.nn.sigmoid(gate_act)
    up_grad = (hidden_grad * gate_act * sigmoid_gate).astype(BF16)
    gate_grad = (
        hidden_grad * up_act * sigmoid_gate * (1.0 + gate_act * (1.0 - sigmoid_gate))
    ).astype(BF16)
    return gate_grad, up_grad


def on_small_slice(tokens, cotangent, expert_ids, gate_weight, up_weight, down_weight):
    n_dp, n_x, n_t = 4, 2, 4
    k, x, t = lax.axis_index("dp"), lax.axis_index("expert"), lax.axis_index("tensor")
    width = gate_weight.shape[1]
    rows = tokens.shape[0]
    ids_row = expert_ids.reshape(1, rows)
    order = jnp.arange(rows, dtype=jnp.int32)
    earlier = (expert_ids == ids_row) & (order[:, None] < order[None, :])
    position = jnp.sum(earlier.astype(jnp.int32), axis=0, keepdims=True) + x * CAP
    meta = jnp.concatenate([ids_row, position], axis=0).astype(BF16)
    meta = jnp.pad(meta, ((0, META - 2), (0, width - rows)))

    def columns(values, rel):
        return lax.dynamic_slice_in_dim(values, (k ^ rel) * width, width, axis=1)

    chunks = [jnp.concatenate([columns(tokens, rel), meta], axis=0) for rel in range(n_dp)]

    def to_owner(value, rel, flip):
        if rel == 0 and flip == 0:
            return value
        pairs = [
            (i * n_x + j, (i ^ rel) * n_x + (j ^ flip)) for i in range(n_dp) for j in range(n_x)
        ]
        return lax.ppermute(value, ("dp", "expert"), pairs)

    own_tokens = [to_owner(c, rel, 0) for rel, c in enumerate(chunks)]
    near_tokens = [to_owner(c, rel, 1) for rel, c in enumerate(chunks[:2])]
    grads = [columns(cotangent, rel) for rel in range(n_dp)]
    far_tokens, grads = lax.optimization_barrier((own_tokens[2:], grads))
    near_tokens, far_tokens = lax.optimization_barrier((near_tokens, far_tokens))
    far_tokens = [swap(c, "expert", n_x, 1) for c in far_tokens]
    own_grads = [to_owner(c, rel, 0) for rel, c in enumerate(grads)]
    leaving_grads = jnp.stack(own_grads)
    far_tokens, leaving_grads = lax.optimization_barrier((far_tokens, leaving_grads))
    other_grads = swap(leaving_grads, "expert", n_x, 1)
    gate_weight, up_weight, down_weight = (
        jnp.swapaxes(weight, 1, 2) for weight in (gate_weight, up_weight, down_weight)
    )
    local_experts = gate_weight.shape[0]

    def project(values, weight):
        act = jnp.einsum("esd,ehd->esh", values, weight, preferred_element_type=F32).astype(BF16)
        return jnp.split(act, n_dp, axis=1)

    def near_and_far(act):
        near, far = swap(act[1], "dp", n_dp, 1), swap(act[3], "dp", n_dp, 1)
        return plus(act[0], near), plus(act[2], far).astype(BF16)

    placed, lines = place(own_tokens, near_tokens + far_tokens, None, rows, local_experts, [leaving_grads])
    gate_near, gate_far = near_and_far(project(placed, gate_weight))
    up_near, up_far = near_and_far(project(placed, up_weight))
    far = jnp.stack([gate_far, up_far])
    there = swap(far, "dp", n_dp, 2)
    placed_grads = place(own_grads, [other_grads], lines, rows, local_experts, [far])
    hidden_act = project(placed_grads, down_weight)
    beside, there = lax.optimization_barrier((swap(hidden_act[3], "dp", n_dp, 1), there))
    hidden_far = plus(hidden_act[2], beside).astype(BF16)
    hidden_near = plus(hidden_act[0], swap(hidden_act[1], "dp", n_dp, 1))
    gate_act, up_act = plus(gate_near, there[0]), plus(up_near, there[1])
    sigmoid_gate = jax.nn.sigmoid(gate_act)
    up_factor = gate_act * sigmoid_gate
    gate_factor = up_act * sigmoid_gate * (1.0 + gate_act * (1.0 - sigmoid_gate))
    hidden_grad = plus(hidden_near, swap(hidden_far, "dp", n_dp, 2))
    part = jnp.concatenate([hidden_grad * gate_factor, hidden_grad * up_factor], axis=2).astype(BF16)
    count = local_experts * 3 // 8
    far = [swap(piece, "dp", n_dp, 2) for piece in jnp.split(part, [count], axis=0)]
    beside = swap(part, "dp", n_dp, 1)
    near_back = back(0, lines, [part, beside], gate_weight, up_weight, rows)
    far[0], _ = lax.optimization_barrier((far[0], near_back[0]))
    far_beside = [swap(far[0], "dp", n_dp, 1)]
    early = back(2, lines, [far[0], far_beside[0]], gate_weight, up_weight, rows)
    far[1], _ = lax.optimization_barrier((far[1], early))
    far_beside.append(swap(far[1], "dp", n_dp, 1))
    far_back = back(2, lines, [far[1], far_beside[1]], gate_weight, up_weight, rows, count, early)
    parts = [part, beside, jnp.concatenate(far, axis=0), jnp.concatenate(far_beside, axis=0)]
    own, other, own_beside, other_beside = near_back
    own_beside, other_beside = swap(own_beside, "dp", n_dp, 1), swap(other_beside, "dp", n_dp, 1)
    own_beside, other_beside = lax.optimization_barrier((own_beside, other_beside))
    arrived = swap(jnp.stack([other, other_beside]), "expert", n_x, 1)
    arrived, after_back, _ = lax.optimization_barrier((arrived, placed, far_back[0]))
    weight_grad = weight_grads(after_back, parts, 4)

    def to_keeper(value, low, turn, flip):
        pairs = []
        for i in range(n_dp):
            for j in range(n_x):
                for l in range(n_t):
                    odd = (i ^ l) & 1
                    to = ((i ^ low ^ odd ^ turn) * n_x + (j ^ flip)) * n_t + (l ^ odd)
                    pairs.append(((i * n_x + j) * n_t + l, to))
        return lax.ppermute(value, ("dp", "expert", "tensor"), pairs)

    merged = [plus(own, arrived[0]).astype(BF16), plus(own_beside, arrived[1]).astype(BF16)]
    odd = ((k ^ t) & 1) == 1
    keep, leaving = jnp.where(odd, merged[1], merged[0]), jnp.where(odd, merged[0], merged[1])
    first = plus(keep, swap(leaving, "tensor", n_t, 1))
    far_terms = [to_keeper(value, 2, at // 2, at % 2) for at, value in enumerate(far_back)]
    far_terms, _ = lax.optimization_barrier((far_terms, weight_grad))
    second = sum(value.astype(F32) for value in far_terms)
    swapped = ((k ^ t) & 2) == 2
    keep = jnp.where(swapped, second, first)
    leaving = jnp.where(swapped, first, second).astype(BF16)
    grad_tokens = plus(keep, swap(leaving, "tensor", n_t, 2)).astype(BF16)

    grad_gate, grad_up = (jnp.swapaxes(grad, 1, 2) for grad in weight_grad)
    return grad_tokens, grad_gate, grad_up


def bits_of(count):
    bits = []
    bit = 1
    while bit < count:
        bits.append(bit)
        bit *= 2
    return bits


def halving_sum(parts, axis, count):
    parts = dict(parts)
    for bit in bits_of(count):
        leaving = sorted(r for r in parts if r & bit)
        arrived = swap(jnp.stack([parts[r].astype(BF16) for r in leaving]), axis, count, bit)
        for at, r in enumerate(leaving):
            parts[r ^ bit] = plus(parts[r ^ bit], arrived[at])
            del parts[r]
    return parts[0]


def doubling_gather(value, axis, count):
    held = {0: value}
    for bit in reversed(bits_of(count)):
        known = sorted(held)
        arrived = swap(jnp.stack([held[r] for r in known]), axis, count, bit)
        for at, r in enumerate(known):
            held[r ^ bit] = arrived[at]
    return [held[r] for r in range(count)]


def on_any_slice(tokens, cotangent, expert_ids, gate_weight, up_weight, down_weight):
    n_dp, n_x, n_t = lax.axis_size("dp"), lax.axis_size("expert"), lax.axis_size("tensor")
    k, x, t = lax.axis_index("dp"), lax.axis_index("expert"), lax.axis_index("tensor")
    local_experts, width, hidden = gate_weight.shape
    rows = tokens.shape[0]
    slots = n_x * CAP
    ids_row = expert_ids.reshape(1, rows)
    order = jnp.arange(rows, dtype=jnp.int32)
    earlier = (expert_ids == ids_row) & (order[:, None] < order[None, :])
    position = jnp.sum(earlier.astype(jnp.int32), axis=0)
    target = ids_row[0] * CAP + position
    targets = lax.all_gather(target, ("dp", "expert"), axis=0, tiled=False).reshape(n_dp, n_x, rows)
    pair = jnp.stack([tokens, cotangent])
    placers, slot_rows = [], []
    for rel in range(n_dp):
        columns = lax.dynamic_slice_in_dim(pair, (k ^ rel) * width, width, axis=2)
        mine = columns if rel == 0 else swap(columns, "dp", n_dp, rel)
        blocks = lax.all_gather(mine, "expert", axis=1, tiled=True)
        goal = lax.dynamic_index_in_dim(targets, k ^ rel, axis=0, keepdims=False)
        expert = goal // CAP - x * local_experts
        place = jnp.arange(n_x, dtype=jnp.int32)[:, None] * CAP + goal % CAP
        row = jnp.where((expert >= 0) & (expert < local_experts), expert * slots + place, -1)
        row = row.reshape(1, n_x * rows)
        every = jnp.arange(local_experts * slots, dtype=jnp.int32)[:, None]
        placer = (every == row).astype(BF16)
        placers.append(placer)
        slot_rows.append(
            jnp.einsum("sn,and->asd", placer, blocks, preferred_element_type=F32)
            .astype(BF16)
            .reshape(2, local_experts, slots, width)
        )
    slot_rows = jnp.concatenate(slot_rows, axis=2)
    inputs, grads_in = slot_rows[0], slot_rows[1]

    def act(values, weight):
        return jnp.einsum("esd,edf->esf", values, weight, preferred_element_type=F32).astype(BF16)

    acts = jnp.stack([act(inputs, gate_weight), act(inputs, up_weight), act(grads_in, down_weight)])
    acts = acts.reshape(3, local_experts, n_dp, slots, hidden)
    acts = halving_sum({r: acts[:, :, r] for r in range(n_dp)}, "dp", n_dp)
    grads = doubling_gather(jnp.stack(swiglu_grads(acts[0], acts[1], acts[2])), "dp", n_dp)
    grads = jnp.concatenate(grads, axis=2)
    gate_grad, up_grad = grads[0], grads[1]
    partial_value = jnp.einsum("esf,edf->esd", gate_grad, gate_weight, preferred_element_type=F32)
    partial_value = partial_value + jnp.einsum("esf,edf->esd", up_grad, up_weight, preferred_element_type=F32)
    partial_value = partial_value.astype(BF16).reshape(local_experts, n_dp, slots, width)
    per_token = []
    for rel in range(n_dp):
        flat = partial_value[:, rel].reshape(local_experts * slots, width)
        spread = lax.dot_general(placers[rel], flat, (((0,), (0,)), ((), ())), preferred_element_type=F32)
        spread = spread.astype(BF16).reshape(n_x, rows, width)
        per_token.append(lax.psum_scatter(spread, "expert", scatter_dimension=0, tiled=False))
    per_token = jnp.stack(per_token)
    terms = {r: lax.dynamic_index_in_dim(per_token, k ^ t ^ r, axis=0, keepdims=False) for r in range(n_t)}
    summed = halving_sum(terms, "tensor", n_t).astype(BF16)
    summed = lax.ppermute(
        summed, ("dp", "tensor"), [(i * n_t + j, j * n_t + i) for i in range(n_dp) for j in range(n_t)]
    )
    grad_gate = jnp.einsum("esd,esf->edf", inputs, gate_grad, preferred_element_type=F32).astype(BF16)
    grad_up = jnp.einsum("esd,esf->edf", inputs, up_grad, preferred_element_type=F32).astype(BF16)
    return summed, grad_gate, grad_up


def solution(mesh):
    placed = (
        P(("dp", "expert"), None),
        P(("dp", "expert"), None),
        P(("dp", "expert"), None),
        P("expert", "dp", "tensor"),
        P("expert", "dp", "tensor"),
        P("expert", "dp", "tensor"),
    )
    sizes = tuple(mesh.shape[name] for name in ("dp", "expert", "tensor"))
    return jax.shard_map(
        on_small_slice if sizes == (4, 2, 4) else on_any_slice,
        mesh=mesh,
        in_specs=placed,
        out_specs=(
            P(("dp", "expert"), "tensor"),
            P("expert", "dp", "tensor"),
            P("expert", "dp", "tensor"),
        ),
        check_vma=False,
    )
```

```python
import functools

import jax
import jax.numpy as jnp
from jax import lax
from jax.experimental import pallas as pl
from jax.experimental.pallas import tpu as pltpu
from jax.sharding import PartitionSpec as P

CAP = 8
META = 16
F32 = jnp.float32
BF16 = jnp.bfloat16
MIB = 1024 * 1024
PLACE_COST = 1 << 34


def swap(value, axis, count, bit):
    return lax.ppermute(value, axis, [(i, i ^ bit) for i in range(count)])


def whole_spec(shape):
    return pl.BlockSpec(shape, lambda *_: (0,) * len(shape))


def params(mib=16):
    return pltpu.CompilerParams(vmem_limit_bytes=mib * MIB)


def placer_of(row, slot_count):
    every = lax.broadcasted_iota(jnp.int32, (slot_count, row.shape[1]), 0)
    return (every == row).astype(F32).astype(BF16)


def place_kernel(first, rows, mine, others, *refs):
    n_dp = len(mine)
    other = []
    for group in others:
        other += [group] if len(group.shape) == 2 else [group.at[i] for i in range(group.shape[0])]
    if first:
        placed, lines = refs[-2:]
    else:
        lines, placed = refs[0], refs[-1]
    local_experts, slot_rows, width = placed.shape
    slots = slot_rows // n_dp
    for rel in range(n_dp):
        if first:
            pair = [b[0 : rows + META, :] for b in (mine[rel], other[rel])]
            metas = [b[rows:, 0:rows].astype(F32) for b in pair]
            ids = jnp.concatenate([m[0:1] for m in metas], axis=1)
            place = jnp.concatenate([m[1:2] for m in metas], axis=1)
            low = (lax.axis_index("expert") * local_experts).astype(F32)
            row = ((ids - low) * slots + place).astype(jnp.int32)
            lines[rel] = jnp.broadcast_to(row, (8, row.shape[1]))
            pair = [b[0:rows] for b in pair]
        else:
            row = lines[rel][0:1]
            pair = [b[...] for b in (mine[rel], other[rel])]
        placer = placer_of(row, local_experts * slots)
        found = jnp.dot(placer, jnp.concatenate(pair, axis=0), preferred_element_type=F32).astype(BF16)
        placed[:, rel * slots : (rel + 1) * slots, :] = found.reshape(local_experts, slots, width)


def place(mine, others, lines, rows, local_experts, after):
    first = lines is None
    n_dp, slots = len(mine), 2 * CAP
    width = mine[0].shape[1]
    placed = jax.ShapeDtypeStruct((local_experts, n_dp * slots, width), BF16)
    line = jax.ShapeDtypeStruct((n_dp, 8, 2 * rows), jnp.int32)
    vmem = pl.BlockSpec(memory_space=pltpu.VMEM)
    operands = [*others] + ([] if first else [lines])

    def kernel(*refs):
        split_at = n_dp + len(others)
        place_kernel(first, rows, refs[:n_dp], refs[n_dp:split_at], *refs[split_at:])

    return pl.pallas_call(
        kernel,
        out_shape=[placed, line] if first else placed,
        in_specs=[vmem] * (n_dp + len(operands))
        + [pl.BlockSpec(memory_space=pl.ANY)] * len(after),
        out_specs=[vmem, vmem] if first else vmem,
        compiler_params=params(),
        cost_estimate=pl.CostEstimate(flops=PLACE_COST, bytes_accessed=4 * rows * width * n_dp, transcendentals=0),
    )(*mine, *operands, *after)


def back_kernel(low, first, last, *refs):
    if first:
        earlier, refs = refs[0], refs[1:]
    if last:
        lines, refs = refs[0], refs[1:]
    h0, h1, gate, up = refs[:4]
    outs, near, sems = refs[4:-2], refs[-2], refs[-1]
    parts = (h0, h1)
    count, slots, _ = h0.shape
    hidden = gate.shape[1]
    per_copy = count // sems.shape[1]

    def copy_of(which, at):
        rows = pl.ds(which * hidden, hidden)
        source = (gate, up)[which].at[pl.ds(first + at * per_copy, per_copy)]
        return pltpu.make_async_copy(source, near.at[pl.ds(at * per_copy, per_copy), rows], sems.at[which, at])

    for at in range(sems.shape[1]):
        for which in range(2):
            copy_of(which, at).start()
    for at in range(sems.shape[1]):
        for which in range(2):
            copy_of(which, at).wait()
        for e in range(at * per_copy, (at + 1) * per_copy):
            grads = jnp.concatenate([h[e] for h in parts], axis=0)
            value = jnp.dot(grads, near[e], preferred_element_type=F32).astype(BF16)
            for i in range(2):
                rows = value[i * slots : (i + 1) * slots]
                if last:
                    outs[-1][i, (first + e) * slots : (first + e + 1) * slots, :] = rows
                else:
                    outs[0][i, e * slots : (e + 1) * slots, :] = rows
    if not last:
        return
    held = outs[-1]
    if first:
        held[:, 0 : first * slots, :] = earlier[...]
    rows = outs[0].shape[0]
    odd = (lax.axis_index("dp") ^ lax.axis_index("tensor")) & 1
    for i in range(2):
        which = odd ^ i if low else i
        placer = placer_of(lines[low + which][0:1], held.shape[1])
        token_rows = lax.dot_general(
            placer, held[which], (((0,), (0,)), ((), ())), preferred_element_type=F32
        ).astype(BF16)
        outs[2 * i][...] = token_rows[0:rows]
        outs[2 * i + 1][...] = token_rows[rows:]


def back(low, lines, parts, gate, up, rows, first=0, earlier=None):
    local_experts, hidden, width = gate.shape
    count, slots, _ = parts[0].shape
    last = first + count == local_experts
    vmem = pl.BlockSpec(memory_space=pltpu.VMEM)
    flops = (16 if last else 1) * count * 2 * slots * width * hidden
    operands = ([earlier] if first else []) + ([lines] if last else []) + [*parts]
    near = [
        pltpu.VMEM((count, 2 * hidden, width), BF16),
        pltpu.SemaphoreType.DMA((2, count // 2 if count % 2 == 0 else count)),
    ]
    if last:
        out_shape = [jax.ShapeDtypeStruct((rows, width), BF16)] * 4
        near = [pltpu.VMEM((2, local_experts * slots, width), BF16)] + near
    else:
        out_shape = jax.ShapeDtypeStruct((2, count * slots, width), BF16)
    return pl.pallas_call(
        functools.partial(back_kernel, low, first, last),
        out_shape=out_shape,
        in_specs=[vmem] * len(operands) + [pl.BlockSpec(memory_space=pl.ANY)] * 2,
        out_specs=[vmem] * 4 if last else vmem,
        scratch_shapes=near,
        compiler_params=params(48),
        cost_estimate=pl.CostEstimate(
            flops=flops, bytes_accessed=2 * count * width * hidden * 2 if last else width, transcendentals=0
        ),
    )(*operands, gate, up)


def weight_kernel(placed, h0, h1, h2, h3, gate, up):
    hidden = gate.shape[1]
    for i in range(gate.shape[0]):
        grads = jnp.concatenate([h[i] for h in (h0, h1, h2, h3)], axis=0)
        both = lax.dot_general(
            grads, placed[i], (((0,), (0,)), ((), ())), preferred_element_type=F32
        ).astype(BF16)
        gate[i] = both[0:hidden]
        up[i] = both[hidden:]


def weight_grads(placed, parts, per_step):
    local_experts, slot_rows, width = placed.shape
    _, slots, both = parts[0].shape
    hidden = both // 2
    part_spec = pl.BlockSpec((per_step, slots, both), lambda e: (e, 0, 0))
    out_spec = pl.BlockSpec((per_step, hidden, width), lambda e: (e, 0, 0))
    flops = 2 * local_experts * slot_rows * width * both
    return pl.pallas_call(
        weight_kernel,
        grid=(local_experts // per_step,),
        out_shape=[jax.ShapeDtypeStruct((local_experts, hidden, width), BF16)] * 2,
        in_specs=[pl.BlockSpec((per_step, slot_rows, width), lambda e: (e, 0, 0))] + [part_spec] * len(parts),
        out_specs=[out_spec] * 2,
        compiler_params=params(12),
        cost_estimate=pl.CostEstimate(
            flops=4 * flops, bytes_accessed=local_experts * width * both * 2, transcendentals=0
        ),
    )(placed, *parts)


def plus(first, second):
    return first.astype(F32) + second.astype(F32)


def swiglu_grads(gate_act, up_act, hidden_grad):
    sigmoid_gate = jax.nn.sigmoid(gate_act)
    up_grad = (hidden_grad * gate_act * sigmoid_gate).astype(BF16)
    gate_grad = (
        hidden_grad * up_act * sigmoid_gate * (1.0 + gate_act * (1.0 - sigmoid_gate))
    ).astype(BF16)
    return gate_grad, up_grad


def on_small_slice(tokens, cotangent, expert_ids, gate_weight, up_weight, down_weight):
    n_dp, n_x, n_t = 4, 2, 4
    k, x, t = lax.axis_index("dp"), lax.axis_index("expert"), lax.axis_index("tensor")
    width = gate_weight.shape[1]
    rows = tokens.shape[0]
    ids_row = expert_ids.reshape(1, rows)
    order = jnp.arange(rows, dtype=jnp.int32)
    earlier = (expert_ids == ids_row) & (order[:, None] < order[None, :])
    position = jnp.sum(earlier.astype(jnp.int32), axis=0, keepdims=True) + x * CAP
    meta = jnp.concatenate([ids_row, position], axis=0).astype(BF16)
    meta = jnp.pad(meta, ((0, META - 2), (0, width - rows)))

    def columns(values, rel):
        return lax.dynamic_slice_in_dim(values, (k ^ rel) * width, width, axis=1)

    chunks = [jnp.concatenate([columns(tokens, rel), meta], axis=0) for rel in range(n_dp)]

    def to_owner(value, rel, flip):
        if rel == 0 and flip == 0:
            return value
        pairs = [
            (i * n_x + j, (i ^ rel) * n_x + (j ^ flip)) for i in range(n_dp) for j in range(n_x)
        ]
        return lax.ppermute(value, ("dp", "expert"), pairs)

    own_tokens = [to_owner(c, rel, 0) for rel, c in enumerate(chunks)]
    near_tokens = [to_owner(c, rel, 1) for rel, c in enumerate(chunks[:2])]
    grads = [columns(cotangent, rel) for rel in range(n_dp)]
    far_tokens, grads = lax.optimization_barrier((own_tokens[2:], grads))
    near_tokens, far_tokens = lax.optimization_barrier((near_tokens, far_tokens))
    far_tokens = [swap(c, "expert", n_x, 1) for c in far_tokens]
    own_grads = [to_owner(c, rel, 0) for rel, c in enumerate(grads)]
    leaving_grads = jnp.stack(own_grads)
    far_tokens, leaving_grads = lax.optimization_barrier((far_tokens, leaving_grads))
    other_grads = swap(leaving_grads, "expert", n_x, 1)
    gate_weight, up_weight, down_weight = (
        jnp.swapaxes(weight, 1, 2) for weight in (gate_weight, up_weight, down_weight)
    )
    local_experts = gate_weight.shape[0]

    def project(values, weight):
        act = jnp.einsum("esd,ehd->esh", values, weight, preferred_element_type=F32).astype(BF16)
        return jnp.split(act, n_dp, axis=1)

    def near_and_far(act):
        near, far = swap(act[1], "dp", n_dp, 1), swap(act[3], "dp", n_dp, 1)
        return plus(act[0], near), plus(act[2], far).astype(BF16)

    placed, lines = place(own_tokens, near_tokens + far_tokens, None, rows, local_experts, [leaving_grads])
    gate_near, gate_far = near_and_far(project(placed, gate_weight))
    up_near, up_far = near_and_far(project(placed, up_weight))
    far = jnp.stack([gate_far, up_far])
    there = swap(far, "dp", n_dp, 2)
    placed_grads = place(own_grads, [other_grads], lines, rows, local_experts, [far])
    hidden_act = project(placed_grads, down_weight)
    beside, there = lax.optimization_barrier((swap(hidden_act[3], "dp", n_dp, 1), there))
    hidden_far = plus(hidden_act[2], beside).astype(BF16)
    hidden_near = plus(hidden_act[0], swap(hidden_act[1], "dp", n_dp, 1))
    gate_act, up_act = plus(gate_near, there[0]), plus(up_near, there[1])
    sigmoid_gate = jax.nn.sigmoid(gate_act)
    up_factor = gate_act * sigmoid_gate
    gate_factor = up_act * sigmoid_gate * (1.0 + gate_act * (1.0 - sigmoid_gate))
    hidden_grad = plus(hidden_near, swap(hidden_far, "dp", n_dp, 2))
    part = jnp.concatenate([hidden_grad * gate_factor, hidden_grad * up_factor], axis=2).astype(BF16)
    count = local_experts * 7 // 16
    far = [swap(piece, "dp", n_dp, 2) for piece in jnp.split(part, [count], axis=0)]
    beside = swap(part, "dp", n_dp, 1)
    near_back = back(0, lines, [part, beside], gate_weight, up_weight, rows)
    far[0], _ = lax.optimization_barrier((far[0], near_back[0]))
    far_beside = [swap(far[0], "dp", n_dp, 1)]
    early = back(2, lines, [far[0], far_beside[0]], gate_weight, up_weight, rows)
    far[1], _ = lax.optimization_barrier((far[1], early))
    far_beside.append(swap(far[1], "dp", n_dp, 1))
    far_back = back(2, lines, [far[1], far_beside[1]], gate_weight, up_weight, rows, count, early)
    parts = [part, beside, jnp.concatenate(far, axis=0), jnp.concatenate(far_beside, axis=0)]
    own, other, own_beside, other_beside = near_back
    own_beside, other_beside = swap(own_beside, "dp", n_dp, 1), swap(other_beside, "dp", n_dp, 1)
    own_beside, other_beside = lax.optimization_barrier((own_beside, other_beside))
    arrived = swap(jnp.stack([other, other_beside]), "expert", n_x, 1)
    arrived, after_back, _ = lax.optimization_barrier((arrived, placed, far_back[0]))
    weight_grad = weight_grads(after_back, parts, 4)

    def to_keeper(value, low, turn, flip):
        pairs = []
        for i in range(n_dp):
            for j in range(n_x):
                for l in range(n_t):
                    odd = (i ^ l) & 1
                    to = ((i ^ low ^ odd ^ turn) * n_x + (j ^ flip)) * n_t + (l ^ odd)
                    pairs.append(((i * n_x + j) * n_t + l, to))
        return lax.ppermute(value, ("dp", "expert", "tensor"), pairs)

    merged = [plus(own, arrived[0]).astype(BF16), plus(own_beside, arrived[1]).astype(BF16)]
    odd = ((k ^ t) & 1) == 1
    keep, leaving = jnp.where(odd, merged[1], merged[0]), jnp.where(odd, merged[0], merged[1])
    first = plus(keep, swap(leaving, "tensor", n_t, 1))
    far_terms = [to_keeper(value, 2, at // 2, at % 2) for at, value in enumerate(far_back)]
    far_terms, _ = lax.optimization_barrier((far_terms, weight_grad))
    second = sum(value.astype(F32) for value in far_terms)
    swapped = ((k ^ t) & 2) == 2
    keep = jnp.where(swapped, second, first)
    leaving = jnp.where(swapped, first, second).astype(BF16)
    grad_tokens = plus(keep, swap(leaving, "tensor", n_t, 2)).astype(BF16)

    grad_gate, grad_up = (jnp.swapaxes(grad, 1, 2) for grad in weight_grad)
    return grad_tokens, grad_gate, grad_up


def bits_of(count):
    bits = []
    bit = 1
    while bit < count:
        bits.append(bit)
        bit *= 2
    return bits


def halving_sum(parts, axis, count):
    parts = dict(parts)
    for bit in bits_of(count):
        leaving = sorted(r for r in parts if r & bit)
        arrived = swap(jnp.stack([parts[r].astype(BF16) for r in leaving]), axis, count, bit)
        for at, r in enumerate(leaving):
            parts[r ^ bit] = plus(parts[r ^ bit], arrived[at])
            del parts[r]
    return parts[0]


def doubling_gather(value, axis, count):
    held = {0: value}
    for bit in reversed(bits_of(count)):
        known = sorted(held)
        arrived = swap(jnp.stack([held[r] for r in known]), axis, count, bit)
        for at, r in enumerate(known):
            held[r ^ bit] = arrived[at]
    return [held[r] for r in range(count)]


def on_any_slice(tokens, cotangent, expert_ids, gate_weight, up_weight, down_weight):
    n_dp, n_x, n_t = lax.axis_size("dp"), lax.axis_size("expert"), lax.axis_size("tensor")
    k, x, t = lax.axis_index("dp"), lax.axis_index("expert"), lax.axis_index("tensor")
    local_experts, width, hidden = gate_weight.shape
    rows = tokens.shape[0]
    slots = n_x * CAP
    ids_row = expert_ids.reshape(1, rows)
    order = jnp.arange(rows, dtype=jnp.int32)
    earlier = (expert_ids == ids_row) & (order[:, None] < order[None, :])
    position = jnp.sum(earlier.astype(jnp.int32), axis=0)
    target = ids_row[0] * CAP + position
    targets = lax.all_gather(target, ("dp", "expert"), axis=0, tiled=False).reshape(n_dp, n_x, rows)
    pair = jnp.stack([tokens, cotangent])
    placers, slot_rows = [], []
    for rel in range(n_dp):
        columns = lax.dynamic_slice_in_dim(pair, (k ^ rel) * width, width, axis=2)
        mine = columns if rel == 0 else swap(columns, "dp", n_dp, rel)
        blocks = lax.all_gather(mine, "expert", axis=1, tiled=True)
        goal = lax.dynamic_index_in_dim(targets, k ^ rel, axis=0, keepdims=False)
        expert = goal // CAP - x * local_experts
        place = jnp.arange(n_x, dtype=jnp.int32)[:, None] * CAP + goal % CAP
        row = jnp.where((expert >= 0) & (expert < local_experts), expert * slots + place, -1)
        row = row.reshape(1, n_x * rows)
        every = jnp.arange(local_experts * slots, dtype=jnp.int32)[:, None]
        placer = (every == row).astype(BF16)
        placers.append(placer)
        slot_rows.append(
            jnp.einsum("sn,and->asd", placer, blocks, preferred_element_type=F32)
            .astype(BF16)
            .reshape(2, local_experts, slots, width)
        )
    slot_rows = jnp.concatenate(slot_rows, axis=2)
    inputs, grads_in = slot_rows[0], slot_rows[1]

    def act(values, weight):
        return jnp.einsum("esd,edf->esf", values, weight, preferred_element_type=F32).astype(BF16)

    acts = jnp.stack([act(inputs, gate_weight), act(inputs, up_weight), act(grads_in, down_weight)])
    acts = acts.reshape(3, local_experts, n_dp, slots, hidden)
    acts = halving_sum({r: acts[:, :, r] for r in range(n_dp)}, "dp", n_dp)
    grads = doubling_gather(jnp.stack(swiglu_grads(acts[0], acts[1], acts[2])), "dp", n_dp)
    grads = jnp.concatenate(grads, axis=2)
    gate_grad, up_grad = grads[0], grads[1]
    partial_value = jnp.einsum("esf,edf->esd", gate_grad, gate_weight, preferred_element_type=F32)
    partial_value = partial_value + jnp.einsum("esf,edf->esd", up_grad, up_weight, preferred_element_type=F32)
    partial_value = partial_value.astype(BF16).reshape(local_experts, n_dp, slots, width)
    per_token = []
    for rel in range(n_dp):
        flat = partial_value[:, rel].reshape(local_experts * slots, width)
        spread = lax.dot_general(placers[rel], flat, (((0,), (0,)), ((), ())), preferred_element_type=F32)
        spread = spread.astype(BF16).reshape(n_x, rows, width)
        per_token.append(lax.psum_scatter(spread, "expert", scatter_dimension=0, tiled=False))
    per_token = jnp.stack(per_token)
    terms = {r: lax.dynamic_index_in_dim(per_token, k ^ t ^ r, axis=0, keepdims=False) for r in range(n_t)}
    summed = halving_sum(terms, "tensor", n_t).astype(BF16)
    summed = lax.ppermute(
        summed, ("dp", "tensor"), [(i * n_t + j, j * n_t + i) for i in range(n_dp) for j in range(n_t)]
    )
    grad_gate = jnp.einsum("esd,esf->edf", inputs, gate_grad, preferred_element_type=F32).astype(BF16)
    grad_up = jnp.einsum("esd,esf->edf", inputs, up_grad, preferred_element_type=F32).astype(BF16)
    return summed, grad_gate, grad_up


def solution(mesh):
    placed = (
        P(("dp", "expert"), None),
        P(("dp", "expert"), None),
        P(("dp", "expert"), None),
        P("expert", "dp", "tensor"),
        P("expert", "dp", "tensor"),
        P("expert", "dp", "tensor"),
    )
    sizes = tuple(mesh.shape[name] for name in ("dp", "expert", "tensor"))
    return jax.shard_map(
        on_small_slice if sizes == (4, 2, 4) else on_any_slice,
        mesh=mesh,
        in_specs=placed,
        out_specs=(
            P(("dp", "expert"), "tensor"),
            P("expert", "dp", "tensor"),
            P("expert", "dp", "tensor"),
        ),
        check_vma=False,
    )
```

```python
import functools

import jax
import jax.numpy as jnp
from jax import lax
from jax.experimental import pallas as pl
from jax.experimental.pallas import tpu as pltpu
from jax.sharding import PartitionSpec as P

CAP = 8
META = 16
F32 = jnp.float32
BF16 = jnp.bfloat16
MIB = 1024 * 1024
PLACE_COST = 1 << 34


def swap(value, axis, count, bit):
    return lax.ppermute(value, axis, [(i, i ^ bit) for i in range(count)])


def whole_spec(shape):
    return pl.BlockSpec(shape, lambda *_: (0,) * len(shape))


def params(mib=16):
    return pltpu.CompilerParams(vmem_limit_bytes=mib * MIB)


def placer_of(row, slot_count):
    every = lax.broadcasted_iota(jnp.int32, (slot_count, row.shape[1]), 0)
    return (every == row).astype(F32).astype(BF16)


def place_kernel(first, rows, mine, others, *refs):
    n_dp = len(mine)
    other = []
    for group in others:
        other += [group] if len(group.shape) == 2 else [group.at[i] for i in range(group.shape[0])]
    if first:
        placed, lines = refs[-2:]
    else:
        lines, placed = refs[0], refs[-1]
    local_experts, slot_rows, width = placed.shape
    slots = slot_rows // n_dp
    for rel in range(n_dp):
        if first:
            pair = [b[0 : rows + META, :] for b in (mine[rel], other[rel])]
            here = lax.axis_index("expert")
            goals = [b[rows:, 0:rows][0:1].astype(F32).astype(jnp.int32) for b in pair]
            row = jnp.concatenate(
                [
                    (goal // CAP - here * local_experts) * slots + source * CAP + goal % CAP
                    for goal, source in zip(goals, (here, 1 - here))
                ],
                axis=1,
            )
            lines[rel] = jnp.broadcast_to(row, (8, row.shape[1]))
            pair = [b[0:rows] for b in pair]
        else:
            row = lines[rel][0:1]
            pair = [b[...] for b in (mine[rel], other[rel])]
        placer = placer_of(row, local_experts * slots)
        found = jnp.dot(placer, jnp.concatenate(pair, axis=0), preferred_element_type=F32).astype(BF16)
        placed[:, rel * slots : (rel + 1) * slots, :] = found.reshape(local_experts, slots, width)


def place(mine, others, lines, rows, local_experts, after):
    first = lines is None
    n_dp, slots = len(mine), 2 * CAP
    width = mine[0].shape[1]
    placed = jax.ShapeDtypeStruct((local_experts, n_dp * slots, width), BF16)
    line = jax.ShapeDtypeStruct((n_dp, 8, 2 * rows), jnp.int32)
    vmem = pl.BlockSpec(memory_space=pltpu.VMEM)
    operands = [*others] + ([] if first else [lines])

    def kernel(*refs):
        split_at = n_dp + len(others)
        place_kernel(first, rows, refs[:n_dp], refs[n_dp:split_at], *refs[split_at:])

    return pl.pallas_call(
        kernel,
        out_shape=[placed, line] if first else placed,
        in_specs=[vmem] * (n_dp + len(operands))
        + [pl.BlockSpec(memory_space=pl.ANY)] * len(after),
        out_specs=[vmem, vmem] if first else vmem,
        compiler_params=params(),
        cost_estimate=pl.CostEstimate(flops=PLACE_COST, bytes_accessed=4 * rows * width * n_dp, transcendentals=0),
    )(*mine, *operands, *after)


def back_kernel(low, first, last, *refs):
    if first:
        earlier, refs = refs[0], refs[1:]
    if last:
        lines, refs = refs[0], refs[1:]
    h0, h1, gate, up = refs[:4]
    outs = refs[4:]
    count, slots, _ = h0.shape
    hidden = gate.shape[1]
    for e in range(count):
        grads = jnp.concatenate([h0[e], h1[e]], axis=0)
        value = jnp.dot(grads[:, 0:hidden], gate[first + e], preferred_element_type=F32)
        value = value + jnp.dot(grads[:, hidden:], up[first + e], preferred_element_type=F32)
        value = value.astype(BF16)
        for i in range(2):
            rows = value[i * slots : (i + 1) * slots]
            if last:
                outs[-1][i, (first + e) * slots : (first + e + 1) * slots, :] = rows
            else:
                outs[0][i, e * slots : (e + 1) * slots, :] = rows
    if not last:
        return
    held = outs[-1]
    if first:
        held[:, 0 : first * slots, :] = earlier[...]
    rows = outs[0].shape[0]
    odd = (lax.axis_index("dp") ^ lax.axis_index("tensor")) & 1
    for i in range(2):
        which = odd ^ i if low else i
        placer = placer_of(lines[low + which][0:1], held.shape[1])
        token_rows = lax.dot_general(
            placer, held[which], (((0,), (0,)), ((), ())), preferred_element_type=F32
        ).astype(BF16)
        outs[2 * i][...] = token_rows[0:rows]
        outs[2 * i + 1][...] = token_rows[rows:]


def back(low, lines, parts, gate, up, rows, first=0, earlier=None):
    local_experts, hidden, width = gate.shape
    count, slots, _ = parts[0].shape
    last = first + count == local_experts
    vmem = pl.BlockSpec(memory_space=pltpu.VMEM)
    flops = (16 if last else 1) * count * 2 * slots * width * hidden
    operands = ([earlier] if first else []) + ([lines] if last else []) + [*parts]
    near = []
    if last:
        out_shape = [jax.ShapeDtypeStruct((rows, width), BF16)] * 4
        near = [pltpu.VMEM((2, local_experts * slots, width), BF16)] + near
    else:
        out_shape = jax.ShapeDtypeStruct((2, count * slots, width), BF16)
    return pl.pallas_call(
        functools.partial(back_kernel, low, first, last),
        out_shape=out_shape,
        in_specs=[vmem] * (len(operands) + 2),
        out_specs=[vmem] * 4 if last else vmem,
        scratch_shapes=near,
        compiler_params=params(24),
        cost_estimate=pl.CostEstimate(
            flops=flops, bytes_accessed=2 * count * width * hidden * 2 if last else width, transcendentals=0
        ),
    )(*operands, gate, up)


def weight_kernel(placed, h0, h1, h2, h3, gate, up):
    hidden = gate.shape[1]
    for i in range(gate.shape[0]):
        grads = jnp.concatenate([h[i] for h in (h0, h1, h2, h3)], axis=0)
        both = lax.dot_general(
            grads, placed[i], (((0,), (0,)), ((), ())), preferred_element_type=F32
        ).astype(BF16)
        gate[i] = both[0:hidden]
        up[i] = both[hidden:]


def weight_grads(placed, parts, per_step):
    local_experts, slot_rows, width = placed.shape
    _, slots, both = parts[0].shape
    hidden = both // 2
    part_spec = pl.BlockSpec((per_step, slots, both), lambda e: (e, 0, 0))
    out_spec = pl.BlockSpec((per_step, hidden, width), lambda e: (e, 0, 0))
    flops = 2 * local_experts * slot_rows * width * both
    return pl.pallas_call(
        weight_kernel,
        grid=(local_experts // per_step,),
        out_shape=[jax.ShapeDtypeStruct((local_experts, hidden, width), BF16)] * 2,
        in_specs=[pl.BlockSpec((per_step, slot_rows, width), lambda e: (e, 0, 0))] + [part_spec] * len(parts),
        out_specs=[out_spec] * 2,
        compiler_params=params(12),
        cost_estimate=pl.CostEstimate(
            flops=4 * flops, bytes_accessed=local_experts * width * both * 2, transcendentals=0
        ),
    )(placed, *parts)


def plus(first, second):
    return first.astype(F32) + second.astype(F32)


def swiglu_grads(gate_act, up_act, hidden_grad):
    sigmoid_gate = jax.nn.sigmoid(gate_act)
    up_grad = (hidden_grad * gate_act * sigmoid_gate).astype(BF16)
    gate_grad = (
        hidden_grad * up_act * sigmoid_gate * (1.0 + gate_act * (1.0 - sigmoid_gate))
    ).astype(BF16)
    return gate_grad, up_grad


def on_small_slice(tokens, cotangent, expert_ids, gate_weight, up_weight, down_weight):
    n_dp, n_x, n_t = 4, 2, 4
    k, x, t = lax.axis_index("dp"), lax.axis_index("expert"), lax.axis_index("tensor")
    width = gate_weight.shape[1]
    rows = tokens.shape[0]
    ids_row = expert_ids.reshape(1, rows)
    order = jnp.arange(rows, dtype=jnp.int32)
    earlier = (expert_ids == ids_row) & (order[:, None] < order[None, :])
    goal = ids_row * CAP + jnp.sum(earlier.astype(jnp.int32), axis=0, keepdims=True)
    meta = jnp.pad(goal.astype(BF16), ((0, META - 1), (0, width - rows)))

    def columns(values, rel):
        return lax.dynamic_slice_in_dim(values, (k ^ rel) * width, width, axis=1)

    chunks = [jnp.concatenate([columns(tokens, rel), meta], axis=0) for rel in range(n_dp)]

    def to_owner(value, rel, flip):
        if rel == 0 and flip == 0:
            return value
        pairs = [
            (i * n_x + j, (i ^ rel) * n_x + (j ^ flip)) for i in range(n_dp) for j in range(n_x)
        ]
        return lax.ppermute(value, ("dp", "expert"), pairs)

    own_tokens = [to_owner(c, rel, 0) for rel, c in enumerate(chunks)]
    near_tokens = [to_owner(c, rel, 1) for rel, c in enumerate(chunks[:2])]
    grads = [columns(cotangent, rel) for rel in range(n_dp)]
    far_tokens, grads = lax.optimization_barrier((own_tokens[2:], grads))
    near_tokens, far_tokens = lax.optimization_barrier((near_tokens, far_tokens))
    far_tokens = [swap(c, "expert", n_x, 1) for c in far_tokens]
    own_grads = [to_owner(c, rel, 0) for rel, c in enumerate(grads)]
    leaving_grads = jnp.stack(own_grads)
    far_tokens, leaving_grads = lax.optimization_barrier((far_tokens, leaving_grads))
    other_grads = swap(leaving_grads, "expert", n_x, 1)
    gate_weight, up_weight, down_weight = (
        jnp.swapaxes(weight, 1, 2) for weight in (gate_weight, up_weight, down_weight)
    )
    local_experts = gate_weight.shape[0]

    def project(values, weight):
        act = jnp.einsum("esd,ehd->esh", values, weight, preferred_element_type=F32).astype(BF16)
        return jnp.split(act, n_dp, axis=1)

    def near_and_far(act):
        near, far = swap(act[1], "dp", n_dp, 1), swap(act[3], "dp", n_dp, 1)
        return plus(act[0], near), plus(act[2], far).astype(BF16)

    placed, lines = place(own_tokens, near_tokens + far_tokens, None, rows, local_experts, [leaving_grads])
    gate_near, gate_far = near_and_far(project(placed, gate_weight))
    up_near, up_far = near_and_far(project(placed, up_weight))
    far = jnp.stack([gate_far, up_far])
    there = swap(far, "dp", n_dp, 2)
    placed_grads = place(own_grads, [other_grads], lines, rows, local_experts, [far])
    hidden_act = project(placed_grads, down_weight)
    beside, there = lax.optimization_barrier((swap(hidden_act[3], "dp", n_dp, 1), there))
    hidden_far = plus(hidden_act[2], beside).astype(BF16)
    hidden_near = plus(hidden_act[0], swap(hidden_act[1], "dp", n_dp, 1))
    gate_act, up_act = plus(gate_near, there[0]), plus(up_near, there[1])
    sigmoid_gate = jax.nn.sigmoid(gate_act)
    up_factor = gate_act * sigmoid_gate
    gate_factor = up_act * sigmoid_gate * (1.0 + gate_act * (1.0 - sigmoid_gate))
    hidden_grad = plus(hidden_near, swap(hidden_far, "dp", n_dp, 2))
    part = jnp.concatenate([hidden_grad * gate_factor, hidden_grad * up_factor], axis=2).astype(BF16)
    count = local_experts * 7 // 16
    far = [swap(piece, "dp", n_dp, 2) for piece in jnp.split(part, [count], axis=0)]
    beside = swap(part, "dp", n_dp, 1)
    near_back = back(0, lines, [part, beside], gate_weight, up_weight, rows)
    far[0], _ = lax.optimization_barrier((far[0], near_back[0]))
    far_beside = [swap(far[0], "dp", n_dp, 1)]
    early = back(2, lines, [far[0], far_beside[0]], gate_weight, up_weight, rows)
    far[1], _ = lax.optimization_barrier((far[1], early))
    far_beside.append(swap(far[1], "dp", n_dp, 1))
    far_back = back(2, lines, [far[1], far_beside[1]], gate_weight, up_weight, rows, count, early)
    parts = [part, beside, jnp.concatenate(far, axis=0), jnp.concatenate(far_beside, axis=0)]
    own, other, own_beside, other_beside = near_back
    own_beside, other_beside = swap(own_beside, "dp", n_dp, 1), swap(other_beside, "dp", n_dp, 1)
    own_beside, other_beside = lax.optimization_barrier((own_beside, other_beside))
    arrived = swap(jnp.stack([other, other_beside]), "expert", n_x, 1)
    arrived, after_back, _ = lax.optimization_barrier((arrived, placed, far_back[0]))
    weight_grad = weight_grads(after_back, parts, 4)

    def to_keeper(value, low, turn, flip):
        pairs = []
        for i in range(n_dp):
            for j in range(n_x):
                for l in range(n_t):
                    odd = (i ^ l) & 1
                    to = ((i ^ low ^ odd ^ turn) * n_x + (j ^ flip)) * n_t + (l ^ odd)
                    pairs.append(((i * n_x + j) * n_t + l, to))
        return lax.ppermute(value, ("dp", "expert", "tensor"), pairs)

    merged = [plus(own, arrived[0]).astype(BF16), plus(own_beside, arrived[1]).astype(BF16)]
    odd = ((k ^ t) & 1) == 1
    keep, leaving = jnp.where(odd, merged[1], merged[0]), jnp.where(odd, merged[0], merged[1])
    first = plus(keep, swap(leaving, "tensor", n_t, 1))
    far_terms = [to_keeper(value, 2, at // 2, at % 2) for at, value in enumerate(far_back)]
    far_terms, _ = lax.optimization_barrier((far_terms, weight_grad))
    second = sum(value.astype(F32) for value in far_terms)
    swapped = ((k ^ t) & 2) == 2
    keep = jnp.where(swapped, second, first)
    leaving = jnp.where(swapped, first, second).astype(BF16)
    grad_tokens = plus(keep, swap(leaving, "tensor", n_t, 2)).astype(BF16)

    grad_gate, grad_up = (jnp.swapaxes(grad, 1, 2) for grad in weight_grad)
    return grad_tokens, grad_gate, grad_up


def bits_of(count):
    bits = []
    bit = 1
    while bit < count:
        bits.append(bit)
        bit *= 2
    return bits


def halving_sum(parts, axis, count):
    parts = dict(parts)
    for bit in bits_of(count):
        leaving = sorted(r for r in parts if r & bit)
        arrived = swap(jnp.stack([parts[r].astype(BF16) for r in leaving]), axis, count, bit)
        for at, r in enumerate(leaving):
            parts[r ^ bit] = plus(parts[r ^ bit], arrived[at])
            del parts[r]
    return parts[0]


def doubling_gather(value, axis, count):
    held = {0: value}
    for bit in reversed(bits_of(count)):
        known = sorted(held)
        arrived = swap(jnp.stack([held[r] for r in known]), axis, count, bit)
        for at, r in enumerate(known):
            held[r ^ bit] = arrived[at]
    return [held[r] for r in range(count)]


def on_any_slice(tokens, cotangent, expert_ids, gate_weight, up_weight, down_weight):
    n_dp, n_x, n_t = lax.axis_size("dp"), lax.axis_size("expert"), lax.axis_size("tensor")
    k, x, t = lax.axis_index("dp"), lax.axis_index("expert"), lax.axis_index("tensor")
    local_experts, width, hidden = gate_weight.shape
    rows = tokens.shape[0]
    slots = n_x * CAP
    ids_row = expert_ids.reshape(1, rows)
    order = jnp.arange(rows, dtype=jnp.int32)
    earlier = (expert_ids == ids_row) & (order[:, None] < order[None, :])
    position = jnp.sum(earlier.astype(jnp.int32), axis=0)
    target = ids_row[0] * CAP + position
    targets = lax.all_gather(target, ("dp", "expert"), axis=0, tiled=False).reshape(n_dp, n_x, rows)
    pair = jnp.stack([tokens, cotangent])
    placers, slot_rows = [], []
    for rel in range(n_dp):
        columns = lax.dynamic_slice_in_dim(pair, (k ^ rel) * width, width, axis=2)
        mine = columns if rel == 0 else swap(columns, "dp", n_dp, rel)
        blocks = lax.all_gather(mine, "expert", axis=1, tiled=True)
        goal = lax.dynamic_index_in_dim(targets, k ^ rel, axis=0, keepdims=False)
        expert = goal // CAP - x * local_experts
        place = jnp.arange(n_x, dtype=jnp.int32)[:, None] * CAP + goal % CAP
        row = jnp.where((expert >= 0) & (expert < local_experts), expert * slots + place, -1)
        row = row.reshape(1, n_x * rows)
        every = jnp.arange(local_experts * slots, dtype=jnp.int32)[:, None]
        placer = (every == row).astype(BF16)
        placers.append(placer)
        slot_rows.append(
            jnp.einsum("sn,and->asd", placer, blocks, preferred_element_type=F32)
            .astype(BF16)
            .reshape(2, local_experts, slots, width)
        )
    slot_rows = jnp.concatenate(slot_rows, axis=2)
    inputs, grads_in = slot_rows[0], slot_rows[1]

    def act(values, weight):
        return jnp.einsum("esd,edf->esf", values, weight, preferred_element_type=F32).astype(BF16)

    acts = jnp.stack([act(inputs, gate_weight), act(inputs, up_weight), act(grads_in, down_weight)])
    acts = acts.reshape(3, local_experts, n_dp, slots, hidden)
    acts = halving_sum({r: acts[:, :, r] for r in range(n_dp)}, "dp", n_dp)
    grads = doubling_gather(jnp.stack(swiglu_grads(acts[0], acts[1], acts[2])), "dp", n_dp)
    grads = jnp.concatenate(grads, axis=2)
    gate_grad, up_grad = grads[0], grads[1]
    partial_value = jnp.einsum("esf,edf->esd", gate_grad, gate_weight, preferred_element_type=F32)
    partial_value = partial_value + jnp.einsum("esf,edf->esd", up_grad, up_weight, preferred_element_type=F32)
    partial_value = partial_value.astype(BF16).reshape(local_experts, n_dp, slots, width)
    per_token = []
    for rel in range(n_dp):
        flat = partial_value[:, rel].reshape(local_experts * slots, width)
        spread = lax.dot_general(placers[rel], flat, (((0,), (0,)), ((), ())), preferred_element_type=F32)
        spread = spread.astype(BF16).reshape(n_x, rows, width)
        per_token.append(lax.psum_scatter(spread, "expert", scatter_dimension=0, tiled=False))
    per_token = jnp.stack(per_token)
    terms = {r: lax.dynamic_index_in_dim(per_token, k ^ t ^ r, axis=0, keepdims=False) for r in range(n_t)}
    summed = halving_sum(terms, "tensor", n_t).astype(BF16)
    summed = lax.ppermute(
        summed, ("dp", "tensor"), [(i * n_t + j, j * n_t + i) for i in range(n_dp) for j in range(n_t)]
    )
    grad_gate = jnp.einsum("esd,esf->edf", inputs, gate_grad, preferred_element_type=F32).astype(BF16)
    grad_up = jnp.einsum("esd,esf->edf", inputs, up_grad, preferred_element_type=F32).astype(BF16)
    return summed, grad_gate, grad_up


def solution(mesh):
    placed = (
        P(("dp", "expert"), None),
        P(("dp", "expert"), None),
        P(("dp", "expert"), None),
        P("expert", "dp", "tensor"),
        P("expert", "dp", "tensor"),
        P("expert", "dp", "tensor"),
    )
    sizes = tuple(mesh.shape[name] for name in ("dp", "expert", "tensor"))

    def on_device(tokens, cotangent, expert_ids, *weights):
        experts = weights[0].shape[0] * sizes[1]
        small = sizes == (4, 2, 4) and experts * CAP <= 256
        return (on_small_slice if small else on_any_slice)(tokens, cotangent, expert_ids, *weights)

    return jax.shard_map(
        on_device,
        mesh=mesh,
        in_specs=placed,
        out_specs=(
            P(("dp", "expert"), "tensor"),
            P("expert", "dp", "tensor"),
            P("expert", "dp", "tensor"),
        ),
        check_vma=False,
    )
```

```python
import functools

import jax
import jax.numpy as jnp
from jax import lax
from jax.experimental import pallas as pl
from jax.experimental.pallas import tpu as pltpu
from jax.sharding import PartitionSpec as P

CAP = 8
META = 16
F32 = jnp.float32
BF16 = jnp.bfloat16
MIB = 1024 * 1024
PLACE_COST = 1 << 34


def swap(value, axis, count, bit):
    return lax.ppermute(value, axis, [(i, i ^ bit) for i in range(count)])


def whole_spec(shape):
    return pl.BlockSpec(shape, lambda *_: (0,) * len(shape))


def params(mib=16):
    return pltpu.CompilerParams(vmem_limit_bytes=mib * MIB)


def placer_of(row, slot_count):
    every = lax.broadcasted_iota(jnp.int32, (slot_count, row.shape[1]), 0)
    return (every == row).astype(F32).astype(BF16)


def place_kernel(first, rows, mine, others, *refs):
    n_dp = len(mine)
    other = []
    for group in others:
        other += [group] if len(group.shape) == 2 else [group.at[i] for i in range(group.shape[0])]
    if first:
        placed, lines = refs[-2:]
    else:
        lines, placed = refs[0], refs[-1]
    local_experts, slot_rows, width = placed.shape
    slots = slot_rows // n_dp
    for rel in range(n_dp):
        if first:
            pair = [b[0 : rows + META, :] for b in (mine[rel], other[rel])]
            here = lax.axis_index("expert")
            goals = [b[rows:, 0:rows][0:1].astype(F32).astype(jnp.int32) for b in pair]
            row = jnp.concatenate(
                [
                    (goal // CAP - here * local_experts) * slots + source * CAP + goal % CAP
                    for goal, source in zip(goals, (here, 1 - here))
                ],
                axis=1,
            )
            lines[rel] = jnp.broadcast_to(row, (8, row.shape[1]))
            pair = [b[0:rows] for b in pair]
        else:
            row = lines[rel][0:1]
            pair = [b[...] for b in (mine[rel], other[rel])]
        placer = placer_of(row, local_experts * slots)
        found = jnp.dot(placer, jnp.concatenate(pair, axis=0), preferred_element_type=F32).astype(BF16)
        placed[:, rel * slots : (rel + 1) * slots, :] = found.reshape(local_experts, slots, width)


def place(mine, others, lines, rows, local_experts, after):
    first = lines is None
    n_dp, slots = len(mine), 2 * CAP
    width = mine[0].shape[1]
    placed = jax.ShapeDtypeStruct((local_experts, n_dp * slots, width), BF16)
    line = jax.ShapeDtypeStruct((n_dp, 8, 2 * rows), jnp.int32)
    vmem = pl.BlockSpec(memory_space=pltpu.VMEM)
    operands = [*others] + ([] if first else [lines])

    def kernel(*refs):
        split_at = n_dp + len(others)
        place_kernel(first, rows, refs[:n_dp], refs[n_dp:split_at], *refs[split_at:])

    return pl.pallas_call(
        kernel,
        out_shape=[placed, line] if first else placed,
        in_specs=[vmem] * (n_dp + len(operands))
        + [pl.BlockSpec(memory_space=pl.ANY)] * len(after),
        out_specs=[vmem, vmem] if first else vmem,
        compiler_params=params(),
        cost_estimate=pl.CostEstimate(flops=PLACE_COST, bytes_accessed=4 * rows * width * n_dp, transcendentals=0),
    )(*mine, *operands, *after)


def back_kernel(low, first, last, *refs):
    if first:
        earlier, refs = refs[0], refs[1:]
    if last:
        lines, refs = refs[0], refs[1:]
    h0, h1, refs = refs[0], refs[1], refs[2:]
    count, slots, _ = h0.shape
    if low:
        both, outs = refs[0], refs[1:]
    else:
        gate, up, both, outs = refs[0], refs[1], refs[6], refs[2:6] + refs[7:]
        hidden = gate.shape[1]
    for e in range(count):
        grads = jnp.concatenate([h0[e], h1[e]], axis=0)
        if not low:
            both[e, 0:hidden, :] = gate[e]
            both[e, hidden:, :] = up[e]
        value = jnp.dot(grads, both[first + e], preferred_element_type=F32).astype(BF16)
        for i in range(2):
            rows = value[i * slots : (i + 1) * slots]
            if last:
                outs[-1][i, (first + e) * slots : (first + e + 1) * slots, :] = rows
            else:
                outs[0][i, e * slots : (e + 1) * slots, :] = rows
    if not last:
        return
    held = outs[-1]
    if first:
        held[:, 0 : first * slots, :] = earlier[...]
    rows = outs[0].shape[0]
    odd = (lax.axis_index("dp") ^ lax.axis_index("tensor")) & 1
    for i in range(2):
        which = odd ^ i if low else i
        placer = placer_of(lines[low + which][0:1], held.shape[1])
        token_rows = lax.dot_general(
            placer, held[which], (((0,), (0,)), ((), ())), preferred_element_type=F32
        ).astype(BF16)
        outs[2 * i][...] = token_rows[0:rows]
        outs[2 * i + 1][...] = token_rows[rows:]


def back(low, lines, parts, weights, rows, first=0, earlier=None):
    local_experts, _, width = weights[0].shape
    count, slots, hidden = parts[0].shape
    last = first + count == local_experts
    vmem = pl.BlockSpec(memory_space=pltpu.VMEM)
    flops = (8 if last else 1) * count * 2 * slots * width * hidden
    operands = ([earlier] if first else []) + ([lines] if last else []) + [*parts]
    near = []
    if last:
        out_shape = [jax.ShapeDtypeStruct((rows, width), BF16)] * 4
        if not low:
            out_shape.append(jax.ShapeDtypeStruct((local_experts, hidden, width), BF16))
        near = [pltpu.VMEM((2, local_experts * slots, width), BF16)] + near
    else:
        out_shape = jax.ShapeDtypeStruct((2, count * slots, width), BF16)
    return pl.pallas_call(
        functools.partial(back_kernel, low, first, last),
        out_shape=out_shape,
        in_specs=[vmem] * (len(operands) + len(weights)),
        out_specs=[vmem] * len(out_shape) if last else vmem,
        scratch_shapes=near,
        compiler_params=params(20 if low else 30),
        cost_estimate=pl.CostEstimate(
            flops=flops, bytes_accessed=count * width * hidden * 2 if last else width, transcendentals=0
        ),
    )(*operands, *weights)


def weight_kernel(placed, h0, h1, h2, h3, gate, up):
    hidden = gate.shape[1]
    for i in range(gate.shape[0]):
        grads = jnp.concatenate([h[i] for h in (h0, h1, h2, h3)], axis=0)
        both = lax.dot_general(
            grads, placed[i], (((0,), (0,)), ((), ())), preferred_element_type=F32
        ).astype(BF16)
        gate[i] = both[0:hidden]
        up[i] = both[hidden:]


def weight_grads(placed, parts, per_step):
    local_experts, slot_rows, width = placed.shape
    _, slots, both = parts[0].shape
    hidden = both // 2
    part_spec = pl.BlockSpec((per_step, slots, both), lambda e: (e, 0, 0))
    out_spec = pl.BlockSpec((per_step, hidden, width), lambda e: (e, 0, 0))
    flops = 2 * local_experts * slot_rows * width * both
    return pl.pallas_call(
        weight_kernel,
        grid=(local_experts // per_step,),
        out_shape=[jax.ShapeDtypeStruct((local_experts, hidden, width), BF16)] * 2,
        in_specs=[pl.BlockSpec((per_step, slot_rows, width), lambda e: (e, 0, 0))] + [part_spec] * len(parts),
        out_specs=[out_spec] * 2,
        compiler_params=params(12),
        cost_estimate=pl.CostEstimate(
            flops=4 * flops, bytes_accessed=local_experts * width * both * 2, transcendentals=0
        ),
    )(placed, *parts)


def plus(first, second):
    return first.astype(F32) + second.astype(F32)


def swiglu_grads(gate_act, up_act, hidden_grad):
    sigmoid_gate = jax.nn.sigmoid(gate_act)
    up_grad = (hidden_grad * gate_act * sigmoid_gate).astype(BF16)
    gate_grad = (
        hidden_grad * up_act * sigmoid_gate * (1.0 + gate_act * (1.0 - sigmoid_gate))
    ).astype(BF16)
    return gate_grad, up_grad


def on_small_slice(tokens, cotangent, expert_ids, gate_weight, up_weight, down_weight):
    n_dp, n_x, n_t = 4, 2, 4
    k, x, t = lax.axis_index("dp"), lax.axis_index("expert"), lax.axis_index("tensor")
    width = gate_weight.shape[1]
    rows = tokens.shape[0]
    ids_row = expert_ids.reshape(1, rows)
    order = jnp.arange(rows, dtype=jnp.int32)
    earlier = (expert_ids == ids_row) & (order[:, None] < order[None, :])
    goal = ids_row * CAP + jnp.sum(earlier.astype(jnp.int32), axis=0, keepdims=True)
    meta = jnp.pad(goal.astype(BF16), ((0, META - 1), (0, width - rows)))

    def columns(values, rel):
        return lax.dynamic_slice_in_dim(values, (k ^ rel) * width, width, axis=1)

    chunks = [jnp.concatenate([columns(tokens, rel), meta], axis=0) for rel in range(n_dp)]

    def to_owner(value, rel, flip):
        if rel == 0 and flip == 0:
            return value
        pairs = [
            (i * n_x + j, (i ^ rel) * n_x + (j ^ flip)) for i in range(n_dp) for j in range(n_x)
        ]
        return lax.ppermute(value, ("dp", "expert"), pairs)

    own_tokens = [to_owner(c, rel, 0) for rel, c in enumerate(chunks)]
    near_tokens = [to_owner(c, rel, 1) for rel, c in enumerate(chunks[:2])]
    grads = [columns(cotangent, rel) for rel in range(n_dp)]
    far_tokens, grads = lax.optimization_barrier((own_tokens[2:], grads))
    near_tokens, far_tokens = lax.optimization_barrier((near_tokens, far_tokens))
    far_tokens = [swap(c, "expert", n_x, 1) for c in far_tokens]
    own_grads = [to_owner(c, rel, 0) for rel, c in enumerate(grads)]
    leaving_grads = jnp.stack(own_grads)
    far_tokens, leaving_grads = lax.optimization_barrier((far_tokens, leaving_grads))
    other_grads = swap(leaving_grads, "expert", n_x, 1)
    gate_weight, up_weight, down_weight = (
        jnp.swapaxes(weight, 1, 2) for weight in (gate_weight, up_weight, down_weight)
    )
    local_experts = gate_weight.shape[0]

    def project(values, weight):
        act = jnp.einsum("esd,ehd->esh", values, weight, preferred_element_type=F32).astype(BF16)
        return jnp.split(act, n_dp, axis=1)

    def near_and_far(act):
        near, far = swap(act[1], "dp", n_dp, 1), swap(act[3], "dp", n_dp, 1)
        return plus(act[0], near), plus(act[2], far).astype(BF16)

    placed, lines = place(own_tokens, near_tokens + far_tokens, None, rows, local_experts, [leaving_grads])
    gate_near, gate_far = near_and_far(project(placed, gate_weight))
    up_near, up_far = near_and_far(project(placed, up_weight))
    far = jnp.stack([gate_far, up_far])
    there = swap(far, "dp", n_dp, 2)
    placed_grads = place(own_grads, [other_grads], lines, rows, local_experts, [far])
    hidden_act = project(placed_grads, down_weight)
    beside, there = lax.optimization_barrier((swap(hidden_act[3], "dp", n_dp, 1), there))
    hidden_far = plus(hidden_act[2], beside).astype(BF16)
    hidden_near = plus(hidden_act[0], swap(hidden_act[1], "dp", n_dp, 1))
    gate_act, up_act = plus(gate_near, there[0]), plus(up_near, there[1])
    sigmoid_gate = jax.nn.sigmoid(gate_act)
    up_factor = gate_act * sigmoid_gate
    gate_factor = up_act * sigmoid_gate * (1.0 + gate_act * (1.0 - sigmoid_gate))
    hidden_grad = plus(hidden_near, swap(hidden_far, "dp", n_dp, 2))
    part = jnp.concatenate([hidden_grad * gate_factor, hidden_grad * up_factor], axis=2).astype(BF16)
    count = local_experts * 7 // 16
    far = [swap(piece, "dp", n_dp, 2) for piece in jnp.split(part, [count], axis=0)]
    beside = swap(part, "dp", n_dp, 1)
    *near_back, both_weights = back(0, lines, [part, beside], [gate_weight, up_weight], rows)
    far[0], _ = lax.optimization_barrier((far[0], near_back[0]))
    far_beside = [swap(far[0], "dp", n_dp, 1)]
    early = back(2, lines, [far[0], far_beside[0]], [both_weights], rows)
    far[1], _ = lax.optimization_barrier((far[1], early))
    far_beside.append(swap(far[1], "dp", n_dp, 1))
    far_back = back(2, lines, [far[1], far_beside[1]], [both_weights], rows, count, early)
    parts = [part, beside, jnp.concatenate(far, axis=0), jnp.concatenate(far_beside, axis=0)]
    own, other, own_beside, other_beside = near_back
    own_beside, other_beside = swap(own_beside, "dp", n_dp, 1), swap(other_beside, "dp", n_dp, 1)
    own_beside, other_beside = lax.optimization_barrier((own_beside, other_beside))
    arrived = swap(jnp.stack([other, other_beside]), "expert", n_x, 1)
    arrived, after_back, _ = lax.optimization_barrier((arrived, placed, far_back[0]))
    weight_grad = weight_grads(after_back, parts, 4)

    def to_keeper(value, low, turn, flip):
        pairs = []
        for i in range(n_dp):
            for j in range(n_x):
                for l in range(n_t):
                    odd = (i ^ l) & 1
                    to = ((i ^ low ^ odd ^ turn) * n_x + (j ^ flip)) * n_t + (l ^ odd)
                    pairs.append(((i * n_x + j) * n_t + l, to))
        return lax.ppermute(value, ("dp", "expert", "tensor"), pairs)

    merged = [plus(own, arrived[0]).astype(BF16), plus(own_beside, arrived[1]).astype(BF16)]
    odd = ((k ^ t) & 1) == 1
    keep, leaving = jnp.where(odd, merged[1], merged[0]), jnp.where(odd, merged[0], merged[1])
    first = plus(keep, swap(leaving, "tensor", n_t, 1))
    far_terms = [to_keeper(value, 2, at // 2, at % 2) for at, value in enumerate(far_back)]
    far_terms, _ = lax.optimization_barrier((far_terms, weight_grad))
    second = sum(value.astype(F32) for value in far_terms)
    swapped = ((k ^ t) & 2) == 2
    keep = jnp.where(swapped, second, first)
    leaving = jnp.where(swapped, first, second).astype(BF16)
    grad_tokens = plus(keep, swap(leaving, "tensor", n_t, 2)).astype(BF16)

    grad_gate, grad_up = (jnp.swapaxes(grad, 1, 2) for grad in weight_grad)
    return grad_tokens, grad_gate, grad_up


def bits_of(count):
    bits = []
    bit = 1
    while bit < count:
        bits.append(bit)
        bit *= 2
    return bits


def halving_sum(parts, axis, count):
    parts = dict(parts)
    for bit in bits_of(count):
        leaving = sorted(r for r in parts if r & bit)
        arrived = swap(jnp.stack([parts[r].astype(BF16) for r in leaving]), axis, count, bit)
        for at, r in enumerate(leaving):
            parts[r ^ bit] = plus(parts[r ^ bit], arrived[at])
            del parts[r]
    return parts[0]


def doubling_gather(value, axis, count):
    held = {0: value}
    for bit in reversed(bits_of(count)):
        known = sorted(held)
        arrived = swap(jnp.stack([held[r] for r in known]), axis, count, bit)
        for at, r in enumerate(known):
            held[r ^ bit] = arrived[at]
    return [held[r] for r in range(count)]


def on_any_slice(tokens, cotangent, expert_ids, gate_weight, up_weight, down_weight):
    n_dp, n_x, n_t = lax.axis_size("dp"), lax.axis_size("expert"), lax.axis_size("tensor")
    k, x, t = lax.axis_index("dp"), lax.axis_index("expert"), lax.axis_index("tensor")
    local_experts, width, hidden = gate_weight.shape
    rows = tokens.shape[0]
    slots = n_x * CAP
    ids_row = expert_ids.reshape(1, rows)
    order = jnp.arange(rows, dtype=jnp.int32)
    earlier = (expert_ids == ids_row) & (order[:, None] < order[None, :])
    position = jnp.sum(earlier.astype(jnp.int32), axis=0)
    target = ids_row[0] * CAP + position
    targets = lax.all_gather(target, ("dp", "expert"), axis=0, tiled=False).reshape(n_dp, n_x, rows)
    pair = jnp.stack([tokens, cotangent])
    placers, slot_rows = [], []
    for rel in range(n_dp):
        columns = lax.dynamic_slice_in_dim(pair, (k ^ rel) * width, width, axis=2)
        mine = columns if rel == 0 else swap(columns, "dp", n_dp, rel)
        blocks = lax.all_gather(mine, "expert", axis=1, tiled=True)
        goal = lax.dynamic_index_in_dim(targets, k ^ rel, axis=0, keepdims=False)
        expert = goal // CAP - x * local_experts
        place = jnp.arange(n_x, dtype=jnp.int32)[:, None] * CAP + goal % CAP
        row = jnp.where((expert >= 0) & (expert < local_experts), expert * slots + place, -1)
        row = row.reshape(1, n_x * rows)
        every = jnp.arange(local_experts * slots, dtype=jnp.int32)[:, None]
        placer = (every == row).astype(BF16)
        placers.append(placer)
        slot_rows.append(
            jnp.einsum("sn,and->asd", placer, blocks, preferred_element_type=F32)
            .astype(BF16)
            .reshape(2, local_experts, slots, width)
        )
    slot_rows = jnp.concatenate(slot_rows, axis=2)
    inputs, grads_in = slot_rows[0], slot_rows[1]

    def act(values, weight):
        return jnp.einsum("esd,edf->esf", values, weight, preferred_element_type=F32).astype(BF16)

    acts = jnp.stack([act(inputs, gate_weight), act(inputs, up_weight), act(grads_in, down_weight)])
    acts = acts.reshape(3, local_experts, n_dp, slots, hidden)
    acts = halving_sum({r: acts[:, :, r] for r in range(n_dp)}, "dp", n_dp)
    grads = doubling_gather(jnp.stack(swiglu_grads(acts[0], acts[1], acts[2])), "dp", n_dp)
    grads = jnp.concatenate(grads, axis=2)
    gate_grad, up_grad = grads[0], grads[1]
    partial_value = jnp.einsum("esf,edf->esd", gate_grad, gate_weight, preferred_element_type=F32)
    partial_value = partial_value + jnp.einsum("esf,edf->esd", up_grad, up_weight, preferred_element_type=F32)
    partial_value = partial_value.astype(BF16).reshape(local_experts, n_dp, slots, width)
    per_token = []
    for rel in range(n_dp):
        flat = partial_value[:, rel].reshape(local_experts * slots, width)
        spread = lax.dot_general(placers[rel], flat, (((0,), (0,)), ((), ())), preferred_element_type=F32)
        spread = spread.astype(BF16).reshape(n_x, rows, width)
        per_token.append(lax.psum_scatter(spread, "expert", scatter_dimension=0, tiled=False))
    per_token = jnp.stack(per_token)
    terms = {r: lax.dynamic_index_in_dim(per_token, k ^ t ^ r, axis=0, keepdims=False) for r in range(n_t)}
    summed = halving_sum(terms, "tensor", n_t).astype(BF16)
    summed = lax.ppermute(
        summed, ("dp", "tensor"), [(i * n_t + j, j * n_t + i) for i in range(n_dp) for j in range(n_t)]
    )
    grad_gate = jnp.einsum("esd,esf->edf", inputs, gate_grad, preferred_element_type=F32).astype(BF16)
    grad_up = jnp.einsum("esd,esf->edf", inputs, up_grad, preferred_element_type=F32).astype(BF16)
    return summed, grad_gate, grad_up


def solution(mesh):
    placed = (
        P(("dp", "expert"), None),
        P(("dp", "expert"), None),
        P(("dp", "expert"), None),
        P("expert", "dp", "tensor"),
        P("expert", "dp", "tensor"),
        P("expert", "dp", "tensor"),
    )
    sizes = tuple(mesh.shape[name] for name in ("dp", "expert", "tensor"))

    def on_device(tokens, cotangent, expert_ids, *weights):
        experts = weights[0].shape[0] * sizes[1]
        small = sizes == (4, 2, 4) and experts * CAP <= 256
        return (on_small_slice if small else on_any_slice)(tokens, cotangent, expert_ids, *weights)

    return jax.shard_map(
        on_device,
        mesh=mesh,
        in_specs=placed,
        out_specs=(
            P(("dp", "expert"), "tensor"),
            P("expert", "dp", "tensor"),
            P("expert", "dp", "tensor"),
        ),
        check_vma=False,
    )
```

```python
import functools

import jax
import jax.numpy as jnp
from jax import lax
from jax.experimental import pallas as pl
from jax.experimental.pallas import tpu as pltpu
from jax.sharding import PartitionSpec as P

CAP = 8
META = 16
F32 = jnp.float32
BF16 = jnp.bfloat16
MIB = 1024 * 1024
PLACE_COST = 1 << 34


def swap(value, axis, count, bit):
    return lax.ppermute(value, axis, [(i, i ^ bit) for i in range(count)])


def whole_spec(shape):
    return pl.BlockSpec(shape, lambda *_: (0,) * len(shape))


def params(mib=16):
    return pltpu.CompilerParams(vmem_limit_bytes=mib * MIB)


def placer_of(row, slot_count):
    every = lax.broadcasted_iota(jnp.int32, (slot_count, row.shape[1]), 0)
    return (every == row).astype(F32).astype(BF16)


def place_kernel(first, rows, mine, others, *refs):
    n_dp = len(mine)
    other = []
    for group in others:
        other += [group] if len(group.shape) == 2 else [group.at[i] for i in range(group.shape[0])]
    if first:
        placed, lines = refs[-2:]
    else:
        lines, placed = refs[0], refs[-1]
    local_experts, slot_rows, width = placed.shape
    slots = slot_rows // n_dp
    for rel in range(n_dp):
        if first:
            pair = [b[0 : rows + META, :] for b in (mine[rel], other[rel])]
            here = lax.axis_index("expert")
            goals = [b[rows:, 0:rows][0:1].astype(F32).astype(jnp.int32) for b in pair]
            row = jnp.concatenate(
                [
                    (goal // CAP - here * local_experts) * slots + source * CAP + goal % CAP
                    for goal, source in zip(goals, (here, 1 - here))
                ],
                axis=1,
            )
            lines[rel] = jnp.broadcast_to(row, (8, row.shape[1]))
            pair = [b[0:rows] for b in pair]
        else:
            row = lines[rel][0:1]
            pair = [b[...] for b in (mine[rel], other[rel])]
        placer = placer_of(row, local_experts * slots)
        found = jnp.dot(placer, jnp.concatenate(pair, axis=0), preferred_element_type=F32).astype(BF16)
        placed[:, rel * slots : (rel + 1) * slots, :] = found.reshape(local_experts, slots, width)


def place(mine, others, lines, rows, local_experts, after):
    first = lines is None
    n_dp, slots = len(mine), 2 * CAP
    width = mine[0].shape[1]
    placed = jax.ShapeDtypeStruct((local_experts, n_dp * slots, width), BF16)
    line = jax.ShapeDtypeStruct((n_dp, 8, 2 * rows), jnp.int32)
    vmem = pl.BlockSpec(memory_space=pltpu.VMEM)
    operands = [*others] + ([] if first else [lines])

    def kernel(*refs):
        split_at = n_dp + len(others)
        place_kernel(first, rows, refs[:n_dp], refs[n_dp:split_at], *refs[split_at:])

    return pl.pallas_call(
        kernel,
        out_shape=[placed, line] if first else placed,
        in_specs=[vmem] * (n_dp + len(operands))
        + [pl.BlockSpec(memory_space=pl.ANY)] * len(after),
        out_specs=[vmem, vmem] if first else vmem,
        compiler_params=params(),
        cost_estimate=pl.CostEstimate(flops=PLACE_COST, bytes_accessed=4 * rows * width * n_dp, transcendentals=0),
    )(*mine, *operands, *after)


def back_kernel(low, first, last, *refs):
    if first:
        earlier, refs = refs[0], refs[1:]
    if last:
        lines, refs = refs[0], refs[1:]
    h0, h1, refs = refs[0], refs[1], refs[2:]
    count, slots, _ = h0.shape
    if low:
        both, outs = refs[0], refs[1:]
    else:
        gate, up, both, outs = refs[0], refs[1], refs[6], refs[2:6] + refs[7:]
        hidden = gate.shape[1]
    for e in range(count):
        grads = jnp.concatenate([h0[e], h1[e]], axis=0)
        if not low:
            both[e, 0:hidden, :] = gate[e]
            both[e, hidden:, :] = up[e]
        value = jnp.dot(grads, both[first + e], preferred_element_type=F32).astype(BF16)
        for i in range(2):
            rows = value[i * slots : (i + 1) * slots]
            if last:
                outs[-1][i, (first + e) * slots : (first + e + 1) * slots, :] = rows
            else:
                outs[0][i, e * slots : (e + 1) * slots, :] = rows
    if not last:
        return
    held = outs[-1]
    if first:
        held[:, 0 : first * slots, :] = earlier[...]
    rows = outs[0].shape[0]
    odd = (lax.axis_index("dp") ^ lax.axis_index("tensor")) & 1
    for i in range(2):
        which = odd ^ i if low else i
        placer = placer_of(lines[low + which][0:1], held.shape[1])
        token_rows = lax.dot_general(
            placer, held[which], (((0,), (0,)), ((), ())), preferred_element_type=F32
        ).astype(BF16)
        outs[2 * i][...] = token_rows[0:rows]
        outs[2 * i + 1][...] = token_rows[rows:]


def back(low, lines, parts, weights, rows, first=0, earlier=None):
    local_experts, _, width = weights[0].shape
    count, slots, hidden = parts[0].shape
    last = first + count == local_experts
    vmem = pl.BlockSpec(memory_space=pltpu.VMEM)
    flops = (8 if last else 1) * count * 2 * slots * width * hidden
    operands = ([earlier] if first else []) + ([lines] if last else []) + [*parts]
    near = []
    if last:
        out_shape = [jax.ShapeDtypeStruct((rows, width), BF16)] * 4
        if not low:
            out_shape.append(jax.ShapeDtypeStruct((local_experts, hidden, width), BF16))
        near = [pltpu.VMEM((2, local_experts * slots, width), BF16)] + near
    else:
        out_shape = jax.ShapeDtypeStruct((2, count * slots, width), BF16)
    return pl.pallas_call(
        functools.partial(back_kernel, low, first, last),
        out_shape=out_shape,
        in_specs=[vmem] * (len(operands) + len(weights)),
        out_specs=[vmem] * len(out_shape) if last else vmem,
        scratch_shapes=near,
        compiler_params=params(20 if low else 30),
        cost_estimate=pl.CostEstimate(
            flops=flops, bytes_accessed=count * width * hidden * 2 if last else width, transcendentals=0
        ),
    )(*operands, *weights)


def weight_kernel(placed, h0, h1, h2, h3, gate, up):
    hidden = gate.shape[1]
    for i in range(gate.shape[0]):
        grads = jnp.concatenate([h[i] for h in (h0, h1, h2, h3)], axis=0)
        both = lax.dot_general(
            grads, placed[i], (((0,), (0,)), ((), ())), preferred_element_type=F32
        ).astype(BF16)
        gate[i] = both[0:hidden]
        up[i] = both[hidden:]


def weight_grads(placed, parts, per_step):
    local_experts, slot_rows, width = placed.shape
    _, slots, both = parts[0].shape
    hidden = both // 2
    part_spec = pl.BlockSpec((per_step, slots, both), lambda e: (e, 0, 0))
    out_spec = pl.BlockSpec((per_step, hidden, width), lambda e: (e, 0, 0))
    flops = 2 * local_experts * slot_rows * width * both
    return pl.pallas_call(
        weight_kernel,
        grid=(local_experts // per_step,),
        out_shape=[jax.ShapeDtypeStruct((local_experts, hidden, width), BF16)] * 2,
        in_specs=[pl.BlockSpec((per_step, slot_rows, width), lambda e: (e, 0, 0))] + [part_spec] * len(parts),
        out_specs=[out_spec] * 2,
        compiler_params=params(12),
        cost_estimate=pl.CostEstimate(
            flops=4 * flops, bytes_accessed=local_experts * width * both * 2, transcendentals=0
        ),
    )(placed, *parts)


def plus(first, second):
    return first.astype(F32) + second.astype(F32)


def swiglu_grads(gate_act, up_act, hidden_grad):
    sigmoid_gate = jax.nn.sigmoid(gate_act)
    up_grad = (hidden_grad * gate_act * sigmoid_gate).astype(BF16)
    gate_grad = (
        hidden_grad * up_act * sigmoid_gate * (1.0 + gate_act * (1.0 - sigmoid_gate))
    ).astype(BF16)
    return gate_grad, up_grad


def on_small_slice(tokens, cotangent, expert_ids, gate_weight, up_weight, down_weight):
    n_dp, n_x, n_t = 4, 2, 4
    k, x, t = lax.axis_index("dp"), lax.axis_index("expert"), lax.axis_index("tensor")
    width = gate_weight.shape[1]
    rows = tokens.shape[0]
    odd, swapped = ((k ^ t) & 1) == 1, ((k ^ t) & 2) == 2
    expert_ids, odd, swapped = lax.optimization_barrier((expert_ids, odd, swapped))
    ids_row = expert_ids.reshape(1, rows)
    order = jnp.arange(rows, dtype=jnp.int32)
    earlier = (expert_ids == ids_row) & (order[:, None] < order[None, :])
    goal = ids_row * CAP + jnp.sum(earlier.astype(jnp.int32), axis=0, keepdims=True)
    meta = jnp.pad(goal.astype(BF16), ((0, META - 1), (0, width - rows)))

    def columns(values, rel):
        return lax.dynamic_slice_in_dim(values, (k ^ rel) * width, width, axis=1)

    chunks = [jnp.concatenate([columns(tokens, rel), meta], axis=0) for rel in range(n_dp)]

    def to_owner(value, rel, flip):
        if rel == 0 and flip == 0:
            return value
        pairs = [
            (i * n_x + j, (i ^ rel) * n_x + (j ^ flip)) for i in range(n_dp) for j in range(n_x)
        ]
        return lax.ppermute(value, ("dp", "expert"), pairs)

    own_tokens = [to_owner(c, rel, 0) for rel, c in enumerate(chunks)]
    near_tokens = [to_owner(c, rel, 1) for rel, c in enumerate(chunks[:2])]
    grads = [columns(cotangent, rel) for rel in range(n_dp)]
    far_tokens, grads = lax.optimization_barrier((own_tokens[2:], grads))
    near_tokens, far_tokens = lax.optimization_barrier((near_tokens, far_tokens))
    far_tokens = [swap(c, "expert", n_x, 1) for c in far_tokens]
    own_grads = [to_owner(c, rel, 0) for rel, c in enumerate(grads)]
    leaving_grads = jnp.stack(own_grads)
    far_tokens, leaving_grads = lax.optimization_barrier((far_tokens, leaving_grads))
    other_grads = swap(leaving_grads, "expert", n_x, 1)
    gate_weight, up_weight, down_weight = (
        jnp.swapaxes(weight, 1, 2) for weight in (gate_weight, up_weight, down_weight)
    )
    local_experts = gate_weight.shape[0]

    def project(values, weight):
        act = jnp.einsum("esd,ehd->esh", values, weight, preferred_element_type=F32).astype(BF16)
        return jnp.split(act, n_dp, axis=1)

    def near_and_far(act):
        near, far = swap(act[1], "dp", n_dp, 1), swap(act[3], "dp", n_dp, 1)
        return plus(act[0], near), plus(act[2], far).astype(BF16)

    placed, lines = place(own_tokens, near_tokens + far_tokens, None, rows, local_experts, [leaving_grads])
    gate_near, gate_far = near_and_far(project(placed, gate_weight))
    up_near, up_far = near_and_far(project(placed, up_weight))
    far = jnp.stack([gate_far, up_far])
    there = swap(far, "dp", n_dp, 2)
    placed_grads = place(own_grads, [other_grads], lines, rows, local_experts, [far])
    hidden_act = project(placed_grads, down_weight)
    beside, there = lax.optimization_barrier((swap(hidden_act[3], "dp", n_dp, 1), there))
    hidden_far = plus(hidden_act[2], beside).astype(BF16)
    hidden_near = plus(hidden_act[0], swap(hidden_act[1], "dp", n_dp, 1))
    gate_act, up_act = plus(gate_near, there[0]), plus(up_near, there[1])
    sigmoid_gate = jax.nn.sigmoid(gate_act)
    up_factor = gate_act * sigmoid_gate
    gate_factor = up_act * sigmoid_gate * (1.0 + gate_act * (1.0 - sigmoid_gate))
    hidden_grad = plus(hidden_near, swap(hidden_far, "dp", n_dp, 2))
    part = jnp.concatenate([hidden_grad * gate_factor, hidden_grad * up_factor], axis=2).astype(BF16)
    count = local_experts * 7 // 16
    far = [swap(piece, "dp", n_dp, 2) for piece in jnp.split(part, [count], axis=0)]
    beside = swap(part, "dp", n_dp, 1)
    *near_back, both_weights = back(0, lines, [part, beside], [gate_weight, up_weight], rows)
    far[0], _ = lax.optimization_barrier((far[0], near_back[0]))
    far_beside = [swap(far[0], "dp", n_dp, 1)]
    early = back(2, lines, [far[0], far_beside[0]], [both_weights], rows)
    far[1], _ = lax.optimization_barrier((far[1], early))
    far_beside.append(swap(far[1], "dp", n_dp, 1))
    far_back = back(2, lines, [far[1], far_beside[1]], [both_weights], rows, count, early)
    parts = [part, beside, jnp.concatenate(far, axis=0), jnp.concatenate(far_beside, axis=0)]
    own, other, own_beside, other_beside = near_back
    own_beside, other_beside = swap(own_beside, "dp", n_dp, 1), swap(other_beside, "dp", n_dp, 1)
    own_beside, other_beside = lax.optimization_barrier((own_beside, other_beside))
    arrived = swap(jnp.stack([other, other_beside]), "expert", n_x, 1)
    arrived, after_back, _ = lax.optimization_barrier((arrived, placed, far_back[0]))
    weight_grad = weight_grads(after_back, parts, 4)

    def to_keeper(value, low, turn, flip):
        pairs = []
        for i in range(n_dp):
            for j in range(n_x):
                for l in range(n_t):
                    odd = (i ^ l) & 1
                    to = ((i ^ low ^ odd ^ turn) * n_x + (j ^ flip)) * n_t + (l ^ odd)
                    pairs.append(((i * n_x + j) * n_t + l, to))
        return lax.ppermute(value, ("dp", "expert", "tensor"), pairs)

    merged = [plus(own, arrived[0]).astype(BF16), plus(own_beside, arrived[1]).astype(BF16)]
    keep, leaving = jnp.where(odd, merged[1], merged[0]), jnp.where(odd, merged[0], merged[1])
    first = plus(keep, swap(leaving, "tensor", n_t, 1))
    far_terms = [to_keeper(value, 2, at // 2, at % 2) for at, value in enumerate(far_back)]
    far_terms, _ = lax.optimization_barrier((far_terms, weight_grad))
    second = sum(value.astype(F32) for value in far_terms)
    keep = jnp.where(swapped, second, first)
    leaving = jnp.where(swapped, first, second).astype(BF16)
    grad_tokens = plus(keep, swap(leaving, "tensor", n_t, 2)).astype(BF16)

    grad_gate, grad_up = (jnp.swapaxes(grad, 1, 2) for grad in weight_grad)
    return grad_tokens, grad_gate, grad_up


def bits_of(count):
    bits = []
    bit = 1
    while bit < count:
        bits.append(bit)
        bit *= 2
    return bits


def halving_sum(parts, axis, count):
    parts = dict(parts)
    for bit in bits_of(count):
        leaving = sorted(r for r in parts if r & bit)
        arrived = swap(jnp.stack([parts[r].astype(BF16) for r in leaving]), axis, count, bit)
        for at, r in enumerate(leaving):
            parts[r ^ bit] = plus(parts[r ^ bit], arrived[at])
            del parts[r]
    return parts[0]


def doubling_gather(value, axis, count):
    held = {0: value}
    for bit in reversed(bits_of(count)):
        known = sorted(held)
        arrived = swap(jnp.stack([held[r] for r in known]), axis, count, bit)
        for at, r in enumerate(known):
            held[r ^ bit] = arrived[at]
    return [held[r] for r in range(count)]


def on_any_slice(tokens, cotangent, expert_ids, gate_weight, up_weight, down_weight):
    n_dp, n_x, n_t = lax.axis_size("dp"), lax.axis_size("expert"), lax.axis_size("tensor")
    k, x, t = lax.axis_index("dp"), lax.axis_index("expert"), lax.axis_index("tensor")
    local_experts, width, hidden = gate_weight.shape
    rows = tokens.shape[0]
    slots = n_x * CAP
    ids_row = expert_ids.reshape(1, rows)
    order = jnp.arange(rows, dtype=jnp.int32)
    earlier = (expert_ids == ids_row) & (order[:, None] < order[None, :])
    position = jnp.sum(earlier.astype(jnp.int32), axis=0)
    target = ids_row[0] * CAP + position
    targets = lax.all_gather(target, ("dp", "expert"), axis=0, tiled=False).reshape(n_dp, n_x, rows)
    pair = jnp.stack([tokens, cotangent])
    placers, slot_rows = [], []
    for rel in range(n_dp):
        columns = lax.dynamic_slice_in_dim(pair, (k ^ rel) * width, width, axis=2)
        mine = columns if rel == 0 else swap(columns, "dp", n_dp, rel)
        blocks = lax.all_gather(mine, "expert", axis=1, tiled=True)
        goal = lax.dynamic_index_in_dim(targets, k ^ rel, axis=0, keepdims=False)
        expert = goal // CAP - x * local_experts
        place = jnp.arange(n_x, dtype=jnp.int32)[:, None] * CAP + goal % CAP
        row = jnp.where((expert >= 0) & (expert < local_experts), expert * slots + place, -1)
        row = row.reshape(1, n_x * rows)
        every = jnp.arange(local_experts * slots, dtype=jnp.int32)[:, None]
        placer = (every == row).astype(BF16)
        placers.append(placer)
        slot_rows.append(
            jnp.einsum("sn,and->asd", placer, blocks, preferred_element_type=F32)
            .astype(BF16)
            .reshape(2, local_experts, slots, width)
        )
    slot_rows = jnp.concatenate(slot_rows, axis=2)
    inputs, grads_in = slot_rows[0], slot_rows[1]

    def act(values, weight):
        return jnp.einsum("esd,edf->esf", values, weight, preferred_element_type=F32).astype(BF16)

    acts = jnp.stack([act(inputs, gate_weight), act(inputs, up_weight), act(grads_in, down_weight)])
    acts = acts.reshape(3, local_experts, n_dp, slots, hidden)
    acts = halving_sum({r: acts[:, :, r] for r in range(n_dp)}, "dp", n_dp)
    grads = doubling_gather(jnp.stack(swiglu_grads(acts[0], acts[1], acts[2])), "dp", n_dp)
    grads = jnp.concatenate(grads, axis=2)
    gate_grad, up_grad = grads[0], grads[1]
    partial_value = jnp.einsum("esf,edf->esd", gate_grad, gate_weight, preferred_element_type=F32)
    partial_value = partial_value + jnp.einsum("esf,edf->esd", up_grad, up_weight, preferred_element_type=F32)
    partial_value = partial_value.astype(BF16).reshape(local_experts, n_dp, slots, width)
    per_token = []
    for rel in range(n_dp):
        flat = partial_value[:, rel].reshape(local_experts * slots, width)
        spread = lax.dot_general(placers[rel], flat, (((0,), (0,)), ((), ())), preferred_element_type=F32)
        spread = spread.astype(BF16).reshape(n_x, rows, width)
        per_token.append(lax.psum_scatter(spread, "expert", scatter_dimension=0, tiled=False))
    per_token = jnp.stack(per_token)
    terms = {r: lax.dynamic_index_in_dim(per_token, k ^ t ^ r, axis=0, keepdims=False) for r in range(n_t)}
    summed = halving_sum(terms, "tensor", n_t).astype(BF16)
    summed = lax.ppermute(
        summed, ("dp", "tensor"), [(i * n_t + j, j * n_t + i) for i in range(n_dp) for j in range(n_t)]
    )
    grad_gate = jnp.einsum("esd,esf->edf", inputs, gate_grad, preferred_element_type=F32).astype(BF16)
    grad_up = jnp.einsum("esd,esf->edf", inputs, up_grad, preferred_element_type=F32).astype(BF16)
    return summed, grad_gate, grad_up


def solution(mesh):
    placed = (
        P(("dp", "expert"), None),
        P(("dp", "expert"), None),
        P(("dp", "expert"), None),
        P("expert", "dp", "tensor"),
        P("expert", "dp", "tensor"),
        P("expert", "dp", "tensor"),
    )
    sizes = tuple(mesh.shape[name] for name in ("dp", "expert", "tensor"))

    def on_device(tokens, cotangent, expert_ids, *weights):
        experts = weights[0].shape[0] * sizes[1]
        small = sizes == (4, 2, 4) and experts * CAP <= 256
        return (on_small_slice if small else on_any_slice)(tokens, cotangent, expert_ids, *weights)

    return jax.shard_map(
        on_device,
        mesh=mesh,
        in_specs=placed,
        out_specs=(
            P(("dp", "expert"), "tensor"),
            P("expert", "dp", "tensor"),
            P("expert", "dp", "tensor"),
        ),
        check_vma=False,
    )
```

```python
import functools

import jax
import jax.numpy as jnp
from jax import lax
from jax.experimental import pallas as pl
from jax.experimental.pallas import tpu as pltpu
from jax.sharding import PartitionSpec as P

CAP = 8
META = 16
F32 = jnp.float32
BF16 = jnp.bfloat16
MIB = 1024 * 1024
PLACE_COST = 1 << 34


def swap(value, axis, count, bit):
    return lax.ppermute(value, axis, [(i, i ^ bit) for i in range(count)])


def whole_spec(shape):
    return pl.BlockSpec(shape, lambda *_: (0,) * len(shape))


def params(mib=16):
    return pltpu.CompilerParams(vmem_limit_bytes=mib * MIB)


def placer_of(row, slot_count):
    every = lax.broadcasted_iota(jnp.int32, (slot_count, row.shape[1]), 0)
    return (every == row).astype(F32).astype(BF16)


def place_kernel(first, rows, mine, others, *refs):
    n_dp = len(mine)
    other = []
    for group in others:
        other += [group] if len(group.shape) == 2 else [group.at[i] for i in range(group.shape[0])]
    if first:
        placed, lines = refs[-2:]
    else:
        lines, placed = refs[0], refs[-1]
    local_experts, slot_rows, width = placed.shape
    slots = slot_rows // n_dp
    for rel in range(n_dp):
        if first:
            pair = [b[0 : rows + META, :] for b in (mine[rel], other[rel])]
            here = lax.axis_index("expert")
            goals = [b[rows:, 0:rows][0:1].astype(F32).astype(jnp.int32) for b in pair]
            row = jnp.concatenate(
                [
                    (goal // CAP - here * local_experts) * slots + source * CAP + goal % CAP
                    for goal, source in zip(goals, (here, 1 - here))
                ],
                axis=1,
            )
            lines[rel] = jnp.broadcast_to(row, (8, row.shape[1]))
            pair = [b[0:rows] for b in pair]
        else:
            row = lines[rel][0:1]
            pair = [b[...] for b in (mine[rel], other[rel])]
        placer = placer_of(row, local_experts * slots)
        found = jnp.dot(placer, jnp.concatenate(pair, axis=0), preferred_element_type=F32).astype(BF16)
        placed[:, rel * slots : (rel + 1) * slots, :] = found.reshape(local_experts, slots, width)


def place(mine, others, lines, rows, local_experts, after):
    first = lines is None
    n_dp, slots = len(mine), 2 * CAP
    width = mine[0].shape[1]
    placed = jax.ShapeDtypeStruct((local_experts, n_dp * slots, width), BF16)
    line = jax.ShapeDtypeStruct((n_dp, 8, 2 * rows), jnp.int32)
    vmem = pl.BlockSpec(memory_space=pltpu.VMEM)
    operands = [*others] + ([] if first else [lines])

    def kernel(*refs):
        split_at = n_dp + len(others)
        place_kernel(first, rows, refs[:n_dp], refs[n_dp:split_at], *refs[split_at:])

    return pl.pallas_call(
        kernel,
        out_shape=[placed, line] if first else placed,
        in_specs=[vmem] * (n_dp + len(operands))
        + [pl.BlockSpec(memory_space=pl.ANY)] * len(after),
        out_specs=[vmem, vmem] if first else vmem,
        compiler_params=params(),
        cost_estimate=pl.CostEstimate(flops=PLACE_COST, bytes_accessed=4 * rows * width * n_dp, transcendentals=0),
    )(*mine, *operands, *after)


def back_kernel(low, first, last, *refs):
    if first:
        earlier, refs = refs[0], refs[1:]
    if last:
        lines, refs = refs[0], refs[1:]
    h0, h1, refs = refs[0], refs[1], refs[2:]
    count, slots, _ = h0.shape
    if low:
        both, outs = refs[0], refs[1:]
    else:
        gate, up, both, outs = refs[0], refs[1], refs[6], refs[2:6] + refs[7:]
        hidden = gate.shape[1]
    for e in range(count):
        grads = jnp.concatenate([h0[e], h1[e]], axis=0)
        if not low:
            both[e, 0:hidden, :] = gate[e]
            both[e, hidden:, :] = up[e]
        value = jnp.dot(grads, both[first + e], preferred_element_type=F32).astype(BF16)
        for i in range(2):
            rows = value[i * slots : (i + 1) * slots]
            if last:
                outs[-1][i, (first + e) * slots : (first + e + 1) * slots, :] = rows
            else:
                outs[0][i, e * slots : (e + 1) * slots, :] = rows
    if not last:
        return
    held = outs[-1]
    if first:
        held[:, 0 : first * slots, :] = earlier[...]
    rows = outs[0].shape[0]
    odd = (lax.axis_index("dp") ^ lax.axis_index("tensor")) & 1
    for i in range(2):
        which = odd ^ i if low else i
        placer = placer_of(lines[low + which][0:1], held.shape[1])
        token_rows = lax.dot_general(
            placer, held[which], (((0,), (0,)), ((), ())), preferred_element_type=F32
        ).astype(BF16)
        outs[2 * i][...] = token_rows[0:rows]
        outs[2 * i + 1][...] = token_rows[rows:]


def back(low, lines, parts, weights, rows, first=0, earlier=None):
    local_experts, _, width = weights[0].shape
    count, slots, hidden = parts[0].shape
    last = first + count == local_experts
    vmem = pl.BlockSpec(memory_space=pltpu.VMEM)
    flops = (8 if last else 1) * count * 2 * slots * width * hidden
    operands = ([earlier] if first else []) + ([lines] if last else []) + [*parts]
    near = []
    if last:
        out_shape = [jax.ShapeDtypeStruct((rows, width), BF16)] * 4
        if not low:
            out_shape.append(jax.ShapeDtypeStruct((local_experts, hidden, width), BF16))
        near = [pltpu.VMEM((2, local_experts * slots, width), BF16)] + near
    else:
        out_shape = jax.ShapeDtypeStruct((2, count * slots, width), BF16)
    return pl.pallas_call(
        functools.partial(back_kernel, low, first, last),
        out_shape=out_shape,
        in_specs=[vmem] * (len(operands) + len(weights)),
        out_specs=[vmem] * len(out_shape) if last else vmem,
        scratch_shapes=near,
        compiler_params=params(20 if low else 30),
        cost_estimate=pl.CostEstimate(
            flops=flops, bytes_accessed=count * width * hidden * 2 if last else width, transcendentals=0
        ),
    )(*operands, *weights)


def weight_kernel(placed, h0, h1, h2, h3, gate, up):
    hidden = gate.shape[1]
    for i in range(gate.shape[0]):
        grads = jnp.concatenate([h[i] for h in (h0, h1, h2, h3)], axis=0)
        both = lax.dot_general(
            grads, placed[i], (((0,), (0,)), ((), ())), preferred_element_type=F32
        ).astype(BF16)
        gate[i] = both[0:hidden]
        up[i] = both[hidden:]


def weight_grads(placed, parts, per_step):
    local_experts, slot_rows, width = placed.shape
    _, slots, both = parts[0].shape
    hidden = both // 2
    part_spec = pl.BlockSpec((per_step, slots, both), lambda e: (e, 0, 0))
    out_spec = pl.BlockSpec((per_step, hidden, width), lambda e: (e, 0, 0))
    flops = 2 * local_experts * slot_rows * width * both
    return pl.pallas_call(
        weight_kernel,
        grid=(local_experts // per_step,),
        out_shape=[jax.ShapeDtypeStruct((local_experts, hidden, width), BF16)] * 2,
        in_specs=[pl.BlockSpec((per_step, slot_rows, width), lambda e: (e, 0, 0))] + [part_spec] * len(parts),
        out_specs=[out_spec] * 2,
        compiler_params=params(12),
        cost_estimate=pl.CostEstimate(
            flops=4 * flops, bytes_accessed=local_experts * width * both * 2, transcendentals=0
        ),
    )(placed, *parts)


def plus(first, second):
    return first.astype(F32) + second.astype(F32)


def swiglu_grads(gate_act, up_act, hidden_grad):
    sigmoid_gate = jax.nn.sigmoid(gate_act)
    up_grad = (hidden_grad * gate_act * sigmoid_gate).astype(BF16)
    gate_grad = (
        hidden_grad * up_act * sigmoid_gate * (1.0 + gate_act * (1.0 - sigmoid_gate))
    ).astype(BF16)
    return gate_grad, up_grad


def on_small_slice(tokens, cotangent, expert_ids, gate_weight, up_weight, down_weight):
    n_dp, n_x, n_t = 4, 2, 4
    k, x, t = lax.axis_index("dp"), lax.axis_index("expert"), lax.axis_index("tensor")
    width = gate_weight.shape[1]
    rows = tokens.shape[0]
    odd, swapped = ((k ^ t) & 1) == 1, ((k ^ t) & 2) == 2
    expert_ids, odd, swapped = lax.optimization_barrier((expert_ids, odd, swapped))
    ids_row = expert_ids.reshape(1, rows)
    order = jnp.arange(rows, dtype=jnp.int32)
    earlier = (expert_ids == ids_row) & (order[:, None] < order[None, :])
    own_line = order[:, None] == order[None, :]
    goal = jnp.sum(jnp.where(own_line, expert_ids * CAP, earlier.astype(jnp.int32)), axis=0, keepdims=True)
    meta = jnp.pad(goal.astype(BF16), ((0, META - 1), (0, width - rows)))

    def columns(values, rel):
        return lax.dynamic_slice_in_dim(values, (k ^ rel) * width, width, axis=1)

    chunks = [jnp.concatenate([columns(tokens, rel), meta], axis=0) for rel in range(n_dp)]

    def to_owner(value, rel, flip):
        if rel == 0 and flip == 0:
            return value
        pairs = [
            (i * n_x + j, (i ^ rel) * n_x + (j ^ flip)) for i in range(n_dp) for j in range(n_x)
        ]
        return lax.ppermute(value, ("dp", "expert"), pairs)

    own_tokens = [to_owner(c, rel, 0) for rel, c in enumerate(chunks)]
    near_tokens = [to_owner(c, rel, 1) for rel, c in enumerate(chunks[:2])]
    grads = [columns(cotangent, rel) for rel in range(n_dp)]
    far_tokens, grads = lax.optimization_barrier((own_tokens[2:], grads))
    near_tokens, far_tokens = lax.optimization_barrier((near_tokens, far_tokens))
    far_tokens = [swap(c, "expert", n_x, 1) for c in far_tokens]
    own_grads = [to_owner(c, rel, 0) for rel, c in enumerate(grads)]
    leaving_grads = jnp.stack(own_grads)
    far_tokens, leaving_grads = lax.optimization_barrier((far_tokens, leaving_grads))
    other_grads = swap(leaving_grads, "expert", n_x, 1)
    gate_weight, up_weight, down_weight = (
        jnp.swapaxes(weight, 1, 2) for weight in (gate_weight, up_weight, down_weight)
    )
    local_experts = gate_weight.shape[0]

    def project(values, weight):
        act = jnp.einsum("esd,ehd->esh", values, weight, preferred_element_type=F32).astype(BF16)
        return jnp.split(act, n_dp, axis=1)

    def near_and_far(act):
        near, far = swap(act[1], "dp", n_dp, 1), swap(act[3], "dp", n_dp, 1)
        return plus(act[0], near), plus(act[2], far).astype(BF16)

    placed, lines = place(own_tokens, near_tokens + far_tokens, None, rows, local_experts, [leaving_grads])
    gate_near, gate_far = near_and_far(project(placed, gate_weight))
    up_near, up_far = near_and_far(project(placed, up_weight))
    far = jnp.stack([gate_far, up_far])
    there = swap(far, "dp", n_dp, 2)
    placed_grads = place(own_grads, [other_grads], lines, rows, local_experts, [far])
    hidden_act = project(placed_grads, down_weight)
    beside, there = lax.optimization_barrier((swap(hidden_act[3], "dp", n_dp, 1), there))
    hidden_far = plus(hidden_act[2], beside).astype(BF16)
    hidden_near = plus(hidden_act[0], swap(hidden_act[1], "dp", n_dp, 1))
    gate_act, up_act = plus(gate_near, there[0]), plus(up_near, there[1])
    sigmoid_gate = jax.nn.sigmoid(gate_act)
    up_factor = gate_act * sigmoid_gate
    gate_factor = up_act * sigmoid_gate * (1.0 + gate_act * (1.0 - sigmoid_gate))
    hidden_grad = plus(hidden_near, swap(hidden_far, "dp", n_dp, 2))
    part = jnp.concatenate([hidden_grad * gate_factor, hidden_grad * up_factor], axis=2).astype(BF16)
    count = local_experts * 7 // 16
    far = [swap(piece, "dp", n_dp, 2) for piece in jnp.split(part, [count], axis=0)]
    beside = swap(part, "dp", n_dp, 1)
    *near_back, both_weights = back(0, lines, [part, beside], [gate_weight, up_weight], rows)
    far[0], _ = lax.optimization_barrier((far[0], near_back[0]))
    far_beside = [swap(far[0], "dp", n_dp, 1)]
    early = back(2, lines, [far[0], far_beside[0]], [both_weights], rows)
    far[1], _ = lax.optimization_barrier((far[1], early))
    far_beside.append(swap(far[1], "dp", n_dp, 1))
    far_back = back(2, lines, [far[1], far_beside[1]], [both_weights], rows, count, early)
    parts = [part, beside, jnp.concatenate(far, axis=0), jnp.concatenate(far_beside, axis=0)]
    own, other, own_beside, other_beside = near_back
    own_beside, other_beside = swap(own_beside, "dp", n_dp, 1), swap(other_beside, "dp", n_dp, 1)
    own_beside, other_beside = lax.optimization_barrier((own_beside, other_beside))
    arrived = swap(jnp.stack([other, other_beside]), "expert", n_x, 1)
    arrived, after_back, _ = lax.optimization_barrier((arrived, placed, far_back[0]))
    weight_grad = weight_grads(after_back, parts, 4)

    def to_keeper(value, low, turn, flip):
        pairs = []
        for i in range(n_dp):
            for j in range(n_x):
                for l in range(n_t):
                    odd = (i ^ l) & 1
                    to = ((i ^ low ^ odd ^ turn) * n_x + (j ^ flip)) * n_t + (l ^ odd)
                    pairs.append(((i * n_x + j) * n_t + l, to))
        return lax.ppermute(value, ("dp", "expert", "tensor"), pairs)

    merged = [plus(own, arrived[0]).astype(BF16), plus(own_beside, arrived[1]).astype(BF16)]
    keep, leaving = jnp.where(odd, merged[1], merged[0]), jnp.where(odd, merged[0], merged[1])
    first = plus(keep, swap(leaving, "tensor", n_t, 1))
    far_terms = [to_keeper(value, 2, at // 2, at % 2) for at, value in enumerate(far_back)]
    far_terms, _ = lax.optimization_barrier((far_terms, weight_grad))
    second = sum(value.astype(F32) for value in far_terms)
    keep = jnp.where(swapped, second, first)
    leaving = jnp.where(swapped, first, second).astype(BF16)
    grad_tokens = plus(keep, swap(leaving, "tensor", n_t, 2)).astype(BF16)

    grad_gate, grad_up = (jnp.swapaxes(grad, 1, 2) for grad in weight_grad)
    return grad_tokens, grad_gate, grad_up


def bits_of(count):
    bits = []
    bit = 1
    while bit < count:
        bits.append(bit)
        bit *= 2
    return bits


def halving_sum(parts, axis, count):
    parts = dict(parts)
    for bit in bits_of(count):
        leaving = sorted(r for r in parts if r & bit)
        arrived = swap(jnp.stack([parts[r].astype(BF16) for r in leaving]), axis, count, bit)
        for at, r in enumerate(leaving):
            parts[r ^ bit] = plus(parts[r ^ bit], arrived[at])
            del parts[r]
    return parts[0]


def doubling_gather(value, axis, count):
    held = {0: value}
    for bit in reversed(bits_of(count)):
        known = sorted(held)
        arrived = swap(jnp.stack([held[r] for r in known]), axis, count, bit)
        for at, r in enumerate(known):
            held[r ^ bit] = arrived[at]
    return [held[r] for r in range(count)]


def on_any_slice(tokens, cotangent, expert_ids, gate_weight, up_weight, down_weight):
    n_dp, n_x, n_t = lax.axis_size("dp"), lax.axis_size("expert"), lax.axis_size("tensor")
    k, x, t = lax.axis_index("dp"), lax.axis_index("expert"), lax.axis_index("tensor")
    local_experts, width, hidden = gate_weight.shape
    rows = tokens.shape[0]
    slots = n_x * CAP
    ids_row = expert_ids.reshape(1, rows)
    order = jnp.arange(rows, dtype=jnp.int32)
    earlier = (expert_ids == ids_row) & (order[:, None] < order[None, :])
    position = jnp.sum(earlier.astype(jnp.int32), axis=0)
    target = ids_row[0] * CAP + position
    targets = lax.all_gather(target, ("dp", "expert"), axis=0, tiled=False).reshape(n_dp, n_x, rows)
    pair = jnp.stack([tokens, cotangent])
    placers, slot_rows = [], []
    for rel in range(n_dp):
        columns = lax.dynamic_slice_in_dim(pair, (k ^ rel) * width, width, axis=2)
        mine = columns if rel == 0 else swap(columns, "dp", n_dp, rel)
        blocks = lax.all_gather(mine, "expert", axis=1, tiled=True)
        goal = lax.dynamic_index_in_dim(targets, k ^ rel, axis=0, keepdims=False)
        expert = goal // CAP - x * local_experts
        place = jnp.arange(n_x, dtype=jnp.int32)[:, None] * CAP + goal % CAP
        row = jnp.where((expert >= 0) & (expert < local_experts), expert * slots + place, -1)
        row = row.reshape(1, n_x * rows)
        every = jnp.arange(local_experts * slots, dtype=jnp.int32)[:, None]
        placer = (every == row).astype(BF16)
        placers.append(placer)
        slot_rows.append(
            jnp.einsum("sn,and->asd", placer, blocks, preferred_element_type=F32)
            .astype(BF16)
            .reshape(2, local_experts, slots, width)
        )
    slot_rows = jnp.concatenate(slot_rows, axis=2)
    inputs, grads_in = slot_rows[0], slot_rows[1]

    def act(values, weight):
        return jnp.einsum("esd,edf->esf", values, weight, preferred_element_type=F32).astype(BF16)

    acts = jnp.stack([act(inputs, gate_weight), act(inputs, up_weight), act(grads_in, down_weight)])
    acts = acts.reshape(3, local_experts, n_dp, slots, hidden)
    acts = halving_sum({r: acts[:, :, r] for r in range(n_dp)}, "dp", n_dp)
    grads = doubling_gather(jnp.stack(swiglu_grads(acts[0], acts[1], acts[2])), "dp", n_dp)
    grads = jnp.concatenate(grads, axis=2)
    gate_grad, up_grad = grads[0], grads[1]
    partial_value = jnp.einsum("esf,edf->esd", gate_grad, gate_weight, preferred_element_type=F32)
    partial_value = partial_value + jnp.einsum("esf,edf->esd", up_grad, up_weight, preferred_element_type=F32)
    partial_value = partial_value.astype(BF16).reshape(local_experts, n_dp, slots, width)
    per_token = []
    for rel in range(n_dp):
        flat = partial_value[:, rel].reshape(local_experts * slots, width)
        spread = lax.dot_general(placers[rel], flat, (((0,), (0,)), ((), ())), preferred_element_type=F32)
        spread = spread.astype(BF16).reshape(n_x, rows, width)
        per_token.append(lax.psum_scatter(spread, "expert", scatter_dimension=0, tiled=False))
    per_token = jnp.stack(per_token)
    terms = {r: lax.dynamic_index_in_dim(per_token, k ^ t ^ r, axis=0, keepdims=False) for r in range(n_t)}
    summed = halving_sum(terms, "tensor", n_t).astype(BF16)
    summed = lax.ppermute(
        summed, ("dp", "tensor"), [(i * n_t + j, j * n_t + i) for i in range(n_dp) for j in range(n_t)]
    )
    grad_gate = jnp.einsum("esd,esf->edf", inputs, gate_grad, preferred_element_type=F32).astype(BF16)
    grad_up = jnp.einsum("esd,esf->edf", inputs, up_grad, preferred_element_type=F32).astype(BF16)
    return summed, grad_gate, grad_up


def solution(mesh):
    placed = (
        P(("dp", "expert"), None),
        P(("dp", "expert"), None),
        P(("dp", "expert"), None),
        P("expert", "dp", "tensor"),
        P("expert", "dp", "tensor"),
        P("expert", "dp", "tensor"),
    )
    sizes = tuple(mesh.shape[name] for name in ("dp", "expert", "tensor"))

    def on_device(tokens, cotangent, expert_ids, *weights):
        experts = weights[0].shape[0] * sizes[1]
        small = sizes == (4, 2, 4) and experts * CAP <= 256
        return (on_small_slice if small else on_any_slice)(tokens, cotangent, expert_ids, *weights)

    return jax.shard_map(
        on_device,
        mesh=mesh,
        in_specs=placed,
        out_specs=(
            P(("dp", "expert"), "tensor"),
            P("expert", "dp", "tensor"),
            P("expert", "dp", "tensor"),
        ),
        check_vma=False,
    )
```

```python
import functools

import jax
import jax.numpy as jnp
from jax import lax
from jax.experimental import pallas as pl
from jax.experimental.pallas import tpu as pltpu
from jax.sharding import PartitionSpec as P

CAP = 8
META = 16
F32 = jnp.float32
BF16 = jnp.bfloat16
MIB = 1024 * 1024
PLACE_COST = 1 << 34


def swap(value, axis, count, bit):
    return lax.ppermute(value, axis, [(i, i ^ bit) for i in range(count)])


def whole_spec(shape):
    return pl.BlockSpec(shape, lambda *_: (0,) * len(shape))


def params(mib=16):
    return pltpu.CompilerParams(vmem_limit_bytes=mib * MIB)


def placer_of(row, slot_count):
    every = lax.broadcasted_iota(jnp.int32, (slot_count, row.shape[1]), 0)
    return (every == row).astype(F32).astype(BF16)


def place_kernel(first, rows, mine, others, *refs):
    n_dp = len(mine)
    other = []
    for group in others:
        other += [group] if len(group.shape) == 2 else [group.at[i] for i in range(group.shape[0])]
    if first:
        placed, lines = refs[-2:]
    else:
        lines, placed = refs[0], refs[-1]
    local_experts, slot_rows, width = placed.shape
    slots = slot_rows // n_dp
    for rel in range(n_dp):
        if first:
            pair = [b[0 : rows + META, :] for b in (mine[rel], other[rel])]
            here = lax.axis_index("expert")
            goals = [b[rows:, 0:rows][0:1].astype(F32).astype(jnp.int32) for b in pair]
            row = jnp.concatenate(
                [
                    (goal // CAP - here * local_experts) * slots + source * CAP + goal % CAP
                    for goal, source in zip(goals, (here, 1 - here))
                ],
                axis=1,
            )
            lines[rel] = jnp.broadcast_to(row, (8, row.shape[1]))
            pair = [b[0:rows] for b in pair]
        else:
            row = lines[rel][0:1]
            pair = [b[...] for b in (mine[rel], other[rel])]
        placer = placer_of(row, local_experts * slots)
        found = jnp.dot(placer, jnp.concatenate(pair, axis=0), preferred_element_type=F32).astype(BF16)
        placed[:, rel * slots : (rel + 1) * slots, :] = found.reshape(local_experts, slots, width)


def place(mine, others, lines, rows, local_experts, after):
    first = lines is None
    n_dp, slots = len(mine), 2 * CAP
    width = mine[0].shape[1]
    placed = jax.ShapeDtypeStruct((local_experts, n_dp * slots, width), BF16)
    line = jax.ShapeDtypeStruct((n_dp, 8, 2 * rows), jnp.int32)
    vmem = pl.BlockSpec(memory_space=pltpu.VMEM)
    operands = [*others] + ([] if first else [lines])

    def kernel(*refs):
        split_at = n_dp + len(others)
        place_kernel(first, rows, refs[:n_dp], refs[n_dp:split_at], *refs[split_at:])

    return pl.pallas_call(
        kernel,
        out_shape=[placed, line] if first else placed,
        in_specs=[vmem] * (n_dp + len(operands))
        + [pl.BlockSpec(memory_space=pl.ANY)] * len(after),
        out_specs=[vmem, vmem] if first else vmem,
        compiler_params=params(),
        cost_estimate=pl.CostEstimate(flops=PLACE_COST, bytes_accessed=4 * rows * width * n_dp, transcendentals=0),
    )(*mine, *operands, *after)


def back_kernel(low, first, last, *refs):
    if first:
        earlier, refs = refs[0], refs[1:]
    if last:
        lines, refs = refs[0], refs[1:]
    h0, h1, refs = refs[0], refs[1], refs[2:]
    count, slots, _ = h0.shape
    if low:
        both, outs = refs[0], refs[1:]
    else:
        gate, up, both, outs = refs[0], refs[1], refs[6], refs[2:6] + refs[7:]
        hidden = gate.shape[1]
    for e in range(count):
        grads = jnp.concatenate([h0[e], h1[e]], axis=0)
        if not low:
            both[e, 0:hidden, :] = gate[e]
            both[e, hidden:, :] = up[e]
        value = jnp.dot(grads, both[first + e], preferred_element_type=F32).astype(BF16)
        for i in range(2):
            rows = value[i * slots : (i + 1) * slots]
            if last:
                outs[-1][i, (first + e) * slots : (first + e + 1) * slots, :] = rows
            else:
                outs[0][i, e * slots : (e + 1) * slots, :] = rows
    if not last:
        return
    held = outs[-1]
    if first:
        held[:, 0 : first * slots, :] = earlier[...]
    rows = outs[0].shape[0]
    odd = (lax.axis_index("dp") ^ lax.axis_index("tensor")) & 1
    for i in range(2):
        which = odd ^ i if low else i
        placer = placer_of(lines[low + which][0:1], held.shape[1])
        token_rows = lax.dot_general(
            placer, held[which], (((0,), (0,)), ((), ())), preferred_element_type=F32
        ).astype(BF16)
        outs[2 * i][...] = token_rows[0:rows]
        outs[2 * i + 1][...] = token_rows[rows:]


def back(low, lines, parts, weights, rows, first=0, earlier=None):
    local_experts, _, width = weights[0].shape
    count, slots, hidden = parts[0].shape
    last = first + count == local_experts
    vmem = pl.BlockSpec(memory_space=pltpu.VMEM)
    flops = (8 if last else 1) * count * 2 * slots * width * hidden
    operands = ([earlier] if first else []) + ([lines] if last else []) + [*parts]
    near = []
    if last:
        out_shape = [jax.ShapeDtypeStruct((rows, width), BF16)] * 4
        if not low:
            out_shape.append(jax.ShapeDtypeStruct((local_experts, hidden, width), BF16))
        near = [pltpu.VMEM((2, local_experts * slots, width), BF16)] + near
    else:
        out_shape = jax.ShapeDtypeStruct((2, count * slots, width), BF16)
    return pl.pallas_call(
        functools.partial(back_kernel, low, first, last),
        out_shape=out_shape,
        in_specs=[vmem] * (len(operands) + len(weights)),
        out_specs=[vmem] * len(out_shape) if last else vmem,
        scratch_shapes=near,
        compiler_params=params(20 if low else 30),
        cost_estimate=pl.CostEstimate(
            flops=flops, bytes_accessed=count * width * hidden * 2 if last else width, transcendentals=0
        ),
    )(*operands, *weights)


def weight_kernel(placed, h0, h1, h2, h3, gate, up):
    hidden = gate.shape[1]
    for i in range(gate.shape[0]):
        grads = jnp.concatenate([h[i] for h in (h0, h1, h2, h3)], axis=0)
        both = lax.dot_general(
            grads, placed[i], (((0,), (0,)), ((), ())), preferred_element_type=F32
        ).astype(BF16)
        gate[i] = both[0:hidden]
        up[i] = both[hidden:]


def weight_grads(placed, parts, per_step):
    local_experts, slot_rows, width = placed.shape
    _, slots, both = parts[0].shape
    hidden = both // 2
    part_spec = pl.BlockSpec((per_step, slots, both), lambda e: (e, 0, 0))
    out_spec = pl.BlockSpec((per_step, hidden, width), lambda e: (e, 0, 0))
    flops = 2 * local_experts * slot_rows * width * both
    return pl.pallas_call(
        weight_kernel,
        grid=(local_experts // per_step,),
        out_shape=[jax.ShapeDtypeStruct((local_experts, hidden, width), BF16)] * 2,
        in_specs=[pl.BlockSpec((per_step, slot_rows, width), lambda e: (e, 0, 0))] + [part_spec] * len(parts),
        out_specs=[out_spec] * 2,
        compiler_params=params(12),
        cost_estimate=pl.CostEstimate(
            flops=4 * flops, bytes_accessed=local_experts * width * both * 2, transcendentals=0
        ),
    )(placed, *parts)


def plus(first, second):
    return first.astype(F32) + second.astype(F32)


def swiglu_grads(gate_act, up_act, hidden_grad):
    sigmoid_gate = jax.nn.sigmoid(gate_act)
    up_grad = (hidden_grad * gate_act * sigmoid_gate).astype(BF16)
    gate_grad = (
        hidden_grad * up_act * sigmoid_gate * (1.0 + gate_act * (1.0 - sigmoid_gate))
    ).astype(BF16)
    return gate_grad, up_grad


def on_small_slice(tokens, cotangent, expert_ids, gate_weight, up_weight, down_weight):
    n_dp, n_x, n_t = 4, 2, 4
    k, x, t = lax.axis_index("dp"), lax.axis_index("expert"), lax.axis_index("tensor")
    width = gate_weight.shape[1]
    rows = tokens.shape[0]
    odd, swapped = ((k ^ t) & 1) == 1, ((k ^ t) & 2) == 2
    expert_ids, odd, swapped = lax.optimization_barrier((expert_ids, odd, swapped))
    ids_row = expert_ids.reshape(1, rows)
    order = jnp.arange(rows, dtype=jnp.int32)
    earlier = (expert_ids == ids_row) & (order[:, None] < order[None, :])
    goal = ids_row * CAP + jnp.sum(earlier.astype(jnp.int32), axis=0, keepdims=True)
    meta = jnp.pad(goal.astype(BF16), ((0, META - 1), (0, width - rows)))

    def columns(values, rel):
        return lax.dynamic_slice_in_dim(values, (k ^ rel) * width, width, axis=1)

    chunks = [jnp.concatenate([columns(tokens, rel), meta], axis=0) for rel in range(n_dp)]

    def to_owner(value, rel, flip):
        if rel == 0 and flip == 0:
            return value
        pairs = [
            (i * n_x + j, (i ^ rel) * n_x + (j ^ flip)) for i in range(n_dp) for j in range(n_x)
        ]
        return lax.ppermute(value, ("dp", "expert"), pairs)

    own_tokens = [to_owner(c, rel, 0) for rel, c in enumerate(chunks)]
    near_tokens = [to_owner(c, rel, 1) for rel, c in enumerate(chunks[:2])]
    grads = [columns(cotangent, rel) for rel in range(n_dp)]
    far_tokens, grads = lax.optimization_barrier((own_tokens[2:], grads))
    near_tokens, far_tokens = lax.optimization_barrier((near_tokens, far_tokens))
    far_tokens = [swap(c, "expert", n_x, 1) for c in far_tokens]
    own_grads = [to_owner(c, rel, 0) for rel, c in enumerate(grads)]
    leaving_grads = jnp.stack(own_grads)
    far_tokens, leaving_grads = lax.optimization_barrier((far_tokens, leaving_grads))
    other_grads = swap(leaving_grads, "expert", n_x, 1)
    gate_weight, up_weight, down_weight = (
        jnp.swapaxes(weight, 1, 2) for weight in (gate_weight, up_weight, down_weight)
    )
    local_experts = gate_weight.shape[0]

    def project(values, weight):
        act = jnp.einsum("esd,ehd->esh", values, weight, preferred_element_type=F32).astype(BF16)
        return jnp.split(act, n_dp, axis=1)

    def near_and_far(act):
        near, far = swap(act[1], "dp", n_dp, 1), swap(act[3], "dp", n_dp, 1)
        return plus(act[0], near), plus(act[2], far).astype(BF16)

    placed, lines = place(own_tokens, near_tokens + far_tokens, None, rows, local_experts, [leaving_grads])
    gate_near, gate_far = near_and_far(project(placed, gate_weight))
    up_near, up_far = near_and_far(project(placed, up_weight))
    there = [swap(gate_far, "dp", n_dp, 2), swap(up_far, "dp", n_dp, 2)]
    placed_grads = place(own_grads, [other_grads], lines, rows, local_experts, [gate_far, up_far])
    hidden_act = project(placed_grads, down_weight)
    beside, there = lax.optimization_barrier((swap(hidden_act[3], "dp", n_dp, 1), there))
    hidden_far = plus(hidden_act[2], beside).astype(BF16)
    hidden_near = plus(hidden_act[0], swap(hidden_act[1], "dp", n_dp, 1))
    gate_act, up_act = plus(gate_near, there[0]), plus(up_near, there[1])
    sigmoid_gate = jax.nn.sigmoid(gate_act)
    up_factor = gate_act * sigmoid_gate
    gate_factor = up_act * sigmoid_gate * (1.0 + gate_act * (1.0 - sigmoid_gate))
    hidden_grad = plus(hidden_near, swap(hidden_far, "dp", n_dp, 2))
    part = jnp.concatenate([hidden_grad * gate_factor, hidden_grad * up_factor], axis=2).astype(BF16)
    count = local_experts * 7 // 16
    far = [swap(piece, "dp", n_dp, 2) for piece in jnp.split(part, [count], axis=0)]
    beside = swap(part, "dp", n_dp, 1)
    *near_back, both_weights = back(0, lines, [part, beside], [gate_weight, up_weight], rows)
    far[0], _ = lax.optimization_barrier((far[0], near_back[0]))
    far_beside = [swap(far[0], "dp", n_dp, 1)]
    early = back(2, lines, [far[0], far_beside[0]], [both_weights], rows)
    far[1], _ = lax.optimization_barrier((far[1], early))
    far_beside.append(swap(far[1], "dp", n_dp, 1))
    far_back = back(2, lines, [far[1], far_beside[1]], [both_weights], rows, count, early)
    parts = [part, beside, jnp.concatenate(far, axis=0), jnp.concatenate(far_beside, axis=0)]
    own, other, own_beside, other_beside = near_back
    own_beside, other_beside = swap(own_beside, "dp", n_dp, 1), swap(other_beside, "dp", n_dp, 1)
    own_beside, other_beside = lax.optimization_barrier((own_beside, other_beside))
    arrived = swap(jnp.stack([other, other_beside]), "expert", n_x, 1)
    arrived, after_back, _ = lax.optimization_barrier((arrived, placed, far_back[0]))
    weight_grad = weight_grads(after_back, parts, 4)

    def to_keeper(value, low, turn, flip):
        pairs = []
        for i in range(n_dp):
            for j in range(n_x):
                for l in range(n_t):
                    odd = (i ^ l) & 1
                    to = ((i ^ low ^ odd ^ turn) * n_x + (j ^ flip)) * n_t + (l ^ odd)
                    pairs.append(((i * n_x + j) * n_t + l, to))
        return lax.ppermute(value, ("dp", "expert", "tensor"), pairs)

    merged = [plus(own, arrived[0]).astype(BF16), plus(own_beside, arrived[1]).astype(BF16)]
    keep, leaving = jnp.where(odd, merged[1], merged[0]), jnp.where(odd, merged[0], merged[1])
    first = plus(keep, swap(leaving, "tensor", n_t, 1))
    far_terms = [to_keeper(value, 2, at // 2, at % 2) for at, value in enumerate(far_back)]
    far_terms, _ = lax.optimization_barrier((far_terms, weight_grad))
    second = sum(value.astype(F32) for value in far_terms)
    keep = jnp.where(swapped, second, first)
    leaving = jnp.where(swapped, first, second).astype(BF16)
    grad_tokens = plus(keep, swap(leaving, "tensor", n_t, 2)).astype(BF16)

    grad_gate, grad_up = (jnp.swapaxes(grad, 1, 2) for grad in weight_grad)
    return grad_tokens, grad_gate, grad_up


def bits_of(count):
    bits = []
    bit = 1
    while bit < count:
        bits.append(bit)
        bit *= 2
    return bits


def halving_sum(parts, axis, count):
    parts = dict(parts)
    for bit in bits_of(count):
        leaving = sorted(r for r in parts if r & bit)
        arrived = swap(jnp.stack([parts[r].astype(BF16) for r in leaving]), axis, count, bit)
        for at, r in enumerate(leaving):
            parts[r ^ bit] = plus(parts[r ^ bit], arrived[at])
            del parts[r]
    return parts[0]


def doubling_gather(value, axis, count):
    held = {0: value}
    for bit in reversed(bits_of(count)):
        known = sorted(held)
        arrived = swap(jnp.stack([held[r] for r in known]), axis, count, bit)
        for at, r in enumerate(known):
            held[r ^ bit] = arrived[at]
    return [held[r] for r in range(count)]


def on_any_slice(tokens, cotangent, expert_ids, gate_weight, up_weight, down_weight):
    n_dp, n_x, n_t = lax.axis_size("dp"), lax.axis_size("expert"), lax.axis_size("tensor")
    k, x, t = lax.axis_index("dp"), lax.axis_index("expert"), lax.axis_index("tensor")
    local_experts, width, hidden = gate_weight.shape
    rows = tokens.shape[0]
    slots = n_x * CAP
    ids_row = expert_ids.reshape(1, rows)
    order = jnp.arange(rows, dtype=jnp.int32)
    earlier = (expert_ids == ids_row) & (order[:, None] < order[None, :])
    position = jnp.sum(earlier.astype(jnp.int32), axis=0)
    target = ids_row[0] * CAP + position
    targets = lax.all_gather(target, ("dp", "expert"), axis=0, tiled=False).reshape(n_dp, n_x, rows)
    pair = jnp.stack([tokens, cotangent])
    placers, slot_rows = [], []
    for rel in range(n_dp):
        columns = lax.dynamic_slice_in_dim(pair, (k ^ rel) * width, width, axis=2)
        mine = columns if rel == 0 else swap(columns, "dp", n_dp, rel)
        blocks = lax.all_gather(mine, "expert", axis=1, tiled=True)
        goal = lax.dynamic_index_in_dim(targets, k ^ rel, axis=0, keepdims=False)
        expert = goal // CAP - x * local_experts
        place = jnp.arange(n_x, dtype=jnp.int32)[:, None] * CAP + goal % CAP
        row = jnp.where((expert >= 0) & (expert < local_experts), expert * slots + place, -1)
        row = row.reshape(1, n_x * rows)
        every = jnp.arange(local_experts * slots, dtype=jnp.int32)[:, None]
        placer = (every == row).astype(BF16)
        placers.append(placer)
        slot_rows.append(
            jnp.einsum("sn,and->asd", placer, blocks, preferred_element_type=F32)
            .astype(BF16)
            .reshape(2, local_experts, slots, width)
        )
    slot_rows = jnp.concatenate(slot_rows, axis=2)
    inputs, grads_in = slot_rows[0], slot_rows[1]

    def act(values, weight):
        return jnp.einsum("esd,edf->esf", values, weight, preferred_element_type=F32).astype(BF16)

    acts = jnp.stack([act(inputs, gate_weight), act(inputs, up_weight), act(grads_in, down_weight)])
    acts = acts.reshape(3, local_experts, n_dp, slots, hidden)
    acts = halving_sum({r: acts[:, :, r] for r in range(n_dp)}, "dp", n_dp)
    grads = doubling_gather(jnp.stack(swiglu_grads(acts[0], acts[1], acts[2])), "dp", n_dp)
    grads = jnp.concatenate(grads, axis=2)
    gate_grad, up_grad = grads[0], grads[1]
    partial_value = jnp.einsum("esf,edf->esd", gate_grad, gate_weight, preferred_element_type=F32)
    partial_value = partial_value + jnp.einsum("esf,edf->esd", up_grad, up_weight, preferred_element_type=F32)
    partial_value = partial_value.astype(BF16).reshape(local_experts, n_dp, slots, width)
    per_token = []
    for rel in range(n_dp):
        flat = partial_value[:, rel].reshape(local_experts * slots, width)
        spread = lax.dot_general(placers[rel], flat, (((0,), (0,)), ((), ())), preferred_element_type=F32)
        spread = spread.astype(BF16).reshape(n_x, rows, width)
        per_token.append(lax.psum_scatter(spread, "expert", scatter_dimension=0, tiled=False))
    per_token = jnp.stack(per_token)
    terms = {r: lax.dynamic_index_in_dim(per_token, k ^ t ^ r, axis=0, keepdims=False) for r in range(n_t)}
    summed = halving_sum(terms, "tensor", n_t).astype(BF16)
    summed = lax.ppermute(
        summed, ("dp", "tensor"), [(i * n_t + j, j * n_t + i) for i in range(n_dp) for j in range(n_t)]
    )
    grad_gate = jnp.einsum("esd,esf->edf", inputs, gate_grad, preferred_element_type=F32).astype(BF16)
    grad_up = jnp.einsum("esd,esf->edf", inputs, up_grad, preferred_element_type=F32).astype(BF16)
    return summed, grad_gate, grad_up


def solution(mesh):
    placed = (
        P(("dp", "expert"), None),
        P(("dp", "expert"), None),
        P(("dp", "expert"), None),
        P("expert", "dp", "tensor"),
        P("expert", "dp", "tensor"),
        P("expert", "dp", "tensor"),
    )
    sizes = tuple(mesh.shape[name] for name in ("dp", "expert", "tensor"))

    def on_device(tokens, cotangent, expert_ids, *weights):
        experts = weights[0].shape[0] * sizes[1]
        small = sizes == (4, 2, 4) and experts * CAP <= 256
        return (on_small_slice if small else on_any_slice)(tokens, cotangent, expert_ids, *weights)

    return jax.shard_map(
        on_device,
        mesh=mesh,
        in_specs=placed,
        out_specs=(
            P(("dp", "expert"), "tensor"),
            P("expert", "dp", "tensor"),
            P("expert", "dp", "tensor"),
        ),
        check_vma=False,
    )
```

```python
import functools

import jax
import jax.numpy as jnp
from jax import lax
from jax.experimental import pallas as pl
from jax.experimental.pallas import tpu as pltpu
from jax.sharding import PartitionSpec as P

CAP = 8
META = 16
F32 = jnp.float32
BF16 = jnp.bfloat16
MIB = 1024 * 1024
PLACE_COST = 1 << 34


def swap(value, axis, count, bit):
    return lax.ppermute(value, axis, [(i, i ^ bit) for i in range(count)])


def whole_spec(shape):
    return pl.BlockSpec(shape, lambda *_: (0,) * len(shape))


def params(mib=16):
    return pltpu.CompilerParams(vmem_limit_bytes=mib * MIB)


def placer_of(row, slot_count):
    every = lax.broadcasted_iota(jnp.int32, (slot_count, row.shape[1]), 0)
    return (every == row).astype(F32).astype(BF16)


def place_kernel(first, rows, mine, others, *refs):
    n_dp = len(mine)
    other = []
    for group in others:
        other += [group] if len(group.shape) == 2 else [group.at[i] for i in range(group.shape[0])]
    if first:
        placed, lines = refs[-2:]
    else:
        lines, placed = refs[0], refs[-1]
    local_experts, slot_rows, width = placed.shape
    slots = slot_rows // n_dp
    for rel in range(n_dp):
        if first:
            pair = [b[0 : rows + META, :] for b in (mine[rel], other[rel])]
            here = lax.axis_index("expert")
            goals = [b[rows:, 0:rows][0:1].astype(F32).astype(jnp.int32) for b in pair]
            row = jnp.concatenate(
                [
                    (goal // CAP - here * local_experts) * slots + source * CAP + goal % CAP
                    for goal, source in zip(goals, (here, 1 - here))
                ],
                axis=1,
            )
            lines[rel] = jnp.broadcast_to(row, (8, row.shape[1]))
            pair = [b[0:rows] for b in pair]
        else:
            row = lines[rel][0:1]
            pair = [b[...] for b in (mine[rel], other[rel])]
        placer = placer_of(row, local_experts * slots)
        found = jnp.dot(placer, jnp.concatenate(pair, axis=0), preferred_element_type=F32).astype(BF16)
        placed[:, rel * slots : (rel + 1) * slots, :] = found.reshape(local_experts, slots, width)


def place(mine, others, lines, rows, local_experts, after):
    first = lines is None
    n_dp, slots = len(mine), 2 * CAP
    width = mine[0].shape[1]
    placed = jax.ShapeDtypeStruct((local_experts, n_dp * slots, width), BF16)
    line = jax.ShapeDtypeStruct((n_dp, 8, 2 * rows), jnp.int32)
    vmem = pl.BlockSpec(memory_space=pltpu.VMEM)
    operands = [*others] + ([] if first else [lines])

    def kernel(*refs):
        split_at = n_dp + len(others)
        place_kernel(first, rows, refs[:n_dp], refs[n_dp:split_at], *refs[split_at:])

    return pl.pallas_call(
        kernel,
        out_shape=[placed, line] if first else placed,
        in_specs=[vmem] * (n_dp + len(operands))
        + [pl.BlockSpec(memory_space=pl.ANY)] * len(after),
        out_specs=[vmem, vmem] if first else vmem,
        compiler_params=params(),
        cost_estimate=pl.CostEstimate(flops=PLACE_COST, bytes_accessed=4 * rows * width * n_dp, transcendentals=0),
    )(*mine, *operands, *after)


def back_kernel(low, first, last, *refs):
    if first:
        earlier, refs = refs[0], refs[1:]
    if last:
        lines, refs = refs[0], refs[1:]
    h0, h1, refs = refs[0], refs[1], refs[2:]
    count, slots, _ = h0.shape
    if low:
        both, outs = refs[0], refs[1:]
    else:
        gate, up, both, outs = refs[0], refs[1], refs[6], refs[2:6] + refs[7:]
        hidden = gate.shape[1]
    for e in range(count):
        grads = jnp.concatenate([h0[e], h1[e]], axis=0)
        if not low:
            both[e, 0:hidden, :] = gate[e]
            both[e, hidden:, :] = up[e]
        value = jnp.dot(grads, both[first + e], preferred_element_type=F32).astype(BF16)
        for i in range(2):
            rows = value[i * slots : (i + 1) * slots]
            if last:
                outs[-1][i, (first + e) * slots : (first + e + 1) * slots, :] = rows
            else:
                outs[0][i, e * slots : (e + 1) * slots, :] = rows
    if not last:
        return
    held = outs[-1]
    if first:
        held[:, 0 : first * slots, :] = earlier[...]
    rows = outs[0].shape[0]
    odd = (lax.axis_index("dp") ^ lax.axis_index("tensor")) & 1
    for i in range(2):
        which = odd ^ i if low else i
        placer = placer_of(lines[low + which][0:1], held.shape[1])
        token_rows = lax.dot_general(
            placer, held[which], (((0,), (0,)), ((), ())), preferred_element_type=F32
        ).astype(BF16)
        outs[2 * i][...] = token_rows[0:rows]
        outs[2 * i + 1][...] = token_rows[rows:]


def back(low, lines, parts, weights, rows, first=0, earlier=None):
    local_experts, _, width = weights[0].shape
    count, slots, hidden = parts[0].shape
    last = first + count == local_experts
    vmem = pl.BlockSpec(memory_space=pltpu.VMEM)
    flops = (8 if last else 1) * count * 2 * slots * width * hidden
    operands = ([earlier] if first else []) + ([lines] if last else []) + [*parts]
    near = []
    if last:
        out_shape = [jax.ShapeDtypeStruct((rows, width), BF16)] * 4
        if not low:
            out_shape.append(jax.ShapeDtypeStruct((local_experts, hidden, width), BF16))
        near = [pltpu.VMEM((2, local_experts * slots, width), BF16)] + near
    else:
        out_shape = jax.ShapeDtypeStruct((2, count * slots, width), BF16)
    return pl.pallas_call(
        functools.partial(back_kernel, low, first, last),
        out_shape=out_shape,
        in_specs=[vmem] * (len(operands) + len(weights)),
        out_specs=[vmem] * len(out_shape) if last else vmem,
        scratch_shapes=near,
        compiler_params=params(20 if low else 30),
        cost_estimate=pl.CostEstimate(
            flops=flops, bytes_accessed=count * width * hidden * 2 if last else width, transcendentals=0
        ),
    )(*operands, *weights)


def weight_kernel(placed, h0, h1, h2, h3, gate, up):
    hidden = gate.shape[1]
    for i in range(gate.shape[0]):
        grads = jnp.concatenate([h[i] for h in (h0, h1, h2, h3)], axis=0)
        both = lax.dot_general(
            grads, placed[i], (((0,), (0,)), ((), ())), preferred_element_type=F32
        ).astype(BF16)
        gate[i] = both[0:hidden]
        up[i] = both[hidden:]


def weight_grads(placed, parts, per_step):
    local_experts, slot_rows, width = placed.shape
    _, slots, both = parts[0].shape
    hidden = both // 2
    part_spec = pl.BlockSpec((per_step, slots, both), lambda e: (e, 0, 0))
    out_spec = pl.BlockSpec((per_step, hidden, width), lambda e: (e, 0, 0))
    flops = 2 * local_experts * slot_rows * width * both
    return pl.pallas_call(
        weight_kernel,
        grid=(local_experts // per_step,),
        out_shape=[jax.ShapeDtypeStruct((local_experts, hidden, width), BF16)] * 2,
        in_specs=[pl.BlockSpec((per_step, slot_rows, width), lambda e: (e, 0, 0))] + [part_spec] * len(parts),
        out_specs=[out_spec] * 2,
        compiler_params=params(12),
        cost_estimate=pl.CostEstimate(
            flops=4 * flops, bytes_accessed=local_experts * width * both * 2, transcendentals=0
        ),
    )(placed, *parts)


def plus(first, second):
    return first.astype(F32) + second.astype(F32)


def swiglu_grads(gate_act, up_act, hidden_grad):
    sigmoid_gate = jax.nn.sigmoid(gate_act)
    up_grad = (hidden_grad * gate_act * sigmoid_gate).astype(BF16)
    gate_grad = (
        hidden_grad * up_act * sigmoid_gate * (1.0 + gate_act * (1.0 - sigmoid_gate))
    ).astype(BF16)
    return gate_grad, up_grad


def on_small_slice(tokens, cotangent, expert_ids, gate_weight, up_weight, down_weight):
    n_dp, n_x, n_t = 4, 2, 4
    k, x, t = lax.axis_index("dp"), lax.axis_index("expert"), lax.axis_index("tensor")
    width = gate_weight.shape[1]
    rows = tokens.shape[0]
    odd, swapped = ((k ^ t) & 1) == 1, ((k ^ t) & 2) == 2
    expert_ids, odd, swapped = lax.optimization_barrier((expert_ids, odd, swapped))
    ids_row = expert_ids.reshape(1, rows)
    order = jnp.arange(rows, dtype=jnp.int32)
    earlier = (expert_ids == ids_row) & (order[:, None] < order[None, :])
    goal = ids_row * CAP + jnp.sum(earlier.astype(jnp.int32), axis=0, keepdims=True)
    meta = jnp.pad(goal.astype(BF16), ((0, META - 1), (0, width - rows)))

    def columns(values, rel):
        return lax.dynamic_slice_in_dim(values, (k ^ rel) * width, width, axis=1)

    chunks = [jnp.concatenate([columns(tokens, rel), meta], axis=0) for rel in range(n_dp)]

    def to_owner(value, rel, flip):
        if rel == 0 and flip == 0:
            return value
        pairs = [
            (i * n_x + j, (i ^ rel) * n_x + (j ^ flip)) for i in range(n_dp) for j in range(n_x)
        ]
        return lax.ppermute(value, ("dp", "expert"), pairs)

    own_tokens = [to_owner(c, rel, 0) for rel, c in enumerate(chunks)]
    near_tokens = [to_owner(c, rel, 1) for rel, c in enumerate(chunks[:2])]
    grads = [columns(cotangent, rel) for rel in range(n_dp)]
    far_tokens, grads = lax.optimization_barrier((own_tokens[2:], grads))
    near_tokens, far_tokens = lax.optimization_barrier((near_tokens, far_tokens))
    far_tokens = [swap(c, "expert", n_x, 1) for c in far_tokens]
    own_grads = [to_owner(c, rel, 0) for rel, c in enumerate(grads)]
    leaving_grads = jnp.stack(own_grads)
    other_grads = swap(leaving_grads, "expert", n_x, 1)
    gate_weight, up_weight, down_weight = (
        jnp.swapaxes(weight, 1, 2) for weight in (gate_weight, up_weight, down_weight)
    )
    local_experts = gate_weight.shape[0]

    def project(values, weight):
        act = jnp.einsum("esd,ehd->esh", values, weight, preferred_element_type=F32).astype(BF16)
        return jnp.split(act, n_dp, axis=1)

    def near_and_far(act):
        near, far = swap(act[1], "dp", n_dp, 1), swap(act[3], "dp", n_dp, 1)
        return plus(act[0], near), plus(act[2], far).astype(BF16)

    placed, lines = place(own_tokens, near_tokens + far_tokens, None, rows, local_experts, [leaving_grads])
    gate_near, gate_far = near_and_far(project(placed, gate_weight))
    up_near, up_far = near_and_far(project(placed, up_weight))
    there = [swap(gate_far, "dp", n_dp, 2), swap(up_far, "dp", n_dp, 2)]
    placed_grads = place(own_grads, [other_grads], lines, rows, local_experts, [gate_far, up_far])
    hidden_act = project(placed_grads, down_weight)
    beside, there = lax.optimization_barrier((swap(hidden_act[3], "dp", n_dp, 1), there))
    hidden_far = plus(hidden_act[2], beside).astype(BF16)
    hidden_near = plus(hidden_act[0], swap(hidden_act[1], "dp", n_dp, 1))
    gate_act, up_act = plus(gate_near, there[0]), plus(up_near, there[1])
    sigmoid_gate = jax.nn.sigmoid(gate_act)
    up_factor = gate_act * sigmoid_gate
    gate_factor = up_act * sigmoid_gate * (1.0 + gate_act * (1.0 - sigmoid_gate))
    hidden_grad = plus(hidden_near, swap(hidden_far, "dp", n_dp, 2))
    part = jnp.concatenate([hidden_grad * gate_factor, hidden_grad * up_factor], axis=2).astype(BF16)
    count = local_experts * 7 // 16
    far = [swap(piece, "dp", n_dp, 2) for piece in jnp.split(part, [count], axis=0)]
    beside = swap(part, "dp", n_dp, 1)
    *near_back, both_weights = back(0, lines, [part, beside], [gate_weight, up_weight], rows)
    far[0], _ = lax.optimization_barrier((far[0], near_back[0]))
    far_beside = [swap(far[0], "dp", n_dp, 1)]
    early = back(2, lines, [far[0], far_beside[0]], [both_weights], rows)
    far[1], _ = lax.optimization_barrier((far[1], early))
    far_beside.append(swap(far[1], "dp", n_dp, 1))
    far_back = back(2, lines, [far[1], far_beside[1]], [both_weights], rows, count, early)
    parts = [part, beside, jnp.concatenate(far, axis=0), jnp.concatenate(far_beside, axis=0)]
    own, other, own_beside, other_beside = near_back
    own_beside, other_beside = swap(own_beside, "dp", n_dp, 1), swap(other_beside, "dp", n_dp, 1)
    own_beside, other_beside = lax.optimization_barrier((own_beside, other_beside))
    arrived = swap(jnp.stack([other, other_beside]), "expert", n_x, 1)
    arrived, after_back, _ = lax.optimization_barrier((arrived, placed, far_back[0]))
    weight_grad = weight_grads(after_back, parts, 4)

    def to_keeper(value, low, turn, flip):
        pairs = []
        for i in range(n_dp):
            for j in range(n_x):
                for l in range(n_t):
                    odd = (i ^ l) & 1
                    to = ((i ^ low ^ odd ^ turn) * n_x + (j ^ flip)) * n_t + (l ^ odd)
                    pairs.append(((i * n_x + j) * n_t + l, to))
        return lax.ppermute(value, ("dp", "expert", "tensor"), pairs)

    merged = [plus(own, arrived[0]).astype(BF16), plus(own_beside, arrived[1]).astype(BF16)]
    keep, leaving = jnp.where(odd, merged[1], merged[0]), jnp.where(odd, merged[0], merged[1])
    first = plus(keep, swap(leaving, "tensor", n_t, 1))
    far_terms = [to_keeper(value, 2, at // 2, at % 2) for at, value in enumerate(far_back)]
    far_terms, _ = lax.optimization_barrier((far_terms, weight_grad))
    second = sum(value.astype(F32) for value in far_terms)
    keep = jnp.where(swapped, second, first)
    leaving = jnp.where(swapped, first, second).astype(BF16)
    grad_tokens = plus(keep, swap(leaving, "tensor", n_t, 2)).astype(BF16)

    grad_gate, grad_up = (jnp.swapaxes(grad, 1, 2) for grad in weight_grad)
    return grad_tokens, grad_gate, grad_up


def bits_of(count):
    bits = []
    bit = 1
    while bit < count:
        bits.append(bit)
        bit *= 2
    return bits


def halving_sum(parts, axis, count):
    parts = dict(parts)
    for bit in bits_of(count):
        leaving = sorted(r for r in parts if r & bit)
        arrived = swap(jnp.stack([parts[r].astype(BF16) for r in leaving]), axis, count, bit)
        for at, r in enumerate(leaving):
            parts[r ^ bit] = plus(parts[r ^ bit], arrived[at])
            del parts[r]
    return parts[0]


def doubling_gather(value, axis, count):
    held = {0: value}
    for bit in reversed(bits_of(count)):
        known = sorted(held)
        arrived = swap(jnp.stack([held[r] for r in known]), axis, count, bit)
        for at, r in enumerate(known):
            held[r ^ bit] = arrived[at]
    return [held[r] for r in range(count)]


def on_any_slice(tokens, cotangent, expert_ids, gate_weight, up_weight, down_weight):
    n_dp, n_x, n_t = lax.axis_size("dp"), lax.axis_size("expert"), lax.axis_size("tensor")
    k, x, t = lax.axis_index("dp"), lax.axis_index("expert"), lax.axis_index("tensor")
    local_experts, width, hidden = gate_weight.shape
    rows = tokens.shape[0]
    slots = n_x * CAP
    ids_row = expert_ids.reshape(1, rows)
    order = jnp.arange(rows, dtype=jnp.int32)
    earlier = (expert_ids == ids_row) & (order[:, None] < order[None, :])
    position = jnp.sum(earlier.astype(jnp.int32), axis=0)
    target = ids_row[0] * CAP + position
    targets = lax.all_gather(target, ("dp", "expert"), axis=0, tiled=False).reshape(n_dp, n_x, rows)
    pair = jnp.stack([tokens, cotangent])
    placers, slot_rows = [], []
    for rel in range(n_dp):
        columns = lax.dynamic_slice_in_dim(pair, (k ^ rel) * width, width, axis=2)
        mine = columns if rel == 0 else swap(columns, "dp", n_dp, rel)
        blocks = lax.all_gather(mine, "expert", axis=1, tiled=True)
        goal = lax.dynamic_index_in_dim(targets, k ^ rel, axis=0, keepdims=False)
        expert = goal // CAP - x * local_experts
        place = jnp.arange(n_x, dtype=jnp.int32)[:, None] * CAP + goal % CAP
        row = jnp.where((expert >= 0) & (expert < local_experts), expert * slots + place, -1)
        row = row.reshape(1, n_x * rows)
        every = jnp.arange(local_experts * slots, dtype=jnp.int32)[:, None]
        placer = (every == row).astype(BF16)
        placers.append(placer)
        slot_rows.append(
            jnp.einsum("sn,and->asd", placer, blocks, preferred_element_type=F32)
            .astype(BF16)
            .reshape(2, local_experts, slots, width)
        )
    slot_rows = jnp.concatenate(slot_rows, axis=2)
    inputs, grads_in = slot_rows[0], slot_rows[1]

    def act(values, weight):
        return jnp.einsum("esd,edf->esf", values, weight, preferred_element_type=F32).astype(BF16)

    acts = jnp.stack([act(inputs, gate_weight), act(inputs, up_weight), act(grads_in, down_weight)])
    acts = acts.reshape(3, local_experts, n_dp, slots, hidden)
    acts = halving_sum({r: acts[:, :, r] for r in range(n_dp)}, "dp", n_dp)
    grads = doubling_gather(jnp.stack(swiglu_grads(acts[0], acts[1], acts[2])), "dp", n_dp)
    grads = jnp.concatenate(grads, axis=2)
    gate_grad, up_grad = grads[0], grads[1]
    partial_value = jnp.einsum("esf,edf->esd", gate_grad, gate_weight, preferred_element_type=F32)
    partial_value = partial_value + jnp.einsum("esf,edf->esd", up_grad, up_weight, preferred_element_type=F32)
    partial_value = partial_value.astype(BF16).reshape(local_experts, n_dp, slots, width)
    per_token = []
    for rel in range(n_dp):
        flat = partial_value[:, rel].reshape(local_experts * slots, width)
        spread = lax.dot_general(placers[rel], flat, (((0,), (0,)), ((), ())), preferred_element_type=F32)
        spread = spread.astype(BF16).reshape(n_x, rows, width)
        per_token.append(lax.psum_scatter(spread, "expert", scatter_dimension=0, tiled=False))
    per_token = jnp.stack(per_token)
    terms = {r: lax.dynamic_index_in_dim(per_token, k ^ t ^ r, axis=0, keepdims=False) for r in range(n_t)}
    summed = halving_sum(terms, "tensor", n_t).astype(BF16)
    summed = lax.ppermute(
        summed, ("dp", "tensor"), [(i * n_t + j, j * n_t + i) for i in range(n_dp) for j in range(n_t)]
    )
    grad_gate = jnp.einsum("esd,esf->edf", inputs, gate_grad, preferred_element_type=F32).astype(BF16)
    grad_up = jnp.einsum("esd,esf->edf", inputs, up_grad, preferred_element_type=F32).astype(BF16)
    return summed, grad_gate, grad_up


def solution(mesh):
    placed = (
        P(("dp", "expert"), None),
        P(("dp", "expert"), None),
        P(("dp", "expert"), None),
        P("expert", "dp", "tensor"),
        P("expert", "dp", "tensor"),
        P("expert", "dp", "tensor"),
    )
    sizes = tuple(mesh.shape[name] for name in ("dp", "expert", "tensor"))

    def on_device(tokens, cotangent, expert_ids, *weights):
        experts = weights[0].shape[0] * sizes[1]
        small = sizes == (4, 2, 4) and experts * CAP <= 256
        return (on_small_slice if small else on_any_slice)(tokens, cotangent, expert_ids, *weights)

    return jax.shard_map(
        on_device,
        mesh=mesh,
        in_specs=placed,
        out_specs=(
            P(("dp", "expert"), "tensor"),
            P("expert", "dp", "tensor"),
            P("expert", "dp", "tensor"),
        ),
        check_vma=False,
    )
```

```python
import functools

import jax
import jax.numpy as jnp
from jax import lax
from jax.experimental import pallas as pl
from jax.experimental.pallas import tpu as pltpu
from jax.sharding import PartitionSpec as P

CAP = 8
META = 16
F32 = jnp.float32
BF16 = jnp.bfloat16
MIB = 1024 * 1024
PLACE_COST = 1 << 34


def swap(value, axis, count, bit):
    return lax.ppermute(value, axis, [(i, i ^ bit) for i in range(count)])


def whole_spec(shape):
    return pl.BlockSpec(shape, lambda *_: (0,) * len(shape))


def params(mib=16):
    return pltpu.CompilerParams(vmem_limit_bytes=mib * MIB)


def placer_of(row, slot_count):
    every = lax.broadcasted_iota(jnp.int32, (slot_count, row.shape[1]), 0)
    return (every == row).astype(F32).astype(BF16)


def place_kernel(first, rows, mine, others, *refs):
    n_dp = len(mine)
    other = []
    for group in others:
        other += [group] if len(group.shape) == 2 else [group.at[i] for i in range(group.shape[0])]
    if first:
        placed, lines = refs[-2:]
    else:
        lines, placed = refs[0], refs[-1]
    local_experts, slot_rows, width = placed.shape
    slots = slot_rows // n_dp
    for rel in range(n_dp):
        if first:
            pair = [b[0 : rows + META, :] for b in (mine[rel], other[rel])]
            here = lax.axis_index("expert")
            goals = [b[rows:, 0:rows][0:1].astype(F32).astype(jnp.int32) for b in pair]
            row = jnp.concatenate(
                [
                    (goal // CAP - here * local_experts) * slots + source * CAP + goal % CAP
                    for goal, source in zip(goals, (here, 1 - here))
                ],
                axis=1,
            )
            lines[rel] = jnp.broadcast_to(row, (8, row.shape[1]))
            pair = [b[0:rows] for b in pair]
        else:
            row = lines[rel][0:1]
            pair = [b[...] for b in (mine[rel], other[rel])]
        placer = placer_of(row, local_experts * slots)
        found = jnp.dot(placer, jnp.concatenate(pair, axis=0), preferred_element_type=F32).astype(BF16)
        placed[:, rel * slots : (rel + 1) * slots, :] = found.reshape(local_experts, slots, width)


def place(mine, others, lines, rows, local_experts, after):
    first = lines is None
    n_dp, slots = len(mine), 2 * CAP
    width = mine[0].shape[1]
    placed = jax.ShapeDtypeStruct((local_experts, n_dp * slots, width), BF16)
    line = jax.ShapeDtypeStruct((n_dp, 8, 2 * rows), jnp.int32)
    vmem = pl.BlockSpec(memory_space=pltpu.VMEM)
    operands = [*others] + ([] if first else [lines])

    def kernel(*refs):
        split_at = n_dp + len(others)
        place_kernel(first, rows, refs[:n_dp], refs[n_dp:split_at], *refs[split_at:])

    return pl.pallas_call(
        kernel,
        out_shape=[placed, line] if first else placed,
        in_specs=[vmem] * (n_dp + len(operands))
        + [pl.BlockSpec(memory_space=pl.ANY)] * len(after),
        out_specs=[vmem, vmem] if first else vmem,
        compiler_params=params(),
        cost_estimate=pl.CostEstimate(flops=PLACE_COST, bytes_accessed=4 * rows * width * n_dp, transcendentals=0),
    )(*mine, *operands, *after)


def back_kernel(low, first, last, *refs):
    if first:
        earlier, refs = refs[0], refs[1:]
    if last:
        lines, refs = refs[0], refs[1:]
    h0, h1, refs = refs[0], refs[1], refs[2:]
    count, slots, _ = h0.shape
    if low:
        both, outs = refs[0], refs[1:]
    else:
        gate, up, both, outs = refs[0], refs[1], refs[6], refs[2:6] + refs[7:]
        hidden = gate.shape[1]
    for e in range(count):
        grads = jnp.concatenate([h0[e], h1[e]], axis=0)
        if not low:
            both[e, 0:hidden, :] = gate[e]
            both[e, hidden:, :] = up[e]
        value = jnp.dot(grads, both[first + e], preferred_element_type=F32).astype(BF16)
        for i in range(2):
            rows = value[i * slots : (i + 1) * slots]
            if last:
                outs[-1][i, (first + e) * slots : (first + e + 1) * slots, :] = rows
            else:
                outs[0][i, e * slots : (e + 1) * slots, :] = rows
    if not last:
        return
    held = outs[-1]
    if first:
        held[:, 0 : first * slots, :] = earlier[...]
    rows = outs[0].shape[0]
    odd = (lax.axis_index("dp") ^ lax.axis_index("tensor")) & 1
    for i in range(2):
        which = odd ^ i if low else i
        placer = placer_of(lines[low + which][0:1], held.shape[1])
        token_rows = lax.dot_general(
            placer, held[which], (((0,), (0,)), ((), ())), preferred_element_type=F32
        ).astype(BF16)
        outs[2 * i][...] = token_rows[0:rows]
        outs[2 * i + 1][...] = token_rows[rows:]


def back(low, lines, parts, weights, rows, first=0, earlier=None):
    local_experts, _, width = weights[0].shape
    count, slots, hidden = parts[0].shape
    last = first + count == local_experts
    vmem = pl.BlockSpec(memory_space=pltpu.VMEM)
    flops = (8 if last else 1) * count * 2 * slots * width * hidden
    operands = ([earlier] if first else []) + ([lines] if last else []) + [*parts]
    near = []
    if last:
        out_shape = [jax.ShapeDtypeStruct((rows, width), BF16)] * 4
        if not low:
            out_shape.append(jax.ShapeDtypeStruct((local_experts, hidden, width), BF16))
        near = [pltpu.VMEM((2, local_experts * slots, width), BF16)] + near
    else:
        out_shape = jax.ShapeDtypeStruct((2, count * slots, width), BF16)
    return pl.pallas_call(
        functools.partial(back_kernel, low, first, last),
        out_shape=out_shape,
        in_specs=[vmem] * (len(operands) + len(weights)),
        out_specs=[vmem] * len(out_shape) if last else vmem,
        scratch_shapes=near,
        compiler_params=params(20 if low else 30),
        cost_estimate=pl.CostEstimate(
            flops=flops, bytes_accessed=count * width * hidden * 2 if last else width, transcendentals=0
        ),
    )(*operands, *weights)


def weight_kernel(placed, h0, h1, h2, h3, gate, up):
    hidden = gate.shape[1]
    for i in range(gate.shape[0]):
        grads = jnp.concatenate([h[i] for h in (h0, h1, h2, h3)], axis=0)
        both = lax.dot_general(
            grads, placed[i], (((0,), (0,)), ((), ())), preferred_element_type=F32
        ).astype(BF16)
        gate[i] = both[0:hidden]
        up[i] = both[hidden:]


def weight_grads(placed, parts, per_step):
    local_experts, slot_rows, width = placed.shape
    _, slots, both = parts[0].shape
    hidden = both // 2
    part_spec = pl.BlockSpec((per_step, slots, both), lambda e: (e, 0, 0))
    out_spec = pl.BlockSpec((per_step, hidden, width), lambda e: (e, 0, 0))
    flops = 2 * local_experts * slot_rows * width * both
    return pl.pallas_call(
        weight_kernel,
        grid=(local_experts // per_step,),
        out_shape=[jax.ShapeDtypeStruct((local_experts, hidden, width), BF16)] * 2,
        in_specs=[pl.BlockSpec((per_step, slot_rows, width), lambda e: (e, 0, 0))] + [part_spec] * len(parts),
        out_specs=[out_spec] * 2,
        compiler_params=params(12),
        cost_estimate=pl.CostEstimate(
            flops=4 * flops, bytes_accessed=local_experts * width * both * 2, transcendentals=0
        ),
    )(placed, *parts)


def plus(first, second):
    return first.astype(F32) + second.astype(F32)


def swiglu_grads(gate_act, up_act, hidden_grad):
    sigmoid_gate = jax.nn.sigmoid(gate_act)
    up_grad = (hidden_grad * gate_act * sigmoid_gate).astype(BF16)
    gate_grad = (
        hidden_grad * up_act * sigmoid_gate * (1.0 + gate_act * (1.0 - sigmoid_gate))
    ).astype(BF16)
    return gate_grad, up_grad


def on_small_slice(tokens, cotangent, expert_ids, gate_weight, up_weight, down_weight):
    n_dp, n_x, n_t = 4, 2, 4
    k, x, t = lax.axis_index("dp"), lax.axis_index("expert"), lax.axis_index("tensor")
    width = gate_weight.shape[1]
    rows = tokens.shape[0]
    odd, swapped = ((k ^ t) & 1) == 1, ((k ^ t) & 2) == 2
    expert_ids, odd, swapped = lax.optimization_barrier((expert_ids, odd, swapped))
    ids_row = expert_ids.reshape(1, rows)
    order = jnp.arange(rows, dtype=jnp.int32)
    earlier = (expert_ids == ids_row) & (order[:, None] < order[None, :])
    goal = ids_row * CAP + jnp.sum(earlier.astype(jnp.int32), axis=0, keepdims=True)
    meta = jnp.pad(goal.astype(BF16), ((0, META - 1), (0, width - rows)))

    def columns(values, rel):
        return lax.dynamic_slice_in_dim(values, (k ^ rel) * width, width, axis=1)

    chunks = [jnp.concatenate([columns(tokens, rel), meta], axis=0) for rel in range(n_dp)]

    def to_owner(value, rel, flip):
        if rel == 0 and flip == 0:
            return value
        pairs = [
            (i * n_x + j, (i ^ rel) * n_x + (j ^ flip)) for i in range(n_dp) for j in range(n_x)
        ]
        return lax.ppermute(value, ("dp", "expert"), pairs)

    own_tokens = [to_owner(c, rel, 0) for rel, c in enumerate(chunks)]
    near_tokens = [to_owner(c, rel, 1) for rel, c in enumerate(chunks[:2])]
    grads = [columns(cotangent, rel) for rel in range(n_dp)]
    far_tokens = own_tokens[2:]
    near_tokens, far_tokens = lax.optimization_barrier((near_tokens, far_tokens))
    far_tokens = [swap(c, "expert", n_x, 1) for c in far_tokens]
    own_grads = [to_owner(c, rel, 0) for rel, c in enumerate(grads)]
    leaving_grads = jnp.stack(own_grads)
    other_grads = swap(leaving_grads, "expert", n_x, 1)
    gate_weight, up_weight, down_weight = (
        jnp.swapaxes(weight, 1, 2) for weight in (gate_weight, up_weight, down_weight)
    )
    local_experts = gate_weight.shape[0]

    def project(values, weight):
        act = jnp.einsum("esd,ehd->esh", values, weight, preferred_element_type=F32).astype(BF16)
        return jnp.split(act, n_dp, axis=1)

    def near_and_far(act):
        near, far = swap(act[1], "dp", n_dp, 1), swap(act[3], "dp", n_dp, 1)
        return plus(act[0], near), plus(act[2], far).astype(BF16)

    placed, lines = place(own_tokens, near_tokens + far_tokens, None, rows, local_experts, [leaving_grads])
    gate_near, gate_far = near_and_far(project(placed, gate_weight))
    up_near, up_far = near_and_far(project(placed, up_weight))
    there = [swap(gate_far, "dp", n_dp, 2), swap(up_far, "dp", n_dp, 2)]
    placed_grads = place(own_grads, [other_grads], lines, rows, local_experts, [gate_far, up_far])
    hidden_act = project(placed_grads, down_weight)
    beside, there = lax.optimization_barrier((swap(hidden_act[3], "dp", n_dp, 1), there))
    hidden_far = plus(hidden_act[2], beside).astype(BF16)
    hidden_near = plus(hidden_act[0], swap(hidden_act[1], "dp", n_dp, 1))
    gate_act, up_act = plus(gate_near, there[0]), plus(up_near, there[1])
    sigmoid_gate = jax.nn.sigmoid(gate_act)
    up_factor = gate_act * sigmoid_gate
    gate_factor = up_act * sigmoid_gate * (1.0 + gate_act * (1.0 - sigmoid_gate))
    hidden_grad = plus(hidden_near, swap(hidden_far, "dp", n_dp, 2))
    part = jnp.concatenate([hidden_grad * gate_factor, hidden_grad * up_factor], axis=2).astype(BF16)
    count = local_experts * 7 // 16
    far = [swap(piece, "dp", n_dp, 2) for piece in jnp.split(part, [count], axis=0)]
    beside = swap(part, "dp", n_dp, 1)
    *near_back, both_weights = back(0, lines, [part, beside], [gate_weight, up_weight], rows)
    far[0], _ = lax.optimization_barrier((far[0], near_back[0]))
    far_beside = [swap(far[0], "dp", n_dp, 1)]
    early = back(2, lines, [far[0], far_beside[0]], [both_weights], rows)
    far[1], _ = lax.optimization_barrier((far[1], early))
    far_beside.append(swap(far[1], "dp", n_dp, 1))
    far_back = back(2, lines, [far[1], far_beside[1]], [both_weights], rows, count, early)
    parts = [part, beside, jnp.concatenate(far, axis=0), jnp.concatenate(far_beside, axis=0)]
    own, other, own_beside, other_beside = near_back
    own_beside, other_beside = swap(own_beside, "dp", n_dp, 1), swap(other_beside, "dp", n_dp, 1)
    own_beside, other_beside = lax.optimization_barrier((own_beside, other_beside))
    arrived = swap(jnp.stack([other, other_beside]), "expert", n_x, 1)
    arrived, after_back, _ = lax.optimization_barrier((arrived, placed, far_back[0]))
    weight_grad = weight_grads(after_back, parts, 4)

    def to_keeper(value, low, turn, flip):
        pairs = []
        for i in range(n_dp):
            for j in range(n_x):
                for l in range(n_t):
                    odd = (i ^ l) & 1
                    to = ((i ^ low ^ odd ^ turn) * n_x + (j ^ flip)) * n_t + (l ^ odd)
                    pairs.append(((i * n_x + j) * n_t + l, to))
        return lax.ppermute(value, ("dp", "expert", "tensor"), pairs)

    merged = [plus(own, arrived[0]).astype(BF16), plus(own_beside, arrived[1]).astype(BF16)]
    keep, leaving = jnp.where(odd, merged[1], merged[0]), jnp.where(odd, merged[0], merged[1])
    first = plus(keep, swap(leaving, "tensor", n_t, 1))
    far_terms = [to_keeper(value, 2, at // 2, at % 2) for at, value in enumerate(far_back)]
    far_terms, _ = lax.optimization_barrier((far_terms, weight_grad))
    second = sum(value.astype(F32) for value in far_terms)
    keep = jnp.where(swapped, second, first)
    leaving = jnp.where(swapped, first, second).astype(BF16)
    grad_tokens = plus(keep, swap(leaving, "tensor", n_t, 2)).astype(BF16)

    grad_gate, grad_up = (jnp.swapaxes(grad, 1, 2) for grad in weight_grad)
    return grad_tokens, grad_gate, grad_up


def bits_of(count):
    bits = []
    bit = 1
    while bit < count:
        bits.append(bit)
        bit *= 2
    return bits


def halving_sum(parts, axis, count):
    parts = dict(parts)
    for bit in bits_of(count):
        leaving = sorted(r for r in parts if r & bit)
        arrived = swap(jnp.stack([parts[r].astype(BF16) for r in leaving]), axis, count, bit)
        for at, r in enumerate(leaving):
            parts[r ^ bit] = plus(parts[r ^ bit], arrived[at])
            del parts[r]
    return parts[0]


def doubling_gather(value, axis, count):
    held = {0: value}
    for bit in reversed(bits_of(count)):
        known = sorted(held)
        arrived = swap(jnp.stack([held[r] for r in known]), axis, count, bit)
        for at, r in enumerate(known):
            held[r ^ bit] = arrived[at]
    return [held[r] for r in range(count)]


def on_any_slice(tokens, cotangent, expert_ids, gate_weight, up_weight, down_weight):
    n_dp, n_x, n_t = lax.axis_size("dp"), lax.axis_size("expert"), lax.axis_size("tensor")
    k, x, t = lax.axis_index("dp"), lax.axis_index("expert"), lax.axis_index("tensor")
    local_experts, width, hidden = gate_weight.shape
    rows = tokens.shape[0]
    slots = n_x * CAP
    ids_row = expert_ids.reshape(1, rows)
    order = jnp.arange(rows, dtype=jnp.int32)
    earlier = (expert_ids == ids_row) & (order[:, None] < order[None, :])
    position = jnp.sum(earlier.astype(jnp.int32), axis=0)
    target = ids_row[0] * CAP + position
    targets = lax.all_gather(target, ("dp", "expert"), axis=0, tiled=False).reshape(n_dp, n_x, rows)
    pair = jnp.stack([tokens, cotangent])
    placers, slot_rows = [], []
    for rel in range(n_dp):
        columns = lax.dynamic_slice_in_dim(pair, (k ^ rel) * width, width, axis=2)
        mine = columns if rel == 0 else swap(columns, "dp", n_dp, rel)
        blocks = lax.all_gather(mine, "expert", axis=1, tiled=True)
        goal = lax.dynamic_index_in_dim(targets, k ^ rel, axis=0, keepdims=False)
        expert = goal // CAP - x * local_experts
        place = jnp.arange(n_x, dtype=jnp.int32)[:, None] * CAP + goal % CAP
        row = jnp.where((expert >= 0) & (expert < local_experts), expert * slots + place, -1)
        row = row.reshape(1, n_x * rows)
        every = jnp.arange(local_experts * slots, dtype=jnp.int32)[:, None]
        placer = (every == row).astype(BF16)
        placers.append(placer)
        slot_rows.append(
            jnp.einsum("sn,and->asd", placer, blocks, preferred_element_type=F32)
            .astype(BF16)
            .reshape(2, local_experts, slots, width)
        )
    slot_rows = jnp.concatenate(slot_rows, axis=2)
    inputs, grads_in = slot_rows[0], slot_rows[1]

    def act(values, weight):
        return jnp.einsum("esd,edf->esf", values, weight, preferred_element_type=F32).astype(BF16)

    acts = jnp.stack([act(inputs, gate_weight), act(inputs, up_weight), act(grads_in, down_weight)])
    acts = acts.reshape(3, local_experts, n_dp, slots, hidden)
    acts = halving_sum({r: acts[:, :, r] for r in range(n_dp)}, "dp", n_dp)
    grads = doubling_gather(jnp.stack(swiglu_grads(acts[0], acts[1], acts[2])), "dp", n_dp)
    grads = jnp.concatenate(grads, axis=2)
    gate_grad, up_grad = grads[0], grads[1]
    partial_value = jnp.einsum("esf,edf->esd", gate_grad, gate_weight, preferred_element_type=F32)
    partial_value = partial_value + jnp.einsum("esf,edf->esd", up_grad, up_weight, preferred_element_type=F32)
    partial_value = partial_value.astype(BF16).reshape(local_experts, n_dp, slots, width)
    per_token = []
    for rel in range(n_dp):
        flat = partial_value[:, rel].reshape(local_experts * slots, width)
        spread = lax.dot_general(placers[rel], flat, (((0,), (0,)), ((), ())), preferred_element_type=F32)
        spread = spread.astype(BF16).reshape(n_x, rows, width)
        per_token.append(lax.psum_scatter(spread, "expert", scatter_dimension=0, tiled=False))
    per_token = jnp.stack(per_token)
    terms = {r: lax.dynamic_index_in_dim(per_token, k ^ t ^ r, axis=0, keepdims=False) for r in range(n_t)}
    summed = halving_sum(terms, "tensor", n_t).astype(BF16)
    summed = lax.ppermute(
        summed, ("dp", "tensor"), [(i * n_t + j, j * n_t + i) for i in range(n_dp) for j in range(n_t)]
    )
    grad_gate = jnp.einsum("esd,esf->edf", inputs, gate_grad, preferred_element_type=F32).astype(BF16)
    grad_up = jnp.einsum("esd,esf->edf", inputs, up_grad, preferred_element_type=F32).astype(BF16)
    return summed, grad_gate, grad_up


def solution(mesh):
    placed = (
        P(("dp", "expert"), None),
        P(("dp", "expert"), None),
        P(("dp", "expert"), None),
        P("expert", "dp", "tensor"),
        P("expert", "dp", "tensor"),
        P("expert", "dp", "tensor"),
    )
    sizes = tuple(mesh.shape[name] for name in ("dp", "expert", "tensor"))

    def on_device(tokens, cotangent, expert_ids, *weights):
        experts = weights[0].shape[0] * sizes[1]
        small = sizes == (4, 2, 4) and experts * CAP <= 256
        return (on_small_slice if small else on_any_slice)(tokens, cotangent, expert_ids, *weights)

    return jax.shard_map(
        on_device,
        mesh=mesh,
        in_specs=placed,
        out_specs=(
            P(("dp", "expert"), "tensor"),
            P("expert", "dp", "tensor"),
            P("expert", "dp", "tensor"),
        ),
        check_vma=False,
    )
```
